32 devices in a mesh: energy: 16 (over z, y, x), mom: 2 (over core).
Axes of the slice: x: 2, y: 2, z: 4, core: 2. Of those that a mesh axis runs over, the one named last changes fastest.
Arguments:
- lesser_green: bfloat16 [4, 256, 32, 288], P('mom', 'energy'), may hold values from -6 to 6
- partner: int32 [32], replicated, may hold values from 0 to 31, each once
- phonon_green: bfloat16 [4, 32, 192], P(None, 'energy'), may hold values from -0.19921875 to 0.19921875
- coupling: bfloat16 [32, 432], P('energy'), may hold values from -1.75 to 1.75
Outputs:
- self_energy: bfloat16 [4, 256, 32, 288], P('mom', 'energy')
- phonon_self: float32 [4, 32, 192], P('mom', 'energy')
The draws below stay inside these ranges and needn't reach their ends.
Inputs may be any that keep to these rules, and one draw needn't show every extreme that they name: Every pair is the partner of exactly one pair.
All inputs are finite; a program needn't handle non-finite values.
Results may differ from the reference program's by a relative error of at most 0.0057.
Values may be sent and summed in bfloat16 or wider, within the bound.
No kernel may reach another device: no remote copies, remote signals or barrier semaphores. Data moves between devices by JAX's collectives and lax.ppermute only.
A program may use at most 128 MiB of HBM per device.

```python
import jax
import jax.numpy as jnp
from jax import lax

ORB = 12
BRANCH = 3
FREQ = 64
MOMENTA = 4
ENERGIES = 256
PAIRS = 32
COMP = 288


def levels(stream_key, dims, split, smallest, top_value):
    level, own = 1.0, jax.random.fold_in(stream_key, 6)
    for position, blocks in split:
        draws = jnp.exp(jax.random.uniform(jax.random.fold_in(own, position), (blocks,), jnp.float32, smallest / len(split), top_value / len(split)))
        level = level * jnp.repeat(draws, dims[position] // blocks).reshape([-1 if axis == position else 1 for axis in range(len(dims))])
    return level


def centred(key, dims, width, bound, pieces=(), kind=jnp.bfloat16):
    entries = jax.random.normal(key, dims, jnp.float32) * width
    if len(pieces) > 0:
        entries = levels(key, dims, pieces, -0.22, 0.18) * entries
    return jnp.clip(entries, min=-bound, max=bound).astype(kind)


def setup_inputs(seed: int = 0) -> dict:
    streams_of = jax.random.split(jax.random.key(seed), 5)
    lesser_green = centred(streams_of[0], (MOMENTA, ENERGIES, PAIRS, COMP), 1.0, 6.0, ((0, 2), (1, 16)))
    partner = jax.random.permutation(streams_of[1], PAIRS).astype(jnp.int32)
    phonon_green = centred(streams_of[2], (MOMENTA, PAIRS, BRANCH * FREQ), 0.03125, 0.19921875, ((1, 16),))
    coupling = centred(streams_of[3], (PAIRS, BRANCH * ORB * ORB), ORB ** -0.5, 1.75, ((0, 16),))
    return {"lesser_green": lesser_green, "partner": partner, "phonon_green": phonon_green, "coupling": coupling}


HIGHEST = lax.Precision.HIGHEST


def blocks_behind(values):
    leading = values.shape[0]
    trailing = values.shape[2:]
    padded = jnp.concatenate([jnp.zeros((leading, FREQ) + trailing, values.dtype), values], axis=1)
    stacked = padded.reshape((leading, values.shape[1] // FREQ + 1, FREQ) + trailing)
    return jnp.concatenate([stacked[:, :-1], stacked[:, 1:]], axis=2)


def blocks_ahead(values):
    leading = values.shape[0]
    trailing = values.shape[2:]
    padded = jnp.concatenate([values, jnp.zeros((leading, FREQ) + trailing, values.dtype)], axis=1)
    stacked = padded.reshape((leading, values.shape[1] // FREQ + 1, FREQ) + trailing)
    return jnp.concatenate([stacked[:, :-1], stacked[:, 1:]], axis=2)


def diagonals(matrix):
    leading = matrix.shape[:-2]
    band_width = matrix.shape[-2]
    flattened = matrix.reshape(leading + (2 * band_width * band_width,))
    flattened = jnp.concatenate([flattened, jnp.zeros(leading + (band_width,), flattened.dtype)], axis=-1)
    return flattened.reshape(leading + (band_width, 2 * band_width + 1))[..., :band_width].sum(axis=-2)


def reference(lesser_green, partner, phonon_green, coupling):
    square = ORB * ORB
    nblocks = ENERGIES // FREQ
    couple = coupling.astype(jnp.float32).reshape(PAIRS, BRANCH, ORB, ORB)
    phonon_table = phonon_green.astype(jnp.float32).reshape(MOMENTA, PAIRS, BRANCH, FREQ)
    lag_table = jnp.arange(FREQ)[:, None] + FREQ - jnp.arange(2 * FREQ)[None, :]
    picker = (lag_table[None] == jnp.arange(FREQ)[:, None, None]).astype(jnp.float32)
    toeplitz = jnp.einsum("qpiw,wrj->pqirj", phonon_table, picker, precision=HIGHEST)
    mom_index = jnp.arange(MOMENTA)
    back_lag = (mom_index[:, None] - mom_index[None, :]) % MOMENTA
    ahead_map = (mom_index[:, None] + mom_index[None, :]) % MOMENTA
    paired = jnp.take(lesser_green, partner, axis=2)

    def one_pair(inputs):
        own_slab, partner_slab, band_table, pair_couple = inputs
        sandwich = jnp.einsum("iac,ibd->iabcd", pair_couple, pair_couple, precision=HIGHEST)
        sandwich = sandwich.reshape(BRANCH, square, square).astype(jnp.bfloat16).astype(jnp.float32)
        kernel = band_table[back_lag]
        behind = blocks_behind(own_slab).astype(jnp.float32)
        sigma_sum = jnp.einsum("xyirj,ybjc->xbric", kernel, behind)
        sigma_sum = sigma_sum.astype(jnp.bfloat16).astype(jnp.float32)
        sigma_sum = sigma_sum.reshape(MOMENTA, ENERGIES, BRANCH, 2, square)
        sigma_out = jnp.einsum("irs,xeiks->xekr", sandwich, sigma_sum)
        sigma_out = sigma_out.reshape(MOMENTA, ENERGIES, COMP).astype(jnp.bfloat16)
        halves = own_slab.astype(jnp.float32).reshape(MOMENTA, ENERGIES, 2, square)
        applied = jnp.einsum("irs,yeks->yeikr", sandwich, halves).astype(jnp.bfloat16)
        applied = applied.reshape(MOMENTA, ENERGIES, BRANCH, COMP)
        partner_blocks = partner_slab.astype(jnp.float32).reshape(MOMENTA, nblocks, FREQ, COMP)
        correlated = jnp.einsum("xbrc,ybjic->ixyrj", partner_blocks, blocks_ahead(applied).astype(jnp.float32))
        diag = diagonals(correlated)
        picked = diag[:, mom_index[:, None], ahead_map]
        return sigma_out, picked.sum(axis=1)

    sigma_all, spectra = lax.map(one_pair, (jnp.moveaxis(lesser_green, 2, 0), jnp.moveaxis(paired, 2, 0), toeplitz, couple))
    self_energy = jnp.moveaxis(sigma_all, 0, 2)
    norming = (MOMENTA * ENERGIES * COMP) ** -0.5
    phonon_self = jnp.transpose(spectra, (2, 0, 1, 3)).reshape(MOMENTA, PAIRS, BRANCH * FREQ) * norming
    return self_energy, phonon_self
```

```python
import functools

import jax
import jax.numpy as jnp
import numpy as np
from jax import lax
from jax.experimental import pallas as pl
from jax.experimental.pallas import tpu as pltpu
from jax.sharding import PartitionSpec as P

ORB = 12
BRANCH = 3
FREQ = 64
COMP = 288
SQUARE = ORB * ORB
MAIN = 256
TAIL = COMP - MAIN
LANES = 128
SLOTS = LANES // TAIL
WIDE = MAIN + LANES
VMEM_LIMIT = 48 * 1024 * 1024

BF16 = jnp.bfloat16
F32 = jnp.float32


class Plan:
    def __init__(self, green, phonon, n_energy, n_mom):
        self.n_energy, self.n_mom = n_energy, n_mom
        self.mom_dev, self.steps, self.pairs, _ = green.shape
        self.momenta = self.mom_dev * n_mom
        self.pairs_dev = phonon.shape[1]
        self.group = -(-FREQ // self.steps)
        self.n_groups = n_energy // self.group
        self.peers = self.group * n_mom
        self.sub = self.pairs_dev // n_mom
        self.own = self.n_groups * self.sub
        self.block = self.group * self.pairs_dev
        self.main_rows = self.mom_dev * self.own * self.steps
        self.rows = self.main_rows + self.own // SLOTS * self.steps
        assert self.group * self.steps == FREQ and n_energy % self.group == 0
        assert self.pairs_dev % n_mom == 0 and self.own % SLOTS == 0
        assert self.mom_dev * LANES == MAIN and 16 % self.block == 0

    def main_row(self, k, u):
        return (k * self.own + u) * self.steps

    def tail_row(self, u):
        return self.main_rows + u // SLOTS * self.steps

    def place(self, p):
        z, rest = divmod(p, self.block)
        j, rest = divmod(rest, self.pairs_dev)
        m, b = divmod(rest, self.sub)
        return j * self.n_mom + m, z * self.sub + b


def dot(a, b):
    return lax.dot_general(a, b, (((1,), (0,)), ((), ())), preferred_element_type=F32)


def dot_nt(a, b):
    return lax.dot_general(a, b, (((1,), (1,)), ((), ())), preferred_element_type=F32)


def swap_matrix(outer, inner, flip=False):
    n = outer * inner
    row = lax.broadcasted_iota(jnp.int32, (n, n), 0)
    col = lax.broadcasted_iota(jnp.int32, (n, n), 1)
    shift = outer.bit_length() - 1
    place = row & (outer - 1)
    source = (outer - 1 - place if flip else place) * inner + (row >> shift)
    return (col == source).astype(F32).astype(BF16)


def pack_rows(plan, load, out_ref, flip=False):
    swap = swap_matrix(plan.steps, 16, flip)
    for k in range(plan.mom_dev):
        tails = {}
        for h in range(plan.pairs // 16):
            moved = dot(swap, load(k, h)).astype(BF16)
            for i in range(16):
                peer, u = plan.place(16 * h + i)
                piece = moved[i * plan.steps : (i + 1) * plan.steps]
                row = plan.main_row(k, u)
                out_ref[peer, row : row + plan.steps, :] = piece[:, :MAIN]
                tails[peer, u] = piece[:, MAIN:]
        for peer in range(plan.peers):
            for u in range(0, plan.own, SLOTS):
                row = plan.tail_row(u)
                joined = jnp.concatenate([tails[peer, u + s] for s in range(SLOTS)], axis=1)
                out_ref[peer, row : row + plan.steps, k * LANES : (k + 1) * LANES] = joined


def pack_own_kernel(plan, green_ref, out_ref):
    def load(k, h):
        return green_ref[k, :, 16 * h : 16 * h + 16, :].reshape(plan.steps * 16, COMP)

    pack_rows(plan, load, out_ref)


def pack_partner_kernel(plan, take_ref, green_ref, out_ref, taken):
    chunk = take_ref.shape[0] // plan.pairs
    take = take_ref[...]
    for k in range(plan.mom_dev):
        for e in range(0, plan.steps, chunk):
            rows = green_ref[k, e : e + chunk].reshape(chunk * plan.pairs, COMP)
            taken[k, e : e + chunk] = dot(take, rows).astype(BF16).reshape(chunk, plan.pairs, COMP)

    def load(k, h):
        return taken[k, :, 16 * h : 16 * h + 16, :].reshape(plan.steps * 16, COMP)

    pack_rows(plan, load, out_ref, flip=True)


def tail_tables():
    first = np.zeros((SLOTS, WIDE, 16), np.float32)
    second = np.zeros((SLOTS, WIDE, 16), np.float32)
    for slot in range(SLOTS):
        for c in range(COMP):
            place = c if c < MAIN else c + TAIL * slot
            first[slot, place, c % SQUARE // ORB] = 1
            second[slot, place, c % ORB] = 1
    return first.astype(BF16), second.astype(BF16)


def prep_kernel(plan, couple_ref, phonon_ref, first_ref, second_ref, sand_ref, toep_ref):
    couple = couple_ref[0].reshape(BRANCH * 16, 16)
    first, second = first_ref[0], second_ref[0]
    row = lax.broadcasted_iota(jnp.int32, (WIDE, WIDE), 0)
    col = lax.broadcasted_iota(jnp.int32, (WIDE, WIDE), 1)
    same_half = (row < SQUARE) == (col < SQUARE)
    left = dot_nt(couple, first).astype(BF16)
    right = dot_nt(couple, second).astype(BF16)
    for i in range(BRANCH):
        rows = slice(16 * i, 16 * i + 16)
        product = dot(first, left[rows]) * dot(second, right[rows])
        sand_ref[0, i] = jnp.where(same_half, product, 0.0).astype(BF16)
    mirror = (
        lax.broadcasted_iota(jnp.int32, (FREQ, 2 * FREQ), 0)
        + lax.broadcasted_iota(jnp.int32, (FREQ, 2 * FREQ), 1)
        == FREQ
    )
    lags = dot(phonon_ref[0], mirror.astype(F32).astype(BF16))
    for q in range(plan.momenta):
        for i in range(BRANCH):
            n = q * BRANCH + i
            band = jnp.broadcast_to(lags[n : n + 1], (FREQ, 2 * FREQ))
            band = pltpu.roll(band, 0, 1, stride=1, stride_axis=0)
            toep_ref[0, q, i * FREQ : (i + 1) * FREQ, :] = band.astype(BF16)


def gather_rows(plan, ref, u, y, flip=False):
    m, k = divmod(y, plan.mom_dev)
    row = pl.multiple_of(plan.main_row(k, u), plan.steps)
    tail = pl.multiple_of(plan.tail_row(u), plan.steps)
    pieces = []
    for j in reversed(range(plan.group)) if flip else range(plan.group):
        peer = j * plan.n_mom + m
        main = ref[peer, pl.ds(row, plan.steps), :]
        rest = ref[peer, pl.ds(tail, plan.steps), k * LANES : (k + 1) * LANES]
        pieces.append(jnp.concatenate([main, rest], axis=1))
    return jnp.concatenate(pieces, axis=0)


def self_kernel(plan, before_ref, own_ref, toep_ref, sand_ref, out_ref):
    u = pl.program_id(0)
    green = jnp.concatenate(
        [gather_rows(plan, ref, u, y) for y in range(plan.momenta) for ref in (before_ref, own_ref)], axis=0
    )
    total = None
    for i in range(BRANCH):
        band = jnp.concatenate(
            [
                jnp.concatenate(
                    [
                        toep_ref[0, (k - y) % plan.momenta, i * FREQ : (i + 1) * FREQ, :]
                        for y in range(plan.momenta)
                    ],
                    axis=1,
                )
                for k in range(plan.momenta)
            ],
            axis=0,
        )
        summed = dot(band, green).astype(BF16)
        term = dot_nt(summed, sand_ref[0, i])
        total = term if total is None else total + term
    total = total.astype(BF16)
    tail = pl.multiple_of(plan.tail_row(u), plan.steps)

    @pl.when(u % SLOTS == 0)
    def _():
        for peer in range(plan.peers):
            out_ref[peer, pl.ds(tail, plan.steps), :] = jnp.zeros((plan.steps, MAIN), BF16)

    for y in range(plan.momenta):
        m, k = divmod(y, plan.mom_dev)
        row = pl.multiple_of(plan.main_row(k, u), plan.steps)
        for j in range(plan.group):
            peer = j * plan.n_mom + m
            start = y * FREQ + j * plan.steps
            piece = total[start : start + plan.steps]
            out_ref[peer, pl.ds(row, plan.steps), :] = piece[:, :MAIN]
            out_ref[peer, pl.ds(tail, plan.steps), k * LANES : (k + 1) * LANES] += piece[:, MAIN:]


def phonon_kernel(plan, scale, partner_ref, own_ref, after_ref, sand_ref, out_ref):
    u = pl.program_id(0)
    partner = jnp.concatenate([gather_rows(plan, partner_ref, u, k, flip=True) for k in range(plan.momenta)], axis=0)
    green = jnp.concatenate(
        [gather_rows(plan, ref, u, y) for y in range(plan.momenta) for ref in (own_ref, after_ref)], axis=0
    )
    for i in range(BRANCH):
        applied = dot(partner, sand_ref[0, i]).astype(BF16)
        lagged = dot_nt(applied, green)
        for q in range(plan.momenta):
            acc = None
            for k in range(plan.momenta):
                y = (k + q) % plan.momenta
                part = lagged[k * FREQ : (k + 1) * FREQ, y * 2 * FREQ : (y + 1) * 2 * FREQ]
                acc = part if acc is None else acc + part
            acc = pltpu.roll(acc, FREQ + 1, 1, stride=1, stride_axis=0)
            n = q * BRANCH + i
            out_ref[0, n : n + 1, :] = jnp.sum(acc, axis=0, keepdims=True) * scale


def unpack_kernel(plan, wire_ref, out_ref):
    swap = swap_matrix(16, plan.steps)
    lane = lax.broadcasted_iota(jnp.int32, (plan.steps, LANES), 1)
    for k in range(plan.mom_dev):
        for h in range(plan.pairs // 16):
            mains, tails = [], []
            for i in range(16):
                peer, u = plan.place(16 * h + i)
                row, tail = plan.main_row(k, u), plan.tail_row(u)
                mains.append(wire_ref[peer, row : row + plan.steps, :])
                rest = wire_ref[peer, tail : tail + plan.steps, k * LANES : (k + 1) * LANES]
                slot = u % SLOTS
                tails.append(rest[:, slot * TAIL : (slot + 1) * TAIL])
            rows = jnp.concatenate([jnp.concatenate(mains, axis=0), jnp.concatenate(tails, axis=0)], axis=1)
            moved = dot(swap, rows).astype(BF16)
            out_ref[k, :, 16 * h : 16 * h + 16, :] = moved.reshape(plan.steps, 16, COMP)


def call(kernel, out_shape, *args, grid=None, in_specs=None, out_specs=None, scratch=(), flops=0):
    moved = sum(a.size * a.dtype.itemsize for a in jax.tree.leaves((args, out_shape)))
    whole = pl.BlockSpec(memory_space=pltpu.VMEM)
    return pl.pallas_call(
        kernel,
        out_shape=out_shape,
        grid=grid or (),
        in_specs=in_specs or [whole] * len(args),
        out_specs=out_specs if out_specs is not None else whole,
        scratch_shapes=list(scratch),
        compiler_params=pltpu.CompilerParams(vmem_limit_bytes=VMEM_LIMIT),
        cost_estimate=pl.CostEstimate(flops=flops, bytes_accessed=moved, transcendentals=0),
    )(*args)


def shape(dims, dtype):
    return jax.ShapeDtypeStruct(dims, dtype)


def shards(lesser_green, partner, phonon_green, coupling):
    n_energy, n_mom = lax.axis_size("energy"), lax.axis_size("mom")
    plan = Plan(lesser_green, phonon_green, n_energy, n_mom)
    axes = ("energy", "mom")
    me = lax.axis_index("mom")
    wire = shape((plan.peers, plan.rows, MAIN), BF16)
    planes = [[s * plan.peers + i for i in range(plan.peers)] for s in range(plan.n_groups)]
    columns = [[s * plan.group + j for s in range(plan.n_groups)] for j in range(plan.group)]

    def exchange(blocks):
        return lax.all_to_all(blocks, axes, split_axis=0, concat_axis=0, axis_index_groups=planes, tiled=True)

    def shifted(blocks, distance):
        route = [(e, e + distance) for e in range(n_energy) if 0 <= e + distance < n_energy]
        return lax.ppermute(blocks, "energy", route)

    own = exchange(call(functools.partial(pack_own_kernel, plan), wire, lesser_green))
    before = shifted(own, plan.group)
    after = shifted(own, -plan.group)

    chunk = max(1, 256 // plan.pairs)
    source = (jnp.arange(chunk)[:, None] * plan.pairs + partner[None, :]).reshape(-1)
    take = (source[:, None] == jnp.arange(chunk * plan.pairs)[None, :]).astype(BF16)
    partner_blocks = exchange(
        call(
            functools.partial(pack_partner_kernel, plan),
            wire,
            take,
            lesser_green,
            scratch=[pltpu.VMEM(lesser_green.shape, BF16)],
        )
    )

    couple = coupling.reshape(plan.pairs_dev, BRANCH, ORB, ORB)
    couple = jnp.pad(couple, ((0, 0), (0, 0), (0, 16 - ORB), (0, 16 - ORB)))
    phonon = phonon_green.reshape(plan.momenta, plan.pairs_dev, BRANCH, FREQ)
    phonon = jnp.moveaxis(phonon, 1, 0).reshape(plan.pairs_dev, plan.momenta * BRANCH, FREQ)
    lag_rows = -(-plan.momenta * BRANCH // 16) * 16
    phonon = jnp.pad(phonon, ((0, 0), (0, lag_rows - plan.momenta * BRANCH), (0, 0)))

    def of_pairs(values):
        every = lax.all_gather(values, "energy", axis_index_groups=columns)
        mine = lax.dynamic_slice_in_dim(every, me * plan.sub, plan.sub, axis=1)
        return mine.reshape((plan.own,) + values.shape[1:])

    first, second = tail_tables()
    sand, toep = call(
        functools.partial(prep_kernel, plan),
        [
            shape((plan.own, BRANCH, WIDE, WIDE), BF16),
            shape((plan.own, plan.momenta, BRANCH * FREQ, 2 * FREQ), BF16),
        ],
        of_pairs(couple),
        of_pairs(phonon),
        jnp.asarray(first),
        jnp.asarray(second),
        grid=(plan.own,),
        in_specs=[
            pl.BlockSpec((1, BRANCH, 16, 16), lambda u: (u, 0, 0, 0)),
            pl.BlockSpec((1, lag_rows, FREQ), lambda u: (u, 0, 0)),
            pl.BlockSpec((1, WIDE, 16), lambda u: (u % SLOTS, 0, 0)),
            pl.BlockSpec((1, WIDE, 16), lambda u: (u % SLOTS, 0, 0)),
        ],
        out_specs=[
            pl.BlockSpec((1, BRANCH, WIDE, WIDE), lambda u: (u, 0, 0, 0)),
            pl.BlockSpec((1, plan.momenta, BRANCH * FREQ, 2 * FREQ), lambda u: (u, 0, 0, 0)),
        ],
    )

    whole = pl.BlockSpec(wire.shape, lambda u: (0, 0, 0))
    sand_spec = pl.BlockSpec((1, BRANCH, WIDE, WIDE), lambda u: (u, 0, 0, 0))
    toep_spec = pl.BlockSpec((1, plan.momenta, BRANCH * FREQ, 2 * FREQ), lambda u: (u, 0, 0, 0))
    sigma = call(
        functools.partial(self_kernel, plan),
        wire,
        before,
        own,
        toep,
        sand,
        grid=(plan.own,),
        in_specs=[whole, whole, toep_spec, sand_spec],
        out_specs=whole,
    )
    arrived = exchange(sigma)

    energies = n_energy * plan.steps
    scale = (plan.momenta * energies * COMP) ** -0.5
    lag_count = plan.momenta * BRANCH
    spectra = call(
        functools.partial(phonon_kernel, plan, scale),
        shape((plan.own, lag_count, 2 * FREQ), F32),
        partner_blocks,
        own,
        after,
        sand,
        grid=(plan.own,),
        in_specs=[whole, whole, whole, sand_spec],
        out_specs=pl.BlockSpec((1, lag_count, 2 * FREQ), lambda u: (u, 0, 0)),
    )
    spectra = spectra[..., :FREQ].reshape(plan.n_groups, 1, plan.sub, n_mom, plan.mom_dev, BRANCH * FREQ)
    mine = (jnp.arange(n_mom) == me)[None, :, None, None, None, None]
    spectra = jnp.where(mine, spectra, 0.0)
    spectra = jnp.transpose(spectra, (0, 3, 4, 1, 2, 5))
    spectra = spectra.reshape(plan.n_groups * n_mom, plan.mom_dev, plan.pairs_dev, BRANCH * FREQ)
    members = [[e * n_mom + m for e in column for m in range(n_mom)] for column in columns]
    phonon_self = lax.psum_scatter(spectra, axes, scatter_dimension=0, axis_index_groups=members)

    self_energy = call(
        functools.partial(unpack_kernel, plan), shape(lesser_green.shape, BF16), arrived
    )
    return self_energy, phonon_self


def solution(mesh):
    in_specs = (P("mom", "energy", None, None), P(), P(None, "energy", None), P("energy", None))
    out_specs = (P("mom", "energy", None, None), P("mom", "energy", None))
    return jax.shard_map(shards, mesh=mesh, in_specs=in_specs, out_specs=out_specs, check_vma=False)
```

```python
import functools

import jax
import jax.numpy as jnp
import numpy as np
from jax import lax
from jax.experimental import pallas as pl
from jax.experimental.pallas import tpu as pltpu
from jax.sharding import PartitionSpec as P

ORB = 12
BRANCH = 3
FREQ = 64
COMP = 288
SQUARE = ORB * ORB
MAIN = 256
TAIL = COMP - MAIN
LANES = 128
SLOTS = LANES // TAIL
WIDE = MAIN + LANES
VMEM_LIMIT = 48 * 1024 * 1024

BF16 = jnp.bfloat16
F32 = jnp.float32


class Plan:
    def __init__(self, green, phonon, n_energy, n_mom):
        self.n_energy, self.n_mom = n_energy, n_mom
        self.mom_dev, self.steps, self.pairs, _ = green.shape
        self.momenta = self.mom_dev * n_mom
        self.pairs_dev = phonon.shape[1]
        self.group = -(-FREQ // self.steps)
        self.n_groups = n_energy // self.group
        self.peers = self.group * n_mom
        self.sub = self.pairs_dev // n_mom
        self.own = self.n_groups * self.sub
        self.block = self.group * self.pairs_dev
        self.main_rows = self.mom_dev * self.own * self.steps
        self.rows = self.main_rows + self.own // SLOTS * self.steps
        assert self.group * self.steps == FREQ and n_energy % self.group == 0
        assert self.pairs_dev % n_mom == 0 and self.own % SLOTS == 0
        assert self.mom_dev * LANES == MAIN and 16 % self.block == 0

    def main_row(self, k, u):
        return (k * self.own + u) * self.steps

    def tail_row(self, u):
        return self.main_rows + u // SLOTS * self.steps

    def place(self, p):
        z, rest = divmod(p, self.block)
        j, rest = divmod(rest, self.pairs_dev)
        m, b = divmod(rest, self.sub)
        return j * self.n_mom + m, z * self.sub + b


def dot(a, b):
    return lax.dot_general(a, b, (((1,), (0,)), ((), ())), preferred_element_type=F32)


def dot_nt(a, b):
    return lax.dot_general(a, b, (((1,), (1,)), ((), ())), preferred_element_type=F32)


def swap_matrix(outer, inner, flip=False):
    n = outer * inner
    row = lax.broadcasted_iota(jnp.int32, (n, n), 0)
    col = lax.broadcasted_iota(jnp.int32, (n, n), 1)
    shift = outer.bit_length() - 1
    place = row & (outer - 1)
    source = (outer - 1 - place if flip else place) * inner + (row >> shift)
    return (col == source).astype(F32).astype(BF16)


def pack_rows(plan, load, out_ref, flip=False):
    swap = swap_matrix(plan.steps, 16, flip)
    for k in range(plan.mom_dev):
        tails = {}
        for h in range(plan.pairs // 16):
            moved = dot(swap, load(k, h)).astype(BF16)
            for i in range(16):
                peer, u = plan.place(16 * h + i)
                piece = moved[i * plan.steps : (i + 1) * plan.steps]
                row = plan.main_row(k, u)
                out_ref[peer, row : row + plan.steps, :] = piece[:, :MAIN]
                tails[peer, u] = piece[:, MAIN:]
        for peer in range(plan.peers):
            for u in range(0, plan.own, SLOTS):
                row = plan.tail_row(u)
                joined = jnp.concatenate([tails[peer, u + s] for s in range(SLOTS)], axis=1)
                out_ref[peer, row : row + plan.steps, k * LANES : (k + 1) * LANES] = joined


def pack_own_kernel(plan, green_ref, out_ref):
    def load(k, h):
        return green_ref[k, :, 16 * h : 16 * h + 16, :].reshape(plan.steps * 16, COMP)

    pack_rows(plan, load, out_ref)


def pack_partner_kernel(plan, take_ref, green_ref, out_ref, taken):
    chunk = take_ref.shape[0] // plan.pairs
    take = take_ref[...]
    for k in range(plan.mom_dev):
        for e in range(0, plan.steps, chunk):
            rows = green_ref[k, e : e + chunk].reshape(chunk * plan.pairs, COMP)
            taken[k, e : e + chunk] = dot(take, rows).astype(BF16).reshape(chunk, plan.pairs, COMP)

    def load(k, h):
        return taken[k, :, 16 * h : 16 * h + 16, :].reshape(plan.steps * 16, COMP)

    pack_rows(plan, load, out_ref, flip=True)


def tail_tables():
    first = np.zeros((SLOTS, WIDE, 16), np.float32)
    second = np.zeros((SLOTS, WIDE, 16), np.float32)
    for slot in range(SLOTS):
        for c in range(COMP):
            place = c if c < MAIN else c + TAIL * slot
            first[slot, place, c % SQUARE // ORB] = 1
            second[slot, place, c % ORB] = 1
    return first.astype(BF16), second.astype(BF16)


def prep_kernel(plan, tables_ref, first_ref, second_ref, sand_ref, toep_ref):
    couple = tables_ref[0, : BRANCH * 16, :16]
    first, second = first_ref[0], second_ref[0]
    row = lax.broadcasted_iota(jnp.int32, (WIDE, WIDE), 0)
    col = lax.broadcasted_iota(jnp.int32, (WIDE, WIDE), 1)
    same_half = (row < SQUARE) == (col < SQUARE)
    left = dot_nt(couple, first).astype(BF16)
    right = dot_nt(couple, second).astype(BF16)
    for i in range(BRANCH):
        rows = slice(16 * i, 16 * i + 16)
        product = dot(first, left[rows]) * dot(second, right[rows])
        sand_ref[0, i] = jnp.where(same_half, product, 0.0).astype(BF16)
    mirror = (
        lax.broadcasted_iota(jnp.int32, (FREQ, 2 * FREQ), 0)
        + lax.broadcasted_iota(jnp.int32, (FREQ, 2 * FREQ), 1)
        == FREQ
    )
    lags = dot(tables_ref[0, BRANCH * 16 :, :], mirror.astype(F32).astype(BF16))
    for q in range(plan.momenta):
        for i in range(BRANCH):
            n = q * BRANCH + i
            band = jnp.broadcast_to(lags[n : n + 1], (FREQ, 2 * FREQ))
            band = pltpu.roll(band, 0, 1, stride=1, stride_axis=0)
            toep_ref[0, q, i * FREQ : (i + 1) * FREQ, :] = band.astype(BF16)


def gather_rows(plan, ref, u, y, flip=False):
    m, k = divmod(y, plan.mom_dev)
    row = pl.multiple_of(plan.main_row(k, u), plan.steps)
    tail = pl.multiple_of(plan.tail_row(u), plan.steps)
    pieces = []
    for j in reversed(range(plan.group)) if flip else range(plan.group):
        peer = j * plan.n_mom + m
        main = ref[peer, pl.ds(row, plan.steps), :]
        rest = ref[peer, pl.ds(tail, plan.steps), k * LANES : (k + 1) * LANES]
        pieces.append(jnp.concatenate([main, rest], axis=1))
    return jnp.concatenate(pieces, axis=0)


def self_kernel(plan, before_ref, own_ref, toep_ref, sand_ref, out_ref):
    u = pl.program_id(0)
    green = jnp.concatenate(
        [gather_rows(plan, ref, u, y) for y in range(plan.momenta) for ref in (before_ref, own_ref)], axis=0
    )
    total = None
    for i in range(BRANCH):
        band = jnp.concatenate(
            [
                jnp.concatenate(
                    [
                        toep_ref[0, (k - y) % plan.momenta, i * FREQ : (i + 1) * FREQ, :]
                        for y in range(plan.momenta)
                    ],
                    axis=1,
                )
                for k in range(plan.momenta)
            ],
            axis=0,
        )
        summed = dot(band, green).astype(BF16)
        term = dot_nt(summed, sand_ref[0, i])
        total = term if total is None else total + term
    total = total.astype(BF16)
    tail = pl.multiple_of(plan.tail_row(u), plan.steps)

    @pl.when(u % SLOTS == 0)
    def _():
        for peer in range(plan.peers):
            out_ref[peer, pl.ds(tail, plan.steps), :] = jnp.zeros((plan.steps, MAIN), BF16)

    for y in range(plan.momenta):
        m, k = divmod(y, plan.mom_dev)
        row = pl.multiple_of(plan.main_row(k, u), plan.steps)
        for j in range(plan.group):
            peer = j * plan.n_mom + m
            start = y * FREQ + j * plan.steps
            piece = total[start : start + plan.steps]
            out_ref[peer, pl.ds(row, plan.steps), :] = piece[:, :MAIN]
            out_ref[peer, pl.ds(tail, plan.steps), k * LANES : (k + 1) * LANES] += piece[:, MAIN:]


def phonon_kernel(plan, scale, partner_ref, own_ref, after_ref, sand_ref, out_ref):
    u = pl.program_id(0)
    partner = jnp.concatenate([gather_rows(plan, partner_ref, u, k, flip=True) for k in range(plan.momenta)], axis=0)
    green = jnp.concatenate(
        [gather_rows(plan, ref, u, y) for y in range(plan.momenta) for ref in (own_ref, after_ref)], axis=0
    )
    for i in range(BRANCH):
        applied = dot(partner, sand_ref[0, i]).astype(BF16)
        lagged = dot_nt(applied, green)
        for q in range(plan.momenta):
            acc = None
            for k in range(plan.momenta):
                y = (k + q) % plan.momenta
                part = lagged[k * FREQ : (k + 1) * FREQ, y * 2 * FREQ : (y + 1) * 2 * FREQ]
                acc = part if acc is None else acc + part
            acc = pltpu.roll(acc, FREQ + 1, 1, stride=1, stride_axis=0)
            n = q * BRANCH + i
            out_ref[0, n : n + 1, :] = jnp.sum(acc, axis=0, keepdims=True) * scale


def unpack_kernel(plan, wire_ref, out_ref):
    swap = swap_matrix(16, plan.steps)
    lane = lax.broadcasted_iota(jnp.int32, (plan.steps, LANES), 1)
    for k in range(plan.mom_dev):
        for h in range(plan.pairs // 16):
            mains, tails = [], []
            for i in range(16):
                peer, u = plan.place(16 * h + i)
                row, tail = plan.main_row(k, u), plan.tail_row(u)
                mains.append(wire_ref[peer, row : row + plan.steps, :])
                rest = wire_ref[peer, tail : tail + plan.steps, k * LANES : (k + 1) * LANES]
                slot = u % SLOTS
                tails.append(rest[:, slot * TAIL : (slot + 1) * TAIL])
            rows = jnp.concatenate([jnp.concatenate(mains, axis=0), jnp.concatenate(tails, axis=0)], axis=1)
            moved = dot(swap, rows).astype(BF16)
            out_ref[k, :, 16 * h : 16 * h + 16, :] = moved.reshape(plan.steps, 16, COMP)


def call(kernel, out_shape, *args, grid=None, in_specs=None, out_specs=None, scratch=(), flops=0):
    moved = sum(a.size * a.dtype.itemsize for a in jax.tree.leaves((args, out_shape)))
    whole = pl.BlockSpec(memory_space=pltpu.VMEM)
    return pl.pallas_call(
        kernel,
        out_shape=out_shape,
        grid=grid or (),
        in_specs=in_specs or [whole] * len(args),
        out_specs=out_specs if out_specs is not None else whole,
        scratch_shapes=list(scratch),
        compiler_params=pltpu.CompilerParams(vmem_limit_bytes=VMEM_LIMIT),
        cost_estimate=pl.CostEstimate(flops=flops, bytes_accessed=moved, transcendentals=0),
    )(*args)


def shape(dims, dtype):
    return jax.ShapeDtypeStruct(dims, dtype)


def shards(lesser_green, partner, phonon_green, coupling):
    n_energy, n_mom = lax.axis_size("energy"), lax.axis_size("mom")
    plan = Plan(lesser_green, phonon_green, n_energy, n_mom)
    axes = ("energy", "mom")
    me = lax.axis_index("mom")
    wire = shape((plan.peers, plan.rows, MAIN), BF16)
    planes = [[s * plan.peers + i for i in range(plan.peers)] for s in range(plan.n_groups)]
    columns = [[s * plan.group + j for s in range(plan.n_groups)] for j in range(plan.group)]

    def exchange(blocks):
        return lax.all_to_all(blocks, axes, split_axis=0, concat_axis=0, axis_index_groups=planes, tiled=True)

    group_of = lax.axis_index("energy") // plan.group
    place = lax.axis_index("energy") % plan.group

    def swapped(blocks, shift):
        route = []
        for e in range(n_energy):
            s, j = divmod(e, plan.group)
            other = ((s - shift) ^ 1) + shift
            route.append((e, other * plan.group + j if 0 <= other < plan.n_groups else e))
        return lax.ppermute(blocks, "energy", route)

    own = exchange(call(functools.partial(pack_own_kernel, plan), wire, lesser_green))
    even, odd = swapped(own, 0), swapped(own, 1)
    before = jnp.where(group_of % 2 == 1, even, jnp.where(group_of == 0, 0, odd))
    after = jnp.where(group_of % 2 == 0, even, jnp.where(group_of == plan.n_groups - 1, 0, odd))

    chunk = max(1, 256 // plan.pairs)
    source = (jnp.arange(chunk)[:, None] * plan.pairs + partner[None, :]).reshape(-1)
    take = (source[:, None] == jnp.arange(chunk * plan.pairs)[None, :]).astype(BF16)
    partner_blocks = exchange(
        call(
            functools.partial(pack_partner_kernel, plan),
            wire,
            take,
            lesser_green,
            scratch=[pltpu.VMEM(lesser_green.shape, BF16)],
        )
    )

    couple = coupling.reshape(plan.pairs_dev, BRANCH, ORB, ORB)
    couple = jnp.pad(couple, ((0, 0), (0, 0), (0, 16 - ORB), (0, 16 - ORB)))
    phonon = phonon_green.reshape(plan.momenta, plan.pairs_dev, BRANCH, FREQ)
    phonon = jnp.moveaxis(phonon, 1, 0).reshape(plan.pairs_dev, plan.momenta * BRANCH, FREQ)
    lag_rows = -(-plan.momenta * BRANCH // 16) * 16
    phonon = jnp.pad(phonon, ((0, 0), (0, lag_rows - plan.momenta * BRANCH), (0, 0)))

    couple = jnp.pad(couple, ((0, 0), (0, 0), (0, 0), (0, FREQ - 16)))
    tables = jnp.concatenate([couple.reshape(plan.pairs_dev, BRANCH * 16, FREQ), phonon], axis=1)
    tables = lax.dynamic_slice_in_dim(tables, me * plan.sub, plan.sub, axis=0)
    tables = lax.all_gather(tables, "energy")
    tables = tables.reshape((plan.n_groups, plan.group) + tables.shape[1:])
    tables = lax.dynamic_index_in_dim(tables, place, axis=1, keepdims=False)
    tables = tables.reshape((plan.own,) + tables.shape[2:])

    first, second = tail_tables()
    sand, toep = call(
        functools.partial(prep_kernel, plan),
        [
            shape((plan.own, BRANCH, WIDE, WIDE), BF16),
            shape((plan.own, plan.momenta, BRANCH * FREQ, 2 * FREQ), BF16),
        ],
        tables,
        jnp.asarray(first),
        jnp.asarray(second),
        grid=(plan.own,),
        in_specs=[
            pl.BlockSpec((1, BRANCH * 16 + lag_rows, FREQ), lambda u: (u, 0, 0)),
            pl.BlockSpec((1, WIDE, 16), lambda u: (u % SLOTS, 0, 0)),
            pl.BlockSpec((1, WIDE, 16), lambda u: (u % SLOTS, 0, 0)),
        ],
        out_specs=[
            pl.BlockSpec((1, BRANCH, WIDE, WIDE), lambda u: (u, 0, 0, 0)),
            pl.BlockSpec((1, plan.momenta, BRANCH * FREQ, 2 * FREQ), lambda u: (u, 0, 0, 0)),
        ],
    )

    whole = pl.BlockSpec(wire.shape, lambda u: (0, 0, 0))
    sand_spec = pl.BlockSpec((1, BRANCH, WIDE, WIDE), lambda u: (u, 0, 0, 0))
    toep_spec = pl.BlockSpec((1, plan.momenta, BRANCH * FREQ, 2 * FREQ), lambda u: (u, 0, 0, 0))
    sigma = call(
        functools.partial(self_kernel, plan),
        wire,
        before,
        own,
        toep,
        sand,
        grid=(plan.own,),
        in_specs=[whole, whole, toep_spec, sand_spec],
        out_specs=whole,
    )
    arrived = exchange(sigma)

    energies = n_energy * plan.steps
    scale = (plan.momenta * energies * COMP) ** -0.5
    lag_count = plan.momenta * BRANCH
    spectra = call(
        functools.partial(phonon_kernel, plan, scale),
        shape((plan.own, lag_count, 2 * FREQ), F32),
        partner_blocks,
        own,
        after,
        sand,
        grid=(plan.own,),
        in_specs=[whole, whole, whole, sand_spec],
        out_specs=pl.BlockSpec((1, lag_count, 2 * FREQ), lambda u: (u, 0, 0)),
    )
    spectra = spectra[..., :FREQ].reshape(plan.n_groups, plan.sub, n_mom, plan.mom_dev, BRANCH * FREQ)
    spectra = jnp.transpose(spectra, (0, 2, 3, 1, 4))
    spectra = spectra.reshape((plan.n_groups * n_mom, plan.mom_dev, plan.sub, BRANCH * FREQ))
    seat = group_of * n_mom + me
    sums = [None] * n_mom
    for distance in range(plan.n_groups * n_mom):
        part = lax.dynamic_index_in_dim(spectra, seat ^ distance, axis=0, keepdims=False)
        if distance:
            route = []
            for e in range(n_energy):
                for m in range(n_mom):
                    s, j = divmod(e, plan.group)
                    s, t = divmod((s * n_mom + m) ^ distance, n_mom)
                    route.append((e * n_mom + m, (s * plan.group + j) * n_mom + t))
            part = lax.ppermute(part, axes, route)
        which = distance % n_mom
        sums[which] = part if sums[which] is None else sums[which] + part
    phonon_self = lax.dynamic_update_slice_in_dim(
        jnp.zeros((plan.mom_dev, plan.pairs_dev, BRANCH * FREQ), F32), sums[0], me * plan.sub, axis=1
    )
    for d in range(1, n_mom):
        phonon_self = lax.dynamic_update_slice_in_dim(phonon_self, sums[d], (me ^ d) * plan.sub, axis=1)

    self_energy = call(
        functools.partial(unpack_kernel, plan), shape(lesser_green.shape, BF16), arrived
    )
    return self_energy, phonon_self


def solution(mesh):
    in_specs = (P("mom", "energy", None, None), P(), P(None, "energy", None), P("energy", None))
    out_specs = (P("mom", "energy", None, None), P("mom", "energy", None))
    return jax.shard_map(shards, mesh=mesh, in_specs=in_specs, out_specs=out_specs, check_vma=False)
```

```python
import functools

import jax
import jax.numpy as jnp
from jax import lax
from jax.experimental import pallas as pl
from jax.experimental.pallas import tpu as pltpu
from jax.sharding import PartitionSpec as P

ORB = 12
BRANCH = 3
FREQ = 64
COMP = 288
SQUARE = ORB * ORB
LANES = 128
MAIN = 256
TAIL = COMP - MAIN
SLOTS = LANES // TAIL
WIDE = MAIN + LANES
TILE = 16
VMEM_LIMIT = 56 * 1024 * 1024

BF16 = jnp.bfloat16
F32 = jnp.float32
I32 = jnp.int32


class Plan:
    def __init__(self, green, phonon, n_energy, n_mom):
        self.n_energy, self.n_mom = n_energy, n_mom
        self.mom_dev, self.steps, self.pairs, _ = green.shape
        self.momenta = self.mom_dev * n_mom
        self.pairs_dev = phonon.shape[1]
        self.half = FREQ // self.steps
        self.group = 2 * self.half
        self.n_groups = n_energy // self.group
        self.peers = self.group * n_mom
        self.sub = self.pairs_dev // n_mom
        self.own = self.n_groups * self.sub
        self.main_rows = self.mom_dev * self.own * 2 * self.steps
        self.rows = self.main_rows + self.mom_dev * self.own // SLOTS * self.steps
        assert self.half * self.steps == FREQ and n_energy % self.group == 0
        assert self.pairs_dev % n_mom == 0 and self.group * self.pairs_dev == TILE
        assert self.mom_dev * self.own % SLOTS == 0 and self.n_groups % 2 == 0

    def main_row(self, k, u):
        return (k * self.own + u) * 2 * self.steps

    def tail_row(self, k, u):
        return self.main_rows + (k * self.own + u) // SLOTS * self.steps

    def shift(self, k):
        return k * self.own % SLOTS * TAIL

    def place(self, h, i):
        j, rest = divmod(i, self.pairs_dev)
        m, b = divmod(rest, self.sub)
        return j * self.n_mom + m, h * self.sub + b


def dot(a, b):
    return lax.dot_general(a, b, (((1,), (0,)), ((), ())), preferred_element_type=F32)


def dot_nt(a, b):
    return lax.dot_general(a, b, (((1,), (1,)), ((), ())), preferred_element_type=F32)


def iota(dims, axis):
    return lax.broadcasted_iota(I32, dims, axis)


def swap_matrix(outer, inner, flip=False):
    n = outer * inner
    row, col = iota((n, n), 0), iota((n, n), 1)
    place = row & (outer - 1)
    source = (outer - 1 - place if flip else place) * inner + (row >> (outer.bit_length() - 1))
    return (col == source).astype(F32).astype(BF16)


def pack_rows(plan, load, out_ref, flip=False):
    swap = swap_matrix(plan.steps, TILE, flip)
    tails = {}
    for k in range(plan.mom_dev):
        for h in range(plan.pairs // TILE):
            moved = dot(swap, load(k, h)).astype(BF16)
            for i in range(TILE):
                peer, u = plan.place(h, i)
                piece = moved[i * plan.steps : (i + 1) * plan.steps]
                row = plan.main_row(k, u)
                out_ref[peer, row : row + plan.steps, :] = piece[:, :LANES]
                out_ref[peer, row + plan.steps : row + 2 * plan.steps, :] = piece[:, LANES:MAIN]
                tails[peer, k * plan.own + u] = piece[:, MAIN:]
    for peer in range(plan.peers):
        for first in range(0, plan.mom_dev * plan.own, SLOTS):
            row = plan.main_rows + first // SLOTS * plan.steps
            joined = jnp.concatenate([tails[peer, first + s] for s in range(SLOTS)], axis=1)
            out_ref[peer, row : row + plan.steps, :] = joined


def pack_own_kernel(plan, green_ref, out_ref, tiles, sems):
    copies = {}
    for k in range(plan.mom_dev):
        for h in range(plan.pairs // TILE):
            copies[k, h] = pltpu.make_async_copy(
                green_ref.at[k, :, TILE * h : TILE * (h + 1), :], tiles.at[k, h], sems.at[k, h]
            )
            copies[k, h].start()

    def load(k, h):
        copies[k, h].wait()
        return tiles[k, h].reshape(plan.steps * TILE, COMP)

    pack_rows(plan, load, out_ref)


def pack_partner_kernel(plan, take_ref, green_ref, out_ref, taken):
    chunk = take_ref.shape[0] // plan.pairs
    take = take_ref[...]
    for k in range(plan.mom_dev):
        for e in range(0, plan.steps, chunk):
            rows = green_ref[k, e : e + chunk].reshape(chunk * plan.pairs, COMP)
            taken[k, e : e + chunk] = dot(take, rows).astype(BF16).reshape(chunk, plan.pairs, COMP)

    def load(k, h):
        return taken[k, :, TILE * h : TILE * (h + 1), :].reshape(plan.steps * TILE, COMP)

    pack_rows(plan, load, out_ref, flip=True)


def prep_kernel(plan, where_ref, tables_ref, sand_ref, toep_ref):
    slot = pl.program_id(0) % SLOTS
    place, want = iota((WIDE, 16), 0), iota((WIDE, 16), 1)
    comp = jnp.where(place < MAIN, place, place - TAIL * slot)
    valid = (place < MAIN) | ((comp >= MAIN) & (comp < COMP))
    comp = jnp.where(comp >= SQUARE, comp - SQUARE, comp)
    quotient = (comp * 171) >> 11
    first = (valid & (quotient == want)).astype(F32).astype(BF16)
    second = (valid & (comp - ORB * quotient == want)).astype(F32).astype(BF16)
    row, col = iota((WIDE, WIDE), 0), iota((WIDE, WIDE), 1)
    same_half = (row < SQUARE) == (col < SQUARE)
    couple = tables_ref[0, : BRANCH * 16, :16]
    left = dot_nt(couple, first).astype(BF16)
    right = dot_nt(couple, second).astype(BF16)
    for i in range(BRANCH):
        rows = slice(16 * i, 16 * i + 16)
        product = dot(first, left[rows]) * dot(second, right[rows])
        sand_ref[0, i] = jnp.where(same_half, product, 0.0).astype(BF16)
    mirror = iota((FREQ, 2 * FREQ), 0) + iota((FREQ, 2 * FREQ), 1) == FREQ
    lags = dot(tables_ref[0, BRANCH * 16 :, :], mirror.astype(F32).astype(BF16))
    for q in range(plan.momenta):
        for i in range(BRANCH):
            n = q * BRANCH + i
            band = jnp.broadcast_to(lags[n : n + 1], (FREQ, 2 * FREQ))
            band = pltpu.roll(band, 0, 1, stride=1, stride_axis=0)
            toep_ref[0, q, i * FREQ : (i + 1) * FREQ, :] = band.astype(BF16)


def gather_rows(plan, ref, u, y, first, flip=False):
    m, k = divmod(y, plan.mom_dev)
    row = pl.multiple_of(plan.main_row(k, u), 2 * plan.steps)
    tail = pl.multiple_of(plan.tail_row(k, u), plan.steps)
    order = range(plan.half)
    mains, tails = [], []
    for j in reversed(order) if flip else order:
        peer = (first + j) * plan.n_mom + m
        left = ref[peer, pl.ds(row, plan.steps), :]
        right = ref[peer, pl.ds(row + plan.steps, plan.steps), :]
        mains.append(jnp.concatenate([left, right], axis=1))
        tails.append(ref[peer, pl.ds(tail, plan.steps), :])
    tails = jnp.concatenate(tails, axis=0)
    if plan.shift(k):
        tails = pltpu.roll(tails.astype(F32), LANES - plan.shift(k), 1).astype(BF16)
    return jnp.concatenate([jnp.concatenate(mains, axis=0), tails], axis=1)


def self_block(plan, u, windows, toep_ref, sand_ref, stage, first):
    green = jnp.concatenate([windows(y) for y in range(plan.momenta)], axis=0)
    total = None
    for i in range(BRANCH):
        rows = slice(i * FREQ, (i + 1) * FREQ)
        band = jnp.concatenate(
            [
                jnp.concatenate([toep_ref[0, (k - y) % plan.momenta, rows, :] for y in range(plan.momenta)], axis=1)
                for k in range(plan.momenta)
            ],
            axis=0,
        )
        summed = dot(band, green).astype(BF16)
        term = dot_nt(summed, sand_ref[0, i])
        total = term if total is None else total + term

    @pl.when(u == 0)
    def _():
        for peer in range(plan.half * plan.n_mom):
            stage[peer, plan.main_rows :, :] = jnp.zeros((plan.rows - plan.main_rows, LANES), BF16)

    for y in range(plan.momenta):
        m, k = divmod(y, plan.mom_dev)
        row = pl.multiple_of(plan.main_row(k, u), 2 * plan.steps)
        tail = pl.multiple_of(plan.tail_row(k, u), plan.steps)
        mine = total[y * FREQ : (y + 1) * FREQ]
        rest = mine[:, MAIN:]
        if plan.shift(k):
            rest = pltpu.roll(rest, plan.shift(k), 1)
        mine, rest = mine.astype(BF16), rest.astype(BF16)
        for j in range(plan.half):
            peer = j * plan.n_mom + m
            here = slice(j * plan.steps, (j + 1) * plan.steps)
            stage[peer, pl.ds(row, plan.steps), :] = mine[here, :LANES]
            stage[peer, pl.ds(row + plan.steps, plan.steps), :] = mine[here, LANES:MAIN]
            stage[peer, pl.ds(tail, plan.steps), :] += rest[here]


def flush(plan, u, stage, out_ref, sem, first):
    @pl.when(u == plan.own - 1)
    def _():
        peers = plan.half * plan.n_mom
        copy = pltpu.make_async_copy(stage, out_ref.at[pl.ds(first * plan.n_mom, peers)], sem)
        copy.start()
        copy.wait()


def self_late_kernel(plan, own_ref, toep_ref, sand_ref, out_ref, stage, sem):
    u = pl.program_id(0)

    def windows(y):
        return jnp.concatenate([gather_rows(plan, own_ref, u, y, first) for first in (0, plan.half)], axis=0)

    self_block(plan, u, windows, toep_ref, sand_ref, stage, plan.half)
    flush(plan, u, stage, out_ref, sem, plan.half)


def self_early_kernel(plan, where_ref, own_ref, halo_ref, toep_ref, sand_ref, late_ref, out_ref, stage, sem):
    u = pl.program_id(0)
    has = (where_ref[0] > 0).astype(F32).astype(BF16)

    def windows(y):
        before = gather_rows(plan, halo_ref, u, y, 0) * has
        return jnp.concatenate([before, gather_rows(plan, own_ref, u, y, 0)], axis=0)

    self_block(plan, u, windows, toep_ref, sand_ref, stage, 0)
    flush(plan, u, stage, out_ref, sem, 0)


def lag_sums(plan, partner, green, sand_ref, store):
    for i in range(BRANCH):
        applied = dot(partner, sand_ref[0, i]).astype(BF16)
        lagged = dot_nt(applied, green)
        for q in range(plan.momenta):
            acc = None
            for k in range(plan.momenta):
                y = (k + q) % plan.momenta
                part = lagged[k * FREQ : (k + 1) * FREQ, y * 2 * FREQ : (y + 1) * 2 * FREQ]
                acc = part if acc is None else acc + part
            acc = pltpu.roll(acc, FREQ + 1, 1, stride=1, stride_axis=0)
            store(q, i, jnp.sum(acc, axis=0, keepdims=True))


def phonon_early_kernel(plan, partner_ref, own_ref, sand_ref, out_ref):
    u = pl.program_id(0)
    partner = [gather_rows(plan, partner_ref, u, k, 0, flip=True) for k in range(plan.momenta)]
    green = [gather_rows(plan, own_ref, u, y, first) for y in range(plan.momenta) for first in (0, plan.half)]

    def store(q, i, lags):
        out_ref[0, q * BRANCH + i : q * BRANCH + i + 1, :] = lags

    lag_sums(plan, jnp.concatenate(partner, axis=0), jnp.concatenate(green, axis=0), sand_ref, store)


def phonon_late_kernel(plan, scale, where_ref, partner_ref, own_ref, halo_ref, sand_ref, early_ref, out_ref):
    u = pl.program_id(0)
    has = (where_ref[0] < plan.n_groups - 1).astype(F32).astype(BF16)
    partner = [gather_rows(plan, partner_ref, u, k, plan.half, flip=True) for k in range(plan.momenta)]
    green = []
    for y in range(plan.momenta):
        green.append(gather_rows(plan, own_ref, u, y, plan.half))
        green.append(gather_rows(plan, halo_ref, u, y, 0) * has)

    def store(q, i, lags):
        n = q * BRANCH + i
        side, row = divmod(n, plan.mom_dev * BRANCH)
        out_ref[0, side ^ where_ref[1], row : row + 1, :] = (lags + early_ref[0, n : n + 1, :]) * scale

    lag_sums(plan, jnp.concatenate(partner, axis=0), jnp.concatenate(green, axis=0), sand_ref, store)


def collect_kernel(plan, where_ref, *refs):
    parts, out_ref = refs[:-1], refs[-1]
    for d in range(plan.n_mom):
        total = sum(ref[...] for ref in parts[d :: plan.n_mom])
        for b in range(plan.sub):
            pair = (where_ref[1] ^ d) * plan.sub + b
            for q in range(plan.mom_dev):
                rows = [total[b, q * BRANCH + i : q * BRANCH + i + 1, :FREQ] for i in range(BRANCH)]
                out_ref[q, pl.ds(pair, 1), :] = jnp.concatenate(rows, axis=1)


def unpack_kernel(plan, wire_ref, out_ref, wire, tiles, in_sems, out_sems):
    keys = [(k, h) for k in range(plan.mom_dev) for h in range(plan.pairs // TILE)]
    tail_copy = pltpu.make_async_copy(
        wire_ref.at[:, plan.main_rows :, :], wire.at[:, plan.main_rows :, :], in_sems.at[len(keys)]
    )
    tail_copy.start()
    loads = []
    span = plan.sub * 2 * plan.steps
    for n, (k, h) in enumerate(keys):
        row = plan.main_row(k, h * plan.sub)
        copy = pltpu.make_async_copy(
            wire_ref.at[:, row : row + span, :], wire.at[:, row : row + span, :], in_sems.at[n]
        )
        copy.start()
        loads.append(copy)
    swap = swap_matrix(TILE, plan.steps)
    tail_copy.wait()
    stores = []
    for n, (k, h) in enumerate(keys):
        loads[n].wait()
        lefts, rights, tails = [], [], []
        for i in range(TILE):
            peer, u = plan.place(h, i)
            row, tail = plan.main_row(k, u), plan.tail_row(k, u)
            lefts.append(wire[peer, row : row + plan.steps, :])
            rights.append(wire[peer, row + plan.steps : row + 2 * plan.steps, :])
            lane = (k * plan.own + u) % SLOTS * TAIL
            tails.append(wire[peer, tail : tail + plan.steps, :][:, lane : lane + TAIL])
        rows = jnp.concatenate([jnp.concatenate(part, axis=0) for part in (lefts, rights, tails)], axis=1)
        tiles[k, h] = dot(swap, rows).astype(BF16).reshape(plan.steps, TILE, COMP)
        copy = pltpu.make_async_copy(
            tiles.at[k, h], out_ref.at[k, :, TILE * h : TILE * (h + 1), :], out_sems.at[n]
        )
        copy.start()
        stores.append(copy)
    for copy in stores:
        copy.wait()


ANY = pl.BlockSpec(memory_space=pl.ANY)
VMEM = pl.BlockSpec(memory_space=pltpu.VMEM)
SMEM = pl.BlockSpec(memory_space=pltpu.SMEM)


def call(kernel, out_shape, *args, in_specs, out_specs, grid=(), scratch=(), flops=0, **options):
    moved = sum(a.size * a.dtype.itemsize for a in jax.tree.leaves((args, out_shape)))
    return pl.pallas_call(
        kernel,
        out_shape=out_shape,
        grid=grid,
        in_specs=in_specs,
        out_specs=out_specs,
        scratch_shapes=list(scratch),
        compiler_params=pltpu.CompilerParams(vmem_limit_bytes=VMEM_LIMIT),
        cost_estimate=pl.CostEstimate(flops=flops, bytes_accessed=moved, transcendentals=0),
        **options,
    )(*args)


def shape(dims, dtype):
    return jax.ShapeDtypeStruct(dims, dtype)


def shards(lesser_green, partner, phonon_green, coupling):
    n_energy, n_mom = lax.axis_size("energy"), lax.axis_size("mom")
    plan = Plan(lesser_green, phonon_green, n_energy, n_mom)
    axes = ("energy", "mom")
    me = lax.axis_index("mom")
    s = lax.axis_index("energy") // plan.group
    where = jnp.stack([s, me]).astype(I32)
    wire = shape((plan.peers, plan.rows, LANES), BF16)
    near = (plan.half * n_mom, plan.rows, LANES)
    groups = [[g * plan.peers + i for i in range(plan.peers)] for g in range(plan.n_groups)]
    tiles = (plan.mom_dev, plan.pairs // TILE)

    def exchange(blocks):
        return lax.all_to_all(blocks, axes, split_axis=0, concat_axis=0, axis_index_groups=groups, tiled=True)

    def swap_groups(values, other):
        route = []
        for e in range(n_energy):
            g, j = divmod(e, plan.group)
            to = other(g) if 0 <= other(g) < plan.n_groups else g
            route.append((e, to * plan.group + j))
        return lax.ppermute(values, "energy", route)

    own = exchange(
        call(
            functools.partial(pack_own_kernel, plan),
            wire,
            lesser_green,
            in_specs=[ANY],
            out_specs=VMEM,
            scratch=[pltpu.VMEM(tiles + (plan.steps, TILE, COMP), BF16), pltpu.SemaphoreType.DMA(tiles)],
        )
    )

    odd = s % 2
    edge = lax.dynamic_slice_in_dim(own, (1 - odd) * near[0], near[0], axis=0)
    halo = swap_groups(edge, lambda g: g ^ 1)
    before = after = halo
    if plan.n_groups > 2:
        edge = lax.dynamic_slice_in_dim(own, odd * near[0], near[0], axis=0)
        outer = swap_groups(edge, lambda g: ((g - 1) ^ 1) + 1)
        before = jnp.where(odd == 1, halo, outer)
        after = jnp.where(odd == 1, outer, halo)

    chunk = max(1, 256 // plan.pairs)
    source = (jnp.arange(chunk)[:, None] * plan.pairs + partner[None, :]).reshape(-1)
    take = (source[:, None] == jnp.arange(chunk * plan.pairs)[None, :]).astype(BF16)
    partner_blocks = exchange(
        call(
            functools.partial(pack_partner_kernel, plan),
            wire,
            take,
            lesser_green,
            in_specs=[VMEM, VMEM],
            out_specs=VMEM,
            scratch=[pltpu.VMEM(lesser_green.shape, BF16)],
        )
    )

    lag_count = plan.momenta * BRANCH
    lag_rows = -(-lag_count // 16) * 16
    couple = coupling.reshape(plan.pairs_dev, BRANCH, ORB, ORB)
    couple = jnp.pad(couple, ((0, 0), (0, 0), (0, 16 - ORB), (0, FREQ - ORB)))
    phonon = phonon_green.reshape(plan.momenta, plan.pairs_dev, BRANCH, FREQ)
    phonon = jnp.moveaxis(phonon, 1, 0).reshape(plan.pairs_dev, lag_count, FREQ)
    phonon = jnp.pad(phonon, ((0, 0), (0, lag_rows - lag_count), (0, 0)))
    table = jnp.concatenate([couple.reshape(plan.pairs_dev, BRANCH * 16, FREQ), phonon], axis=1)
    table = lax.dynamic_slice_in_dim(table, me * plan.sub, plan.sub, axis=0)
    tables = [table]
    for d in range(1, plan.n_groups):
        tables.append(swap_groups(table, functools.partial(lambda d, g: g ^ d, d)))
    tables = jnp.concatenate(tables, axis=0)

    def by_distance(u, where_ref):
        return (u // plan.sub ^ where_ref[0]) * plan.sub + u % plan.sub

    sand_shape = (1, BRANCH, WIDE, WIDE)
    toep_shape = (1, plan.momenta, BRANCH * FREQ, 2 * FREQ)
    sand_spec = pl.BlockSpec(sand_shape, lambda u, *_: (u, 0, 0, 0))
    toep_spec = pl.BlockSpec(toep_shape, lambda u, *_: (u, 0, 0, 0))
    whole = pl.BlockSpec(wire.shape, lambda u, *_: (0, 0, 0))
    near_spec = pl.BlockSpec(near, lambda u, *_: (0, 0, 0))
    lag_spec = pl.BlockSpec((1, lag_count, LANES), lambda u, *_: (u, 0, 0))

    def staged(kernel, out_shape, *args, in_specs, out_specs, scratch=(), scalars=1, flops=0, **options):
        moved = sum(a.size * a.dtype.itemsize for a in jax.tree.leaves((args, out_shape)))
        return pl.pallas_call(
            kernel,
            out_shape=out_shape,
            grid_spec=pltpu.PrefetchScalarGridSpec(
                num_scalar_prefetch=scalars,
                grid=(plan.own,),
                in_specs=in_specs,
                out_specs=out_specs,
                scratch_shapes=list(scratch),
            ),
            compiler_params=pltpu.CompilerParams(vmem_limit_bytes=VMEM_LIMIT),
            cost_estimate=pl.CostEstimate(flops=flops, bytes_accessed=moved, transcendentals=0),
            **options,
        )(*args)

    sand, toep = staged(
        functools.partial(prep_kernel, plan),
        [shape((plan.own,) + sand_shape[1:], BF16), shape((plan.own,) + toep_shape[1:], BF16)],
        where,
        tables,
        in_specs=[
            pl.BlockSpec((1, BRANCH * 16 + lag_rows, FREQ), lambda u, w: (by_distance(u, w), 0, 0)),
        ],
        out_specs=[sand_spec, toep_spec],
    )

    stage = [pltpu.VMEM(near, BF16), pltpu.SemaphoreType.DMA]
    work = plan.own * 2 * plan.momenta * BRANCH * FREQ * WIDE * (plan.momenta * 2 * FREQ + WIDE)
    late = staged(
        functools.partial(self_late_kernel, plan),
        wire,
        own,
        toep,
        sand,
        in_specs=[whole, toep_spec, sand_spec],
        out_specs=ANY,
        scratch=stage,
        scalars=0,
        flops=work,
    )
    sigma = staged(
        functools.partial(self_early_kernel, plan),
        wire,
        where,
        own,
        before,
        toep,
        sand,
        late,
        in_specs=[whole, near_spec, toep_spec, sand_spec, ANY],
        out_specs=ANY,
        scratch=stage,
        flops=work,
        input_output_aliases={5: 0},
    )
    arrived = exchange(sigma)

    scale = (plan.momenta * n_energy * plan.steps * COMP) ** -0.5
    early = staged(
        functools.partial(phonon_early_kernel, plan),
        shape((plan.own, lag_count, LANES), F32),
        partner_blocks,
        own,
        sand,
        in_specs=[whole, whole, sand_spec],
        out_specs=lag_spec,
        scalars=0,
        flops=work,
    )
    side_rows = plan.mom_dev * BRANCH
    spectra = staged(
        functools.partial(phonon_late_kernel, plan, scale),
        shape((plan.own, n_mom, side_rows, LANES), F32),
        where,
        partner_blocks,
        own,
        after,
        sand,
        early,
        in_specs=[whole, whole, near_spec, sand_spec, lag_spec],
        out_specs=pl.BlockSpec((1, n_mom, side_rows, LANES), lambda u, w: (by_distance(u, w), 0, 0, 0)),
        flops=work,
    )
    parts = []
    for d in range(plan.n_groups):
        for t in range(n_mom):
            part = spectra[d * plan.sub : (d + 1) * plan.sub, t]
            if d or t:
                route = []
                for e in range(n_energy):
                    g, j = divmod(e, plan.group)
                    for m in range(n_mom):
                        route.append((e * n_mom + m, ((g ^ d) * plan.group + j) * n_mom + (m ^ t)))
                part = lax.ppermute(part, axes, route)
            parts.append(part)
    phonon_self = call(
        functools.partial(collect_kernel, plan),
        shape((plan.mom_dev, plan.pairs_dev, BRANCH * FREQ), F32),
        where,
        *parts,
        in_specs=[SMEM] + [VMEM] * len(parts),
        out_specs=VMEM,
    )

    self_energy = call(
        functools.partial(unpack_kernel, plan),
        shape(lesser_green.shape, BF16),
        arrived,
        in_specs=[ANY],
        out_specs=ANY,
        scratch=[
            pltpu.VMEM(wire.shape, BF16),
            pltpu.VMEM(tiles + (plan.steps, TILE, COMP), BF16),
            pltpu.SemaphoreType.DMA((tiles[0] * tiles[1] + 1,)),
            pltpu.SemaphoreType.DMA((tiles[0] * tiles[1],)),
        ],
    )
    return self_energy, phonon_self


def solution(mesh):
    in_specs = (P("mom", "energy", None, None), P(), P(None, "energy", None), P("energy", None))
    out_specs = (P("mom", "energy", None, None), P("mom", "energy", None))
    return jax.shard_map(shards, mesh=mesh, in_specs=in_specs, out_specs=out_specs, check_vma=False)
```

```python
import functools

import jax
import jax.numpy as jnp
from jax import lax
from jax.experimental import pallas as pl
from jax.experimental.pallas import tpu as pltpu
from jax.sharding import PartitionSpec as P

ORB = 12
BRANCH = 3
FREQ = 64
COMP = 288
SQUARE = ORB * ORB
LANES = 128
REST = SQUARE - LANES
TAIL = 2 * REST
SLOTS = LANES // TAIL
TILE = 16
SMALL_GRANT = 16 * 1024 * 1024

BF16 = jnp.bfloat16
F32 = jnp.float32
I32 = jnp.int32


class Plan:
    def __init__(self, green, phonon, n_energy, n_mom):
        self.n_energy, self.n_mom = n_energy, n_mom
        self.mom_dev, self.steps, self.pairs, _ = green.shape
        self.momenta = self.mom_dev * n_mom
        self.pairs_dev = phonon.shape[1]
        self.half = FREQ // self.steps
        self.group = 2 * self.half
        self.n_groups = n_energy // self.group
        self.peers = self.group * n_mom
        self.sub = self.pairs_dev // n_mom
        self.own = self.n_groups * self.sub
        self.main_rows = self.mom_dev * self.own * 2 * self.steps
        self.rows = self.main_rows + self.mom_dev * self.own // SLOTS * self.steps
        assert self.half * self.steps == FREQ and n_energy % self.group == 0
        assert self.pairs_dev % n_mom == 0 and self.group * self.pairs_dev == TILE
        assert self.mom_dev * self.own % SLOTS == 0 and self.n_groups % 2 == 0

    def main_row(self, k, u):
        return (k * self.own + u) * 2 * self.steps

    def tail_row(self, k, u):
        return self.main_rows + (k * self.own + u) // SLOTS * self.steps

    def shift(self, k):
        return k * self.own % SLOTS * TAIL

    def place(self, h, i):
        j, rest = divmod(i, self.pairs_dev)
        m, b = divmod(rest, self.sub)
        return j * self.n_mom + m, h * self.sub + b


def dot(a, b):
    return lax.dot_general(a, b, (((1,), (0,)), ((), ())), preferred_element_type=F32)


def dot_nt(a, b):
    return lax.dot_general(a, b, (((1,), (1,)), ((), ())), preferred_element_type=F32)


def iota(dims, axis):
    return lax.broadcasted_iota(I32, dims, axis)


def swap_matrix(outer, inner, flip=False):
    n = outer * inner
    row, col = iota((n, n), 0), iota((n, n), 1)
    place = row & (outer - 1)
    source = (outer - 1 - place if flip else place) * inner + (row >> (outer.bit_length() - 1))
    return (col == source).astype(F32).astype(BF16)


def to_wire(rows):
    tail = jnp.concatenate([rows[:, LANES:SQUARE], rows[:, SQUARE + LANES :]], axis=1)
    return rows[:, :LANES], rows[:, SQUARE : SQUARE + LANES], tail


def pack_rows(plan, load, out_ref, stage, sems, flip=False):
    swap = swap_matrix(plan.steps, TILE, flip)
    tails, copies = {}, []

    def send(first, count):
        rows = slice(first, first + count)
        copy = pltpu.make_async_copy(stage.at[:, rows, :], out_ref.at[:, rows, :], sems.at[len(copies)])
        copy.start()
        copies.append(copy)

    for k in range(plan.mom_dev):
        for h in range(plan.pairs // TILE):
            left, right, tail = to_wire(dot(swap, load(k, h)).astype(BF16))
            for i in range(TILE):
                peer, u = plan.place(h, i)
                here = slice(i * plan.steps, (i + 1) * plan.steps)
                row = plan.main_row(k, u)
                stage[peer, row : row + plan.steps, :] = left[here]
                stage[peer, row + plan.steps : row + 2 * plan.steps, :] = right[here]
                tails[peer, k * plan.own + u] = tail[here]
            send(plan.main_row(k, h * plan.sub), plan.sub * 2 * plan.steps)
    for peer in range(plan.peers):
        for first in range(0, plan.mom_dev * plan.own, SLOTS):
            row = plan.main_rows + first // SLOTS * plan.steps
            joined = jnp.concatenate([tails[peer, first + t] for t in range(SLOTS)], axis=1)
            stage[peer, row : row + plan.steps, :] = joined
    send(plan.main_rows, plan.rows - plan.main_rows)
    for copy in copies:
        copy.wait()


def load_tiles(plan, green_ref, tiles, sems):
    copies = {}
    for k in range(plan.mom_dev):
        for h in range(plan.pairs // TILE):
            copies[k, h] = pltpu.make_async_copy(
                green_ref.at[k, :, TILE * h : TILE * (h + 1), :], tiles.at[k, h], sems.at[k, h]
            )
            copies[k, h].start()
    return copies


def pack_own_kernel(plan, green_ref, out_ref, stage, out_sems, tiles, sems):
    copies = load_tiles(plan, green_ref, tiles, sems)

    def load(k, h):
        copies[k, h].wait()
        return tiles[k, h].reshape(plan.steps * TILE, COMP)

    pack_rows(plan, load, out_ref, stage, out_sems)


def pack_partner_kernel(plan, take_ref, green_ref, out_ref, stage, out_sems, taken):
    chunk = take_ref.shape[0] // plan.pairs
    take = take_ref[...]
    for k in range(plan.mom_dev):
        for e in range(0, plan.steps, chunk):
            rows = green_ref[k, e : e + chunk].reshape(chunk * plan.pairs, COMP)
            taken[k, e : e + chunk] = dot(take, rows).astype(BF16).reshape(chunk, plan.pairs, COMP)

    def load(k, h):
        return taken[k, :, TILE * h : TILE * (h + 1), :].reshape(plan.steps * TILE, COMP)

    pack_rows(plan, load, out_ref, stage, out_sems, flip=True)


def each_pair(plan, body):
    if plan.own <= 2:
        for u in range(plan.own):
            body(u)
    else:
        lax.fori_loop(0, plan.own, lambda u, _: body(u), None)


def rows_at(row, count):
    return pl.ds(row if isinstance(row, int) else pl.multiple_of(row, count), count)


def prep_kernel(plan, tables_ref, sand_ref, toep_ref):
    group = lax.axis_index("energy") // plan.group
    place, want = iota((2 * LANES, 16), 0), iota((2 * LANES, 16), 1)
    mirror = iota((FREQ, 2 * FREQ), 0) + iota((FREQ, 2 * FREQ), 1) == FREQ
    mirror = mirror.astype(F32).astype(BF16)

    def body(u):
        source = (u // plan.sub ^ group) * plan.sub + u % plan.sub
        table = tables_ref[source]
        couple = table[: BRANCH * 16, :16]
        for h in range(2):
            comp = jnp.where(place < LANES, place, place - (u % SLOTS * TAIL + h * REST))
            valid = (place < LANES) | ((comp >= LANES) & (comp < SQUARE))
            quotient = (comp * 171) >> 11
            first = (valid & (quotient == want)).astype(F32).astype(BF16)
            second = (valid & (comp - ORB * quotient == want)).astype(F32).astype(BF16)
            left = dot_nt(couple, first).astype(BF16)
            right = dot_nt(couple, second).astype(BF16)
            for i in range(BRANCH):
                rows = slice(16 * i, 16 * i + 16)
                product = dot(first, left[rows]) * dot(second, right[rows])
                sand_ref[u, h, :, 2 * LANES * i : 2 * LANES * (i + 1)] = product.astype(BF16)
        lags = dot(table[BRANCH * 16 :, :], mirror)
        for q in range(plan.momenta):
            for i in range(BRANCH):
                n = q * BRANCH + i
                band = jnp.broadcast_to(lags[n : n + 1], (FREQ, 2 * FREQ))
                band = pltpu.roll(band, 0, 1, stride=1, stride_axis=0)
                toep_ref[u, q, i * FREQ : (i + 1) * FREQ, :] = band.astype(BF16)

    each_pair(plan, body)


def gather_rows(plan, ref, u, y, first, flip=False):
    m, k = divmod(y, plan.mom_dev)
    row, tail = plan.main_row(k, u), plan.tail_row(k, u)
    order = range(plan.half)
    lefts, rights, tails = [], [], []
    for j in reversed(order) if flip else order:
        peer = (first + j) * plan.n_mom + m
        lefts.append(ref[peer, rows_at(row, plan.steps), :])
        rights.append(ref[peer, rows_at(row + plan.steps, plan.steps), :])
        tails.append(ref[peer, rows_at(tail, plan.steps), :])
    tails = jnp.concatenate(tails, axis=0)
    if plan.shift(k):
        tails = pltpu.roll(tails.astype(F32), LANES - plan.shift(k), 1).astype(BF16)
    return jnp.concatenate([jnp.concatenate(lefts, axis=0), jnp.concatenate(rights, axis=0), tails], axis=1)


def half_and_tail(rows, h):
    return jnp.concatenate([rows[:, h * LANES : (h + 1) * LANES], rows[:, 2 * LANES :]], axis=1)


def self_block(plan, u, green, toep_ref, sand_ref, out_ref):
    summed = []
    for i in range(BRANCH):
        rows = slice(i * FREQ, (i + 1) * FREQ)
        band = jnp.concatenate(
            [
                jnp.concatenate([toep_ref[u, (k - y) % plan.momenta, rows, :] for y in range(plan.momenta)], axis=1)
                for k in range(plan.momenta)
            ],
            axis=0,
        )
        summed.append(dot(band, green).astype(BF16))
    left, right = [
        dot_nt(jnp.concatenate([half_and_tail(rows, h) for rows in summed], axis=1), sand_ref[u, h])
        for h in range(2)
    ]
    tails = left[:, LANES:] + right[:, LANES:]
    left, right = left[:, :LANES].astype(BF16), right[:, :LANES].astype(BF16)
    for y in range(plan.momenta):
        m, k = divmod(y, plan.mom_dev)
        row, tail = plan.main_row(k, u), plan.tail_row(k, u)
        rest = tails[y * FREQ : (y + 1) * FREQ]
        if plan.shift(k):
            rest = pltpu.roll(rest, plan.shift(k), 1)
        rest = rest.astype(BF16)
        for j in range(plan.half):
            peer = j * plan.n_mom + m
            here = slice(j * plan.steps, (j + 1) * plan.steps)
            there = slice(y * FREQ + j * plan.steps, y * FREQ + (j + 1) * plan.steps)
            out_ref[peer, rows_at(row, plan.steps), :] = left[there]
            out_ref[peer, rows_at(row + plan.steps, plan.steps), :] = right[there]
            out_ref[peer, rows_at(tail, plan.steps), :] += rest[here]


def clear_tails(plan, out_ref):
    for peer in range(plan.half * plan.n_mom):
        out_ref[peer, plan.main_rows :, :] = jnp.zeros((plan.rows - plan.main_rows, LANES), BF16)


def self_late_kernel(plan, own_ref, toep_ref, sand_ref, out_ref):
    clear_tails(plan, out_ref)

    def body(u):
        green = [gather_rows(plan, own_ref, u, y, first) for y in range(plan.momenta) for first in (0, plan.half)]
        self_block(plan, u, jnp.concatenate(green, axis=0), toep_ref, sand_ref, out_ref)

    each_pair(plan, body)


def self_early_kernel(plan, own_ref, halo_ref, toep_ref, sand_ref, late_ref, out_ref):
    group = lax.axis_index("energy") // plan.group
    has = (group > 0).astype(F32).astype(BF16)
    clear_tails(plan, out_ref)
    near = plan.half * plan.n_mom
    out_ref[near:] = late_ref[...]

    def body(u):
        green = []
        for y in range(plan.momenta):
            green.append(gather_rows(plan, halo_ref, u, y, 0) * has)
            green.append(gather_rows(plan, own_ref, u, y, 0))
        self_block(plan, u, jnp.concatenate(green, axis=0), toep_ref, sand_ref, out_ref)

    each_pair(plan, body)


def lag_sums(plan, u, partner, green, sand_ref, store):
    partner, green = jnp.concatenate(partner, axis=0), jnp.concatenate(green, axis=0)
    left, right = [dot(half_and_tail(partner, h), sand_ref[u, h]) for h in range(2)]
    for i in range(BRANCH):
        here = slice(2 * LANES * i, 2 * LANES * i + LANES)
        rest = slice(2 * LANES * i + LANES, 2 * LANES * (i + 1))
        applied = jnp.concatenate([left[:, here], right[:, here], left[:, rest] + right[:, rest]], axis=1)
        lagged = dot_nt(applied.astype(BF16), green)
        for q in range(plan.momenta):
            acc = None
            for k in range(plan.momenta):
                y = (k + q) % plan.momenta
                part = lagged[k * FREQ : (k + 1) * FREQ, y * 2 * FREQ : (y + 1) * 2 * FREQ]
                acc = part if acc is None else acc + part
            acc = pltpu.roll(acc, FREQ + 1, 1, stride=1, stride_axis=0)
            store(q, i, jnp.sum(acc, axis=0, keepdims=True))


def phonon_early_kernel(plan, partner_ref, own_ref, sand_ref, out_ref):
    def body(u):
        partner = [gather_rows(plan, partner_ref, u, k, 0, flip=True) for k in range(plan.momenta)]
        green = [gather_rows(plan, own_ref, u, y, first) for y in range(plan.momenta) for first in (0, plan.half)]

        def store(q, i, lags):
            out_ref[u, q * BRANCH + i : q * BRANCH + i + 1, :] = lags

        lag_sums(plan, u, partner, green, sand_ref, store)

    each_pair(plan, body)


def phonon_late_kernel(plan, partner_ref, own_ref, halo_ref, sand_ref, early_ref, *refs, scale):
    outs, sums = refs[:-1], refs[-1]
    group = lax.axis_index("energy") // plan.group
    me = lax.axis_index("mom")
    has = (group < plan.n_groups - 1).astype(F32).astype(BF16)

    def body(u):
        partner = [gather_rows(plan, partner_ref, u, k, plan.half, flip=True) for k in range(plan.momenta)]
        green = []
        for y in range(plan.momenta):
            green.append(gather_rows(plan, own_ref, u, y, plan.half))
            green.append(gather_rows(plan, halo_ref, u, y, 0) * has)

        def store(q, i, lags):
            n = q * BRANCH + i
            side, row = divmod(n, plan.mom_dev * BRANCH)
            sums[u, side, row : row + 1, :] = (lags + early_ref[u, n : n + 1, :]) * scale

        lag_sums(plan, u, partner, green, sand_ref, store)

    each_pair(plan, body)
    for d in range(plan.n_groups):
        for t in range(plan.n_mom):
            for b in range(plan.sub):
                outs[d * plan.n_mom + t][b] = sums[(group ^ d) * plan.sub + b, me ^ t]


def collect_kernel(plan, *refs):
    parts, out_ref = refs[:-1], refs[-1]
    me = lax.axis_index("mom")
    for d in range(plan.n_mom):
        total = sum(ref[...] for ref in parts[d :: plan.n_mom])
        for b in range(plan.sub):
            pair = (me ^ d) * plan.sub + b
            for q in range(plan.mom_dev):
                rows = [total[b, q * BRANCH + i : q * BRANCH + i + 1, :FREQ] for i in range(BRANCH)]
                out_ref[q, pl.ds(pair, 1), :] = jnp.concatenate(rows, axis=1)


def unpack_kernel(plan, wire, out_ref, tiles, sems):
    swap = swap_matrix(TILE, plan.steps)
    copies = []
    for k in range(plan.mom_dev):
        for h in range(plan.pairs // TILE):
            lefts, rights, tails = [], [], []
            for i in range(TILE):
                peer, u = plan.place(h, i)
                row, tail = plan.main_row(k, u), plan.tail_row(k, u)
                lefts.append(wire[peer, row : row + plan.steps, :])
                rights.append(wire[peer, row + plan.steps : row + 2 * plan.steps, :])
                lane = (k * plan.own + u) % SLOTS * TAIL
                tails.append(wire[peer, tail : tail + plan.steps, :][:, lane : lane + TAIL])
            rows = jnp.concatenate([jnp.concatenate(part, axis=0) for part in (lefts, rights, tails)], axis=1)
            moved = dot(swap, rows).astype(BF16)
            left, right = moved[:, :LANES], moved[:, LANES : 2 * LANES]
            tail = moved[:, 2 * LANES :]
            moved = jnp.concatenate([left, tail[:, :REST], right, tail[:, REST:]], axis=1)
            tiles[k, h] = moved.reshape(plan.steps, TILE, COMP)
            copy = pltpu.make_async_copy(
                tiles.at[k, h], out_ref.at[k, :, TILE * h : TILE * (h + 1), :], sems.at[k, h]
            )
            copy.start()
            copies.append(copy)
    for copy in copies:
        copy.wait()


ANY = pl.BlockSpec(memory_space=pl.ANY)
VMEM = pl.BlockSpec(memory_space=pltpu.VMEM)


def call(plan, kernel, out_shape, *args, in_specs=None, out_specs=None, scratch=(), flops=0):
    arrays = jax.tree.leaves((args, out_shape))
    outs = jax.tree.map(lambda _: VMEM, out_shape)
    return pl.pallas_call(
        functools.partial(kernel, plan),
        out_shape=out_shape,
        in_specs=in_specs or [VMEM] * len(args),
        out_specs=out_specs or outs,
        scratch_shapes=list(scratch),
        compiler_params=pltpu.CompilerParams(vmem_limit_bytes=SMALL_GRANT * max(1, plan.own // 4)),
        cost_estimate=pl.CostEstimate(
            flops=flops, bytes_accessed=sum(a.size * a.dtype.itemsize for a in arrays), transcendentals=0
        ),
    )(*args)


def shape(dims, dtype):
    return jax.ShapeDtypeStruct(dims, dtype)


def shards(lesser_green, partner, phonon_green, coupling):
    n_energy, n_mom = lax.axis_size("energy"), lax.axis_size("mom")
    plan = Plan(lesser_green, phonon_green, n_energy, n_mom)
    axes = ("energy", "mom")
    me = lax.axis_index("mom")
    s = lax.axis_index("energy") // plan.group
    wire = shape((plan.peers, plan.rows, LANES), BF16)
    near = shape((plan.half * n_mom, plan.rows, LANES), BF16)
    groups = [[g * plan.peers + i for i in range(plan.peers)] for g in range(plan.n_groups)]
    tiles = (plan.mom_dev, plan.pairs // TILE)

    def exchange(blocks):
        return lax.all_to_all(blocks, axes, split_axis=0, concat_axis=0, axis_index_groups=groups, tiled=True)

    def swap_groups(values, other):
        route = []
        for e in range(n_energy):
            g, j = divmod(e, plan.group)
            to = other(g) if 0 <= other(g) < plan.n_groups else g
            route.append((e, to * plan.group + j))
        return lax.ppermute(values, "energy", route)

    staging = [pltpu.VMEM(wire.shape, BF16), pltpu.SemaphoreType.DMA((tiles[0] * tiles[1] + 1,))]
    tile_scratch = [pltpu.VMEM(tiles + (plan.steps, TILE, COMP), BF16), pltpu.SemaphoreType.DMA(tiles)]
    own = exchange(
        call(
            plan,
            pack_own_kernel,
            wire,
            lesser_green,
            in_specs=[ANY],
            out_specs=ANY,
            scratch=staging + tile_scratch,
        )
    )

    lag_count = plan.momenta * BRANCH
    lag_rows = -(-lag_count // 16) * 16
    couple = coupling.reshape(plan.pairs_dev, BRANCH, ORB, ORB)
    couple = jnp.pad(couple, ((0, 0), (0, 0), (0, 16 - ORB), (0, FREQ - ORB)))
    phonon = phonon_green.reshape(plan.momenta, plan.pairs_dev, BRANCH, FREQ)
    phonon = jnp.moveaxis(phonon, 1, 0).reshape(plan.pairs_dev, lag_count, FREQ)
    phonon = jnp.pad(phonon, ((0, 0), (0, lag_rows - lag_count), (0, 0)))
    table = jnp.concatenate([couple.reshape(plan.pairs_dev, BRANCH * 16, FREQ), phonon], axis=1)
    table = lax.dynamic_slice_in_dim(table, me * plan.sub, plan.sub, axis=0)
    tables = [table]
    for d in range(1, plan.n_groups):
        tables.append(swap_groups(table, functools.partial(lambda d, g: g ^ d, d)))
    sand, toep = call(
        plan,
        prep_kernel,
        [
            shape((plan.own, 2, 2 * LANES, BRANCH * 2 * LANES), BF16),
            shape((plan.own, plan.momenta, BRANCH * FREQ, 2 * FREQ), BF16),
        ],
        jnp.concatenate(tables, axis=0),
    )

    chunk = max(1, 256 // plan.pairs)
    source = (jnp.arange(chunk)[:, None] * plan.pairs + partner[None, :]).reshape(-1)
    take = (source[:, None] == jnp.arange(chunk * plan.pairs)[None, :]).astype(BF16)
    partner_wire = call(
        plan,
        pack_partner_kernel,
        wire,
        take,
        lesser_green,
        out_specs=ANY,
        scratch=staging + [pltpu.VMEM(lesser_green.shape, BF16)],
    )
    own, sand, toep, partner_wire = lax.optimization_barrier((own, sand, toep, partner_wire))

    odd = s % 2
    edge = lax.dynamic_slice_in_dim(own, (1 - odd) * near.shape[0], near.shape[0], axis=0)
    edge, partner_wire = lax.optimization_barrier((edge, partner_wire))
    halo = swap_groups(edge, lambda g: g ^ 1)
    before = after = halo
    if plan.n_groups > 2:
        edge = lax.dynamic_slice_in_dim(own, odd * near.shape[0], near.shape[0], axis=0)
        outer = swap_groups(edge, lambda g: ((g - 1) ^ 1) + 1)
        before = jnp.where(odd == 1, halo, outer)
        after = jnp.where(odd == 1, outer, halo)
    partner_blocks = exchange(partner_wire)

    work = 4_000_000_000 * plan.own // 2
    late = call(plan, self_late_kernel, near, own, toep, sand, flops=work)
    sigma = call(plan, self_early_kernel, wire, own, before, toep, sand, late, flops=work)
    arrived = exchange(sigma)

    scale = (plan.momenta * n_energy * plan.steps * COMP) ** -0.5
    early = call(
        plan,
        phonon_early_kernel,
        shape((plan.own, lag_count, LANES), F32),
        partner_blocks,
        own,
        sand,
        flops=work,
    )
    side_rows = plan.mom_dev * BRANCH
    parts = list(call(
        plan,
        functools.partial(phonon_late_kernel, scale=scale),
        [shape((plan.sub, side_rows, LANES), F32)] * (plan.n_groups * n_mom),
        partner_blocks,
        own,
        after,
        sand,
        early,
        scratch=[pltpu.VMEM((plan.own, n_mom, side_rows, LANES), F32)],
        flops=work,
    ))
    for d in range(plan.n_groups):
        for t in range(n_mom):
            if d or t:
                route = []
                for e in range(n_energy):
                    g, j = divmod(e, plan.group)
                    for m in range(n_mom):
                        route.append((e * n_mom + m, ((g ^ d) * plan.group + j) * n_mom + (m ^ t)))
                parts[d * n_mom + t] = lax.ppermute(parts[d * n_mom + t], axes, route)
    phonon_self = call(
        plan, collect_kernel, shape((plan.mom_dev, plan.pairs_dev, BRANCH * FREQ), F32), *parts
    )

    self_energy = call(
        plan,
        unpack_kernel,
        shape(lesser_green.shape, BF16),
        arrived,
        out_specs=ANY,
        scratch=tile_scratch,
    )
    return self_energy, phonon_self


def solution(mesh):
    in_specs = (P("mom", "energy", None, None), P(), P(None, "energy", None), P("energy", None))
    out_specs = (P("mom", "energy", None, None), P("mom", "energy", None))
    return jax.shard_map(shards, mesh=mesh, in_specs=in_specs, out_specs=out_specs, check_vma=False)
```

```python
import functools

import jax
import jax.numpy as jnp
from jax import lax
from jax.experimental import pallas as pl
from jax.experimental.pallas import tpu as pltpu
from jax.sharding import PartitionSpec as P

ORB = 12
BRANCH = 3
FREQ = 64
COMP = 288
SQUARE = ORB * ORB
LANES = 128
REST = SQUARE - LANES
TAIL = 2 * REST
SLOTS = LANES // TAIL
TILE = 16
SMALL_GRANT = 16 * 1024 * 1024
LARGE_GRANT = 60 * 1024 * 1024

BF16 = jnp.bfloat16
F32 = jnp.float32
I32 = jnp.int32


class Plan:
    def __init__(self, green, phonon, n_energy, n_mom):
        self.n_energy, self.n_mom = n_energy, n_mom
        self.mom_dev, self.steps, self.pairs, _ = green.shape
        self.momenta = self.mom_dev * n_mom
        self.pairs_dev = phonon.shape[1]
        self.half = FREQ // self.steps
        self.group = 2 * self.half
        self.n_groups = n_energy // self.group
        self.peers = self.group * n_mom
        self.sub = self.pairs_dev // n_mom
        self.own = self.n_groups * self.sub
        self.main_rows = self.own * 2 * self.steps
        self.tail_rows = self.mom_dev * self.own // SLOTS * self.steps
        self.rows = self.mom_dev * self.main_rows + self.tail_rows
        assert self.half * self.steps == FREQ and n_energy % self.group == 0
        assert self.pairs_dev % n_mom == 0 and self.group * self.pairs_dev == TILE
        assert self.mom_dev * self.own % SLOTS == 0 and self.n_groups % 2 == 0

    def main_row(self, k, u):
        return (k * self.own + u) * 2 * self.steps

    def tail_row(self, k, u):
        return (k * self.own + u) // SLOTS * self.steps

    def spots(self, refs, k, u):
        if len(refs) == 1:
            return refs[0], self.main_row(k, u), refs[0], self.mom_dev * self.main_rows + self.tail_row(k, u)
        return refs[k], self.main_row(0, u), refs[-1], self.main_rows + self.tail_row(k, u)

    def shift(self, k):
        return k * self.own % SLOTS * TAIL

    def place(self, h, i):
        j, rest = divmod(i, self.pairs_dev)
        m, b = divmod(rest, self.sub)
        return j * self.n_mom + m, h * self.sub + b


def dot(a, b):
    return lax.dot_general(a, b, (((1,), (0,)), ((), ())), preferred_element_type=F32)


def dot_nt(a, b):
    return lax.dot_general(a, b, (((1,), (1,)), ((), ())), preferred_element_type=F32)


def iota(dims, axis):
    return lax.broadcasted_iota(I32, dims, axis)


def swap_matrix(outer, inner, flip=False):
    n = outer * inner
    row, col = iota((n, n), 0), iota((n, n), 1)
    place = row & (outer - 1)
    source = (outer - 1 - place if flip else place) * inner + (row >> (outer.bit_length() - 1))
    return (col == source).astype(F32).astype(BF16)


def to_wire(rows):
    tail = jnp.concatenate([rows[:, LANES:SQUARE], rows[:, SQUARE + LANES :]], axis=1)
    return rows[:, :LANES], rows[:, SQUARE : SQUARE + LANES], tail


def pack_rows(plan, load, out_ref, stage, sems, momenta, tail_momenta, flip=False):
    swap = swap_matrix(plan.steps, TILE, flip)
    tails, copies = {}, []

    def send(first, count):
        rows = slice(first, first + count)
        copy = pltpu.make_async_copy(stage.at[:, rows, :], out_ref.at[:, rows, :], sems.at[len(copies)])
        copy.start()
        copies.append(copy)

    for k in sorted({*momenta, *tail_momenta}):
        for h in range(plan.pairs // TILE):
            left, right, tail = to_wire(dot(swap, load(k, h)).astype(BF16))
            for i in range(TILE):
                peer, u = plan.place(h, i)
                here = slice(i * plan.steps, (i + 1) * plan.steps)
                tails[peer, k * plan.own + u] = tail[here]
                if k in momenta:
                    row = plan.main_row(momenta.index(k), u)
                    stage[peer, row : row + plan.steps, :] = left[here]
                    stage[peer, row + plan.steps : row + 2 * plan.steps, :] = right[here]
            if k in momenta:
                send(plan.main_row(momenta.index(k), h * plan.sub), plan.sub * 2 * plan.steps)
    if tail_momenta:
        base = len(momenta) * plan.main_rows
        for peer in range(plan.peers):
            for first in range(0, plan.mom_dev * plan.own, SLOTS):
                row = base + first // SLOTS * plan.steps
                joined = jnp.concatenate([tails[peer, first + t] for t in range(SLOTS)], axis=1)
                stage[peer, row : row + plan.steps, :] = joined
        send(base, plan.tail_rows)
    for copy in copies:
        copy.wait()


def pack_own_kernel(plan, green_ref, out_ref, stage, out_sems, tiles, sems, *, momenta, tail_momenta):
    copies = {}
    for k in sorted({*momenta, *tail_momenta}):
        for h in range(plan.pairs // TILE):
            copies[k, h] = pltpu.make_async_copy(
                green_ref.at[k, :, TILE * h : TILE * (h + 1), :], tiles.at[k, h], sems.at[k, h]
            )
            copies[k, h].start()

    def load(k, h):
        copies[k, h].wait()
        return tiles[k, h].reshape(plan.steps * TILE, COMP)

    pack_rows(plan, load, out_ref, stage, out_sems, momenta, tail_momenta)


def pack_partner_kernel(plan, take_ref, green_ref, out_ref, stage, out_sems, taken):
    chunk = take_ref.shape[0] // plan.pairs
    take = take_ref[...]
    for k in range(plan.mom_dev):
        for e in range(0, plan.steps, chunk):
            rows = green_ref[k, e : e + chunk].reshape(chunk * plan.pairs, COMP)
            taken[k, e : e + chunk] = dot(take, rows).astype(BF16).reshape(chunk, plan.pairs, COMP)

    def load(k, h):
        return taken[k, :, TILE * h : TILE * (h + 1), :].reshape(plan.steps * TILE, COMP)

    every = list(range(plan.mom_dev))
    pack_rows(plan, load, out_ref, stage, out_sems, every, every, flip=True)


def each_pair(plan, body):
    if plan.own <= 2:
        for u in range(plan.own):
            body(u)
    else:
        lax.fori_loop(0, plan.own, lambda u, _: body(u), None)


def rows_at(row, count):
    return pl.ds(row if isinstance(row, int) else pl.multiple_of(row, count), count)


def prep_kernel(plan, tables_ref, sand_ref, toep_ref):
    group = lax.axis_index("energy") // plan.group
    place, want = iota((2 * LANES, 16), 0), iota((2 * LANES, 16), 1)
    mirror = iota((FREQ, 2 * FREQ), 0) + iota((FREQ, 2 * FREQ), 1) == FREQ
    mirror = mirror.astype(F32).astype(BF16)

    def body(u):
        source = (u // plan.sub ^ group) * plan.sub + u % plan.sub
        table = tables_ref[source]
        couple = table[: BRANCH * 16, :16]
        for h in range(2):
            comp = jnp.where(place < LANES, place, place - (u % SLOTS * TAIL + h * REST))
            valid = (place < LANES) | ((comp >= LANES) & (comp < SQUARE))
            quotient = (comp * 171) >> 11
            first = (valid & (quotient == want)).astype(F32).astype(BF16)
            second = (valid & (comp - ORB * quotient == want)).astype(F32).astype(BF16)
            left = dot_nt(couple, first).astype(BF16)
            right = dot_nt(couple, second).astype(BF16)
            for i in range(BRANCH):
                rows = slice(16 * i, 16 * i + 16)
                product = dot(first, left[rows]) * dot(second, right[rows])
                sand_ref[u, h, :, 2 * LANES * i : 2 * LANES * (i + 1)] = product.astype(BF16)
        lags = dot(table[BRANCH * 16 :, :], mirror)
        for q in range(plan.momenta):
            for i in range(BRANCH):
                n = q * BRANCH + i
                band = jnp.broadcast_to(lags[n : n + 1], (FREQ, 2 * FREQ))
                band = pltpu.roll(band, 0, 1, stride=1, stride_axis=0)
                toep_ref[u, q, i * FREQ : (i + 1) * FREQ, :] = band.astype(BF16)

    each_pair(plan, body)


def gather_rows(plan, refs, u, y, first, flip=False):
    m, k = divmod(y, plan.mom_dev)
    ref, row, tail_ref, tail = plan.spots(refs, k, u)
    order = range(plan.half)
    lefts, rights, tails = [], [], []
    for j in reversed(order) if flip else order:
        peer = (first + j) * plan.n_mom + m
        lefts.append(ref[peer, rows_at(row, plan.steps), :])
        rights.append(ref[peer, rows_at(row + plan.steps, plan.steps), :])
        tails.append(tail_ref[peer, rows_at(tail, plan.steps), :])
    tails = jnp.concatenate(tails, axis=0)
    if plan.shift(k):
        tails = pltpu.roll(tails.astype(F32), LANES - plan.shift(k), 1).astype(BF16)
    return jnp.concatenate([jnp.concatenate(lefts, axis=0), jnp.concatenate(rights, axis=0), tails], axis=1)


def half_and_tail(rows, h):
    return jnp.concatenate([rows[:, h * LANES : (h + 1) * LANES], rows[:, 2 * LANES :]], axis=1)


def self_block(plan, u, green, toep_ref, sand_ref, out_ref):
    summed = []
    for i in range(BRANCH):
        rows = slice(i * FREQ, (i + 1) * FREQ)
        band = jnp.concatenate(
            [
                jnp.concatenate([toep_ref[u, (k - y) % plan.momenta, rows, :] for y in range(plan.momenta)], axis=1)
                for k in range(plan.momenta)
            ],
            axis=0,
        )
        summed.append(dot(band, green).astype(BF16))
    left, right = [
        dot_nt(jnp.concatenate([half_and_tail(rows, h) for rows in summed], axis=1), sand_ref[u, h])
        for h in range(2)
    ]
    tails = left[:, LANES:] + right[:, LANES:]
    left, right = left[:, :LANES].astype(BF16), right[:, :LANES].astype(BF16)
    for y in range(plan.momenta):
        m, k = divmod(y, plan.mom_dev)
        _, row, _, tail = plan.spots([out_ref], k, u)
        rest = tails[y * FREQ : (y + 1) * FREQ]
        if plan.shift(k):
            rest = pltpu.roll(rest, plan.shift(k), 1)
        rest = rest.astype(BF16)
        for j in range(plan.half):
            peer = j * plan.n_mom + m
            here = slice(j * plan.steps, (j + 1) * plan.steps)
            there = slice(y * FREQ + j * plan.steps, y * FREQ + (j + 1) * plan.steps)
            out_ref[peer, rows_at(row, plan.steps), :] = left[there]
            out_ref[peer, rows_at(row + plan.steps, plan.steps), :] = right[there]
            out_ref[peer, rows_at(tail, plan.steps), :] += rest[here]


def clear_tails(plan, out_ref):
    for peer in range(plan.half * plan.n_mom):
        out_ref[peer, plan.rows - plan.tail_rows :, :] = jnp.zeros((plan.tail_rows, LANES), BF16)


def self_late_kernel(plan, *refs):
    own, (toep_ref, sand_ref, out_ref) = refs[: plan.mom_dev], refs[plan.mom_dev :]
    clear_tails(plan, out_ref)

    def body(u):
        green = [gather_rows(plan, own, u, y, first) for y in range(plan.momenta) for first in (0, plan.half)]
        self_block(plan, u, jnp.concatenate(green, axis=0), toep_ref, sand_ref, out_ref)

    each_pair(plan, body)


def self_early_kernel(plan, *refs):
    own, halo = refs[: plan.mom_dev], refs[plan.mom_dev : 2 * plan.mom_dev]
    toep_ref, sand_ref, late_ref, out_ref = refs[2 * plan.mom_dev :]
    group = lax.axis_index("energy") // plan.group
    has = (group > 0).astype(F32).astype(BF16)
    clear_tails(plan, out_ref)
    out_ref[plan.half * plan.n_mom :] = late_ref[...]

    def body(u):
        green = []
        for y in range(plan.momenta):
            green.append(gather_rows(plan, halo, u, y, 0) * has)
            green.append(gather_rows(plan, own, u, y, 0))
        self_block(plan, u, jnp.concatenate(green, axis=0), toep_ref, sand_ref, out_ref)

    each_pair(plan, body)


def lag_sums(plan, u, partner, green, sand_ref, store):
    partner, green = jnp.concatenate(partner, axis=0), jnp.concatenate(green, axis=0)
    left, right = [dot(half_and_tail(partner, h), sand_ref[u, h]) for h in range(2)]
    for i in range(BRANCH):
        here = slice(2 * LANES * i, 2 * LANES * i + LANES)
        rest = slice(2 * LANES * i + LANES, 2 * LANES * (i + 1))
        applied = jnp.concatenate([left[:, here], right[:, here], left[:, rest] + right[:, rest]], axis=1)
        lagged = dot_nt(applied.astype(BF16), green)
        for q in range(plan.momenta):
            acc = None
            for k in range(plan.momenta):
                y = (k + q) % plan.momenta
                part = lagged[k * FREQ : (k + 1) * FREQ, y * 2 * FREQ : (y + 1) * 2 * FREQ]
                acc = part if acc is None else acc + part
            acc = pltpu.roll(acc, FREQ + 1, 1, stride=1, stride_axis=0)
            store(q, i, jnp.sum(acc, axis=0, keepdims=True))


def phonon_early_kernel(plan, *refs):
    own, (partner_ref, sand_ref, out_ref) = refs[: plan.mom_dev], refs[plan.mom_dev :]

    def body(u):
        partner = [gather_rows(plan, [partner_ref], u, k, 0, flip=True) for k in range(plan.momenta)]
        green = [gather_rows(plan, own, u, y, first) for y in range(plan.momenta) for first in (0, plan.half)]

        def store(q, i, lags):
            out_ref[u, q * BRANCH + i : q * BRANCH + i + 1, :] = lags

        lag_sums(plan, u, partner, green, sand_ref, store)

    each_pair(plan, body)


def phonon_late_kernel(plan, *refs, scale):
    own, halo = refs[: plan.mom_dev], refs[plan.mom_dev : 2 * plan.mom_dev]
    partner_ref, sand_ref, early_ref, *refs = refs[2 * plan.mom_dev :]
    outs, sums = refs[:-1], refs[-1]
    group = lax.axis_index("energy") // plan.group
    me = lax.axis_index("mom")
    has = (group < plan.n_groups - 1).astype(F32).astype(BF16)

    def body(u):
        partner = [gather_rows(plan, [partner_ref], u, k, plan.half, flip=True) for k in range(plan.momenta)]
        green = []
        for y in range(plan.momenta):
            green.append(gather_rows(plan, own, u, y, plan.half))
            green.append(gather_rows(plan, halo, u, y, 0) * has)

        def store(q, i, lags):
            n = q * BRANCH + i
            side, row = divmod(n, plan.mom_dev * BRANCH)
            sums[u, side, row : row + 1, :] = (lags + early_ref[u, n : n + 1, :]) * scale

        lag_sums(plan, u, partner, green, sand_ref, store)

    each_pair(plan, body)
    for d in range(plan.n_groups):
        for t in range(plan.n_mom):
            for b in range(plan.sub):
                outs[d * plan.n_mom + t][b] = sums[(group ^ d) * plan.sub + b, me ^ t]


def collect_kernel(plan, *refs):
    parts, out_ref = refs[:-1], refs[-1]
    me = lax.axis_index("mom")
    for d in range(plan.n_mom):
        total = sum(ref[...] for ref in parts[d :: plan.n_mom])
        for b in range(plan.sub):
            pair = (me ^ d) * plan.sub + b
            for q in range(plan.mom_dev):
                rows = [total[b, q * BRANCH + i : q * BRANCH + i + 1, :FREQ] for i in range(BRANCH)]
                out_ref[q, pl.ds(pair, 1), :] = jnp.concatenate(rows, axis=1)


def unpack_kernel(plan, wire, out_ref, tiles, sems):
    swap = swap_matrix(TILE, plan.steps)
    copies = []
    for k in range(plan.mom_dev):
        for h in range(plan.pairs // TILE):
            lefts, rights, tails = [], [], []
            for i in range(TILE):
                peer, u = plan.place(h, i)
                _, row, _, tail = plan.spots([wire], k, u)
                lefts.append(wire[peer, row : row + plan.steps, :])
                rights.append(wire[peer, row + plan.steps : row + 2 * plan.steps, :])
                lane = (k * plan.own + u) % SLOTS * TAIL
                tails.append(wire[peer, tail : tail + plan.steps, :][:, lane : lane + TAIL])
            rows = jnp.concatenate([jnp.concatenate(part, axis=0) for part in (lefts, rights, tails)], axis=1)
            moved = dot(swap, rows).astype(BF16)
            left, right = moved[:, :LANES], moved[:, LANES : 2 * LANES]
            tail = moved[:, 2 * LANES :]
            moved = jnp.concatenate([left, tail[:, :REST], right, tail[:, REST:]], axis=1)
            tiles[k, h] = moved.reshape(plan.steps, TILE, COMP)
            copy = pltpu.make_async_copy(
                tiles.at[k, h], out_ref.at[k, :, TILE * h : TILE * (h + 1), :], sems.at[k, h]
            )
            copy.start()
            copies.append(copy)
    for copy in copies:
        copy.wait()


ANY = pl.BlockSpec(memory_space=pl.ANY)
VMEM = pl.BlockSpec(memory_space=pltpu.VMEM)


def call(plan, kernel, out_shape, *args, in_specs=None, out_specs=None, scratch=(), flops=0, grant=None):
    arrays = jax.tree.leaves((args, out_shape))
    outs = jax.tree.map(lambda _: VMEM, out_shape)
    return pl.pallas_call(
        functools.partial(kernel, plan),
        out_shape=out_shape,
        in_specs=in_specs or [VMEM] * len(args),
        out_specs=out_specs or outs,
        scratch_shapes=list(scratch),
        compiler_params=pltpu.CompilerParams(vmem_limit_bytes=grant or SMALL_GRANT * max(1, plan.own // 4)),
        cost_estimate=pl.CostEstimate(
            flops=flops, bytes_accessed=sum(a.size * a.dtype.itemsize for a in arrays), transcendentals=0
        ),
    )(*args)


def shape(dims, dtype):
    return jax.ShapeDtypeStruct(dims, dtype)


def shards(lesser_green, partner, phonon_green, coupling):
    n_energy, n_mom = lax.axis_size("energy"), lax.axis_size("mom")
    plan = Plan(lesser_green, phonon_green, n_energy, n_mom)
    axes = ("energy", "mom")
    me = lax.axis_index("mom")
    s = lax.axis_index("energy") // plan.group
    wire = shape((plan.peers, plan.rows, LANES), BF16)
    half_peers = plan.half * n_mom
    groups = [[g * plan.peers + i for i in range(plan.peers)] for g in range(plan.n_groups)]
    tiles = (plan.mom_dev, plan.pairs // TILE)

    def exchange(blocks):
        return lax.all_to_all(blocks, axes, split_axis=0, concat_axis=0, axis_index_groups=groups, tiled=True)

    def swap_groups(values, other):
        route = []
        for e in range(n_energy):
            g, j = divmod(e, plan.group)
            to = other(g) if 0 <= other(g) < plan.n_groups else g
            route.append((e, to * plan.group + j))
        return lax.ppermute(values, "energy", route)

    staging = [pltpu.VMEM(wire.shape, BF16), pltpu.SemaphoreType.DMA((tiles[0] * tiles[1] + 1,))]
    tile_scratch = [pltpu.VMEM(tiles + (plan.steps, TILE, COMP), BF16), pltpu.SemaphoreType.DMA(tiles)]
    every = list(range(plan.mom_dev))

    def pack_own(k):
        last = k == every[-1]
        rows = plan.main_rows + (plan.tail_rows if last else 0)
        return call(
            plan,
            functools.partial(pack_own_kernel, momenta=[k], tail_momenta=every if last else []),
            shape((plan.peers, rows, LANES), BF16),
            lesser_green,
            in_specs=[ANY],
            out_specs=ANY,
            scratch=[pltpu.VMEM((plan.peers, rows, LANES), BF16), staging[1]] + tile_scratch,
            grant=LARGE_GRANT,
        )

    odd = s % 2

    def neighbours(blocks):
        def edge(side):
            return lax.dynamic_slice_in_dim(blocks, side * half_peers, half_peers, axis=0)

        inner = swap_groups(edge(1 - odd), lambda g: g ^ 1)
        if plan.n_groups == 2:
            return inner, inner
        outer = swap_groups(edge(odd), lambda g: ((g - 1) ^ 1) + 1)
        return jnp.where(odd == 1, inner, outer), jnp.where(odd == 1, outer, inner)

    lag_count = plan.momenta * BRANCH
    lag_rows = -(-lag_count // 16) * 16
    couple = coupling.reshape(plan.pairs_dev, BRANCH, ORB, ORB)
    couple = jnp.pad(couple, ((0, 0), (0, 0), (0, 16 - ORB), (0, FREQ - ORB)))
    phonon = phonon_green.reshape(plan.momenta, plan.pairs_dev, BRANCH, FREQ)
    phonon = jnp.moveaxis(phonon, 1, 0).reshape(plan.pairs_dev, lag_count, FREQ)
    phonon = jnp.pad(phonon, ((0, 0), (0, lag_rows - lag_count), (0, 0)))
    table = jnp.concatenate([couple.reshape(plan.pairs_dev, BRANCH * 16, FREQ), phonon], axis=1)
    table = lax.dynamic_slice_in_dim(table, me * plan.sub, plan.sub, axis=0)
    tables = [table]
    for d in range(1, plan.n_groups):
        tables.append(swap_groups(table, functools.partial(lambda d, g: g ^ d, d)))
    sand, toep = call(
        plan,
        prep_kernel,
        [
            shape((plan.own, 2, 2 * LANES, BRANCH * 2 * LANES), BF16),
            shape((plan.own, plan.momenta, BRANCH * FREQ, 2 * FREQ), BF16),
        ],
        jnp.concatenate(tables, axis=0),
    )

    chunk = max(1, 256 // plan.pairs)
    source = (jnp.arange(chunk)[:, None] * plan.pairs + partner[None, :]).reshape(-1)
    take = (source[:, None] == jnp.arange(chunk * plan.pairs)[None, :]).astype(BF16)
    partner_wire = call(
        plan,
        pack_partner_kernel,
        wire,
        take,
        lesser_green,
        out_specs=ANY,
        scratch=staging + [pltpu.VMEM(lesser_green.shape, BF16)],
    )
    own, before, after = [], [], []
    for k in every:
        blocks = exchange(pack_own(k))
        if k == 0:
            blocks, partner_wire = lax.optimization_barrier((blocks, partner_wire))
        else:
            blocks, sand, toep = lax.optimization_barrier((blocks, sand, toep))
        ahead, behind = neighbours(blocks)
        own.append(blocks)
        before.append(ahead)
        after.append(behind)

    work = 4_000_000_000 * plan.own // 2
    half_wire = shape((half_peers, plan.rows, LANES), BF16)
    late = call(plan, self_late_kernel, half_wire, *own, toep, sand, flops=work)
    late, partner_wire = lax.optimization_barrier((late, partner_wire))
    partner_blocks = exchange(partner_wire)
    sigma = call(plan, self_early_kernel, wire, *own, *before, toep, sand, late, flops=work)
    arrived = exchange(sigma)

    scale = (plan.momenta * n_energy * plan.steps * COMP) ** -0.5
    early = call(
        plan,
        phonon_early_kernel,
        shape((plan.own, lag_count, LANES), F32),
        *own,
        partner_blocks,
        sand,
        flops=work,
    )
    side_rows = plan.mom_dev * BRANCH
    parts = list(call(
        plan,
        functools.partial(phonon_late_kernel, scale=scale),
        [shape((plan.sub, side_rows, LANES), F32)] * (plan.n_groups * n_mom),
        *own,
        *after,
        partner_blocks,
        sand,
        early,
        scratch=[pltpu.VMEM((plan.own, n_mom, side_rows, LANES), F32)],
        flops=work,
    ))
    for d in range(plan.n_groups):
        for t in range(n_mom):
            if d or t:
                route = []
                for e in range(n_energy):
                    g, j = divmod(e, plan.group)
                    for m in range(n_mom):
                        route.append((e * n_mom + m, ((g ^ d) * plan.group + j) * n_mom + (m ^ t)))
                parts[d * n_mom + t] = lax.ppermute(parts[d * n_mom + t], axes, route)
    phonon_self = call(
        plan, collect_kernel, shape((plan.mom_dev, plan.pairs_dev, BRANCH * FREQ), F32), *parts
    )

    self_energy = call(
        plan,
        unpack_kernel,
        shape(lesser_green.shape, BF16),
        arrived,
        out_specs=ANY,
        scratch=tile_scratch,
    )
    return self_energy, phonon_self


def solution(mesh):
    in_specs = (P("mom", "energy", None, None), P(), P(None, "energy", None), P("energy", None))
    out_specs = (P("mom", "energy", None, None), P("mom", "energy", None))
    return jax.shard_map(shards, mesh=mesh, in_specs=in_specs, out_specs=out_specs, check_vma=False)
```

```python
import functools

import jax
import jax.numpy as jnp
from jax import lax
from jax.experimental import pallas as pl
from jax.experimental.pallas import tpu as pltpu
from jax.sharding import PartitionSpec as P

ORB = 12
BRANCH = 3
FREQ = 64
COMP = 288
SQUARE = ORB * ORB
LANES = 128
REST = SQUARE - LANES
TAIL = 2 * REST
SLOTS = LANES // TAIL
TILE = 16
SMALL_GRANT = 16 * 1024 * 1024
LARGE_GRANT = 60 * 1024 * 1024

BF16 = jnp.bfloat16
F32 = jnp.float32
I32 = jnp.int32


class Plan:
    def __init__(self, green, phonon, n_energy, n_mom):
        self.n_energy, self.n_mom = n_energy, n_mom
        self.mom_dev, self.steps, self.pairs, _ = green.shape
        self.momenta = self.mom_dev * n_mom
        self.pairs_dev = phonon.shape[1]
        self.half = FREQ // self.steps
        self.group = 2 * self.half
        self.n_groups = n_energy // self.group
        self.peers = self.group * n_mom
        self.sub = self.pairs_dev // n_mom
        self.own = self.n_groups * self.sub
        self.main_rows = self.own * 2 * self.steps
        self.tail_rows = self.mom_dev * self.own // SLOTS * self.steps
        self.rows = self.mom_dev * self.main_rows + self.tail_rows
        assert self.half * self.steps == FREQ and n_energy % self.group == 0
        assert self.pairs_dev % n_mom == 0 and self.group * self.pairs_dev == TILE
        assert self.mom_dev * self.own % SLOTS == 0 and self.n_groups % 2 == 0

    def main_row(self, k, u):
        return (k * self.own + u) * 2 * self.steps

    def tail_row(self, k, u):
        return (k * self.own + u) // SLOTS * self.steps

    def spots(self, refs, k, u):
        if len(refs) == 1:
            return refs[0], self.main_row(k, u), refs[0], self.mom_dev * self.main_rows + self.tail_row(k, u)
        return refs[k], self.main_row(0, u), refs[-1], self.main_rows + self.tail_row(k, u)

    def shift(self, k):
        return k * self.own % SLOTS * TAIL

    def place(self, h, i):
        j, rest = divmod(i, self.pairs_dev)
        m, b = divmod(rest, self.sub)
        return j * self.n_mom + m, h * self.sub + b


def dot(a, b):
    return lax.dot_general(a, b, (((1,), (0,)), ((), ())), preferred_element_type=F32)


def dot_nt(a, b):
    return lax.dot_general(a, b, (((1,), (1,)), ((), ())), preferred_element_type=F32)


def iota(dims, axis):
    return lax.broadcasted_iota(I32, dims, axis)


def swap_matrix(outer, inner, flip=False):
    n = outer * inner
    row, col = iota((n, n), 0), iota((n, n), 1)
    place = row & (outer - 1)
    source = (outer - 1 - place if flip else place) * inner + (row >> (outer.bit_length() - 1))
    return (col == source).astype(F32).astype(BF16)


def to_wire(rows):
    tail = jnp.concatenate([rows[:, LANES:SQUARE], rows[:, SQUARE + LANES :]], axis=1)
    return rows[:, :LANES], rows[:, SQUARE : SQUARE + LANES], tail


def pack_rows(plan, load, out_ref, stage, sems, momenta, tail_momenta, flip=False):
    swap = swap_matrix(plan.steps, TILE, flip)
    tails, copies = {}, []

    def send(first, count):
        rows = slice(first, first + count)
        copy = pltpu.make_async_copy(stage.at[:, rows, :], out_ref.at[:, rows, :], sems.at[len(copies)])
        copy.start()
        copies.append(copy)

    for k in sorted({*momenta, *tail_momenta}):
        for h in range(plan.pairs // TILE):
            left, right, tail = to_wire(dot(swap, load(k, h)).astype(BF16))
            for i in range(TILE):
                peer, u = plan.place(h, i)
                here = slice(i * plan.steps, (i + 1) * plan.steps)
                tails[peer, k * plan.own + u] = tail[here]
                if k in momenta:
                    row = plan.main_row(momenta.index(k), u)
                    stage[peer, row : row + plan.steps, :] = left[here]
                    stage[peer, row + plan.steps : row + 2 * plan.steps, :] = right[here]
            if k in momenta:
                send(plan.main_row(momenta.index(k), h * plan.sub), plan.sub * 2 * plan.steps)
    if tail_momenta:
        base = len(momenta) * plan.main_rows
        for peer in range(plan.peers):
            for first in range(0, plan.mom_dev * plan.own, SLOTS):
                row = base + first // SLOTS * plan.steps
                joined = jnp.concatenate([tails[peer, first + t] for t in range(SLOTS)], axis=1)
                stage[peer, row : row + plan.steps, :] = joined
        send(base, plan.tail_rows)
    for copy in copies:
        copy.wait()


def pack_own_kernel(plan, green_ref, out_ref, stage, out_sems, tiles, sems, *, momenta, tail_momenta):
    copies = {}
    for k in sorted({*momenta, *tail_momenta}):
        for h in range(plan.pairs // TILE):
            copies[k, h] = pltpu.make_async_copy(
                green_ref.at[k, :, TILE * h : TILE * (h + 1), :], tiles.at[k, h], sems.at[k, h]
            )
            copies[k, h].start()

    def load(k, h):
        copies[k, h].wait()
        return tiles[k, h].reshape(plan.steps * TILE, COMP)

    pack_rows(plan, load, out_ref, stage, out_sems, momenta, tail_momenta)


def pack_partner_kernel(plan, take_ref, green_ref, out_ref, stage, out_sems, taken):
    chunk = take_ref.shape[0] // plan.pairs
    take = take_ref[...]
    for k in range(plan.mom_dev):
        for e in range(0, plan.steps, chunk):
            rows = green_ref[k, e : e + chunk].reshape(chunk * plan.pairs, COMP)
            taken[k, e : e + chunk] = dot(take, rows).astype(BF16).reshape(chunk, plan.pairs, COMP)

    def load(k, h):
        return taken[k, :, TILE * h : TILE * (h + 1), :].reshape(plan.steps * TILE, COMP)

    every = list(range(plan.mom_dev))
    pack_rows(plan, load, out_ref, stage, out_sems, every, every, flip=True)


def each_pair(plan, body):
    if plan.own <= 2:
        for u in range(plan.own):
            body(u)
    else:
        lax.fori_loop(0, plan.own, lambda u, _: body(u), None)


def rows_at(row, count):
    return pl.ds(row if isinstance(row, int) else pl.multiple_of(row, count), count)


def prep_kernel(plan, tables_ref, sand_ref, toep_ref):
    group = lax.axis_index("energy") // plan.group
    place, want = iota((2 * LANES, 16), 0), iota((2 * LANES, 16), 1)
    mirror = iota((FREQ, 2 * FREQ), 0) + iota((FREQ, 2 * FREQ), 1) == FREQ
    mirror = mirror.astype(F32).astype(BF16)

    def body(u):
        source = (u // plan.sub ^ group) * plan.sub + u % plan.sub
        table = tables_ref[source]
        couple = table[: BRANCH * 16, :16]
        for h in range(2):
            comp = jnp.where(place < LANES, place, place - (u % SLOTS * TAIL + h * REST))
            valid = (place < LANES) | ((comp >= LANES) & (comp < SQUARE))
            quotient = (comp * 171) >> 11
            first = (valid & (quotient == want)).astype(F32).astype(BF16)
            second = (valid & (comp - ORB * quotient == want)).astype(F32).astype(BF16)
            left = dot_nt(couple, first).astype(BF16)
            right = dot_nt(couple, second).astype(BF16)
            for i in range(BRANCH):
                rows = slice(16 * i, 16 * i + 16)
                product = dot(first, left[rows]) * dot(second, right[rows])
                sand_ref[u, h, :, 2 * LANES * i : 2 * LANES * (i + 1)] = product.astype(BF16)
        lags = dot(table[BRANCH * 16 :, :], mirror)
        for q in range(plan.momenta):
            for i in range(BRANCH):
                n = q * BRANCH + i
                band = jnp.broadcast_to(lags[n : n + 1], (FREQ, 2 * FREQ))
                band = pltpu.roll(band, 0, 1, stride=1, stride_axis=0)
                toep_ref[u, q, i * FREQ : (i + 1) * FREQ, :] = band.astype(BF16)

    each_pair(plan, body)


def gather_rows(plan, refs, u, y, first, flip=False):
    m, k = divmod(y, plan.mom_dev)
    ref, row, tail_ref, tail = plan.spots(refs, k, u)
    order = range(plan.half)
    lefts, rights, tails = [], [], []
    for j in reversed(order) if flip else order:
        peer = (first + j) * plan.n_mom + m
        lefts.append(ref[peer, rows_at(row, plan.steps), :])
        rights.append(ref[peer, rows_at(row + plan.steps, plan.steps), :])
        tails.append(tail_ref[peer, rows_at(tail, plan.steps), :])
    tails = jnp.concatenate(tails, axis=0)
    if plan.shift(k):
        tails = pltpu.roll(tails.astype(F32), LANES - plan.shift(k), 1).astype(BF16)
    return jnp.concatenate([jnp.concatenate(lefts, axis=0), jnp.concatenate(rights, axis=0), tails], axis=1)


def half_and_tail(rows, h):
    return jnp.concatenate([rows[:, h * LANES : (h + 1) * LANES], rows[:, 2 * LANES :]], axis=1)


def self_block(plan, u, green, toep_ref, sand_ref, out_ref):
    summed = []
    for i in range(BRANCH):
        rows = slice(i * FREQ, (i + 1) * FREQ)
        band = jnp.concatenate(
            [
                jnp.concatenate([toep_ref[u, (k - y) % plan.momenta, rows, :] for y in range(plan.momenta)], axis=1)
                for k in range(plan.momenta)
            ],
            axis=0,
        )
        summed.append(dot(band, green).astype(BF16))
    left, right = [
        dot_nt(jnp.concatenate([half_and_tail(rows, h) for rows in summed], axis=1), sand_ref[u, h])
        for h in range(2)
    ]
    tails = left[:, LANES:] + right[:, LANES:]
    left, right = left[:, :LANES].astype(BF16), right[:, :LANES].astype(BF16)
    for y in range(plan.momenta):
        m, k = divmod(y, plan.mom_dev)
        _, row, _, tail = plan.spots([out_ref], k, u)
        rest = tails[y * FREQ : (y + 1) * FREQ]
        if plan.shift(k):
            rest = pltpu.roll(rest, plan.shift(k), 1)
        rest = rest.astype(BF16)
        for j in range(plan.half):
            peer = j * plan.n_mom + m
            here = slice(j * plan.steps, (j + 1) * plan.steps)
            there = slice(y * FREQ + j * plan.steps, y * FREQ + (j + 1) * plan.steps)
            out_ref[peer, rows_at(row, plan.steps), :] = left[there]
            out_ref[peer, rows_at(row + plan.steps, plan.steps), :] = right[there]
            out_ref[peer, rows_at(tail, plan.steps), :] += rest[here]


def clear_tails(plan, out_ref):
    for peer in range(plan.half * plan.n_mom):
        out_ref[peer, plan.rows - plan.tail_rows :, :] = jnp.zeros((plan.tail_rows, LANES), BF16)


def self_late_kernel(plan, *refs):
    own, (toep_ref, sand_ref, out_ref) = refs[: plan.mom_dev], refs[plan.mom_dev :]
    clear_tails(plan, out_ref)

    def body(u):
        green = [gather_rows(plan, own, u, y, first) for y in range(plan.momenta) for first in (0, plan.half)]
        self_block(plan, u, jnp.concatenate(green, axis=0), toep_ref, sand_ref, out_ref)

    each_pair(plan, body)


def self_early_kernel(plan, *refs):
    own, halo = refs[: plan.mom_dev], refs[plan.mom_dev : 2 * plan.mom_dev]
    toep_ref, sand_ref, late_ref, out_ref = refs[2 * plan.mom_dev :]
    group = lax.axis_index("energy") // plan.group
    has = (group > 0).astype(F32).astype(BF16)
    clear_tails(plan, out_ref)
    out_ref[plan.half * plan.n_mom :] = late_ref[...]

    def body(u):
        green = []
        for y in range(plan.momenta):
            green.append(gather_rows(plan, halo, u, y, 0) * has)
            green.append(gather_rows(plan, own, u, y, 0))
        self_block(plan, u, jnp.concatenate(green, axis=0), toep_ref, sand_ref, out_ref)

    each_pair(plan, body)


def lag_sums(plan, u, partner, green, sand_ref, store):
    partner, green = jnp.concatenate(partner, axis=0), jnp.concatenate(green, axis=0)
    left, right = [dot(half_and_tail(partner, h), sand_ref[u, h]) for h in range(2)]
    for i in range(BRANCH):
        here = slice(2 * LANES * i, 2 * LANES * i + LANES)
        rest = slice(2 * LANES * i + LANES, 2 * LANES * (i + 1))
        applied = jnp.concatenate([left[:, here], right[:, here], left[:, rest] + right[:, rest]], axis=1)
        lagged = dot_nt(applied.astype(BF16), green)
        for q in range(plan.momenta):
            acc = None
            for k in range(plan.momenta):
                y = (k + q) % plan.momenta
                part = lagged[k * FREQ : (k + 1) * FREQ, y * 2 * FREQ : (y + 1) * 2 * FREQ]
                acc = part if acc is None else acc + part
            acc = pltpu.roll(acc, FREQ + 1, 1, stride=1, stride_axis=0)
            store(q, i, jnp.sum(acc, axis=0, keepdims=True))


def phonon_early_kernel(plan, *refs):
    own, (partner_ref, sand_ref, out_ref) = refs[: plan.mom_dev], refs[plan.mom_dev :]

    def body(u):
        partner = [gather_rows(plan, [partner_ref], u, k, 0, flip=True) for k in range(plan.momenta)]
        green = [gather_rows(plan, own, u, y, first) for y in range(plan.momenta) for first in (0, plan.half)]

        def store(q, i, lags):
            out_ref[u, q * BRANCH + i : q * BRANCH + i + 1, :] = lags

        lag_sums(plan, u, partner, green, sand_ref, store)

    each_pair(plan, body)


def phonon_late_kernel(plan, *refs, scale):
    own, halo = refs[: plan.mom_dev], refs[plan.mom_dev : 2 * plan.mom_dev]
    partner_ref, sand_ref, early_ref, *refs = refs[2 * plan.mom_dev :]
    outs, sums = refs[:-1], refs[-1]
    group = lax.axis_index("energy") // plan.group
    me = lax.axis_index("mom")
    has = (group < plan.n_groups - 1).astype(F32).astype(BF16)

    def body(u):
        partner = [gather_rows(plan, [partner_ref], u, k, plan.half, flip=True) for k in range(plan.momenta)]
        green = []
        for y in range(plan.momenta):
            green.append(gather_rows(plan, own, u, y, plan.half))
            green.append(gather_rows(plan, halo, u, y, 0) * has)

        def store(q, i, lags):
            n = q * BRANCH + i
            side, row = divmod(n, plan.mom_dev * BRANCH)
            sums[u, side, row : row + 1, :] = (lags + early_ref[u, n : n + 1, :]) * scale

        lag_sums(plan, u, partner, green, sand_ref, store)

    each_pair(plan, body)
    for d in range(plan.n_groups):
        for t in range(plan.n_mom):
            for b in range(plan.sub):
                outs[d * plan.n_mom + t][b] = sums[(group ^ d) * plan.sub + b, me ^ t]


def collect_kernel(plan, *refs):
    parts, out_ref = refs[:-1], refs[-1]
    me = lax.axis_index("mom")
    for d in range(plan.n_mom):
        total = sum(ref[...] for ref in parts[d :: plan.n_mom])
        for b in range(plan.sub):
            pair = (me ^ d) * plan.sub + b
            for q in range(plan.mom_dev):
                rows = [total[b, q * BRANCH + i : q * BRANCH + i + 1, :FREQ] for i in range(BRANCH)]
                out_ref[q, pl.ds(pair, 1), :] = jnp.concatenate(rows, axis=1)


def unpack_kernel(plan, wire, out_ref, tiles, sems):
    swap = swap_matrix(TILE, plan.steps)
    copies = []
    for k in range(plan.mom_dev):
        for h in range(plan.pairs // TILE):
            lefts, rights, tails = [], [], []
            for i in range(TILE):
                peer, u = plan.place(h, i)
                _, row, _, tail = plan.spots([wire], k, u)
                lefts.append(wire[peer, row : row + plan.steps, :])
                rights.append(wire[peer, row + plan.steps : row + 2 * plan.steps, :])
                lane = (k * plan.own + u) % SLOTS * TAIL
                tails.append(wire[peer, tail : tail + plan.steps, :][:, lane : lane + TAIL])
            rows = jnp.concatenate([jnp.concatenate(part, axis=0) for part in (lefts, rights, tails)], axis=1)
            moved = dot(swap, rows).astype(BF16)
            left, right = moved[:, :LANES], moved[:, LANES : 2 * LANES]
            tail = moved[:, 2 * LANES :]
            moved = jnp.concatenate([left, tail[:, :REST], right, tail[:, REST:]], axis=1)
            tiles[k, h] = moved.reshape(plan.steps, TILE, COMP)
            copy = pltpu.make_async_copy(
                tiles.at[k, h], out_ref.at[k, :, TILE * h : TILE * (h + 1), :], sems.at[k, h]
            )
            copy.start()
            copies.append(copy)
    for copy in copies:
        copy.wait()


ANY = pl.BlockSpec(memory_space=pl.ANY)
VMEM = pl.BlockSpec(memory_space=pltpu.VMEM)


def call(plan, kernel, out_shape, *args, in_specs=None, out_specs=None, scratch=(), grant=None):
    outs = jax.tree.map(lambda _: VMEM, out_shape)
    return pl.pallas_call(
        functools.partial(kernel, plan),
        out_shape=out_shape,
        in_specs=in_specs or [VMEM] * len(args),
        out_specs=out_specs or outs,
        scratch_shapes=list(scratch),
        compiler_params=pltpu.CompilerParams(vmem_limit_bytes=grant or SMALL_GRANT * max(1, plan.own // 4)),
        cost_estimate=pl.CostEstimate(flops=1, bytes_accessed=1, transcendentals=0),
    )(*args)


def shape(dims, dtype):
    return jax.ShapeDtypeStruct(dims, dtype)


def shards(lesser_green, partner, phonon_green, coupling):
    n_energy, n_mom = lax.axis_size("energy"), lax.axis_size("mom")
    plan = Plan(lesser_green, phonon_green, n_energy, n_mom)
    axes = ("energy", "mom")
    me = lax.axis_index("mom")
    s = lax.axis_index("energy") // plan.group
    wire = shape((plan.peers, plan.rows, LANES), BF16)
    half_peers = plan.half * n_mom
    groups = [[g * plan.peers + i for i in range(plan.peers)] for g in range(plan.n_groups)]
    tiles = (plan.mom_dev, plan.pairs // TILE)

    def exchange(blocks):
        return lax.all_to_all(blocks, axes, split_axis=0, concat_axis=0, axis_index_groups=groups, tiled=True)

    def swap_groups(values, other):
        route = []
        for e in range(n_energy):
            g, j = divmod(e, plan.group)
            to = other(g) if 0 <= other(g) < plan.n_groups else g
            route.append((e, to * plan.group + j))
        return lax.ppermute(values, "energy", route)

    staging = [pltpu.VMEM(wire.shape, BF16), pltpu.SemaphoreType.DMA((tiles[0] * tiles[1] + 1,))]
    tile_scratch = [pltpu.VMEM(tiles + (plan.steps, TILE, COMP), BF16), pltpu.SemaphoreType.DMA(tiles)]
    every = list(range(plan.mom_dev))

    def pack_own(k):
        last = k == every[-1]
        rows = plan.main_rows + (plan.tail_rows if last else 0)
        return call(
            plan,
            functools.partial(pack_own_kernel, momenta=[k], tail_momenta=every if last else []),
            shape((plan.peers, rows, LANES), BF16),
            lesser_green,
            in_specs=[ANY],
            out_specs=ANY,
            scratch=[pltpu.VMEM((plan.peers, rows, LANES), BF16), staging[1]] + tile_scratch,
            grant=LARGE_GRANT,
        )

    odd = s % 2

    def neighbours(blocks):
        def edge(side):
            return lax.dynamic_slice_in_dim(blocks, side * half_peers, half_peers, axis=0)

        inner = swap_groups(edge(1 - odd), lambda g: g ^ 1)
        if plan.n_groups == 2:
            return inner, inner
        outer = swap_groups(edge(odd), lambda g: ((g - 1) ^ 1) + 1)
        return jnp.where(odd == 1, inner, outer), jnp.where(odd == 1, outer, inner)

    lag_count = plan.momenta * BRANCH
    lag_rows = -(-lag_count // 16) * 16
    couple = coupling.reshape(plan.pairs_dev, BRANCH, ORB, ORB)
    couple = jnp.pad(couple, ((0, 0), (0, 0), (0, 16 - ORB), (0, FREQ - ORB)))
    phonon = phonon_green.reshape(plan.momenta, plan.pairs_dev, BRANCH, FREQ)
    phonon = jnp.moveaxis(phonon, 1, 0).reshape(plan.pairs_dev, lag_count, FREQ)
    phonon = jnp.pad(phonon, ((0, 0), (0, lag_rows - lag_count), (0, 0)))
    table = jnp.concatenate([couple.reshape(plan.pairs_dev, BRANCH * 16, FREQ), phonon], axis=1)
    table = lax.dynamic_slice_in_dim(table, me * plan.sub, plan.sub, axis=0)
    tables = [table]
    for d in range(1, plan.n_groups):
        tables.append(swap_groups(table, functools.partial(lambda d, g: g ^ d, d)))
    sand, toep = call(
        plan,
        prep_kernel,
        [
            shape((plan.own, 2, 2 * LANES, BRANCH * 2 * LANES), BF16),
            shape((plan.own, plan.momenta, BRANCH * FREQ, 2 * FREQ), BF16),
        ],
        jnp.concatenate(tables, axis=0),
    )

    chunk = max(1, 256 // plan.pairs)
    source = (jnp.arange(chunk)[:, None] * plan.pairs + partner[None, :]).reshape(-1)
    take = (source[:, None] == jnp.arange(chunk * plan.pairs)[None, :]).astype(BF16)
    partner_wire = call(
        plan,
        pack_partner_kernel,
        wire,
        take,
        lesser_green,
        out_specs=ANY,
        scratch=staging + [pltpu.VMEM(lesser_green.shape, BF16)],
    )
    own, before, after = [], [], []
    for k in every:
        blocks = exchange(pack_own(k))
        if k == 0:
            blocks, partner_wire = lax.optimization_barrier((blocks, partner_wire))
        else:
            blocks, sand, toep = lax.optimization_barrier((blocks, sand, toep))
        ahead, behind = neighbours(blocks)
        own.append(blocks)
        before.append(ahead)
        after.append(behind)

    half_wire = shape((half_peers, plan.rows, LANES), BF16)
    late = call(plan, self_late_kernel, half_wire, *own, toep, sand)
    late, before[0], partner_wire = lax.optimization_barrier((late, before[0], partner_wire))
    partner_blocks = exchange(partner_wire)
    sigma = call(plan, self_early_kernel, wire, *own, *before, toep, sand, late)
    arrived = exchange(sigma)

    scale = (plan.momenta * n_energy * plan.steps * COMP) ** -0.5
    early = call(
        plan,
        phonon_early_kernel,
        shape((plan.own, lag_count, LANES), F32),
        *own,
        partner_blocks,
        sand,
    )
    side_rows = plan.mom_dev * BRANCH
    parts = list(call(
        plan,
        functools.partial(phonon_late_kernel, scale=scale),
        [shape((plan.sub, side_rows, LANES), F32)] * (plan.n_groups * n_mom),
        *own,
        *after,
        partner_blocks,
        sand,
        early,
        scratch=[pltpu.VMEM((plan.own, n_mom, side_rows, LANES), F32)],
    ))
    for d in range(plan.n_groups):
        for t in range(n_mom):
            if d or t:
                route = []
                for e in range(n_energy):
                    g, j = divmod(e, plan.group)
                    for m in range(n_mom):
                        route.append((e * n_mom + m, ((g ^ d) * plan.group + j) * n_mom + (m ^ t)))
                parts[d * n_mom + t] = lax.ppermute(parts[d * n_mom + t], axes, route)
    phonon_self = call(
        plan, collect_kernel, shape((plan.mom_dev, plan.pairs_dev, BRANCH * FREQ), F32), *parts
    )

    self_energy = call(
        plan,
        unpack_kernel,
        shape(lesser_green.shape, BF16),
        arrived,
        out_specs=ANY,
        scratch=tile_scratch,
    )
    return self_energy, phonon_self


def solution(mesh):
    in_specs = (P("mom", "energy", None, None), P(), P(None, "energy", None), P("energy", None))
    out_specs = (P("mom", "energy", None, None), P("mom", "energy", None))
    return jax.shard_map(shards, mesh=mesh, in_specs=in_specs, out_specs=out_specs, check_vma=False)
```

```python
import functools

import jax
import jax.numpy as jnp
from jax import lax
from jax.experimental import pallas as pl
from jax.experimental.pallas import tpu as pltpu
from jax.sharding import PartitionSpec as P

ORB = 12
BRANCH = 3
FREQ = 64
COMP = 288
SQUARE = ORB * ORB
LANES = 128
REST = SQUARE - LANES
TAIL = 2 * REST
SLOTS = LANES // TAIL
TILE = 16
SMALL_GRANT = 16 * 1024 * 1024
LARGE_GRANT = 60 * 1024 * 1024
LONG = 100_000_000_000

BF16 = jnp.bfloat16
F32 = jnp.float32
I32 = jnp.int32


class Plan:
    def __init__(self, green, phonon, n_energy, n_mom):
        self.n_energy, self.n_mom = n_energy, n_mom
        self.mom_dev, self.steps, self.pairs, _ = green.shape
        self.momenta = self.mom_dev * n_mom
        self.pairs_dev = phonon.shape[1]
        self.half = FREQ // self.steps
        self.group = 2 * self.half
        self.n_groups = n_energy // self.group
        self.peers = self.group * n_mom
        self.sub = self.pairs_dev // n_mom
        self.own = self.n_groups * self.sub
        self.main_rows = self.own * 2 * self.steps
        self.tail_rows = self.mom_dev * self.own // SLOTS * self.steps
        self.rows = self.mom_dev * self.main_rows + self.tail_rows
        assert self.half * self.steps == FREQ and n_energy % self.group == 0
        assert self.pairs_dev % n_mom == 0 and self.group * self.pairs_dev == TILE
        assert self.mom_dev * self.own % SLOTS == 0 and self.n_groups % 2 == 0

    def main_row(self, k, u):
        return (k * self.own + u) * 2 * self.steps

    def tail_row(self, k, u):
        return (k * self.own + u) // SLOTS * self.steps

    def spots(self, refs, k, u):
        if len(refs) == 1:
            return refs[0], self.main_row(k, u), refs[0], self.mom_dev * self.main_rows + self.tail_row(k, u)
        return refs[k], self.main_row(0, u), refs[-1], self.main_rows + self.tail_row(k, u)

    def shift(self, k):
        return k * self.own % SLOTS * TAIL

    def place(self, h, i):
        j, rest = divmod(i, self.pairs_dev)
        m, b = divmod(rest, self.sub)
        return j * self.n_mom + m, h * self.sub + b


def dot(a, b):
    return lax.dot_general(a, b, (((1,), (0,)), ((), ())), preferred_element_type=F32)


def dot_nt(a, b):
    return lax.dot_general(a, b, (((1,), (1,)), ((), ())), preferred_element_type=F32)


def iota(dims, axis):
    return lax.broadcasted_iota(I32, dims, axis)


def swap_matrix(outer, inner, flip=False):
    n = outer * inner
    row, col = iota((n, n), 0), iota((n, n), 1)
    place = row & (outer - 1)
    source = (outer - 1 - place if flip else place) * inner + (row >> (outer.bit_length() - 1))
    return (col == source).astype(F32).astype(BF16)


def to_wire(rows):
    tail = jnp.concatenate([rows[:, LANES:SQUARE], rows[:, SQUARE + LANES :]], axis=1)
    return rows[:, :LANES], rows[:, SQUARE : SQUARE + LANES], tail


def pack_rows(plan, load, out_ref, stage, sems, momenta, tail_momenta, flip=False):
    swap = swap_matrix(plan.steps, TILE, flip)
    tails, copies = {}, []

    def send(first, count):
        rows = slice(first, first + count)
        copy = pltpu.make_async_copy(stage.at[:, rows, :], out_ref.at[:, rows, :], sems.at[len(copies)])
        copy.start()
        copies.append(copy)

    for k in sorted({*momenta, *tail_momenta}):
        for h in range(plan.pairs // TILE):
            left, right, tail = to_wire(dot(swap, load(k, h)).astype(BF16))
            for i in range(TILE):
                peer, u = plan.place(h, i)
                here = slice(i * plan.steps, (i + 1) * plan.steps)
                tails[peer, k * plan.own + u] = tail[here]
                if k in momenta:
                    row = plan.main_row(momenta.index(k), u)
                    stage[peer, row : row + plan.steps, :] = left[here]
                    stage[peer, row + plan.steps : row + 2 * plan.steps, :] = right[here]
            if k in momenta:
                send(plan.main_row(momenta.index(k), h * plan.sub), plan.sub * 2 * plan.steps)
    if tail_momenta:
        base = len(momenta) * plan.main_rows
        for peer in range(plan.peers):
            for first in range(0, plan.mom_dev * plan.own, SLOTS):
                row = base + first // SLOTS * plan.steps
                joined = jnp.concatenate([tails[peer, first + t] for t in range(SLOTS)], axis=1)
                stage[peer, row : row + plan.steps, :] = joined
        send(base, plan.tail_rows)
    for copy in copies:
        copy.wait()


def pack_own_kernel(plan, green_ref, out_ref, stage, out_sems, tiles, sems, *, momenta, tail_momenta):
    copies = {}
    for k in sorted({*momenta, *tail_momenta}):
        for h in range(plan.pairs // TILE):
            copies[k, h] = pltpu.make_async_copy(
                green_ref.at[k, :, TILE * h : TILE * (h + 1), :], tiles.at[k, h], sems.at[k, h]
            )
            copies[k, h].start()

    def load(k, h):
        copies[k, h].wait()
        return tiles[k, h].reshape(plan.steps * TILE, COMP)

    pack_rows(plan, load, out_ref, stage, out_sems, momenta, tail_momenta)


def pack_partner_kernel(plan, take_ref, green_ref, out_ref, stage, out_sems, taken):
    chunk = take_ref.shape[0] // plan.pairs
    take = take_ref[...]
    for k in range(plan.mom_dev):
        for e in range(0, plan.steps, chunk):
            rows = green_ref[k, e : e + chunk].reshape(chunk * plan.pairs, COMP)
            taken[k, e : e + chunk] = dot(take, rows).astype(BF16).reshape(chunk, plan.pairs, COMP)

    def load(k, h):
        return taken[k, :, TILE * h : TILE * (h + 1), :].reshape(plan.steps * TILE, COMP)

    every = list(range(plan.mom_dev))
    pack_rows(plan, load, out_ref, stage, out_sems, every, every, flip=True)


def each_pair(plan, body):
    if plan.own <= 2:
        for u in range(plan.own):
            body(u)
    else:
        lax.fori_loop(0, plan.own, lambda u, _: body(u), None)


def rows_at(row, count):
    return pl.ds(row if isinstance(row, int) else pl.multiple_of(row, count), count)


def prep_kernel(plan, tables_ref, sand_ref, toep_ref):
    group = lax.axis_index("energy") // plan.group
    place, want = iota((2 * LANES, 16), 0), iota((2 * LANES, 16), 1)
    mirror = iota((FREQ, 2 * FREQ), 0) + iota((FREQ, 2 * FREQ), 1) == FREQ
    mirror = mirror.astype(F32).astype(BF16)

    def body(u):
        source = (u // plan.sub ^ group) * plan.sub + u % plan.sub
        table = tables_ref[source]
        couple = table[: BRANCH * 16, :16]
        for h in range(2):
            comp = jnp.where(place < LANES, place, place - (u % SLOTS * TAIL + h * REST))
            valid = (place < LANES) | ((comp >= LANES) & (comp < SQUARE))
            quotient = (comp * 171) >> 11
            first = (valid & (quotient == want)).astype(F32).astype(BF16)
            second = (valid & (comp - ORB * quotient == want)).astype(F32).astype(BF16)
            left = dot_nt(couple, first).astype(BF16)
            right = dot_nt(couple, second).astype(BF16)
            for i in range(BRANCH):
                rows = slice(16 * i, 16 * i + 16)
                product = dot(first, left[rows]) * dot(second, right[rows])
                sand_ref[u, h, :, 2 * LANES * i : 2 * LANES * (i + 1)] = product.astype(BF16)
        lags = dot(table[BRANCH * 16 :, :], mirror)
        for q in range(plan.momenta):
            for i in range(BRANCH):
                n = q * BRANCH + i
                band = jnp.broadcast_to(lags[n : n + 1], (FREQ, 2 * FREQ))
                band = pltpu.roll(band, 0, 1, stride=1, stride_axis=0)
                toep_ref[u, q, i * FREQ : (i + 1) * FREQ, :] = band.astype(BF16)

    each_pair(plan, body)


def gather_rows(plan, refs, u, y, first, flip=False):
    m, k = divmod(y, plan.mom_dev)
    ref, row, tail_ref, tail = plan.spots(refs, k, u)
    order = range(plan.half)
    lefts, rights, tails = [], [], []
    for j in reversed(order) if flip else order:
        peer = (first + j) * plan.n_mom + m
        lefts.append(ref[peer, rows_at(row, plan.steps), :])
        rights.append(ref[peer, rows_at(row + plan.steps, plan.steps), :])
        tails.append(tail_ref[peer, rows_at(tail, plan.steps), :])
    tails = jnp.concatenate(tails, axis=0)
    if plan.shift(k):
        tails = pltpu.roll(tails.astype(F32), LANES - plan.shift(k), 1).astype(BF16)
    return jnp.concatenate([jnp.concatenate(lefts, axis=0), jnp.concatenate(rights, axis=0), tails], axis=1)


def half_and_tail(rows, h):
    return jnp.concatenate([rows[:, h * LANES : (h + 1) * LANES], rows[:, 2 * LANES :]], axis=1)


def self_block(plan, u, green, toep_ref, sand_ref, out_ref):
    summed = []
    for i in range(BRANCH):
        rows = slice(i * FREQ, (i + 1) * FREQ)
        band = jnp.concatenate(
            [
                jnp.concatenate([toep_ref[u, (k - y) % plan.momenta, rows, :] for y in range(plan.momenta)], axis=1)
                for k in range(plan.momenta)
            ],
            axis=0,
        )
        summed.append(dot(band, green).astype(BF16))
    left, right = [
        dot_nt(jnp.concatenate([half_and_tail(rows, h) for rows in summed], axis=1), sand_ref[u, h])
        for h in range(2)
    ]
    tails = left[:, LANES:] + right[:, LANES:]
    left, right = left[:, :LANES].astype(BF16), right[:, :LANES].astype(BF16)
    for y in range(plan.momenta):
        m, k = divmod(y, plan.mom_dev)
        _, row, _, tail = plan.spots([out_ref], k, u)
        rest = tails[y * FREQ : (y + 1) * FREQ]
        if plan.shift(k):
            rest = pltpu.roll(rest, plan.shift(k), 1)
        rest = rest.astype(BF16)
        for j in range(plan.half):
            peer = j * plan.n_mom + m
            here = slice(j * plan.steps, (j + 1) * plan.steps)
            there = slice(y * FREQ + j * plan.steps, y * FREQ + (j + 1) * plan.steps)
            out_ref[peer, rows_at(row, plan.steps), :] = left[there]
            out_ref[peer, rows_at(row + plan.steps, plan.steps), :] = right[there]
            out_ref[peer, rows_at(tail, plan.steps), :] += rest[here]


def clear_tails(plan, out_ref):
    for peer in range(plan.half * plan.n_mom):
        out_ref[peer, plan.rows - plan.tail_rows :, :] = jnp.zeros((plan.tail_rows, LANES), BF16)


def self_late_kernel(plan, *refs):
    own, (toep_ref, sand_ref, out_ref) = refs[: plan.mom_dev], refs[plan.mom_dev :]
    clear_tails(plan, out_ref)

    def body(u):
        green = [gather_rows(plan, own, u, y, first) for y in range(plan.momenta) for first in (0, plan.half)]
        self_block(plan, u, jnp.concatenate(green, axis=0), toep_ref, sand_ref, out_ref)

    each_pair(plan, body)


def self_early_kernel(plan, *refs):
    own, far = refs[: plan.mom_dev], refs[plan.mom_dev : 2 * plan.mom_dev]
    toep_ref, sand_ref, late_ref, out_ref, stage, *halo, in_sems, out_sems = refs[2 * plan.mom_dev :]
    group = lax.axis_index("energy") // plan.group
    has = (group > 0).astype(F32).astype(BF16)
    near = plan.half * plan.n_mom
    loads = [pltpu.make_async_copy(far[k], halo[k], in_sems.at[k]) for k in range(plan.mom_dev)]
    for copy in loads:
        copy.start()
    upper = pltpu.make_async_copy(late_ref, out_ref.at[near:], out_sems.at[0])
    upper.start()
    clear_tails(plan, stage)
    for copy in loads:
        copy.wait()

    def body(u):
        green = []
        for y in range(plan.momenta):
            green.append(gather_rows(plan, halo, u, y, 0) * has)
            green.append(gather_rows(plan, own, u, y, 0))
        self_block(plan, u, jnp.concatenate(green, axis=0), toep_ref, sand_ref, stage)

    each_pair(plan, body)
    lower = pltpu.make_async_copy(stage, out_ref.at[:near], out_sems.at[1])
    lower.start()
    lower.wait()
    upper.wait()


def lag_sums(plan, u, partner, green, sand_ref, store):
    partner, green = jnp.concatenate(partner, axis=0), jnp.concatenate(green, axis=0)
    left, right = [dot(half_and_tail(partner, h), sand_ref[u, h]) for h in range(2)]
    for i in range(BRANCH):
        here = slice(2 * LANES * i, 2 * LANES * i + LANES)
        rest = slice(2 * LANES * i + LANES, 2 * LANES * (i + 1))
        applied = jnp.concatenate([left[:, here], right[:, here], left[:, rest] + right[:, rest]], axis=1)
        lagged = dot_nt(applied.astype(BF16), green)
        for q in range(plan.momenta):
            acc = None
            for k in range(plan.momenta):
                y = (k + q) % plan.momenta
                part = lagged[k * FREQ : (k + 1) * FREQ, y * 2 * FREQ : (y + 1) * 2 * FREQ]
                acc = part if acc is None else acc + part
            acc = pltpu.roll(acc, FREQ + 1, 1, stride=1, stride_axis=0)
            store(q, i, jnp.sum(acc, axis=0, keepdims=True))


def phonon_early_kernel(plan, *refs):
    own, (partner_ref, sand_ref, out_ref) = refs[: plan.mom_dev], refs[plan.mom_dev :]

    def body(u):
        partner = [gather_rows(plan, [partner_ref], u, k, 0, flip=True) for k in range(plan.momenta)]
        green = [gather_rows(plan, own, u, y, first) for y in range(plan.momenta) for first in (0, plan.half)]

        def store(q, i, lags):
            out_ref[u, q * BRANCH + i : q * BRANCH + i + 1, :] = lags

        lag_sums(plan, u, partner, green, sand_ref, store)

    each_pair(plan, body)


def phonon_late_kernel(plan, *refs, scale):
    own, halo = refs[: plan.mom_dev], refs[plan.mom_dev : 2 * plan.mom_dev]
    partner_ref, sand_ref, early_ref, *refs = refs[2 * plan.mom_dev :]
    outs, sums = refs[:-1], refs[-1]
    group = lax.axis_index("energy") // plan.group
    me = lax.axis_index("mom")
    has = (group < plan.n_groups - 1).astype(F32).astype(BF16)

    def body(u):
        partner = [gather_rows(plan, [partner_ref], u, k, plan.half, flip=True) for k in range(plan.momenta)]
        green = []
        for y in range(plan.momenta):
            green.append(gather_rows(plan, own, u, y, plan.half))
            green.append(gather_rows(plan, halo, u, y, 0) * has)

        def store(q, i, lags):
            n = q * BRANCH + i
            side, row = divmod(n, plan.mom_dev * BRANCH)
            sums[u, side, row : row + 1, :] = (lags + early_ref[u, n : n + 1, :]) * scale

        lag_sums(plan, u, partner, green, sand_ref, store)

    each_pair(plan, body)
    for d in range(plan.n_groups):
        for t in range(plan.n_mom):
            for b in range(plan.sub):
                outs[d * plan.n_mom + t][b] = sums[(group ^ d) * plan.sub + b, me ^ t]


def collect_kernel(plan, *refs):
    parts, out_ref = refs[:-1], refs[-1]
    me = lax.axis_index("mom")
    for d in range(plan.n_mom):
        total = sum(ref[...] for ref in parts[d :: plan.n_mom])
        for b in range(plan.sub):
            pair = (me ^ d) * plan.sub + b
            for q in range(plan.mom_dev):
                rows = [total[b, q * BRANCH + i : q * BRANCH + i + 1, :FREQ] for i in range(BRANCH)]
                out_ref[q, pl.ds(pair, 1), :] = jnp.concatenate(rows, axis=1)


def unpack_kernel(plan, wire, out_ref, tiles, sems):
    swap = swap_matrix(TILE, plan.steps)
    copies = []
    for k in range(plan.mom_dev):
        for h in range(plan.pairs // TILE):
            lefts, rights, tails = [], [], []
            for i in range(TILE):
                peer, u = plan.place(h, i)
                _, row, _, tail = plan.spots([wire], k, u)
                lefts.append(wire[peer, row : row + plan.steps, :])
                rights.append(wire[peer, row + plan.steps : row + 2 * plan.steps, :])
                lane = (k * plan.own + u) % SLOTS * TAIL
                tails.append(wire[peer, tail : tail + plan.steps, :][:, lane : lane + TAIL])
            rows = jnp.concatenate([jnp.concatenate(part, axis=0) for part in (lefts, rights, tails)], axis=1)
            moved = dot(swap, rows).astype(BF16)
            left, right = moved[:, :LANES], moved[:, LANES : 2 * LANES]
            tail = moved[:, 2 * LANES :]
            moved = jnp.concatenate([left, tail[:, :REST], right, tail[:, REST:]], axis=1)
            tiles[k, h] = moved.reshape(plan.steps, TILE, COMP)
            copy = pltpu.make_async_copy(
                tiles.at[k, h], out_ref.at[k, :, TILE * h : TILE * (h + 1), :], sems.at[k, h]
            )
            copy.start()
            copies.append(copy)
    for copy in copies:
        copy.wait()


ANY = pl.BlockSpec(memory_space=pl.ANY)
HBM = pl.BlockSpec(memory_space=pltpu.HBM)
VMEM = pl.BlockSpec(memory_space=pltpu.VMEM)


def call(plan, kernel, out_shape, *args, in_specs=None, out_specs=None, scratch=(), flops=1, grant=None):
    outs = jax.tree.map(lambda _: VMEM, out_shape)
    return pl.pallas_call(
        functools.partial(kernel, plan),
        out_shape=out_shape,
        in_specs=in_specs or [VMEM] * len(args),
        out_specs=out_specs or outs,
        scratch_shapes=list(scratch),
        compiler_params=pltpu.CompilerParams(vmem_limit_bytes=grant or SMALL_GRANT * max(1, plan.own // 4)),
        cost_estimate=pl.CostEstimate(flops=flops, bytes_accessed=1, transcendentals=0),
    )(*args)


def shape(dims, dtype):
    return jax.ShapeDtypeStruct(dims, dtype)


def in_hbm(struct):
    return pltpu.HBM(struct.shape, struct.dtype)


def shards(lesser_green, partner, phonon_green, coupling):
    n_energy, n_mom = lax.axis_size("energy"), lax.axis_size("mom")
    plan = Plan(lesser_green, phonon_green, n_energy, n_mom)
    axes = ("energy", "mom")
    me = lax.axis_index("mom")
    s = lax.axis_index("energy") // plan.group
    wire = shape((plan.peers, plan.rows, LANES), BF16)
    half_peers = plan.half * n_mom
    groups = [[g * plan.peers + i for i in range(plan.peers)] for g in range(plan.n_groups)]
    tiles = (plan.mom_dev, plan.pairs // TILE)

    def exchange(blocks):
        return lax.all_to_all(blocks, axes, split_axis=0, concat_axis=0, axis_index_groups=groups, tiled=True)

    def swap_groups(values, other):
        route = []
        for e in range(n_energy):
            g, j = divmod(e, plan.group)
            to = other(g) if 0 <= other(g) < plan.n_groups else g
            route.append((e, to * plan.group + j))
        return lax.ppermute(values, "energy", route)

    staging = [pltpu.VMEM(wire.shape, BF16), pltpu.SemaphoreType.DMA((tiles[0] * tiles[1] + 1,))]
    tile_scratch = [pltpu.VMEM(tiles + (plan.steps, TILE, COMP), BF16), pltpu.SemaphoreType.DMA(tiles)]
    every = list(range(plan.mom_dev))

    def pack_own(k):
        last = k == every[-1]
        rows = plan.main_rows + (plan.tail_rows if last else 0)
        return call(
            plan,
            functools.partial(pack_own_kernel, momenta=[k], tail_momenta=every if last else []),
            in_hbm(shape((plan.peers, rows, LANES), BF16)),
            lesser_green,
            in_specs=[HBM],
            out_specs=HBM,
            scratch=[pltpu.VMEM((plan.peers, rows, LANES), BF16), staging[1]] + tile_scratch,
            grant=LARGE_GRANT,
        )

    odd = s % 2

    def neighbours(blocks):
        def edge(side):
            return lax.dynamic_slice_in_dim(blocks, side * half_peers, half_peers, axis=0)

        inner = swap_groups(edge(1 - odd), lambda g: g ^ 1)
        if plan.n_groups == 2:
            return inner, inner
        outer = swap_groups(edge(odd), lambda g: ((g - 1) ^ 1) + 1)
        return jnp.where(odd == 1, inner, outer), jnp.where(odd == 1, outer, inner)

    lag_count = plan.momenta * BRANCH
    lag_rows = -(-lag_count // 16) * 16
    couple = coupling.reshape(plan.pairs_dev, BRANCH, ORB, ORB)
    couple = jnp.pad(couple, ((0, 0), (0, 0), (0, 16 - ORB), (0, FREQ - ORB)))
    phonon = phonon_green.reshape(plan.momenta, plan.pairs_dev, BRANCH, FREQ)
    phonon = jnp.moveaxis(phonon, 1, 0).reshape(plan.pairs_dev, lag_count, FREQ)
    phonon = jnp.pad(phonon, ((0, 0), (0, lag_rows - lag_count), (0, 0)))
    table = jnp.concatenate([couple.reshape(plan.pairs_dev, BRANCH * 16, FREQ), phonon], axis=1)
    table = lax.dynamic_slice_in_dim(table, me * plan.sub, plan.sub, axis=0)
    tables = [table]
    for d in range(1, plan.n_groups):
        tables.append(swap_groups(table, functools.partial(lambda d, g: g ^ d, d)))
    tables = jnp.concatenate(tables, axis=0)

    chunk = max(1, 256 // plan.pairs)
    source = (jnp.arange(chunk)[:, None] * plan.pairs + partner[None, :]).reshape(-1)
    take = (source[:, None] == jnp.arange(chunk * plan.pairs)[None, :]).astype(BF16)
    partner_wire = call(
        plan,
        pack_partner_kernel,
        in_hbm(wire),
        take,
        lesser_green,
        out_specs=HBM,
        scratch=staging + [pltpu.VMEM(lesser_green.shape, BF16)],
    )
    own, before, after = [], [], []
    for k in every:
        blocks = exchange(pack_own(k))
        if k == every[-1]:
            blocks, sand, toep, partner_wire = lax.optimization_barrier((blocks, sand, toep, partner_wire))
        ahead, behind = neighbours(blocks)
        if k == 0:
            ahead, behind, tables = lax.optimization_barrier((ahead, behind, tables))
            sand, toep = call(
                plan,
                prep_kernel,
                [
                    shape((plan.own, 2, 2 * LANES, BRANCH * 2 * LANES), BF16),
                    shape((plan.own, plan.momenta, BRANCH * FREQ, 2 * FREQ), BF16),
                ],
                tables,
                flops=LONG,
            )
        own.append(blocks)
        before.append(ahead)
        after.append(behind)

    half_wire = shape((half_peers, plan.rows, LANES), BF16)
    late = call(plan, self_late_kernel, half_wire, *own, toep, sand, flops=LONG)
    partner_blocks = exchange(partner_wire)
    sigma = call(
        plan,
        self_early_kernel,
        in_hbm(wire),
        *own,
        *before,
        toep,
        sand,
        late,
        in_specs=[VMEM] * len(own) + [ANY] * len(before) + [VMEM] * 3,
        out_specs=HBM,
        scratch=[pltpu.VMEM(half_wire.shape, BF16)]
        + [pltpu.VMEM((half_peers,) + b.shape[1:], BF16) for b in before]
        + [pltpu.SemaphoreType.DMA((len(before),)), pltpu.SemaphoreType.DMA((2,))],
        flops=LONG,
    )
    arrived = exchange(sigma)

    scale = (plan.momenta * n_energy * plan.steps * COMP) ** -0.5
    early = call(
        plan,
        phonon_early_kernel,
        shape((plan.own, lag_count, LANES), F32),
        *own,
        partner_blocks,
        sand,
    )
    side_rows = plan.mom_dev * BRANCH
    parts = list(call(
        plan,
        functools.partial(phonon_late_kernel, scale=scale),
        [shape((plan.sub, side_rows, LANES), F32)] * (plan.n_groups * n_mom),
        *own,
        *after,
        partner_blocks,
        sand,
        early,
        scratch=[pltpu.VMEM((plan.own, n_mom, side_rows, LANES), F32)],
    ))
    for d in range(plan.n_groups):
        for t in range(n_mom):
            if d or t:
                route = []
                for e in range(n_energy):
                    g, j = divmod(e, plan.group)
                    for m in range(n_mom):
                        route.append((e * n_mom + m, ((g ^ d) * plan.group + j) * n_mom + (m ^ t)))
                parts[d * n_mom + t] = lax.ppermute(parts[d * n_mom + t], axes, route)
    phonon_self = call(
        plan, collect_kernel, shape((plan.mom_dev, plan.pairs_dev, BRANCH * FREQ), F32), *parts
    )

    self_energy = call(
        plan,
        unpack_kernel,
        shape(lesser_green.shape, BF16),
        arrived,
        out_specs=ANY,
        scratch=tile_scratch,
    )
    return self_energy, phonon_self


def solution(mesh):
    in_specs = (P("mom", "energy", None, None), P(), P(None, "energy", None), P("energy", None))
    out_specs = (P("mom", "energy", None, None), P("mom", "energy", None))
    return jax.shard_map(shards, mesh=mesh, in_specs=in_specs, out_specs=out_specs, check_vma=False)
```

```python
import functools

import jax
import jax.numpy as jnp
from jax import lax
from jax.experimental import pallas as pl
from jax.experimental.pallas import tpu as pltpu
from jax.sharding import PartitionSpec as P

ORB = 12
BRANCH = 3
FREQ = 64
COMP = 288
SQUARE = ORB * ORB
LANES = 128
REST = SQUARE - LANES
TAIL = 2 * REST
SLOTS = LANES // TAIL
TILE = 16
SMALL_GRANT = 16 * 1024 * 1024
LARGE_GRANT = 60 * 1024 * 1024
LONG = 100_000_000_000

BF16 = jnp.bfloat16
F32 = jnp.float32
I32 = jnp.int32


class Plan:
    def __init__(self, green, phonon, n_energy, n_mom):
        self.n_energy, self.n_mom = n_energy, n_mom
        self.mom_dev, self.steps, self.pairs, _ = green.shape
        self.momenta = self.mom_dev * n_mom
        self.pairs_dev = phonon.shape[1]
        self.half = FREQ // self.steps
        self.group = 2 * self.half
        self.n_groups = n_energy // self.group
        self.peers = self.group * n_mom
        self.sub = self.pairs_dev // n_mom
        self.own = self.n_groups * self.sub
        self.main_rows = self.mom_dev * self.own * 2 * self.steps
        self.tail_rows = self.mom_dev * self.own // SLOTS * self.steps
        self.rows = self.main_rows + self.tail_rows
        assert self.half * self.steps == FREQ and n_energy % self.group == 0
        assert self.peers & (self.peers - 1) == 0 and self.n_groups & (self.n_groups - 1) == 0
        assert self.pairs_dev % n_mom == 0 and self.group * self.pairs_dev == TILE
        assert self.mom_dev * self.own % SLOTS == 0 and self.n_groups % 2 == 0

    def main_row(self, k, u):
        return (k * self.own + u) * 2 * self.steps

    def tail_row(self, k, u):
        return self.main_rows + (k * self.own + u) // SLOTS * self.steps

    def shift(self, k):
        return k * self.own % SLOTS * TAIL

    def place(self, h, i):
        j, rest = divmod(i, self.pairs_dev)
        m, b = divmod(rest, self.sub)
        return j * self.n_mom + m, h * self.sub + b


def dot(a, b):
    return lax.dot_general(a, b, (((1,), (0,)), ((), ())), preferred_element_type=F32)


def dot_nt(a, b):
    return lax.dot_general(a, b, (((1,), (1,)), ((), ())), preferred_element_type=F32)


def iota(dims, axis):
    return lax.broadcasted_iota(I32, dims, axis)


def swap_matrix(outer, inner, flip=False):
    n = outer * inner
    row, col = iota((n, n), 0), iota((n, n), 1)
    place = row & (outer - 1)
    source = (outer - 1 - place if flip else place) * inner + (row >> (outer.bit_length() - 1))
    return (col == source).astype(F32).astype(BF16)


def to_wire(rows):
    tail = jnp.concatenate([rows[:, LANES:SQUARE], rows[:, SQUARE + LANES :]], axis=1)
    return rows[:, :LANES], rows[:, SQUARE : SQUARE + LANES], tail


def pack_rows(plan, load, stage, flip=False, packed=None):
    swap = swap_matrix(plan.steps, TILE, flip)
    tails = {}
    for k in range(plan.mom_dev):
        for h in range(plan.pairs // TILE):
            left, right, tail = to_wire(dot(swap, load(k, h)).astype(BF16))
            for i in range(TILE):
                peer, u = plan.place(h, i)
                here = slice(i * plan.steps, (i + 1) * plan.steps)
                row = plan.main_row(k, u)
                stage[peer, row : row + plan.steps, :] = left[here]
                stage[peer, row + plan.steps : row + 2 * plan.steps, :] = right[here]
                tails[peer, k * plan.own + u] = tail[here]
            if packed is not None:
                packed(plan.main_row(k, h * plan.sub), plan.sub * 2 * plan.steps)
    for peer in range(plan.peers):
        for first in range(0, plan.mom_dev * plan.own, SLOTS):
            row = plan.main_rows + first // SLOTS * plan.steps
            joined = jnp.concatenate([tails[peer, first + t] for t in range(SLOTS)], axis=1)
            stage[peer, row : row + plan.steps, :] = joined
    if packed is not None:
        packed(plan.main_rows, plan.tail_rows)


def my_seat(plan):
    return lax.axis_index("energy") % plan.group * plan.n_mom + lax.axis_index("mom")


def pack_own_kernel(plan, green_ref, *refs):
    outs, (stage, tiles, sems) = refs[: plan.peers], refs[plan.peers :]
    copies = {}
    for k in range(plan.mom_dev):
        for h in range(plan.pairs // TILE):
            copies[k, h] = pltpu.make_async_copy(
                green_ref.at[k, :, TILE * h : TILE * (h + 1), :], tiles.at[k, h], sems.at[k, h]
            )
            copies[k, h].start()

    def load(k, h):
        copies[k, h].wait()
        return tiles[k, h].reshape(plan.steps * TILE, COMP)

    pack_rows(plan, load, stage)
    seat = my_seat(plan)
    for d in range(plan.peers):
        outs[d][...] = stage[seat ^ d]


def gather_kernel(plan, *refs):
    parts, (own_ref, *edges) = refs[: plan.peers], refs[plan.peers :]
    seat = my_seat(plan)
    for d in range(plan.peers):
        own_ref[seat ^ d] = parts[d][...]
    near = plan.half * plan.n_mom
    odd = lax.axis_index("energy") // plan.group % 2
    for edge, side in zip(edges, (1 - odd, odd)):
        for i in range(near):
            edge[i] = own_ref[side * near + i]


def pack_partner_kernel(plan, take_ref, green_ref, out_ref, stage, sems, taken):
    chunk = take_ref.shape[0] // plan.pairs
    take = take_ref[...]
    for k in range(plan.mom_dev):
        for e in range(0, plan.steps, chunk):
            rows = green_ref[k, e : e + chunk].reshape(chunk * plan.pairs, COMP)
            taken[k, e : e + chunk] = dot(take, rows).astype(BF16).reshape(chunk, plan.pairs, COMP)

    def load(k, h):
        return taken[k, :, TILE * h : TILE * (h + 1), :].reshape(plan.steps * TILE, COMP)

    copies = []

    def packed(first, count):
        rows = slice(first, first + count)
        copy = pltpu.make_async_copy(stage.at[:, rows, :], out_ref.at[:, rows, :], sems.at[len(copies)])
        copy.start()
        copies.append(copy)

    pack_rows(plan, load, stage, flip=True, packed=packed)
    for copy in copies:
        copy.wait()


def each_pair(plan, body):
    if plan.own <= 2:
        for u in range(plan.own):
            body(u)
    else:
        lax.fori_loop(0, plan.own, lambda u, _: body(u), None)


def rows_at(row, count):
    return pl.ds(row if isinstance(row, int) else pl.multiple_of(row, count), count)


def prep_kernel(plan, tables_ref, sand_ref, toep_ref):
    group = lax.axis_index("energy") // plan.group
    place, want = iota((2 * LANES, 16), 0), iota((2 * LANES, 16), 1)
    mirror = iota((FREQ, 2 * FREQ), 0) + iota((FREQ, 2 * FREQ), 1) == FREQ
    mirror = mirror.astype(F32).astype(BF16)

    def body(u):
        source = (u // plan.sub ^ group) * plan.sub + u % plan.sub
        table = tables_ref[source]
        couple = table[: BRANCH * 16, :16]
        for h in range(2):
            comp = jnp.where(place < LANES, place, place - (u % SLOTS * TAIL + h * REST))
            valid = (place < LANES) | ((comp >= LANES) & (comp < SQUARE))
            quotient = (comp * 171) >> 11
            first = (valid & (quotient == want)).astype(F32).astype(BF16)
            second = (valid & (comp - ORB * quotient == want)).astype(F32).astype(BF16)
            left = dot_nt(couple, first).astype(BF16)
            right = dot_nt(couple, second).astype(BF16)
            for i in range(BRANCH):
                rows = slice(16 * i, 16 * i + 16)
                product = dot(first, left[rows]) * dot(second, right[rows])
                sand_ref[u, h, :, 2 * LANES * i : 2 * LANES * (i + 1)] = product.astype(BF16)
        lags = dot(table[BRANCH * 16 :, :], mirror)
        for q in range(plan.momenta):
            for i in range(BRANCH):
                n = q * BRANCH + i
                band = jnp.broadcast_to(lags[n : n + 1], (FREQ, 2 * FREQ))
                band = pltpu.roll(band, 0, 1, stride=1, stride_axis=0)
                toep_ref[u, q, i * FREQ : (i + 1) * FREQ, :] = band.astype(BF16)

    each_pair(plan, body)


def gather_rows(plan, ref, u, y, first, flip=False):
    m, k = divmod(y, plan.mom_dev)
    row, tail = plan.main_row(k, u), plan.tail_row(k, u)
    order = range(plan.half)
    lefts, rights, tails = [], [], []
    for j in reversed(order) if flip else order:
        peer = (first + j) * plan.n_mom + m
        lefts.append(ref[peer, rows_at(row, plan.steps), :])
        rights.append(ref[peer, rows_at(row + plan.steps, plan.steps), :])
        tails.append(ref[peer, rows_at(tail, plan.steps), :])
    tails = jnp.concatenate(tails, axis=0)
    if plan.shift(k):
        tails = pltpu.roll(tails.astype(F32), LANES - plan.shift(k), 1).astype(BF16)
    return jnp.concatenate([jnp.concatenate(lefts, axis=0), jnp.concatenate(rights, axis=0), tails], axis=1)


def half_and_tail(rows, h):
    return jnp.concatenate([rows[:, h * LANES : (h + 1) * LANES], rows[:, 2 * LANES :]], axis=1)


def self_block(plan, u, green, toep_ref, sand_ref, out_ref):
    summed = []
    for i in range(BRANCH):
        rows = slice(i * FREQ, (i + 1) * FREQ)
        band = jnp.concatenate(
            [
                jnp.concatenate([toep_ref[u, (k - y) % plan.momenta, rows, :] for y in range(plan.momenta)], axis=1)
                for k in range(plan.momenta)
            ],
            axis=0,
        )
        summed.append(dot(band, green).astype(BF16))
    left, right = [
        dot_nt(jnp.concatenate([half_and_tail(rows, h) for rows in summed], axis=1), sand_ref[u, h])
        for h in range(2)
    ]
    tails = left[:, LANES:] + right[:, LANES:]
    left, right = left[:, :LANES].astype(BF16), right[:, :LANES].astype(BF16)
    for y in range(plan.momenta):
        m, k = divmod(y, plan.mom_dev)
        row, tail = plan.main_row(k, u), plan.tail_row(k, u)
        rest = tails[y * FREQ : (y + 1) * FREQ]
        if plan.shift(k):
            rest = pltpu.roll(rest, plan.shift(k), 1)
        rest = rest.astype(BF16)
        for j in range(plan.half):
            peer = j * plan.n_mom + m
            here = slice(j * plan.steps, (j + 1) * plan.steps)
            there = slice(y * FREQ + j * plan.steps, y * FREQ + (j + 1) * plan.steps)
            out_ref[peer, rows_at(row, plan.steps), :] = left[there]
            out_ref[peer, rows_at(row + plan.steps, plan.steps), :] = right[there]
            out_ref[peer, rows_at(tail, plan.steps), :] += rest[here]


def clear_tails(plan, out_ref):
    for peer in range(plan.half * plan.n_mom):
        out_ref[peer, plan.main_rows :, :] = jnp.zeros((plan.tail_rows, LANES), BF16)


def self_late_kernel(plan, own, toep_ref, sand_ref, out_ref):
    clear_tails(plan, out_ref)

    def body(u):
        green = [gather_rows(plan, own, u, y, first) for y in range(plan.momenta) for first in (0, plan.half)]
        self_block(plan, u, jnp.concatenate(green, axis=0), toep_ref, sand_ref, out_ref)

    each_pair(plan, body)


def self_early_kernel(plan, own, halo, toep_ref, sand_ref, late_ref, *refs):
    outs, (stage,) = refs[: plan.peers], refs[plan.peers :]
    has = (lax.axis_index("energy") // plan.group > 0).astype(F32).astype(BF16)
    clear_tails(plan, stage)
    near = plan.half * plan.n_mom
    for i in range(near):
        stage[near + i] = late_ref[i]

    def body(u):
        green = []
        for y in range(plan.momenta):
            green.append(gather_rows(plan, halo, u, y, 0) * has)
            green.append(gather_rows(plan, own, u, y, 0))
        self_block(plan, u, jnp.concatenate(green, axis=0), toep_ref, sand_ref, stage)

    each_pair(plan, body)
    seat = my_seat(plan)
    for d in range(plan.peers):
        outs[d][...] = stage[seat ^ d]


def lag_sums(plan, u, partner, green, sand_ref, store):
    partner, green = jnp.concatenate(partner, axis=0), jnp.concatenate(green, axis=0)
    left, right = [dot(half_and_tail(partner, h), sand_ref[u, h]) for h in range(2)]
    for i in range(BRANCH):
        here = slice(2 * LANES * i, 2 * LANES * i + LANES)
        rest = slice(2 * LANES * i + LANES, 2 * LANES * (i + 1))
        applied = jnp.concatenate([left[:, here], right[:, here], left[:, rest] + right[:, rest]], axis=1)
        lagged = dot_nt(applied.astype(BF16), green)
        for q in range(plan.momenta):
            acc = None
            for k in range(plan.momenta):
                y = (k + q) % plan.momenta
                part = lagged[k * FREQ : (k + 1) * FREQ, y * 2 * FREQ : (y + 1) * 2 * FREQ]
                acc = part if acc is None else acc + part
            acc = pltpu.roll(acc, FREQ + 1, 1, stride=1, stride_axis=0)
            store(q, i, jnp.sum(acc, axis=0, keepdims=True))


def phonon_early_kernel(plan, own, partner_ref, sand_ref, out_ref):
    def body(u):
        partner = [gather_rows(plan, partner_ref, u, k, 0, flip=True) for k in range(plan.momenta)]
        green = [gather_rows(plan, own, u, y, first) for y in range(plan.momenta) for first in (0, plan.half)]

        def store(q, i, lags):
            out_ref[u, q * BRANCH + i : q * BRANCH + i + 1, :] = lags

        lag_sums(plan, u, partner, green, sand_ref, store)

    each_pair(plan, body)


def phonon_late_kernel(plan, own, halo, partner_ref, sand_ref, early_ref, *refs, scale):
    outs, sums = refs[:-1], refs[-1]
    group = lax.axis_index("energy") // plan.group
    me = lax.axis_index("mom")
    has = (group < plan.n_groups - 1).astype(F32).astype(BF16)

    def body(u):
        partner = [gather_rows(plan, partner_ref, u, k, plan.half, flip=True) for k in range(plan.momenta)]
        green = []
        for y in range(plan.momenta):
            green.append(gather_rows(plan, own, u, y, plan.half))
            green.append(gather_rows(plan, halo, u, y, 0) * has)

        def store(q, i, lags):
            n = q * BRANCH + i
            side, row = divmod(n, plan.mom_dev * BRANCH)
            sums[u, side, row : row + 1, :] = (lags + early_ref[u, n : n + 1, :]) * scale

        lag_sums(plan, u, partner, green, sand_ref, store)

    each_pair(plan, body)
    for d in range(plan.n_groups):
        for t in range(plan.n_mom):
            for b in range(plan.sub):
                outs[d * plan.n_mom + t][b] = sums[(group ^ d) * plan.sub + b, me ^ t]


def collect_kernel(plan, *refs):
    parts, out_ref = refs[:-1], refs[-1]
    me = lax.axis_index("mom")
    for d in range(plan.n_mom):
        total = sum(ref[...] for ref in parts[d :: plan.n_mom])
        for b in range(plan.sub):
            pair = (me ^ d) * plan.sub + b
            for q in range(plan.mom_dev):
                rows = [total[b, q * BRANCH + i : q * BRANCH + i + 1, :FREQ] for i in range(BRANCH)]
                out_ref[q, pl.ds(pair, 1), :] = jnp.concatenate(rows, axis=1)


def unpack_kernel(plan, *refs):
    parts, (out_ref, wire, tiles, sems) = refs[: plan.peers], refs[plan.peers :]
    seat = my_seat(plan)
    for d in range(plan.peers):
        wire[seat ^ d] = parts[d][...]
    swap = swap_matrix(TILE, plan.steps)
    copies = []
    for k in range(plan.mom_dev):
        for h in range(plan.pairs // TILE):
            lefts, rights, tails = [], [], []
            for i in range(TILE):
                peer, u = plan.place(h, i)
                row, tail = plan.main_row(k, u), plan.tail_row(k, u)
                lefts.append(wire[peer, row : row + plan.steps, :])
                rights.append(wire[peer, row + plan.steps : row + 2 * plan.steps, :])
                lane = (k * plan.own + u) % SLOTS * TAIL
                tails.append(wire[peer, tail : tail + plan.steps, :][:, lane : lane + TAIL])
            rows = jnp.concatenate([jnp.concatenate(part, axis=0) for part in (lefts, rights, tails)], axis=1)
            moved = dot(swap, rows).astype(BF16)
            left, right = moved[:, :LANES], moved[:, LANES : 2 * LANES]
            tail = moved[:, 2 * LANES :]
            moved = jnp.concatenate([left, tail[:, :REST], right, tail[:, REST:]], axis=1)
            tiles[k, h] = moved.reshape(plan.steps, TILE, COMP)
            copy = pltpu.make_async_copy(
                tiles.at[k, h], out_ref.at[k, :, TILE * h : TILE * (h + 1), :], sems.at[k, h]
            )
            copy.start()
            copies.append(copy)
    for copy in copies:
        copy.wait()


ANY = pl.BlockSpec(memory_space=pl.ANY)
HBM = pl.BlockSpec(memory_space=pltpu.HBM)
VMEM = pl.BlockSpec(memory_space=pltpu.VMEM)


def call(plan, kernel, out_shape, *args, in_specs=None, out_specs=None, scratch=(), flops=1, grant=None):
    outs = jax.tree.map(lambda _: VMEM, out_shape)
    return pl.pallas_call(
        functools.partial(kernel, plan),
        out_shape=out_shape,
        in_specs=in_specs or [VMEM] * len(args),
        out_specs=out_specs or outs,
        scratch_shapes=list(scratch),
        compiler_params=pltpu.CompilerParams(vmem_limit_bytes=grant or SMALL_GRANT * max(1, plan.own // 4)),
        cost_estimate=pl.CostEstimate(flops=flops, bytes_accessed=1, transcendentals=0),
    )(*args)


def shape(dims, dtype):
    return jax.ShapeDtypeStruct(dims, dtype)


def in_hbm(struct):
    return pltpu.HBM(struct.shape, struct.dtype)


def shards(lesser_green, partner, phonon_green, coupling):
    n_energy, n_mom = lax.axis_size("energy"), lax.axis_size("mom")
    plan = Plan(lesser_green, phonon_green, n_energy, n_mom)
    axes = ("energy", "mom")
    me = lax.axis_index("mom")
    s = lax.axis_index("energy") // plan.group
    wire = shape((plan.peers, plan.rows, LANES), BF16)
    half_peers = plan.half * n_mom
    groups = [[g * plan.peers + i for i in range(plan.peers)] for g in range(plan.n_groups)]
    tiles = (plan.mom_dev, plan.pairs // TILE)

    def exchange(blocks):
        return lax.all_to_all(blocks, axes, split_axis=0, concat_axis=0, axis_index_groups=groups, tiled=True)

    def swap_peers(parts):
        moved = [parts[0]]
        for d in range(1, plan.peers):
            route = [(i, i ^ d) for i in range(n_energy * n_mom)]
            moved.append(lax.ppermute(parts[d], axes, route))
        return moved

    def swap_groups(values, other):
        route = []
        for e in range(n_energy):
            g, j = divmod(e, plan.group)
            to = other(g) if 0 <= other(g) < plan.n_groups else g
            route.append((e, to * plan.group + j))
        return lax.ppermute(values, "energy", route)

    staging = [pltpu.VMEM(wire.shape, BF16), pltpu.SemaphoreType.DMA((tiles[0] * tiles[1] + 1,))]
    tile_scratch = [pltpu.VMEM(tiles + (plan.steps, TILE, COMP), BF16), pltpu.SemaphoreType.DMA(tiles)]
    block = shape((plan.rows, LANES), BF16)
    half_wire = shape((half_peers, plan.rows, LANES), BF16)
    parts = call(
        plan,
        pack_own_kernel,
        [block] * plan.peers,
        lesser_green,
        in_specs=[HBM],
        scratch=[pltpu.VMEM(wire.shape, BF16)] + tile_scratch,
        grant=LARGE_GRANT,
    )
    own, *edges = call(
        plan, gather_kernel, [wire] + [half_wire] * (1 if plan.n_groups == 2 else 2), *swap_peers(parts)
    )
    inner = swap_groups(edges[0], lambda g: g ^ 1)
    before = after = inner
    if plan.n_groups > 2:
        outer = swap_groups(edges[1], lambda g: ((g - 1) ^ 1) + 1)
        odd = s % 2
        before = jnp.where(odd == 1, inner, outer)
        after = jnp.where(odd == 1, outer, inner)

    lag_count = plan.momenta * BRANCH
    lag_rows = -(-lag_count // 16) * 16
    couple = coupling.reshape(plan.pairs_dev, BRANCH, ORB, ORB)
    couple = jnp.pad(couple, ((0, 0), (0, 0), (0, 16 - ORB), (0, FREQ - ORB)))
    phonon = phonon_green.reshape(plan.momenta, plan.pairs_dev, BRANCH, FREQ)
    phonon = jnp.moveaxis(phonon, 1, 0).reshape(plan.pairs_dev, lag_count, FREQ)
    phonon = jnp.pad(phonon, ((0, 0), (0, lag_rows - lag_count), (0, 0)))
    table = jnp.concatenate([couple.reshape(plan.pairs_dev, BRANCH * 16, FREQ), phonon], axis=1)
    table = lax.dynamic_slice_in_dim(table, me * plan.sub, plan.sub, axis=0)
    tables = [table]
    for d in range(1, plan.n_groups):
        tables.append(swap_groups(table, functools.partial(lambda d, g: g ^ d, d)))
    tables, own = lax.optimization_barrier((jnp.concatenate(tables, axis=0), own))
    sand, toep = call(
        plan,
        prep_kernel,
        [
            shape((plan.own, 2, 2 * LANES, BRANCH * 2 * LANES), BF16),
            shape((plan.own, plan.momenta, BRANCH * FREQ, 2 * FREQ), BF16),
        ],
        tables,
        flops=LONG,
    )
    chunk = max(1, 256 // plan.pairs)
    source = (jnp.arange(chunk)[:, None] * plan.pairs + partner[None, :]).reshape(-1)
    take = (source[:, None] == jnp.arange(chunk * plan.pairs)[None, :]).astype(BF16)
    take, sand = lax.optimization_barrier((take, sand))
    partner_wire = call(
        plan,
        pack_partner_kernel,
        in_hbm(wire),
        take,
        lesser_green,
        out_specs=HBM,
        scratch=staging + [pltpu.VMEM(lesser_green.shape, BF16)],
    )
    partner_blocks = exchange(partner_wire)

    late = call(plan, self_late_kernel, half_wire, own, toep, sand)
    sigma = call(
        plan,
        self_early_kernel,
        [block] * plan.peers,
        own,
        before,
        toep,
        sand,
        late,
        scratch=[pltpu.VMEM(wire.shape, BF16)],
        flops=LONG,
    )
    arrived = swap_peers(sigma)

    scale = (plan.momenta * n_energy * plan.steps * COMP) ** -0.5
    early = call(
        plan,
        phonon_early_kernel,
        shape((plan.own, lag_count, LANES), F32),
        own,
        partner_blocks,
        sand,
    )
    side_rows = plan.mom_dev * BRANCH
    parts = list(call(
        plan,
        functools.partial(phonon_late_kernel, scale=scale),
        [shape((plan.sub, side_rows, LANES), F32)] * (plan.n_groups * n_mom),
        own,
        after,
        partner_blocks,
        sand,
        early,
        scratch=[pltpu.VMEM((plan.own, n_mom, side_rows, LANES), F32)],
    ))
    for d in range(plan.n_groups):
        for t in range(n_mom):
            if d or t:
                route = []
                for e in range(n_energy):
                    g, j = divmod(e, plan.group)
                    for m in range(n_mom):
                        route.append((e * n_mom + m, ((g ^ d) * plan.group + j) * n_mom + (m ^ t)))
                parts[d * n_mom + t] = lax.ppermute(parts[d * n_mom + t], axes, route)
    phonon_self = call(
        plan, collect_kernel, shape((plan.mom_dev, plan.pairs_dev, BRANCH * FREQ), F32), *parts
    )

    self_energy = call(
        plan,
        unpack_kernel,
        shape(lesser_green.shape, BF16),
        *arrived,
        out_specs=ANY,
        scratch=[pltpu.VMEM(wire.shape, BF16)] + tile_scratch,
    )
    return self_energy, phonon_self


def solution(mesh):
    in_specs = (P("mom", "energy", None, None), P(), P(None, "energy", None), P("energy", None))
    out_specs = (P("mom", "energy", None, None), P("mom", "energy", None))
    return jax.shard_map(shards, mesh=mesh, in_specs=in_specs, out_specs=out_specs, check_vma=False)
```

```python
import functools

import jax
import jax.numpy as jnp
from jax import lax
from jax.experimental import pallas as pl
from jax.experimental.pallas import tpu as pltpu
from jax.sharding import PartitionSpec as P

ORB = 12
BRANCH = 3
FREQ = 64
COMP = 288
SQUARE = ORB * ORB
LANES = 128
REST = SQUARE - LANES
TAIL = 2 * REST
SLOTS = LANES // TAIL
TILE = 16
SMALL_GRANT = 16 * 1024 * 1024
LARGE_GRANT = 60 * 1024 * 1024
LONG = 100_000_000_000

BF16 = jnp.bfloat16
F32 = jnp.float32
I32 = jnp.int32


class Plan:
    def __init__(self, green, phonon, n_energy, n_mom):
        self.n_energy, self.n_mom = n_energy, n_mom
        self.mom_dev, self.steps, self.pairs, _ = green.shape
        self.momenta = self.mom_dev * n_mom
        self.pairs_dev = phonon.shape[1]
        self.half = FREQ // self.steps
        self.group = 2 * self.half
        self.n_groups = n_energy // self.group
        self.peers = self.group * n_mom
        self.sub = self.pairs_dev // n_mom
        self.own = self.n_groups * self.sub
        self.main_rows = self.mom_dev * self.own * 2 * self.steps
        self.tail_rows = self.mom_dev * self.own // SLOTS * self.steps
        self.rows = self.main_rows + self.tail_rows
        assert self.half * self.steps == FREQ and n_energy % self.group == 0
        assert self.n_groups & (self.n_groups - 1) == 0
        assert self.pairs_dev % n_mom == 0 and self.group * self.pairs_dev == TILE
        assert self.mom_dev * self.own % SLOTS == 0 and self.n_groups % 2 == 0

    def main_row(self, k, u):
        return (k * self.own + u) * 2 * self.steps

    def tail_row(self, k, u):
        return self.main_rows + (k * self.own + u) // SLOTS * self.steps

    def shift(self, k):
        return k * self.own % SLOTS * TAIL

    def place(self, h, i):
        j, rest = divmod(i, self.pairs_dev)
        m, b = divmod(rest, self.sub)
        return j * self.n_mom + m, h * self.sub + b


def dot(a, b):
    return lax.dot_general(a, b, (((1,), (0,)), ((), ())), preferred_element_type=F32)


def dot_nt(a, b):
    return lax.dot_general(a, b, (((1,), (1,)), ((), ())), preferred_element_type=F32)


def iota(dims, axis):
    return lax.broadcasted_iota(I32, dims, axis)


def swap_matrix(outer, inner, flip=False):
    n = outer * inner
    row, col = iota((n, n), 0), iota((n, n), 1)
    place = row & (outer - 1)
    source = (outer - 1 - place if flip else place) * inner + (row >> (outer.bit_length() - 1))
    return (col == source).astype(F32).astype(BF16)


def to_wire(rows):
    tail = jnp.concatenate([rows[:, LANES:SQUARE], rows[:, SQUARE + LANES :]], axis=1)
    return rows[:, :LANES], rows[:, SQUARE : SQUARE + LANES], tail


def pack_rows(plan, load, out_ref, stage, sems, flip=False):
    swap = swap_matrix(plan.steps, TILE, flip)
    tails, copies = {}, []

    def send(first, count):
        rows = slice(first, first + count)
        copy = pltpu.make_async_copy(stage.at[:, rows, :], out_ref.at[:, rows, :], sems.at[len(copies)])
        copy.start()
        copies.append(copy)

    for k in range(plan.mom_dev):
        for h in range(plan.pairs // TILE):
            left, right, tail = to_wire(dot(swap, load(k, h)).astype(BF16))
            for i in range(TILE):
                peer, u = plan.place(h, i)
                here = slice(i * plan.steps, (i + 1) * plan.steps)
                row = plan.main_row(k, u)
                stage[peer, row : row + plan.steps, :] = left[here]
                stage[peer, row + plan.steps : row + 2 * plan.steps, :] = right[here]
                tails[peer, k * plan.own + u] = tail[here]
            send(plan.main_row(k, h * plan.sub), plan.sub * 2 * plan.steps)
    for peer in range(plan.peers):
        for first in range(0, plan.mom_dev * plan.own, SLOTS):
            row = plan.main_rows + first // SLOTS * plan.steps
            joined = jnp.concatenate([tails[peer, first + t] for t in range(SLOTS)], axis=1)
            stage[peer, row : row + plan.steps, :] = joined
    send(plan.main_rows, plan.tail_rows)
    for copy in copies:
        copy.wait()


def pack_own_kernel(plan, green_ref, out_ref, stage, out_sems, tiles, sems):
    copies = {}
    for k in range(plan.mom_dev):
        for h in range(plan.pairs // TILE):
            copies[k, h] = pltpu.make_async_copy(
                green_ref.at[k, :, TILE * h : TILE * (h + 1), :], tiles.at[k, h], sems.at[k, h]
            )
            copies[k, h].start()

    def load(k, h):
        copies[k, h].wait()
        return tiles[k, h].reshape(plan.steps * TILE, COMP)

    pack_rows(plan, load, out_ref, stage, out_sems)


def pack_partner_kernel(plan, take_ref, green_ref, out_ref, stage, sems, taken):
    chunk = take_ref.shape[0] // plan.pairs
    take = take_ref[...]
    for k in range(plan.mom_dev):
        for e in range(0, plan.steps, chunk):
            rows = green_ref[k, e : e + chunk].reshape(chunk * plan.pairs, COMP)
            taken[k, e : e + chunk] = dot(take, rows).astype(BF16).reshape(chunk, plan.pairs, COMP)

    def load(k, h):
        return taken[k, :, TILE * h : TILE * (h + 1), :].reshape(plan.steps * TILE, COMP)

    pack_rows(plan, load, out_ref, stage, sems, flip=True)


def each_pair(plan, body):
    if plan.own <= 2:
        for u in range(plan.own):
            body(u)
    else:
        lax.fori_loop(0, plan.own, lambda u, _: body(u), None)


def rows_at(row, count):
    return pl.ds(row if isinstance(row, int) else pl.multiple_of(row, count), count)


def my_table(plan, tables_ref, u):
    group = lax.axis_index("energy") // plan.group
    return tables_ref[(u // plan.sub ^ group) * plan.sub + u % plan.sub]


def sandwich_kernel(plan, tables_ref, sand_ref):
    place, want = iota((2 * LANES, 16), 0), iota((2 * LANES, 16), 1)

    def body(u):
        couple = my_table(plan, tables_ref, u)[: BRANCH * 16, :16]
        for h in range(2):
            comp = jnp.where(place < LANES, place, place - (u % SLOTS * TAIL + h * REST))
            valid = (place < LANES) | ((comp >= LANES) & (comp < SQUARE))
            quotient = (comp * 171) >> 11
            first = (valid & (quotient == want)).astype(F32).astype(BF16)
            second = (valid & (comp - ORB * quotient == want)).astype(F32).astype(BF16)
            left = dot_nt(couple, first).astype(BF16)
            right = dot_nt(couple, second).astype(BF16)
            for i in range(BRANCH):
                rows = slice(16 * i, 16 * i + 16)
                product = dot(first, left[rows]) * dot(second, right[rows])
                sand_ref[u, h, :, 2 * LANES * i : 2 * LANES * (i + 1)] = product.astype(BF16)

    each_pair(plan, body)


def toeplitz_kernel(plan, tables_ref, toep_ref):
    mirror = iota((FREQ, 2 * FREQ), 0) + iota((FREQ, 2 * FREQ), 1) == FREQ
    mirror = mirror.astype(F32).astype(BF16)

    def body(u):
        lags = dot(my_table(plan, tables_ref, u)[BRANCH * 16 :, :], mirror)
        for q in range(plan.momenta):
            for i in range(BRANCH):
                n = q * BRANCH + i
                band = jnp.broadcast_to(lags[n : n + 1], (FREQ, 2 * FREQ))
                band = pltpu.roll(band, 0, 1, stride=1, stride_axis=0)
                toep_ref[u, q, i * FREQ : (i + 1) * FREQ, :] = band.astype(BF16)

    each_pair(plan, body)


def gather_rows(plan, ref, u, y, first, flip=False):
    m, k = divmod(y, plan.mom_dev)
    row, tail = plan.main_row(k, u), plan.tail_row(k, u)
    order = range(plan.half)
    lefts, rights, tails = [], [], []
    for j in reversed(order) if flip else order:
        peer = (first + j) * plan.n_mom + m
        lefts.append(ref[peer, rows_at(row, plan.steps), :])
        rights.append(ref[peer, rows_at(row + plan.steps, plan.steps), :])
        tails.append(ref[peer, rows_at(tail, plan.steps), :])
    tails = jnp.concatenate(tails, axis=0)
    if plan.shift(k):
        tails = pltpu.roll(tails.astype(F32), LANES - plan.shift(k), 1).astype(BF16)
    return jnp.concatenate([jnp.concatenate(lefts, axis=0), jnp.concatenate(rights, axis=0), tails], axis=1)


def half_and_tail(rows, h):
    return jnp.concatenate([rows[:, h * LANES : (h + 1) * LANES], rows[:, 2 * LANES :]], axis=1)


def self_block(plan, u, green, toep_ref, sand_ref, out_ref):
    summed = []
    for i in range(BRANCH):
        rows = slice(i * FREQ, (i + 1) * FREQ)
        band = jnp.concatenate(
            [
                jnp.concatenate([toep_ref[u, (k - y) % plan.momenta, rows, :] for y in range(plan.momenta)], axis=1)
                for k in range(plan.momenta)
            ],
            axis=0,
        )
        summed.append(dot(band, green).astype(BF16))
    left, right = [
        dot_nt(jnp.concatenate([half_and_tail(rows, h) for rows in summed], axis=1), sand_ref[u, h])
        for h in range(2)
    ]
    tails = left[:, LANES:] + right[:, LANES:]
    left, right = left[:, :LANES].astype(BF16), right[:, :LANES].astype(BF16)
    for y in range(plan.momenta):
        m, k = divmod(y, plan.mom_dev)
        row, tail = plan.main_row(k, u), plan.tail_row(k, u)
        rest = tails[y * FREQ : (y + 1) * FREQ]
        if plan.shift(k):
            rest = pltpu.roll(rest, plan.shift(k), 1)
        rest = rest.astype(BF16)
        for j in range(plan.half):
            peer = j * plan.n_mom + m
            here = slice(j * plan.steps, (j + 1) * plan.steps)
            there = slice(y * FREQ + j * plan.steps, y * FREQ + (j + 1) * plan.steps)
            out_ref[peer, rows_at(row, plan.steps), :] = left[there]
            out_ref[peer, rows_at(row + plan.steps, plan.steps), :] = right[there]
            out_ref[peer, rows_at(tail, plan.steps), :] += rest[here]


def clear_tails(plan, out_ref):
    for peer in range(plan.half * plan.n_mom):
        out_ref[peer, plan.main_rows :, :] = jnp.zeros((plan.tail_rows, LANES), BF16)


def self_late_kernel(plan, own, toep_ref, sand_ref, out_ref):
    clear_tails(plan, out_ref)

    def body(u):
        green = [gather_rows(plan, own, u, y, first) for y in range(plan.momenta) for first in (0, plan.half)]
        self_block(plan, u, jnp.concatenate(green, axis=0), toep_ref, sand_ref, out_ref)

    each_pair(plan, body)


def self_early_kernel(plan, own, far, toep_ref, sand_ref, late_ref, out_ref, stage, halo, sems):
    has = (lax.axis_index("energy") // plan.group > 0).astype(F32).astype(BF16)
    near = plan.half * plan.n_mom
    load = pltpu.make_async_copy(far, halo, sems.at[0])
    load.start()
    upper = pltpu.make_async_copy(late_ref, out_ref.at[near:], sems.at[1])
    upper.start()
    clear_tails(plan, stage)
    load.wait()

    def body(u):
        green = []
        for y in range(plan.momenta):
            green.append(gather_rows(plan, halo, u, y, 0) * has)
            green.append(gather_rows(plan, own, u, y, 0))
        self_block(plan, u, jnp.concatenate(green, axis=0), toep_ref, sand_ref, stage)

    each_pair(plan, body)
    lower = pltpu.make_async_copy(stage, out_ref.at[:near], sems.at[2])
    lower.start()
    lower.wait()
    upper.wait()


def lag_sums(plan, u, partner, green, sand_ref, store):
    partner, green = jnp.concatenate(partner, axis=0), jnp.concatenate(green, axis=0)
    left, right = [dot(half_and_tail(partner, h), sand_ref[u, h]) for h in range(2)]
    for i in range(BRANCH):
        here = slice(2 * LANES * i, 2 * LANES * i + LANES)
        rest = slice(2 * LANES * i + LANES, 2 * LANES * (i + 1))
        applied = jnp.concatenate([left[:, here], right[:, here], left[:, rest] + right[:, rest]], axis=1)
        lagged = dot_nt(applied.astype(BF16), green)
        for q in range(plan.momenta):
            acc = None
            for k in range(plan.momenta):
                y = (k + q) % plan.momenta
                part = lagged[k * FREQ : (k + 1) * FREQ, y * 2 * FREQ : (y + 1) * 2 * FREQ]
                acc = part if acc is None else acc + part
            acc = pltpu.roll(acc, FREQ + 1, 1, stride=1, stride_axis=0)
            store(q, i, jnp.sum(acc, axis=0, keepdims=True))


def phonon_early_kernel(plan, own, partner_ref, sand_ref, out_ref):
    def body(u):
        partner = [gather_rows(plan, partner_ref, u, k, 0, flip=True) for k in range(plan.momenta)]
        green = [gather_rows(plan, own, u, y, first) for y in range(plan.momenta) for first in (0, plan.half)]

        def store(q, i, lags):
            out_ref[u, q * BRANCH + i : q * BRANCH + i + 1, :] = lags

        lag_sums(plan, u, partner, green, sand_ref, store)

    each_pair(plan, body)


def phonon_late_kernel(plan, own, halo, partner_ref, sand_ref, early_ref, *refs, scale):
    outs, sums = refs[:-1], refs[-1]
    group = lax.axis_index("energy") // plan.group
    me = lax.axis_index("mom")
    has = (group < plan.n_groups - 1).astype(F32).astype(BF16)

    def body(u):
        partner = [gather_rows(plan, partner_ref, u, k, plan.half, flip=True) for k in range(plan.momenta)]
        green = []
        for y in range(plan.momenta):
            green.append(gather_rows(plan, own, u, y, plan.half))
            green.append(gather_rows(plan, halo, u, y, 0) * has)

        def store(q, i, lags):
            n = q * BRANCH + i
            side, row = divmod(n, plan.mom_dev * BRANCH)
            sums[u, side, row : row + 1, :] = (lags + early_ref[u, n : n + 1, :]) * scale

        lag_sums(plan, u, partner, green, sand_ref, store)

    each_pair(plan, body)
    for d in range(plan.n_groups):
        for t in range(plan.n_mom):
            for b in range(plan.sub):
                outs[d * plan.n_mom + t][b] = sums[(group ^ d) * plan.sub + b, me ^ t]


def collect_kernel(plan, *refs):
    parts, out_ref = refs[:-1], refs[-1]
    me = lax.axis_index("mom")
    for d in range(plan.n_mom):
        total = sum(ref[...] for ref in parts[d :: plan.n_mom])
        for b in range(plan.sub):
            pair = (me ^ d) * plan.sub + b
            for q in range(plan.mom_dev):
                rows = [total[b, q * BRANCH + i : q * BRANCH + i + 1, :FREQ] for i in range(BRANCH)]
                out_ref[q, pl.ds(pair, 1), :] = jnp.concatenate(rows, axis=1)


def unpack_kernel(plan, wire, out_ref, tiles, sems):
    swap = swap_matrix(TILE, plan.steps)
    copies = []
    for k in range(plan.mom_dev):
        for h in range(plan.pairs // TILE):
            lefts, rights, tails = [], [], []
            for i in range(TILE):
                peer, u = plan.place(h, i)
                row, tail = plan.main_row(k, u), plan.tail_row(k, u)
                lefts.append(wire[peer, row : row + plan.steps, :])
                rights.append(wire[peer, row + plan.steps : row + 2 * plan.steps, :])
                lane = (k * plan.own + u) % SLOTS * TAIL
                tails.append(wire[peer, tail : tail + plan.steps, :][:, lane : lane + TAIL])
            rows = jnp.concatenate([jnp.concatenate(part, axis=0) for part in (lefts, rights, tails)], axis=1)
            moved = dot(swap, rows).astype(BF16)
            left, right = moved[:, :LANES], moved[:, LANES : 2 * LANES]
            tail = moved[:, 2 * LANES :]
            moved = jnp.concatenate([left, tail[:, :REST], right, tail[:, REST:]], axis=1)
            tiles[k, h] = moved.reshape(plan.steps, TILE, COMP)
            copy = pltpu.make_async_copy(
                tiles.at[k, h], out_ref.at[k, :, TILE * h : TILE * (h + 1), :], sems.at[k, h]
            )
            copy.start()
            copies.append(copy)
    for copy in copies:
        copy.wait()


ANY = pl.BlockSpec(memory_space=pl.ANY)
HBM = pl.BlockSpec(memory_space=pltpu.HBM)
VMEM = pl.BlockSpec(memory_space=pltpu.VMEM)


def call(plan, kernel, out_shape, *args, in_specs=None, out_specs=None, scratch=(), flops=1, grant=None):
    outs = jax.tree.map(lambda _: VMEM, out_shape)
    return pl.pallas_call(
        functools.partial(kernel, plan),
        out_shape=out_shape,
        in_specs=in_specs or [VMEM] * len(args),
        out_specs=out_specs or outs,
        scratch_shapes=list(scratch),
        compiler_params=pltpu.CompilerParams(vmem_limit_bytes=grant or SMALL_GRANT * max(1, plan.own // 4)),
        cost_estimate=pl.CostEstimate(flops=flops, bytes_accessed=1, transcendentals=0),
    )(*args)


def shape(dims, dtype):
    return jax.ShapeDtypeStruct(dims, dtype)


def in_hbm(struct):
    return pltpu.HBM(struct.shape, struct.dtype)


def shards(lesser_green, partner, phonon_green, coupling):
    n_energy, n_mom = lax.axis_size("energy"), lax.axis_size("mom")
    plan = Plan(lesser_green, phonon_green, n_energy, n_mom)
    axes = ("energy", "mom")
    me = lax.axis_index("mom")
    s = lax.axis_index("energy") // plan.group
    wire = shape((plan.peers, plan.rows, LANES), BF16)
    half_peers = plan.half * n_mom
    groups = [[g * plan.peers + i for i in range(plan.peers)] for g in range(plan.n_groups)]
    tiles = (plan.mom_dev, plan.pairs // TILE)

    def exchange(blocks):
        return lax.all_to_all(blocks, axes, split_axis=0, concat_axis=0, axis_index_groups=groups, tiled=True)

    def swap_groups(values, other):
        route = []
        for e in range(n_energy):
            g, j = divmod(e, plan.group)
            to = other(g) if 0 <= other(g) < plan.n_groups else g
            route.append((e, to * plan.group + j))
        return lax.ppermute(values, "energy", route)

    staging = [pltpu.VMEM(wire.shape, BF16), pltpu.SemaphoreType.DMA((tiles[0] * tiles[1] + 1,))]
    tile_scratch = [pltpu.VMEM(tiles + (plan.steps, TILE, COMP), BF16), pltpu.SemaphoreType.DMA(tiles)]
    half_wire = shape((half_peers, plan.rows, LANES), BF16)
    own = exchange(
        call(
            plan,
            pack_own_kernel,
            in_hbm(wire),
            lesser_green,
            in_specs=[HBM],
            out_specs=HBM,
            scratch=staging + tile_scratch,
            grant=LARGE_GRANT,
        )
    )

    lag_count = plan.momenta * BRANCH
    lag_rows = -(-lag_count // 16) * 16
    couple = coupling.reshape(plan.pairs_dev, BRANCH, ORB, ORB)
    couple = jnp.pad(couple, ((0, 0), (0, 0), (0, 16 - ORB), (0, FREQ - ORB)))
    phonon = phonon_green.reshape(plan.momenta, plan.pairs_dev, BRANCH, FREQ)
    phonon = jnp.moveaxis(phonon, 1, 0).reshape(plan.pairs_dev, lag_count, FREQ)
    phonon = jnp.pad(phonon, ((0, 0), (0, lag_rows - lag_count), (0, 0)))
    table = jnp.concatenate([couple.reshape(plan.pairs_dev, BRANCH * 16, FREQ), phonon], axis=1)
    table = lax.dynamic_slice_in_dim(table, me * plan.sub, plan.sub, axis=0)
    tables = [table]
    for d in range(1, plan.n_groups):
        tables.append(swap_groups(table, functools.partial(lambda d, g: g ^ d, d)))
    tables = jnp.concatenate(tables, axis=0)
    sand = call(
        plan, sandwich_kernel, shape((plan.own, 2, 2 * LANES, BRANCH * 2 * LANES), BF16), tables
    )
    chunk = max(1, 256 // plan.pairs)
    source = (jnp.arange(chunk)[:, None] * plan.pairs + partner[None, :]).reshape(-1)
    take = (source[:, None] == jnp.arange(chunk * plan.pairs)[None, :]).astype(BF16)
    partner_wire = call(
        plan,
        pack_partner_kernel,
        in_hbm(wire),
        take,
        lesser_green,
        out_specs=HBM,
        scratch=staging + [pltpu.VMEM(lesser_green.shape, BF16)],
    )
    own, tables, sand, partner_wire = lax.optimization_barrier((own, tables, sand, partner_wire))

    odd = s % 2

    def edge(side):
        return lax.dynamic_slice_in_dim(own, side * half_peers, half_peers, axis=0)

    before = after = inner = swap_groups(edge(1 - odd), lambda g: g ^ 1)
    if plan.n_groups > 2:
        outer = swap_groups(edge(odd), lambda g: ((g - 1) ^ 1) + 1)
        before = jnp.where(odd == 1, inner, outer)
        after = jnp.where(odd == 1, outer, inner)

    toep = call(
        plan,
        toeplitz_kernel,
        shape((plan.own, plan.momenta, BRANCH * FREQ, 2 * FREQ), BF16),
        tables,
        flops=LONG,
    )
    toep, partner_wire = lax.optimization_barrier((toep, partner_wire))
    partner_blocks = exchange(partner_wire)

    late = call(plan, self_late_kernel, half_wire, own, toep, sand)
    sigma = call(
        plan,
        self_early_kernel,
        in_hbm(wire),
        own,
        before,
        toep,
        sand,
        late,
        in_specs=[VMEM, ANY, VMEM, VMEM, VMEM],
        out_specs=HBM,
        scratch=[
            pltpu.VMEM(half_wire.shape, BF16),
            pltpu.VMEM(half_wire.shape, BF16),
            pltpu.SemaphoreType.DMA((3,)),
        ],
        flops=LONG,
    )
    arrived = exchange(sigma)

    scale = (plan.momenta * n_energy * plan.steps * COMP) ** -0.5
    early = call(
        plan,
        phonon_early_kernel,
        shape((plan.own, lag_count, LANES), F32),
        own,
        partner_blocks,
        sand,
    )
    side_rows = plan.mom_dev * BRANCH
    parts = list(call(
        plan,
        functools.partial(phonon_late_kernel, scale=scale),
        [shape((plan.sub, side_rows, LANES), F32)] * (plan.n_groups * n_mom),
        own,
        after,
        partner_blocks,
        sand,
        early,
        scratch=[pltpu.VMEM((plan.own, n_mom, side_rows, LANES), F32)],
    ))
    for d in range(plan.n_groups):
        for t in range(n_mom):
            if d or t:
                route = []
                for e in range(n_energy):
                    g, j = divmod(e, plan.group)
                    for m in range(n_mom):
                        route.append((e * n_mom + m, ((g ^ d) * plan.group + j) * n_mom + (m ^ t)))
                parts[d * n_mom + t] = lax.ppermute(parts[d * n_mom + t], axes, route)
    phonon_self = call(
        plan, collect_kernel, shape((plan.mom_dev, plan.pairs_dev, BRANCH * FREQ), F32), *parts
    )

    self_energy = call(
        plan,
        unpack_kernel,
        shape(lesser_green.shape, BF16),
        arrived,
        out_specs=ANY,
        scratch=tile_scratch,
    )
    return self_energy, phonon_self


def solution(mesh):
    in_specs = (P("mom", "energy", None, None), P(), P(None, "energy", None), P("energy", None))
    out_specs = (P("mom", "energy", None, None), P("mom", "energy", None))
    return jax.shard_map(shards, mesh=mesh, in_specs=in_specs, out_specs=out_specs, check_vma=False)
```

```python
import functools

import jax
import jax.numpy as jnp
from jax import lax
from jax.experimental import pallas as pl
from jax.experimental.pallas import tpu as pltpu
from jax.sharding import PartitionSpec as P

ORB = 12
BRANCH = 3
FREQ = 64
COMP = 288
SQUARE = ORB * ORB
LANES = 128
REST = SQUARE - LANES
TAIL = 2 * REST
SLOTS = LANES // TAIL
TILE = 16
SMALL_GRANT = 16 * 1024 * 1024
LARGE_GRANT = 60 * 1024 * 1024

BF16 = jnp.bfloat16
F32 = jnp.float32
I32 = jnp.int32


class Plan:
    def __init__(self, green, phonon, n_energy, n_mom):
        self.n_energy, self.n_mom = n_energy, n_mom
        self.mom_dev, self.steps, self.pairs, _ = green.shape
        self.momenta = self.mom_dev * n_mom
        self.pairs_dev = phonon.shape[1]
        self.half = FREQ // self.steps
        self.group = 2 * self.half
        self.n_groups = n_energy // self.group
        self.peers = self.group * n_mom
        self.sub = self.pairs_dev // n_mom
        self.own = self.n_groups * self.sub
        self.main_rows = self.mom_dev * self.own * 2 * self.steps
        self.tail_rows = self.mom_dev * self.own // SLOTS * self.steps
        self.rows = self.main_rows + self.tail_rows
        assert self.half * self.steps == FREQ and n_energy % self.group == 0
        for count in (self.n_groups, self.half, n_mom):
            assert count & (count - 1) == 0
        self.sides = 1 if self.n_groups == 2 else 2
        assert self.pairs_dev % n_mom == 0 and self.group * self.pairs_dev == TILE
        assert self.mom_dev * self.own % SLOTS == 0 and self.n_groups % 2 == 0

    def main_row(self, k, u):
        return (k * self.own + u) * 2 * self.steps

    def tail_row(self, k, u):
        return self.main_rows + (k * self.own + u) // SLOTS * self.steps

    def hops(self):
        return [(plane, d) for plane in range(2) for d in range(self.half)]

    def shift(self, k):
        return k * self.own % SLOTS * TAIL

    def place(self, h, i):
        j, rest = divmod(i, self.pairs_dev)
        m, b = divmod(rest, self.sub)
        return j * self.n_mom + m, h * self.sub + b


def dot(a, b):
    return lax.dot_general(a, b, (((1,), (0,)), ((), ())), preferred_element_type=F32)


def dot_nt(a, b):
    return lax.dot_general(a, b, (((1,), (1,)), ((), ())), preferred_element_type=F32)


def iota(dims, axis):
    return lax.broadcasted_iota(I32, dims, axis)


def swap_matrix(outer, inner, flip=False):
    n = outer * inner
    row, col = iota((n, n), 0), iota((n, n), 1)
    place = row & (outer - 1)
    source = (outer - 1 - place if flip else place) * inner + (row >> (outer.bit_length() - 1))
    return (col == source).astype(F32).astype(BF16)


def to_wire(rows):
    tail = jnp.concatenate([rows[:, LANES:SQUARE], rows[:, SQUARE + LANES :]], axis=1)
    return rows[:, :LANES], rows[:, SQUARE : SQUARE + LANES], tail


def pack_rows(plan, load, stage, sent, base=0, flip=False):
    swap = swap_matrix(plan.steps, TILE, flip)
    tails = {}
    for k in range(plan.mom_dev):
        for h in range(plan.pairs // TILE):
            left, right, tail = to_wire(dot(swap, load(k, h)).astype(BF16))
            for i in range(TILE):
                peer, u = plan.place(h, i)
                here = slice(i * plan.steps, (i + 1) * plan.steps)
                row = base + plan.main_row(k, u)
                stage[peer, row : row + plan.steps, :] = left[here]
                stage[peer, row + plan.steps : row + 2 * plan.steps, :] = right[here]
                tails[peer, k * plan.own + u] = tail[here]
            sent(base + plan.main_row(k, h * plan.sub), plan.sub * 2 * plan.steps)
    for peer in range(plan.peers):
        for first in range(0, plan.mom_dev * plan.own, SLOTS):
            row = base + plan.main_rows + first // SLOTS * plan.steps
            joined = jnp.concatenate([tails[peer, first + t] for t in range(SLOTS)], axis=1)
            stage[peer, row : row + plan.steps, :] = joined
    sent(base + plan.main_rows, plan.tail_rows)


def pack_kernel(plan, take_ref, green_ref, out_ref, *refs):
    messages, (stage, green, taken, in_sems, out_sems) = refs[:-5], refs[-5:]
    loads = [pltpu.make_async_copy(green_ref.at[k], green.at[k], in_sems.at[k]) for k in range(plan.mom_dev)]
    for copy in loads:
        copy.start()
    copies = []

    def sent(first, count):
        rows = slice(first, first + count)
        copy = pltpu.make_async_copy(stage.at[:, rows, :], out_ref.at[:, rows, :], out_sems.at[len(copies)])
        copy.start()
        copies.append(copy)

    def load(k, h):
        if h == 0:
            loads[k].wait()
        return green[k, :, TILE * h : TILE * (h + 1), :].reshape(plan.steps * TILE, COMP)

    pack_rows(plan, load, stage, sent)

    here = lax.axis_index("energy") % plan.group
    later, seat = here // plan.half, here % plan.half
    for message, (plane, d) in zip(messages, plan.hops()):
        chip = (1 - plane ^ later) * plan.half + (seat ^ d)
        for m in range(plan.n_mom):
            message[m] = stage[chip * plan.n_mom + m, : plan.rows, :]

    chunk = take_ref.shape[0] // plan.pairs
    take = take_ref[...]
    for k in range(plan.mom_dev):
        for e in range(0, plan.steps, chunk):
            rows = green[k, e : e + chunk].reshape(chunk * plan.pairs, COMP)
            taken[k, e : e + chunk] = dot(take, rows).astype(BF16).reshape(chunk, plan.pairs, COMP)

    def load_taken(k, h):
        return taken[k, :, TILE * h : TILE * (h + 1), :].reshape(plan.steps * TILE, COMP)

    pack_rows(plan, load_taken, stage, sent, base=plan.rows, flip=True)
    for copy in copies:
        copy.wait()


def halo_kernel(plan, *refs):
    messages, outs = refs[: 2 * plan.half], refs[2 * plan.half :]
    here = lax.axis_index("energy") % plan.group
    plane, seat = here // plan.half, here % plan.half
    me = lax.axis_index("mom")
    for d in range(plan.half):
        first, second = messages[d], messages[plan.half + d]
        for t in range(plan.n_mom):
            a, b = first[me ^ t], second[me ^ t]
            if plan.sides == 1:
                outs[t][0, seat ^ d] = a + b
            else:
                outs[t][0, seat ^ d] = jnp.where(plane == 0, a, b)
                outs[t][1, seat ^ d] = jnp.where(plane == 0, b, a)


def each_pair(plan, body):
    if plan.own <= 2:
        for u in range(plan.own):
            body(u)
    else:
        lax.fori_loop(0, plan.own, lambda u, _: body(u), None)


def rows_at(row, count):
    return pl.ds(row if isinstance(row, int) else pl.multiple_of(row, count), count)


def my_table(plan, tables_ref, u):
    group = lax.axis_index("energy") // plan.group
    return tables_ref[(u // plan.sub ^ group) * plan.sub + u % plan.sub]


def sandwich_kernel(plan, tables_ref, sand_ref):
    place, want = iota((2 * LANES, 16), 0), iota((2 * LANES, 16), 1)

    def body(u):
        couple = my_table(plan, tables_ref, u)[: BRANCH * 16, :16]
        for h in range(2):
            comp = jnp.where(place < LANES, place, place - (u % SLOTS * TAIL + h * REST))
            valid = (place < LANES) | ((comp >= LANES) & (comp < SQUARE))
            quotient = (comp * 171) >> 11
            first = (valid & (quotient == want)).astype(F32).astype(BF16)
            second = (valid & (comp - ORB * quotient == want)).astype(F32).astype(BF16)
            left = dot_nt(couple, first).astype(BF16)
            right = dot_nt(couple, second).astype(BF16)
            for i in range(BRANCH):
                rows = slice(16 * i, 16 * i + 16)
                product = dot(first, left[rows]) * dot(second, right[rows])
                sand_ref[u, h, :, 2 * LANES * i : 2 * LANES * (i + 1)] = product.astype(BF16)

    each_pair(plan, body)


def toeplitz_kernel(plan, tables_ref, toep_ref):
    mirror = iota((FREQ, 2 * FREQ), 0) + iota((FREQ, 2 * FREQ), 1) == FREQ
    mirror = mirror.astype(F32).astype(BF16)

    def body(u):
        lags = dot(my_table(plan, tables_ref, u)[BRANCH * 16 :, :], mirror)
        for q in range(plan.momenta):
            for i in range(BRANCH):
                n = q * BRANCH + i
                band = jnp.broadcast_to(lags[n : n + 1], (FREQ, 2 * FREQ))
                band = pltpu.roll(band, 0, 1, stride=1, stride_axis=0)
                toep_ref[u, q, i * FREQ : (i + 1) * FREQ, :] = band.astype(BF16)

    each_pair(plan, body)


def gather_rows(plan, ref, u, y, place, base=0, flip=False):
    m, k = divmod(y, plan.mom_dev)
    row, tail = base + plan.main_row(k, u), base + plan.tail_row(k, u)
    order = range(plan.half)
    lefts, rights, tails = [], [], []
    for j in reversed(order) if flip else order:
        peer = place(j, m)
        lefts.append(ref[peer, rows_at(row, plan.steps), :])
        rights.append(ref[peer, rows_at(row + plan.steps, plan.steps), :])
        tails.append(ref[peer, rows_at(tail, plan.steps), :])
    tails = jnp.concatenate(tails, axis=0)
    if plan.shift(k):
        tails = pltpu.roll(tails.astype(F32), LANES - plan.shift(k), 1).astype(BF16)
    return jnp.concatenate([jnp.concatenate(lefts, axis=0), jnp.concatenate(rights, axis=0), tails], axis=1)


def half_and_tail(rows, h):
    return jnp.concatenate([rows[:, h * LANES : (h + 1) * LANES], rows[:, 2 * LANES :]], axis=1)


def own_rows(plan, blocks, u, y, late):
    return gather_rows(plan, blocks, u, y, lambda j, m: (late * plan.half + j) * plan.n_mom + m)


def partner_rows(plan, blocks, u, k, late):
    place = lambda j, m: (late * plan.half + j) * plan.n_mom + m
    return gather_rows(plan, blocks, u, k, place, base=plan.rows, flip=True)


def halo_rows(plan, halo, u, y, side, has):
    side = min(side, plan.sides - 1)
    rows = gather_rows(plan, halo, u, y, lambda j, m: (m * plan.sides + side) * plan.half + j)
    return rows * has.astype(F32).astype(BF16)


def sort_halo(plan, halos, halo):
    me = lax.axis_index("mom")
    count = plan.sides * plan.half
    for t in range(plan.n_mom):
        for side in range(plan.sides):
            for j in range(plan.half):
                halo[(me ^ t) * count + side * plan.half + j] = halos[t][side, j]


def self_block(plan, u, green, toep_ref, sand_ref, out_ref, late):
    green = jnp.concatenate(green, axis=0)
    summed = []
    for i in range(BRANCH):
        rows = slice(i * FREQ, (i + 1) * FREQ)
        band = jnp.concatenate(
            [
                jnp.concatenate([toep_ref[u, (k - y) % plan.momenta, rows, :] for y in range(plan.momenta)], axis=1)
                for k in range(plan.momenta)
            ],
            axis=0,
        )
        summed.append(dot(band, green).astype(BF16))
    left, right = [
        dot_nt(jnp.concatenate([half_and_tail(rows, h) for rows in summed], axis=1), sand_ref[u, h])
        for h in range(2)
    ]
    tails = left[:, LANES:] + right[:, LANES:]
    left, right = left[:, :LANES].astype(BF16), right[:, :LANES].astype(BF16)
    for y in range(plan.momenta):
        m, k = divmod(y, plan.mom_dev)
        row, tail = plan.main_row(k, u), plan.tail_row(k, u)
        rest = tails[y * FREQ : (y + 1) * FREQ]
        if plan.shift(k):
            rest = pltpu.roll(rest, plan.shift(k), 1)
        rest = rest.astype(BF16)
        for j in range(plan.half):
            peer = (late * plan.half + j) * plan.n_mom + m
            here = slice(j * plan.steps, (j + 1) * plan.steps)
            there = slice(y * FREQ + j * plan.steps, y * FREQ + (j + 1) * plan.steps)
            out_ref[peer, rows_at(row, plan.steps), :] = left[there]
            out_ref[peer, rows_at(row + plan.steps, plan.steps), :] = right[there]
            out_ref[peer, rows_at(tail, plan.steps), :] += rest[here]


def self_kernel(plan, blocks, *refs):
    halos, (toep_ref, sand_ref, out_ref, stage, halo, sems) = refs[: plan.n_mom], refs[plan.n_mom :]
    has_before = lax.axis_index("energy") // plan.group > 0
    near = plan.half * plan.n_mom
    sort_halo(plan, halos, halo)
    for peer in range(plan.peers):
        stage[peer, plan.main_rows :, :] = jnp.zeros((plan.tail_rows, LANES), BF16)
    copies = []
    for late in (1, 0):

        def body(u):
            green = []
            for y in range(plan.momenta):
                if late:
                    green.append(own_rows(plan, blocks, u, y, 0))
                else:
                    green.append(halo_rows(plan, halo, u, y, 0, has_before))
                green.append(own_rows(plan, blocks, u, y, late))
            self_block(plan, u, green, toep_ref, sand_ref, stage, late)

        each_pair(plan, body)
        here = pl.ds(late * near, near)
        copies.append(pltpu.make_async_copy(stage.at[here], out_ref.at[here], sems.at[late]))
        copies[-1].start()
    for copy in copies:
        copy.wait()


def lag_sums(plan, u, partner, green, sand_ref, store):
    partner, green = jnp.concatenate(partner, axis=0), jnp.concatenate(green, axis=0)
    left, right = [dot(half_and_tail(partner, h), sand_ref[u, h]) for h in range(2)]
    for i in range(BRANCH):
        here = slice(2 * LANES * i, 2 * LANES * i + LANES)
        rest = slice(2 * LANES * i + LANES, 2 * LANES * (i + 1))
        applied = jnp.concatenate([left[:, here], right[:, here], left[:, rest] + right[:, rest]], axis=1)
        lagged = dot_nt(applied.astype(BF16), green)
        for q in range(plan.momenta):
            acc = None
            for k in range(plan.momenta):
                y = (k + q) % plan.momenta
                part = lagged[k * FREQ : (k + 1) * FREQ, y * 2 * FREQ : (y + 1) * 2 * FREQ]
                acc = part if acc is None else acc + part
            acc = pltpu.roll(acc, FREQ + 1, 1, stride=1, stride_axis=0)
            store(q, i, jnp.sum(acc, axis=0, keepdims=True))


def phonon_kernel(plan, blocks, *refs, scale):
    halos, (sand_ref, *outs, sums, halo) = refs[: plan.n_mom], refs[plan.n_mom :]
    group = lax.axis_index("energy") // plan.group
    me = lax.axis_index("mom")
    has_after = group < plan.n_groups - 1
    sort_halo(plan, halos, halo)

    def body(u):
        for late in range(2):
            partner = [partner_rows(plan, blocks, u, k, late) for k in range(plan.momenta)]
            green = []
            for y in range(plan.momenta):
                green.append(own_rows(plan, blocks, u, y, late))
                if late:
                    green.append(halo_rows(plan, halo, u, y, 1, has_after))
                else:
                    green.append(own_rows(plan, blocks, u, y, 1))

            def store(q, i, lags):
                side, row = divmod(q * BRANCH + i, plan.mom_dev * BRANCH)
                if late:
                    lags = lags + sums[u, side, row : row + 1, :]
                sums[u, side, row : row + 1, :] = lags * scale if late else lags

            lag_sums(plan, u, partner, green, sand_ref, store)

    each_pair(plan, body)
    for d in range(plan.n_groups):
        for t in range(plan.n_mom):
            for b in range(plan.sub):
                outs[d * plan.n_mom + t][b] = sums[(group ^ d) * plan.sub + b, me ^ t]


def collect_kernel(plan, *refs):
    parts, out_ref = refs[:-1], refs[-1]
    me = lax.axis_index("mom")
    for d in range(plan.n_mom):
        total = sum(ref[...] for ref in parts[d :: plan.n_mom])
        for b in range(plan.sub):
            pair = (me ^ d) * plan.sub + b
            for q in range(plan.mom_dev):
                rows = [total[b, q * BRANCH + i : q * BRANCH + i + 1, :FREQ] for i in range(BRANCH)]
                out_ref[q, pl.ds(pair, 1), :] = jnp.concatenate(rows, axis=1)


def unpack_kernel(plan, wire, out_ref, tiles, sems):
    swap = swap_matrix(TILE, plan.steps)
    copies = []
    for k in range(plan.mom_dev):
        for h in range(plan.pairs // TILE):
            lefts, rights, tails = [], [], []
            for i in range(TILE):
                peer, u = plan.place(h, i)
                row, tail = plan.main_row(k, u), plan.tail_row(k, u)
                lefts.append(wire[peer, row : row + plan.steps, :])
                rights.append(wire[peer, row + plan.steps : row + 2 * plan.steps, :])
                lane = (k * plan.own + u) % SLOTS * TAIL
                tails.append(wire[peer, tail : tail + plan.steps, :][:, lane : lane + TAIL])
            rows = jnp.concatenate([jnp.concatenate(part, axis=0) for part in (lefts, rights, tails)], axis=1)
            moved = dot(swap, rows).astype(BF16)
            left, right = moved[:, :LANES], moved[:, LANES : 2 * LANES]
            tail = moved[:, 2 * LANES :]
            moved = jnp.concatenate([left, tail[:, :REST], right, tail[:, REST:]], axis=1)
            tiles[k, h] = moved.reshape(plan.steps, TILE, COMP)
            copy = pltpu.make_async_copy(
                tiles.at[k, h], out_ref.at[k, :, TILE * h : TILE * (h + 1), :], sems.at[k, h]
            )
            copy.start()
            copies.append(copy)
    for copy in copies:
        copy.wait()


ANY = pl.BlockSpec(memory_space=pl.ANY)
HBM = pl.BlockSpec(memory_space=pltpu.HBM)
VMEM = pl.BlockSpec(memory_space=pltpu.VMEM)


def call(plan, kernel, out_shape, *args, in_specs=None, out_specs=None, scratch=(), grant=None):
    outs = jax.tree.map(lambda _: VMEM, out_shape)
    return pl.pallas_call(
        functools.partial(kernel, plan),
        out_shape=out_shape,
        in_specs=in_specs or [VMEM] * len(args),
        out_specs=out_specs or outs,
        scratch_shapes=list(scratch),
        compiler_params=pltpu.CompilerParams(vmem_limit_bytes=grant or SMALL_GRANT * max(1, plan.own // 4)),
        cost_estimate=pl.CostEstimate(flops=1, bytes_accessed=1, transcendentals=0),
    )(*args)


def shape(dims, dtype):
    return jax.ShapeDtypeStruct(dims, dtype)


def in_hbm(struct):
    return pltpu.HBM(struct.shape, struct.dtype)


def shards(lesser_green, partner, phonon_green, coupling):
    n_energy, n_mom = lax.axis_size("energy"), lax.axis_size("mom")
    plan = Plan(lesser_green, phonon_green, n_energy, n_mom)
    axes = ("energy", "mom")
    me = lax.axis_index("mom")
    s = lax.axis_index("energy") // plan.group
    wire = shape((plan.peers, plan.rows, LANES), BF16)
    groups = [[g * plan.peers + i for i in range(plan.peers)] for g in range(plan.n_groups)]
    tiles = (plan.mom_dev, plan.pairs // TILE)

    def exchange(blocks):
        return lax.all_to_all(blocks, axes, split_axis=0, concat_axis=0, axis_index_groups=groups, tiled=True)

    def swap_groups(values, other):
        route = []
        for e in range(n_energy):
            g, j = divmod(e, plan.group)
            to = other(g) if 0 <= other(g) < plan.n_groups else g
            route.append((e, to * plan.group + j))
        return lax.ppermute(values, "energy", route)

    chunk = max(1, 256 // plan.pairs)
    source = (jnp.arange(chunk)[:, None] * plan.pairs + partner[None, :]).reshape(-1)
    take = (source[:, None] == jnp.arange(chunk * plan.pairs)[None, :]).astype(BF16)
    both = (plan.peers, 2 * plan.rows, LANES)
    message = shape((n_mom, plan.rows, LANES), BF16)
    packed, *messages = call(
        plan,
        pack_kernel,
        [in_hbm(shape(both, BF16))] + [message] * len(plan.hops()),
        take,
        lesser_green,
        in_specs=[VMEM, HBM],
        out_specs=[HBM] + [VMEM] * len(plan.hops()),
        scratch=[
            pltpu.VMEM(both, BF16),
            pltpu.VMEM(lesser_green.shape, BF16),
            pltpu.VMEM(lesser_green.shape, BF16),
            pltpu.SemaphoreType.DMA((plan.mom_dev,)),
            pltpu.SemaphoreType.DMA((2 * (tiles[0] * tiles[1] + 1),)),
        ],
        grant=LARGE_GRANT,
    )
    blocks = exchange(packed)

    arrived = []
    for message, (plane, d) in zip(messages, plan.hops()):
        route = []
        for e in range(n_energy):
            g, rest = divmod(e, plan.group)
            later, seat = divmod(rest, plan.half)
            g, to = (g + 1, plane) if later else (g - 1, 1 - plane)
            if 0 <= g < plan.n_groups:
                route.append((e, g * plan.group + to * plan.half + (seat ^ d)))
        arrived.append(lax.ppermute(message, "energy", route))
    side_shape = shape((plan.sides, plan.half, plan.rows, LANES), BF16)
    halos = list(call(plan, halo_kernel, [side_shape] * n_mom, *arrived))
    for t in range(1, n_mom):
        halos[t] = lax.ppermute(halos[t], "mom", [(m, m ^ t) for m in range(n_mom)])

    lag_count = plan.momenta * BRANCH
    lag_rows = -(-lag_count // 16) * 16
    couple = coupling.reshape(plan.pairs_dev, BRANCH, ORB, ORB)
    couple = jnp.pad(couple, ((0, 0), (0, 0), (0, 16 - ORB), (0, FREQ - ORB)))
    phonon = phonon_green.reshape(plan.momenta, plan.pairs_dev, BRANCH, FREQ)
    phonon = jnp.moveaxis(phonon, 1, 0).reshape(plan.pairs_dev, lag_count, FREQ)
    phonon = jnp.pad(phonon, ((0, 0), (0, lag_rows - lag_count), (0, 0)))
    table = jnp.concatenate([couple.reshape(plan.pairs_dev, BRANCH * 16, FREQ), phonon], axis=1)
    table = lax.dynamic_slice_in_dim(table, me * plan.sub, plan.sub, axis=0)
    tables = [table]
    for d in range(1, plan.n_groups):
        tables.append(swap_groups(table, functools.partial(lambda d, g: g ^ d, d)))
    tables = jnp.concatenate(tables, axis=0)
    sand = call(
        plan, sandwich_kernel, shape((plan.own, 2, 2 * LANES, BRANCH * 2 * LANES), BF16), tables
    )
    toep = call(plan, toeplitz_kernel, shape((plan.own, plan.momenta, BRANCH * FREQ, 2 * FREQ), BF16), tables)
    blocks, halos, sand, toep = lax.optimization_barrier((blocks, halos, sand, toep))

    halo_scratch = pltpu.VMEM((n_mom * plan.sides * plan.half, plan.rows, LANES), BF16)
    sigma = call(
        plan,
        self_kernel,
        in_hbm(wire),
        blocks,
        *halos,
        toep,
        sand,
        out_specs=HBM,
        scratch=[pltpu.VMEM(wire.shape, BF16), halo_scratch, pltpu.SemaphoreType.DMA((2,))],
    )
    arrived = exchange(sigma)

    scale = (plan.momenta * n_energy * plan.steps * COMP) ** -0.5
    side_rows = plan.mom_dev * BRANCH
    parts = list(
        call(
            plan,
            functools.partial(phonon_kernel, scale=scale),
            [shape((plan.sub, side_rows, LANES), F32)] * (plan.n_groups * n_mom),
            blocks,
            *halos,
            sand,
            scratch=[pltpu.VMEM((plan.own, n_mom, side_rows, LANES), F32), halo_scratch],
        )
    )
    for d in range(plan.n_groups):
        for t in range(n_mom):
            if d or t:
                route = []
                for e in range(n_energy):
                    g, j = divmod(e, plan.group)
                    for m in range(n_mom):
                        route.append((e * n_mom + m, ((g ^ d) * plan.group + j) * n_mom + (m ^ t)))
                parts[d * n_mom + t] = lax.ppermute(parts[d * n_mom + t], axes, route)
    phonon_self = call(
        plan, collect_kernel, shape((plan.mom_dev, plan.pairs_dev, BRANCH * FREQ), F32), *parts
    )

    self_energy = call(
        plan,
        unpack_kernel,
        shape(lesser_green.shape, BF16),
        arrived,
        out_specs=ANY,
        scratch=[pltpu.VMEM(tiles + (plan.steps, TILE, COMP), BF16), pltpu.SemaphoreType.DMA(tiles)],
    )
    return self_energy, phonon_self


def solution(mesh):
    in_specs = (P("mom", "energy", None, None), P(), P(None, "energy", None), P("energy", None))
    out_specs = (P("mom", "energy", None, None), P("mom", "energy", None))
    return jax.shard_map(shards, mesh=mesh, in_specs=in_specs, out_specs=out_specs, check_vma=False)
```

```python
import functools

import jax
import jax.numpy as jnp
from jax import lax
from jax.experimental import pallas as pl
from jax.experimental.pallas import tpu as pltpu
from jax.sharding import PartitionSpec as P

ORB = 12
BRANCH = 3
FREQ = 64
COMP = 288
SQUARE = ORB * ORB
LANES = 128
REST = SQUARE - LANES
TAIL = 2 * REST
SLOTS = LANES // TAIL
TILE = 16
SMALL_GRANT = 16 * 1024 * 1024
LARGE_GRANT = 60 * 1024 * 1024
LONG = 100_000_000_000

BF16 = jnp.bfloat16
F32 = jnp.float32
I32 = jnp.int32


class Plan:
    def __init__(self, green, phonon, n_energy, n_mom):
        self.n_energy, self.n_mom = n_energy, n_mom
        self.mom_dev, self.steps, self.pairs, _ = green.shape
        self.momenta = self.mom_dev * n_mom
        self.pairs_dev = phonon.shape[1]
        self.group = FREQ // self.steps
        self.n_groups = n_energy // self.group
        self.peers = self.group * n_mom
        self.sub = self.pairs_dev // n_mom
        self.own = self.n_groups * self.sub
        self.block = self.group * self.pairs_dev
        self.main_rows = self.mom_dev * self.own * 2 * self.steps
        self.tail_rows = self.mom_dev * self.own // SLOTS * self.steps
        self.rows = self.main_rows + self.tail_rows
        assert self.group * self.steps == FREQ and n_energy % self.group == 0
        assert self.n_groups & (self.n_groups - 1) == 0
        assert self.pairs_dev % n_mom == 0 and TILE % self.block == 0
        assert self.mom_dev * self.own % SLOTS == 0 and self.n_groups % 2 == 0

    def main_row(self, k, u):
        return (k * self.own + u) * 2 * self.steps

    def tail_row(self, k, u):
        return self.main_rows + (k * self.own + u) // SLOTS * self.steps

    def shift(self, k):
        return k * self.own % SLOTS * TAIL

    def place(self, h, i):
        s, rest = divmod(TILE * h + i, self.block)
        j, rest = divmod(rest, self.pairs_dev)
        m, b = divmod(rest, self.sub)
        return j * self.n_mom + m, s * self.sub + b


def dot(a, b):
    return lax.dot_general(a, b, (((1,), (0,)), ((), ())), preferred_element_type=F32)


def dot_nt(a, b):
    return lax.dot_general(a, b, (((1,), (1,)), ((), ())), preferred_element_type=F32)


def iota(dims, axis):
    return lax.broadcasted_iota(I32, dims, axis)


def swap_matrix(outer, inner, flip=False):
    n = outer * inner
    row, col = iota((n, n), 0), iota((n, n), 1)
    place = row & (outer - 1)
    source = (outer - 1 - place if flip else place) * inner + (row >> (outer.bit_length() - 1))
    return (col == source).astype(F32).astype(BF16)


def to_wire(rows):
    tail = jnp.concatenate([rows[:, LANES:SQUARE], rows[:, SQUARE + LANES :]], axis=1)
    return rows[:, :LANES], rows[:, SQUARE : SQUARE + LANES], tail


def pack_rows(plan, load, out_ref, stage, sems, flip=False):
    swap = swap_matrix(plan.steps, TILE, flip)
    tails, copies = {}, []

    def send(first, count):
        rows = slice(first, first + count)
        copy = pltpu.make_async_copy(stage.at[:, rows, :], out_ref.at[:, rows, :], sems.at[len(copies)])
        copy.start()
        copies.append(copy)

    for k in range(plan.mom_dev):
        for h in range(plan.pairs // TILE):
            left, right, tail = to_wire(dot(swap, load(k, h)).astype(BF16))
            for i in range(TILE):
                peer, u = plan.place(h, i)
                here = slice(i * plan.steps, (i + 1) * plan.steps)
                row = plan.main_row(k, u)
                stage[peer, row : row + plan.steps, :] = left[here]
                stage[peer, row + plan.steps : row + 2 * plan.steps, :] = right[here]
                tails[peer, k * plan.own + u] = tail[here]
            count = TILE // plan.block * plan.sub
            send(plan.main_row(k, h * count), count * 2 * plan.steps)
    for peer in range(plan.peers):
        for first in range(0, plan.mom_dev * plan.own, SLOTS):
            row = plan.main_rows + first // SLOTS * plan.steps
            joined = jnp.concatenate([tails[peer, first + t] for t in range(SLOTS)], axis=1)
            stage[peer, row : row + plan.steps, :] = joined
    send(plan.main_rows, plan.tail_rows)
    for copy in copies:
        copy.wait()


def pack_own_kernel(plan, green_ref, out_ref, stage, out_sems, tiles, sems):
    copies = {}
    for k in range(plan.mom_dev):
        for h in range(plan.pairs // TILE):
            copies[k, h] = pltpu.make_async_copy(
                green_ref.at[k, :, TILE * h : TILE * (h + 1), :], tiles.at[k, h], sems.at[k, h]
            )
            copies[k, h].start()

    def load(k, h):
        copies[k, h].wait()
        return tiles[k, h].reshape(plan.steps * TILE, COMP)

    pack_rows(plan, load, out_ref, stage, out_sems)


def pack_partner_kernel(plan, take_ref, green_ref, out_ref, stage, sems, taken):
    chunk = take_ref.shape[0] // plan.pairs
    take = take_ref[...]
    for k in range(plan.mom_dev):
        for e in range(0, plan.steps, chunk):
            rows = green_ref[k, e : e + chunk].reshape(chunk * plan.pairs, COMP)
            taken[k, e : e + chunk] = dot(take, rows).astype(BF16).reshape(chunk, plan.pairs, COMP)

    def load(k, h):
        return taken[k, :, TILE * h : TILE * (h + 1), :].reshape(plan.steps * TILE, COMP)

    pack_rows(plan, load, out_ref, stage, sems, flip=True)


def each_pair(plan, body):
    if plan.own <= SLOTS:
        for u in range(plan.own):
            body(u)
    else:
        lax.fori_loop(0, plan.own, lambda u, _: body(u), None)


def rows_at(row, count):
    return pl.ds(row if isinstance(row, int) else pl.multiple_of(row, count), count)


def my_table(plan, tables_ref, u):
    group = lax.axis_index("energy") // plan.group
    return tables_ref[(u // plan.sub ^ group) * plan.sub + u % plan.sub]


def sandwich_kernel(plan, tables_ref, sand_ref):
    place, want = iota((2 * LANES, 16), 0), iota((2 * LANES, 16), 1)

    def body(u):
        couple = my_table(plan, tables_ref, u)[: BRANCH * 16, :16]
        for h in range(2):
            comp = jnp.where(place < LANES, place, place - (u % SLOTS * TAIL + h * REST))
            valid = (place < LANES) | ((comp >= LANES) & (comp < SQUARE))
            quotient = (comp * 171) >> 11
            first = (valid & (quotient == want)).astype(F32).astype(BF16)
            second = (valid & (comp - ORB * quotient == want)).astype(F32).astype(BF16)
            left = dot_nt(couple, first).astype(BF16)
            right = dot_nt(couple, second).astype(BF16)
            for i in range(BRANCH):
                rows = slice(16 * i, 16 * i + 16)
                product = dot(first, left[rows]) * dot(second, right[rows])
                sand_ref[u, h, :, 2 * LANES * i : 2 * LANES * (i + 1)] = product.astype(BF16)

    each_pair(plan, body)


def toeplitz_kernel(plan, tables_ref, toep_ref):
    mirror = iota((FREQ, 2 * FREQ), 0) + iota((FREQ, 2 * FREQ), 1) == FREQ
    mirror = mirror.astype(F32).astype(BF16)

    def body(u):
        lags = dot(my_table(plan, tables_ref, u)[BRANCH * 16 :, :], mirror)
        for q in range(plan.momenta):
            for i in range(BRANCH):
                n = q * BRANCH + i
                band = jnp.broadcast_to(lags[n : n + 1], (FREQ, 2 * FREQ))
                band = pltpu.roll(band, 0, 1, stride=1, stride_axis=0)
                toep_ref[u, q, i * FREQ : (i + 1) * FREQ, :] = band.astype(BF16)

    each_pair(plan, body)


def gather_rows(plan, ref, u, y, flip=False):
    m, k = divmod(y, plan.mom_dev)
    row, tail = plan.main_row(k, u), plan.tail_row(k, u)
    order = range(plan.group)
    lefts, rights, tails = [], [], []
    for j in reversed(order) if flip else order:
        peer = j * plan.n_mom + m
        lefts.append(ref[peer, rows_at(row, plan.steps), :])
        rights.append(ref[peer, rows_at(row + plan.steps, plan.steps), :])
        tails.append(ref[peer, rows_at(tail, plan.steps), :])
    tails = jnp.concatenate(tails, axis=0)
    if plan.shift(k):
        tails = pltpu.roll(tails.astype(F32), LANES - plan.shift(k), 1).astype(BF16)
    return jnp.concatenate([jnp.concatenate(lefts, axis=0), jnp.concatenate(rights, axis=0), tails], axis=1)


def half_and_tail(rows, h):
    return jnp.concatenate([rows[:, h * LANES : (h + 1) * LANES], rows[:, 2 * LANES :]], axis=1)


def halo_rows(plan, even, odd, u, y, later):
    group = lax.axis_index("energy") // plan.group
    inner = group % 2 == (0 if later else 1)
    exists = group < plan.n_groups - 1 if later else group > 0
    rows = jnp.where(inner, gather_rows(plan, even, u, y), gather_rows(plan, odd, u, y))
    return rows * exists.astype(F32).astype(BF16)


def self_kernel(plan, own, even, odd, toep_ref, sand_ref, out_ref, stage, sems):
    copies = []

    def send(rows):
        copy = pltpu.make_async_copy(stage.at[:, rows, :], out_ref.at[:, rows, :], sems.at[len(copies)])
        copy.start()
        copies.append(copy)

    for peer in range(plan.peers):
        stage[peer, plan.main_rows :, :] = jnp.zeros((plan.tail_rows, LANES), BF16)

    def body(u):
        green = []
        for y in range(plan.momenta):
            green.append(halo_rows(plan, even, odd, u, y, False))
            green.append(gather_rows(plan, own, u, y))
        green = jnp.concatenate(green, axis=0)
        summed = []
        for i in range(BRANCH):
            rows = slice(i * FREQ, (i + 1) * FREQ)
            band = jnp.concatenate(
                [
                    jnp.concatenate(
                        [toep_ref[u, (k - y) % plan.momenta, rows, :] for y in range(plan.momenta)], axis=1
                    )
                    for k in range(plan.momenta)
                ],
                axis=0,
            )
            summed.append(dot(band, green).astype(BF16))
        left, right = [
            dot_nt(jnp.concatenate([half_and_tail(rows, h) for rows in summed], axis=1), sand_ref[u, h])
            for h in range(2)
        ]
        tails = left[:, LANES:] + right[:, LANES:]
        left, right = left[:, :LANES].astype(BF16), right[:, :LANES].astype(BF16)
        for y in range(plan.momenta):
            m, k = divmod(y, plan.mom_dev)
            row, tail = plan.main_row(k, u), plan.tail_row(k, u)
            rest = tails[y * FREQ : (y + 1) * FREQ]
            if plan.shift(k):
                rest = pltpu.roll(rest, plan.shift(k), 1)
            rest = rest.astype(BF16)
            for j in range(plan.group):
                peer = j * plan.n_mom + m
                here = slice(j * plan.steps, (j + 1) * plan.steps)
                there = slice(y * FREQ + j * plan.steps, y * FREQ + (j + 1) * plan.steps)
                stage[peer, rows_at(row, plan.steps), :] = left[there]
                stage[peer, rows_at(row + plan.steps, plan.steps), :] = right[there]
                stage[peer, rows_at(tail, plan.steps), :] += rest[here]
        if isinstance(u, int):
            for k in range(plan.mom_dev):
                send(pl.ds(plan.main_row(k, u), 2 * plan.steps))

    each_pair(plan, body)
    send(pl.ds(plan.main_rows, plan.tail_rows) if copies else pl.ds(0, plan.rows))
    for copy in copies:
        copy.wait()


def lag_sums(plan, u, partner, green, sand_ref, store):
    partner, green = jnp.concatenate(partner, axis=0), jnp.concatenate(green, axis=0)
    left, right = [dot(half_and_tail(partner, h), sand_ref[u, h]) for h in range(2)]
    for i in range(BRANCH):
        here = slice(2 * LANES * i, 2 * LANES * i + LANES)
        rest = slice(2 * LANES * i + LANES, 2 * LANES * (i + 1))
        applied = jnp.concatenate([left[:, here], right[:, here], left[:, rest] + right[:, rest]], axis=1)
        lagged = dot_nt(applied.astype(BF16), green)
        for q in range(plan.momenta):
            acc = None
            for k in range(plan.momenta):
                y = (k + q) % plan.momenta
                part = lagged[k * FREQ : (k + 1) * FREQ, y * 2 * FREQ : (y + 1) * 2 * FREQ]
                acc = part if acc is None else acc + part
            acc = pltpu.roll(acc, FREQ + 1, 1, stride=1, stride_axis=0)
            store(q, i, jnp.sum(acc, axis=0, keepdims=True))


def phonon_kernel(plan, own, even, odd, partner, sand_ref, *refs, scale):
    outs, sums = refs[:-1], refs[-1]
    group = lax.axis_index("energy") // plan.group
    me = lax.axis_index("mom")

    def body(u):
        rows = [gather_rows(plan, partner, u, k, flip=True) for k in range(plan.momenta)]
        green = []
        for y in range(plan.momenta):
            green.append(gather_rows(plan, own, u, y))
            green.append(halo_rows(plan, even, odd, u, y, True))

        def store(q, i, lags):
            side, row = divmod(q * BRANCH + i, plan.mom_dev * BRANCH)
            sums[u, side, row : row + 1, :] = lags * scale

        lag_sums(plan, u, rows, green, sand_ref, store)

    each_pair(plan, body)
    for d in range(plan.n_groups):
        for t in range(plan.n_mom):
            for b in range(plan.sub):
                outs[d * plan.n_mom + t][b] = sums[(group ^ d) * plan.sub + b, me ^ t]


def collect_kernel(plan, *refs):
    parts, out_ref = refs[:-1], refs[-1]
    me = lax.axis_index("mom")
    for d in range(plan.n_mom):
        total = sum(ref[...] for ref in parts[d :: plan.n_mom])
        for b in range(plan.sub):
            pair = (me ^ d) * plan.sub + b
            for q in range(plan.mom_dev):
                rows = [total[b, q * BRANCH + i : q * BRANCH + i + 1, :FREQ] for i in range(BRANCH)]
                out_ref[q, pl.ds(pair, 1), :] = jnp.concatenate(rows, axis=1)


def unpack_kernel(plan, wire, out_ref, tiles, sems):
    swap = swap_matrix(TILE, plan.steps)
    copies = []
    for k in range(plan.mom_dev):
        for h in range(plan.pairs // TILE):
            lefts, rights, tails = [], [], []
            for i in range(TILE):
                peer, u = plan.place(h, i)
                row, tail = plan.main_row(k, u), plan.tail_row(k, u)
                lefts.append(wire[peer, row : row + plan.steps, :])
                rights.append(wire[peer, row + plan.steps : row + 2 * plan.steps, :])
                lane = (k * plan.own + u) % SLOTS * TAIL
                tails.append(wire[peer, tail : tail + plan.steps, :][:, lane : lane + TAIL])
            rows = jnp.concatenate([jnp.concatenate(part, axis=0) for part in (lefts, rights, tails)], axis=1)
            moved = dot(swap, rows).astype(BF16)
            left, right = moved[:, :LANES], moved[:, LANES : 2 * LANES]
            tail = moved[:, 2 * LANES :]
            moved = jnp.concatenate([left, tail[:, :REST], right, tail[:, REST:]], axis=1)
            tiles[k, h] = moved.reshape(plan.steps, TILE, COMP)
            copy = pltpu.make_async_copy(
                tiles.at[k, h], out_ref.at[k, :, TILE * h : TILE * (h + 1), :], sems.at[k, h]
            )
            copy.start()
            copies.append(copy)
    for copy in copies:
        copy.wait()


ANY = pl.BlockSpec(memory_space=pl.ANY)
HBM = pl.BlockSpec(memory_space=pltpu.HBM)
VMEM = pl.BlockSpec(memory_space=pltpu.VMEM)


def call(plan, kernel, out_shape, *args, in_specs=None, out_specs=None, scratch=(), flops=1, grant=None):
    outs = jax.tree.map(lambda _: VMEM, out_shape)
    return pl.pallas_call(
        functools.partial(kernel, plan),
        out_shape=out_shape,
        in_specs=in_specs or [VMEM] * len(args),
        out_specs=out_specs or outs,
        scratch_shapes=list(scratch),
        compiler_params=pltpu.CompilerParams(vmem_limit_bytes=grant or SMALL_GRANT * max(1, plan.own // 4)),
        cost_estimate=pl.CostEstimate(flops=flops, bytes_accessed=1, transcendentals=0),
    )(*args)


def shape(dims, dtype):
    return jax.ShapeDtypeStruct(dims, dtype)


def in_hbm(struct):
    return pltpu.HBM(struct.shape, struct.dtype)


def shards(lesser_green, partner, phonon_green, coupling):
    n_energy, n_mom = lax.axis_size("energy"), lax.axis_size("mom")
    plan = Plan(lesser_green, phonon_green, n_energy, n_mom)
    axes = ("energy", "mom")
    me = lax.axis_index("mom")
    s = lax.axis_index("energy") // plan.group
    wire = shape((plan.peers, plan.rows, LANES), BF16)
    groups = [[g * plan.peers + i for i in range(plan.peers)] for g in range(plan.n_groups)]
    tiles = (plan.mom_dev, plan.pairs // TILE)

    def exchange(blocks):
        return lax.all_to_all(blocks, axes, split_axis=0, concat_axis=0, axis_index_groups=groups, tiled=True)

    def swap_groups(values, other):
        route = []
        for e in range(n_energy):
            g, j = divmod(e, plan.group)
            to = other(g) if 0 <= other(g) < plan.n_groups else g
            route.append((e, to * plan.group + j))
        return lax.ppermute(values, "energy", route)

    staging = [pltpu.VMEM(wire.shape, BF16), pltpu.SemaphoreType.DMA((tiles[0] * tiles[1] + 1,))]
    tile_scratch = [pltpu.VMEM(tiles + (plan.steps, TILE, COMP), BF16), pltpu.SemaphoreType.DMA(tiles)]
    own = exchange(
        call(
            plan,
            pack_own_kernel,
            in_hbm(wire),
            lesser_green,
            in_specs=[HBM],
            out_specs=HBM,
            scratch=staging + tile_scratch,
            grant=LARGE_GRANT,
        )
    )

    lag_count = plan.momenta * BRANCH
    lag_rows = -(-lag_count // 16) * 16
    couple = coupling.reshape(plan.pairs_dev, BRANCH, ORB, ORB)
    couple = jnp.pad(couple, ((0, 0), (0, 0), (0, 16 - ORB), (0, FREQ - ORB)))
    phonon = phonon_green.reshape(plan.momenta, plan.pairs_dev, BRANCH, FREQ)
    phonon = jnp.moveaxis(phonon, 1, 0).reshape(plan.pairs_dev, lag_count, FREQ)
    phonon = jnp.pad(phonon, ((0, 0), (0, lag_rows - lag_count), (0, 0)))
    table = jnp.concatenate([couple.reshape(plan.pairs_dev, BRANCH * 16, FREQ), phonon], axis=1)
    table = lax.dynamic_slice_in_dim(table, me * plan.sub, plan.sub, axis=0)
    tables = [table]
    for d in range(1, plan.n_groups):
        tables.append(swap_groups(table, functools.partial(lambda d, g: g ^ d, d)))
    tables = jnp.concatenate(tables, axis=0)
    own, tables = lax.optimization_barrier((own, tables))

    def neighbours(shift):
        route = []
        for e in range(n_energy):
            g, j = divmod(e, plan.group)
            to = ((g - shift) ^ 1) + shift
            for m in range(n_mom):
                if 0 <= to < plan.n_groups:
                    route.append((e * n_mom + m, (to * plan.group + j) * n_mom + m))
                else:
                    route.append((e * n_mom + m, e * n_mom + (m ^ 1)))
        return lax.ppermute(own, axes, route)

    even, odd = neighbours(0), neighbours(1)

    chunk = max(1, 256 // plan.pairs)
    source = (jnp.arange(chunk)[:, None] * plan.pairs + partner[None, :]).reshape(-1)
    take = (source[:, None] == jnp.arange(chunk * plan.pairs)[None, :]).astype(BF16)
    own, take = lax.optimization_barrier((own, take))
    partner_blocks = exchange(
        call(
            plan,
            pack_partner_kernel,
            in_hbm(wire),
            take,
            lesser_green,
            out_specs=HBM,
            scratch=staging + [pltpu.VMEM(lesser_green.shape, BF16)],
            flops=LONG,
        )
    )

    sand = call(
        plan, sandwich_kernel, shape((plan.own, 2, 2 * LANES, BRANCH * 2 * LANES), BF16), tables
    )
    toep = call(plan, toeplitz_kernel, shape((plan.own, plan.momenta, BRANCH * FREQ, 2 * FREQ), BF16), tables)
    sigma = call(
        plan,
        self_kernel,
        in_hbm(wire),
        own,
        even,
        odd,
        toep,
        sand,
        out_specs=HBM,
        scratch=[pltpu.VMEM(wire.shape, BF16), pltpu.SemaphoreType.DMA((plan.mom_dev * plan.own + 1,))],
        flops=LONG,
    )
    arrived = exchange(sigma)

    scale = (plan.momenta * n_energy * plan.steps * COMP) ** -0.5
    side_rows = plan.mom_dev * BRANCH
    parts = list(
        call(
            plan,
            functools.partial(phonon_kernel, scale=scale),
            [shape((plan.sub, side_rows, LANES), F32)] * (plan.n_groups * n_mom),
            own,
            even,
            odd,
            partner_blocks,
            sand,
            scratch=[pltpu.VMEM((plan.own, n_mom, side_rows, LANES), F32)],
        )
    )
    for d in range(plan.n_groups):
        for t in range(n_mom):
            if d or t:
                route = []
                for e in range(n_energy):
                    g, j = divmod(e, plan.group)
                    for m in range(n_mom):
                        route.append((e * n_mom + m, ((g ^ d) * plan.group + j) * n_mom + (m ^ t)))
                parts[d * n_mom + t] = lax.ppermute(parts[d * n_mom + t], axes, route)
    phonon_self = call(
        plan, collect_kernel, shape((plan.mom_dev, plan.pairs_dev, BRANCH * FREQ), F32), *parts
    )

    self_energy = call(
        plan,
        unpack_kernel,
        shape(lesser_green.shape, BF16),
        arrived,
        out_specs=ANY,
        scratch=tile_scratch,
    )
    return self_energy, phonon_self


def solution(mesh):
    in_specs = (P("mom", "energy", None, None), P(), P(None, "energy", None), P("energy", None))
    out_specs = (P("mom", "energy", None, None), P("mom", "energy", None))
    return jax.shard_map(shards, mesh=mesh, in_specs=in_specs, out_specs=out_specs, check_vma=False)
```

```python
import functools

import jax
import jax.numpy as jnp
from jax import lax
from jax.experimental import pallas as pl
from jax.experimental.pallas import tpu as pltpu
from jax.sharding import PartitionSpec as P

ORB = 12
BRANCH = 3
FREQ = 64
COMP = 288
SQUARE = ORB * ORB
LANES = 128
REST = SQUARE - LANES
TAIL = 2 * REST
SLOTS = LANES // TAIL
TILE = 16
SMALL_GRANT = 16 * 1024 * 1024
LARGE_GRANT = 60 * 1024 * 1024
LONG = 100_000_000_000

BF16 = jnp.bfloat16
F32 = jnp.float32
I32 = jnp.int32


class Plan:
    def __init__(self, green, phonon, n_energy, n_mom):
        self.n_energy, self.n_mom = n_energy, n_mom
        self.mom_dev, self.steps, self.pairs, _ = green.shape
        self.momenta = self.mom_dev * n_mom
        self.pairs_dev = phonon.shape[1]
        self.half = FREQ // self.steps
        self.group = 2 * self.half
        self.n_groups = n_energy // self.group
        self.peers = self.group * n_mom
        self.sub = self.pairs_dev // n_mom
        self.own = self.n_groups * self.sub
        self.main_rows = self.mom_dev * self.own * 2 * self.steps
        self.tail_rows = self.mom_dev * self.own // SLOTS * self.steps
        self.rows = self.main_rows + self.tail_rows
        assert self.half * self.steps == FREQ and n_energy % self.group == 0
        assert self.n_groups & (self.n_groups - 1) == 0 and self.own % 2 == 0
        self.few = self.own // 2
        self.few_rows = self.mom_dev * self.few * 2 * self.steps
        assert self.pairs_dev % n_mom == 0 and self.group * self.pairs_dev == TILE
        assert self.mom_dev * self.own % SLOTS == 0 and self.n_groups % 2 == 0

    def main_row(self, k, u):
        return (k * self.own + u) * 2 * self.steps

    def tail_row(self, k, u):
        return self.main_rows + (k * self.own + u) // SLOTS * self.steps

    def piece_rows(self, piece):
        return self.few_rows + (self.tail_rows if piece == 0 else 0)

    def shift(self, k):
        return k * self.own % SLOTS * TAIL

    def place(self, h, i):
        j, rest = divmod(i, self.pairs_dev)
        m, b = divmod(rest, self.sub)
        return j * self.n_mom + m, h * self.sub + b


def dot(a, b):
    return lax.dot_general(a, b, (((1,), (0,)), ((), ())), preferred_element_type=F32)


def dot_nt(a, b):
    return lax.dot_general(a, b, (((1,), (1,)), ((), ())), preferred_element_type=F32)


def iota(dims, axis):
    return lax.broadcasted_iota(I32, dims, axis)


def swap_matrix(outer, inner, flip=False):
    n = outer * inner
    row, col = iota((n, n), 0), iota((n, n), 1)
    place = row & (outer - 1)
    source = (outer - 1 - place if flip else place) * inner + (row >> (outer.bit_length() - 1))
    return (col == source).astype(F32).astype(BF16)


def to_wire(rows):
    tail = jnp.concatenate([rows[:, LANES:SQUARE], rows[:, SQUARE + LANES :]], axis=1)
    return rows[:, :LANES], rows[:, SQUARE : SQUARE + LANES], tail


def pack_rows(plan, load, out_ref, stage, sems, flip=False):
    swap = swap_matrix(plan.steps, TILE, flip)
    tails, copies = {}, []

    def send(first, count):
        rows = slice(first, first + count)
        copy = pltpu.make_async_copy(stage.at[:, rows, :], out_ref.at[:, rows, :], sems.at[len(copies)])
        copy.start()
        copies.append(copy)

    for k in range(plan.mom_dev):
        for h in range(plan.pairs // TILE):
            left, right, tail = to_wire(dot(swap, load(k, h)).astype(BF16))
            for i in range(TILE):
                peer, u = plan.place(h, i)
                here = slice(i * plan.steps, (i + 1) * plan.steps)
                row = plan.main_row(k, u)
                stage[peer, row : row + plan.steps, :] = left[here]
                stage[peer, row + plan.steps : row + 2 * plan.steps, :] = right[here]
                tails[peer, k * plan.own + u] = tail[here]
            send(plan.main_row(k, h * plan.sub), plan.sub * 2 * plan.steps)
    for peer in range(plan.peers):
        for first in range(0, plan.mom_dev * plan.own, SLOTS):
            row = plan.main_rows + first // SLOTS * plan.steps
            joined = jnp.concatenate([tails[peer, first + t] for t in range(SLOTS)], axis=1)
            stage[peer, row : row + plan.steps, :] = joined
    send(plan.main_rows, plan.tail_rows)
    for copy in copies:
        copy.wait()


def pack_own_kernel(plan, green_ref, out_ref, stage, out_sems, tiles, sems):
    copies = {}
    for k in range(plan.mom_dev):
        for h in range(plan.pairs // TILE):
            copies[k, h] = pltpu.make_async_copy(
                green_ref.at[k, :, TILE * h : TILE * (h + 1), :], tiles.at[k, h], sems.at[k, h]
            )
            copies[k, h].start()

    def load(k, h):
        copies[k, h].wait()
        return tiles[k, h].reshape(plan.steps * TILE, COMP)

    pack_rows(plan, load, out_ref, stage, out_sems)


def pack_partner_kernel(plan, take_ref, green_ref, out_ref, stage, sems, taken):
    chunk = take_ref.shape[0] // plan.pairs
    take = take_ref[...]
    for k in range(plan.mom_dev):
        for e in range(0, plan.steps, chunk):
            rows = green_ref[k, e : e + chunk].reshape(chunk * plan.pairs, COMP)
            taken[k, e : e + chunk] = dot(take, rows).astype(BF16).reshape(chunk, plan.pairs, COMP)

    def load(k, h):
        return taken[k, :, TILE * h : TILE * (h + 1), :].reshape(plan.steps * TILE, COMP)

    pack_rows(plan, load, out_ref, stage, sems, flip=True)


def each_pair(plan, body, pairs=None):
    first, last = (0, plan.own) if pairs is None else (pairs.start, pairs.stop)
    if plan.own <= 2:
        for u in range(first, last):
            body(u)
    else:
        lax.fori_loop(first, last, lambda u, _: body(u), None)


def pairs_of(plan, piece):
    return range(piece * plan.few, (piece + 1) * plan.few)


def rows_at(row, count):
    return pl.ds(row if isinstance(row, int) else pl.multiple_of(row, count), count)


def my_table(plan, tables_ref, u):
    group = lax.axis_index("energy") // plan.group
    return tables_ref[(u // plan.sub ^ group) * plan.sub + u % plan.sub]


def sandwich_kernel(plan, tables_ref, sand_ref):
    place, want = iota((2 * LANES, 16), 0), iota((2 * LANES, 16), 1)

    def body(u):
        couple = my_table(plan, tables_ref, u)[: BRANCH * 16, :16]
        for h in range(2):
            comp = jnp.where(place < LANES, place, place - (u % SLOTS * TAIL + h * REST))
            valid = (place < LANES) | ((comp >= LANES) & (comp < SQUARE))
            quotient = (comp * 171) >> 11
            first = (valid & (quotient == want)).astype(F32).astype(BF16)
            second = (valid & (comp - ORB * quotient == want)).astype(F32).astype(BF16)
            left = dot_nt(couple, first).astype(BF16)
            right = dot_nt(couple, second).astype(BF16)
            for i in range(BRANCH):
                rows = slice(16 * i, 16 * i + 16)
                product = dot(first, left[rows]) * dot(second, right[rows])
                sand_ref[u, h, :, 2 * LANES * i : 2 * LANES * (i + 1)] = product.astype(BF16)

    each_pair(plan, body)


def toeplitz_kernel(plan, tables_ref, toep_ref):
    mirror = iota((FREQ, 2 * FREQ), 0) + iota((FREQ, 2 * FREQ), 1) == FREQ
    mirror = mirror.astype(F32).astype(BF16)

    def body(u):
        lags = dot(my_table(plan, tables_ref, u)[BRANCH * 16 :, :], mirror)
        for q in range(plan.momenta):
            for i in range(BRANCH):
                n = q * BRANCH + i
                band = jnp.broadcast_to(lags[n : n + 1], (FREQ, 2 * FREQ))
                band = pltpu.roll(band, 0, 1, stride=1, stride_axis=0)
                toep_ref[u, q, i * FREQ : (i + 1) * FREQ, :] = band.astype(BF16)

    each_pair(plan, body)


def edge_kernel(plan, own_ref, *edges):
    odd = lax.axis_index("energy") // plan.group % 2
    near = plan.half * plan.n_mom
    count = plan.few * 2 * plan.steps
    for n in range(0, len(edges), 2):
        side = 1 - odd if n == 0 else odd
        for i in range(near):
            for piece in range(2):
                for k in range(plan.mom_dev):
                    row = plan.main_row(k, piece * plan.few)
                    edges[n + piece][i, k * count : (k + 1) * count, :] = own_ref[
                        side * near + i, row : row + count, :
                    ]
            edges[n][i, plan.few_rows :, :] = own_ref[side * near + i, plan.main_rows :, :]


def gather_rows(plan, ref, u, y, first, flip=False, piece=None, tail_ref=None):
    m, k = divmod(y, plan.mom_dev)
    row, tail = plan.main_row(k, u), plan.tail_row(k, u)
    if piece is not None:
        row = (k * plan.few + u - piece * plan.few) * 2 * plan.steps
        tail = plan.few_rows + tail - plan.main_rows
    order = range(plan.half)
    lefts, rights, tails = [], [], []
    for j in reversed(order) if flip else order:
        peer = (first + j) * plan.n_mom + m
        lefts.append(ref[peer, rows_at(row, plan.steps), :])
        rights.append(ref[peer, rows_at(row + plan.steps, plan.steps), :])
        tails.append((ref if tail_ref is None else tail_ref)[peer, rows_at(tail, plan.steps), :])
    tails = jnp.concatenate(tails, axis=0)
    if plan.shift(k):
        tails = pltpu.roll(tails.astype(F32), LANES - plan.shift(k), 1).astype(BF16)
    return jnp.concatenate([jnp.concatenate(lefts, axis=0), jnp.concatenate(rights, axis=0), tails], axis=1)


def half_and_tail(rows, h):
    return jnp.concatenate([rows[:, h * LANES : (h + 1) * LANES], rows[:, 2 * LANES :]], axis=1)


def self_block(plan, u, green, toep_ref, sand_ref, out_ref):
    summed = []
    for i in range(BRANCH):
        rows = slice(i * FREQ, (i + 1) * FREQ)
        band = jnp.concatenate(
            [
                jnp.concatenate([toep_ref[u, (k - y) % plan.momenta, rows, :] for y in range(plan.momenta)], axis=1)
                for k in range(plan.momenta)
            ],
            axis=0,
        )
        summed.append(dot(band, green).astype(BF16))
    left, right = [
        dot_nt(jnp.concatenate([half_and_tail(rows, h) for rows in summed], axis=1), sand_ref[u, h])
        for h in range(2)
    ]
    tails = left[:, LANES:] + right[:, LANES:]
    left, right = left[:, :LANES].astype(BF16), right[:, :LANES].astype(BF16)
    for y in range(plan.momenta):
        m, k = divmod(y, plan.mom_dev)
        row, tail = plan.main_row(k, u), plan.tail_row(k, u)
        rest = tails[y * FREQ : (y + 1) * FREQ]
        if plan.shift(k):
            rest = pltpu.roll(rest, plan.shift(k), 1)
        rest = rest.astype(BF16)
        for j in range(plan.half):
            peer = j * plan.n_mom + m
            here = slice(j * plan.steps, (j + 1) * plan.steps)
            there = slice(y * FREQ + j * plan.steps, y * FREQ + (j + 1) * plan.steps)
            out_ref[peer, rows_at(row, plan.steps), :] = left[there]
            out_ref[peer, rows_at(row + plan.steps, plan.steps), :] = right[there]
            out_ref[peer, rows_at(tail, plan.steps), :] += rest[here]


def clear_tails(plan, out_ref):
    for peer in range(plan.half * plan.n_mom):
        out_ref[peer, plan.main_rows :, :] = jnp.zeros((plan.tail_rows, LANES), BF16)


def self_late_kernel(plan, own, toep_ref, sand_ref, out_ref):
    clear_tails(plan, out_ref)

    def body(u):
        green = [gather_rows(plan, own, u, y, first) for y in range(plan.momenta) for first in (0, plan.half)]
        self_block(plan, u, jnp.concatenate(green, axis=0), toep_ref, sand_ref, out_ref)

    each_pair(plan, body)


def halo_rows(plan, pieces, u, y, piece, exists):
    rows = gather_rows(plan, pieces[piece], u, y, 0, piece=piece, tail_ref=pieces[0])
    return rows * exists.astype(F32).astype(BF16)


def early_block(plan, own, pieces, toep_ref, sand_ref, stage, piece):
    exists = lax.axis_index("energy") // plan.group > 0

    def body(u):
        green = []
        for y in range(plan.momenta):
            green.append(halo_rows(plan, pieces, u, y, piece, exists))
            green.append(gather_rows(plan, own, u, y, 0))
        self_block(plan, u, jnp.concatenate(green, axis=0), toep_ref, sand_ref, stage)

    each_pair(plan, body, pairs_of(plan, piece))


def send_rows(plan, stage, out_ref, sems, piece, tails):
    near = plan.half * plan.n_mom
    count = plan.few * 2 * plan.steps
    spans = [(plan.main_row(k, piece * plan.few), count) for k in range(plan.mom_dev)]
    if tails:
        spans.append((plan.main_rows, plan.tail_rows))
    copies = []
    for n, (row, rows) in enumerate(spans):
        here = pl.ds(row, rows)
        copies.append(
            pltpu.make_async_copy(stage.at[:, here, :], out_ref.at[pl.ds(0, near), here, :], sems.at[n])
        )
        copies[-1].start()
    return copies


def self_first_kernel(plan, own, piece0, toep_ref, sand_ref, late_ref, out_ref, tails_ref, stage, sems):
    near = plan.half * plan.n_mom
    upper = pltpu.make_async_copy(late_ref, out_ref.at[near:], sems.at[plan.mom_dev])
    upper.start()
    clear_tails(plan, stage)
    early_block(plan, own, [piece0], toep_ref, sand_ref, stage, 0)
    copies = send_rows(plan, stage, out_ref, sems, 0, False)
    tails_ref[...] = stage[:, plan.main_rows :, :]
    for copy in copies:
        copy.wait()
    upper.wait()


def self_second_kernel(plan, own, piece0, piece1, toep_ref, sand_ref, tails_ref, part_ref, out_ref, stage, sems):
    stage[:, plan.main_rows :, :] = tails_ref[...]
    early_block(plan, own, [piece0, piece1], toep_ref, sand_ref, stage, 1)
    for copy in send_rows(plan, stage, out_ref, sems, 1, True):
        copy.wait()


def lag_sums(plan, u, partner, green, sand_ref, store):
    partner, green = jnp.concatenate(partner, axis=0), jnp.concatenate(green, axis=0)
    left, right = [dot(half_and_tail(partner, h), sand_ref[u, h]) for h in range(2)]
    for i in range(BRANCH):
        here = slice(2 * LANES * i, 2 * LANES * i + LANES)
        rest = slice(2 * LANES * i + LANES, 2 * LANES * (i + 1))
        applied = jnp.concatenate([left[:, here], right[:, here], left[:, rest] + right[:, rest]], axis=1)
        lagged = dot_nt(applied.astype(BF16), green)
        for q in range(plan.momenta):
            acc = None
            for k in range(plan.momenta):
                y = (k + q) % plan.momenta
                part = lagged[k * FREQ : (k + 1) * FREQ, y * 2 * FREQ : (y + 1) * 2 * FREQ]
                acc = part if acc is None else acc + part
            acc = pltpu.roll(acc, FREQ + 1, 1, stride=1, stride_axis=0)
            store(q, i, jnp.sum(acc, axis=0, keepdims=True))


def phonon_early_kernel(plan, own, partner_ref, sand_ref, out_ref):
    def body(u):
        partner = [gather_rows(plan, partner_ref, u, k, 0, flip=True) for k in range(plan.momenta)]
        green = [gather_rows(plan, own, u, y, first) for y in range(plan.momenta) for first in (0, plan.half)]

        def store(q, i, lags):
            out_ref[u, q * BRANCH + i : q * BRANCH + i + 1, :] = lags

        lag_sums(plan, u, partner, green, sand_ref, store)

    each_pair(plan, body)


def phonon_late_kernel(plan, own, piece0, piece1, partner_ref, sand_ref, early_ref, *refs, scale):
    outs, sums = refs[:-1], refs[-1]
    group = lax.axis_index("energy") // plan.group
    me = lax.axis_index("mom")
    exists = group < plan.n_groups - 1

    def terms(u, piece):
        partner = [gather_rows(plan, partner_ref, u, k, plan.half, flip=True) for k in range(plan.momenta)]
        green = []
        for y in range(plan.momenta):
            green.append(gather_rows(plan, own, u, y, plan.half))
            green.append(halo_rows(plan, [piece0, piece1], u, y, piece, exists))

        def store(q, i, lags):
            n = q * BRANCH + i
            side, row = divmod(n, plan.mom_dev * BRANCH)
            sums[u, side, row : row + 1, :] = (lags + early_ref[u, n : n + 1, :]) * scale

        lag_sums(plan, u, partner, green, sand_ref, store)

    for piece in range(2):
        each_pair(plan, functools.partial(terms, piece=piece), pairs_of(plan, piece))
    for d in range(plan.n_groups):
        for t in range(plan.n_mom):
            for b in range(plan.sub):
                outs[d * plan.n_mom + t][b] = sums[(group ^ d) * plan.sub + b, me ^ t]


def collect_kernel(plan, *refs):
    parts, out_ref = refs[:-1], refs[-1]
    me = lax.axis_index("mom")
    for d in range(plan.n_mom):
        total = sum(ref[...] for ref in parts[d :: plan.n_mom])
        for b in range(plan.sub):
            pair = (me ^ d) * plan.sub + b
            for q in range(plan.mom_dev):
                rows = [total[b, q * BRANCH + i : q * BRANCH + i + 1, :FREQ] for i in range(BRANCH)]
                out_ref[q, pl.ds(pair, 1), :] = jnp.concatenate(rows, axis=1)


def unpack_kernel(plan, wire, out_ref, tiles, sems):
    swap = swap_matrix(TILE, plan.steps)
    copies = []
    for k in range(plan.mom_dev):
        for h in range(plan.pairs // TILE):
            lefts, rights, tails = [], [], []
            for i in range(TILE):
                peer, u = plan.place(h, i)
                row, tail = plan.main_row(k, u), plan.tail_row(k, u)
                lefts.append(wire[peer, row : row + plan.steps, :])
                rights.append(wire[peer, row + plan.steps : row + 2 * plan.steps, :])
                lane = (k * plan.own + u) % SLOTS * TAIL
                tails.append(wire[peer, tail : tail + plan.steps, :][:, lane : lane + TAIL])
            rows = jnp.concatenate([jnp.concatenate(part, axis=0) for part in (lefts, rights, tails)], axis=1)
            moved = dot(swap, rows).astype(BF16)
            left, right = moved[:, :LANES], moved[:, LANES : 2 * LANES]
            tail = moved[:, 2 * LANES :]
            moved = jnp.concatenate([left, tail[:, :REST], right, tail[:, REST:]], axis=1)
            tiles[k, h] = moved.reshape(plan.steps, TILE, COMP)
            copy = pltpu.make_async_copy(
                tiles.at[k, h], out_ref.at[k, :, TILE * h : TILE * (h + 1), :], sems.at[k, h]
            )
            copy.start()
            copies.append(copy)
    for copy in copies:
        copy.wait()


ANY = pl.BlockSpec(memory_space=pl.ANY)
HBM = pl.BlockSpec(memory_space=pltpu.HBM)
VMEM = pl.BlockSpec(memory_space=pltpu.VMEM)


def call(plan, kernel, out_shape, *args, in_specs=None, out_specs=None, scratch=(), flops=1, grant=None, aliases=None):
    outs = jax.tree.map(lambda _: VMEM, out_shape)
    return pl.pallas_call(
        functools.partial(kernel, plan),
        out_shape=out_shape,
        in_specs=in_specs or [VMEM] * len(args),
        out_specs=out_specs or outs,
        scratch_shapes=list(scratch),
        compiler_params=pltpu.CompilerParams(vmem_limit_bytes=grant or SMALL_GRANT * max(1, plan.own // 4)),
        cost_estimate=pl.CostEstimate(flops=flops, bytes_accessed=1, transcendentals=0),
        input_output_aliases=aliases or {},
    )(*args)


def shape(dims, dtype):
    return jax.ShapeDtypeStruct(dims, dtype)


def in_hbm(struct):
    return pltpu.HBM(struct.shape, struct.dtype)


def shards(lesser_green, partner, phonon_green, coupling):
    n_energy, n_mom = lax.axis_size("energy"), lax.axis_size("mom")
    plan = Plan(lesser_green, phonon_green, n_energy, n_mom)
    axes = ("energy", "mom")
    me = lax.axis_index("mom")
    s = lax.axis_index("energy") // plan.group
    wire = shape((plan.peers, plan.rows, LANES), BF16)
    half_peers = plan.half * n_mom
    groups = [[g * plan.peers + i for i in range(plan.peers)] for g in range(plan.n_groups)]
    tiles = (plan.mom_dev, plan.pairs // TILE)

    def exchange(blocks):
        return lax.all_to_all(blocks, axes, split_axis=0, concat_axis=0, axis_index_groups=groups, tiled=True)

    def swap_groups(values, other):
        route = []
        for e in range(n_energy):
            g, j = divmod(e, plan.group)
            to = other(g) if 0 <= other(g) < plan.n_groups else g
            route.append((e, to * plan.group + j))
        return lax.ppermute(values, "energy", route)

    staging = [pltpu.VMEM(wire.shape, BF16), pltpu.SemaphoreType.DMA((tiles[0] * tiles[1] + 1,))]
    tile_scratch = [pltpu.VMEM(tiles + (plan.steps, TILE, COMP), BF16), pltpu.SemaphoreType.DMA(tiles)]
    half_wire = shape((half_peers, plan.rows, LANES), BF16)
    own = exchange(
        call(
            plan,
            pack_own_kernel,
            in_hbm(wire),
            lesser_green,
            in_specs=[HBM],
            out_specs=HBM,
            scratch=staging + tile_scratch,
            grant=LARGE_GRANT,
        )
    )

    lag_count = plan.momenta * BRANCH
    lag_rows = -(-lag_count // 16) * 16
    couple = coupling.reshape(plan.pairs_dev, BRANCH, ORB, ORB)
    couple = jnp.pad(couple, ((0, 0), (0, 0), (0, 16 - ORB), (0, FREQ - ORB)))
    phonon = phonon_green.reshape(plan.momenta, plan.pairs_dev, BRANCH, FREQ)
    phonon = jnp.moveaxis(phonon, 1, 0).reshape(plan.pairs_dev, lag_count, FREQ)
    phonon = jnp.pad(phonon, ((0, 0), (0, lag_rows - lag_count), (0, 0)))
    table = jnp.concatenate([couple.reshape(plan.pairs_dev, BRANCH * 16, FREQ), phonon], axis=1)
    table = lax.dynamic_slice_in_dim(table, me * plan.sub, plan.sub, axis=0)
    tables = [table]
    for d in range(1, plan.n_groups):
        tables.append(swap_groups(table, functools.partial(lambda d, g: g ^ d, d)))
    tables = jnp.concatenate(tables, axis=0)
    sand = call(
        plan, sandwich_kernel, shape((plan.own, 2, 2 * LANES, BRANCH * 2 * LANES), BF16), tables
    )
    chunk = max(1, 256 // plan.pairs)
    source = (jnp.arange(chunk)[:, None] * plan.pairs + partner[None, :]).reshape(-1)
    take = (source[:, None] == jnp.arange(chunk * plan.pairs)[None, :]).astype(BF16)
    partner_wire = call(
        plan,
        pack_partner_kernel,
        in_hbm(wire),
        take,
        lesser_green,
        out_specs=HBM,
        scratch=staging + [pltpu.VMEM(lesser_green.shape, BF16)],
    )
    own, partner_wire = lax.optimization_barrier((own, partner_wire))
    partner_blocks = exchange(partner_wire)

    sizes = [shape((half_peers, plan.piece_rows(piece), LANES), BF16) for piece in range(2)]
    edges = call(plan, edge_kernel, sizes * (1 if plan.n_groups == 2 else 2), own)
    before = after = [swap_groups(edge, lambda g: g ^ 1) for edge in edges[:2]]
    if plan.n_groups > 2:
        outer = [swap_groups(edge, lambda g: ((g - 1) ^ 1) + 1) for edge in edges[2:]]
        odd = s % 2 == 1
        before, after = (
            [jnp.where(odd, a, b) for a, b in zip(*order)] for order in ((before, outer), (outer, before))
        )

    toep = call(plan, toeplitz_kernel, shape((plan.own, plan.momenta, BRANCH * FREQ, 2 * FREQ), BF16), tables)
    late = call(plan, self_late_kernel, half_wire, own, toep, sand)
    scratch = [pltpu.VMEM(half_wire.shape, BF16), pltpu.SemaphoreType.DMA((plan.mom_dev + 1,))]
    part, tails = call(
        plan,
        self_first_kernel,
        [in_hbm(wire), shape((half_peers, plan.tail_rows, LANES), BF16)],
        own,
        before[0],
        toep,
        sand,
        late,
        out_specs=[HBM, VMEM],
        scratch=scratch,
        flops=LONG,
    )
    sigma = call(
        plan,
        self_second_kernel,
        in_hbm(wire),
        own,
        *before,
        toep,
        sand,
        tails,
        part,
        in_specs=[VMEM] * 6 + [HBM],
        out_specs=HBM,
        scratch=scratch,
        aliases={6: 0},
    )
    arrived = exchange(sigma)

    scale = (plan.momenta * n_energy * plan.steps * COMP) ** -0.5
    early = call(
        plan,
        phonon_early_kernel,
        shape((plan.own, lag_count, LANES), F32),
        own,
        partner_blocks,
        sand,
    )
    side_rows = plan.mom_dev * BRANCH
    parts = list(call(
        plan,
        functools.partial(phonon_late_kernel, scale=scale),
        [shape((plan.sub, side_rows, LANES), F32)] * (plan.n_groups * n_mom),
        own,
        *after,
        partner_blocks,
        sand,
        early,
        scratch=[pltpu.VMEM((plan.own, n_mom, side_rows, LANES), F32)],
    ))
    for d in range(plan.n_groups):
        for t in range(n_mom):
            if d or t:
                route = []
                for e in range(n_energy):
                    g, j = divmod(e, plan.group)
                    for m in range(n_mom):
                        route.append((e * n_mom + m, ((g ^ d) * plan.group + j) * n_mom + (m ^ t)))
                parts[d * n_mom + t] = lax.ppermute(parts[d * n_mom + t], axes, route)
    phonon_self = call(
        plan, collect_kernel, shape((plan.mom_dev, plan.pairs_dev, BRANCH * FREQ), F32), *parts
    )

    self_energy = call(
        plan,
        unpack_kernel,
        shape(lesser_green.shape, BF16),
        arrived,
        out_specs=ANY,
        scratch=tile_scratch,
    )
    return self_energy, phonon_self


def solution(mesh):
    in_specs = (P("mom", "energy", None, None), P(), P(None, "energy", None), P("energy", None))
    out_specs = (P("mom", "energy", None, None), P("mom", "energy", None))
    return jax.shard_map(shards, mesh=mesh, in_specs=in_specs, out_specs=out_specs, check_vma=False)
```

```python
import functools

import jax
import jax.numpy as jnp
from jax import lax
from jax.experimental import pallas as pl
from jax.experimental.pallas import tpu as pltpu
from jax.sharding import PartitionSpec as P

ORB = 12
BRANCH = 3
FREQ = 64
COMP = 288
SQUARE = ORB * ORB
LANES = 128
REST = SQUARE - LANES
TAIL = 2 * REST
SLOTS = LANES // TAIL
TILE = 16
SMALL_GRANT = 16 * 1024 * 1024
LARGE_GRANT = 60 * 1024 * 1024
LONG = 100_000_000_000

BF16 = jnp.bfloat16
F32 = jnp.float32
I32 = jnp.int32


class Plan:
    def __init__(self, green, phonon, n_energy, n_mom):
        self.n_energy, self.n_mom = n_energy, n_mom
        self.mom_dev, self.steps, self.pairs, _ = green.shape
        self.momenta = self.mom_dev * n_mom
        self.pairs_dev = phonon.shape[1]
        self.half = FREQ // self.steps
        self.group = 2 * self.half
        self.n_groups = n_energy // self.group
        self.peers = self.group * n_mom
        self.sub = self.pairs_dev // n_mom
        self.own = self.n_groups * self.sub
        self.main_rows = self.mom_dev * self.own * 2 * self.steps
        self.tail_rows = self.mom_dev * self.own // SLOTS * self.steps
        self.rows = self.main_rows + self.tail_rows
        assert self.half * self.steps == FREQ and n_energy % self.group == 0
        assert self.n_groups & (self.n_groups - 1) == 0 and self.own % 2 == 0
        self.few = self.own // 2
        self.few_rows = self.mom_dev * self.few * 2 * self.steps
        assert self.pairs_dev % n_mom == 0 and self.group * self.pairs_dev == TILE
        assert self.mom_dev * self.own % SLOTS == 0 and self.n_groups % 2 == 0

    def main_row(self, k, u):
        return (k * self.own + u) * 2 * self.steps

    def tail_row(self, k, u):
        return self.main_rows + (k * self.own + u) // SLOTS * self.steps

    def piece_rows(self, piece):
        return self.few_rows + (self.tail_rows if piece == 0 else 0)

    def shift(self, k):
        return k * self.own % SLOTS * TAIL

    def place(self, h, i):
        j, rest = divmod(i, self.pairs_dev)
        m, b = divmod(rest, self.sub)
        return j * self.n_mom + m, h * self.sub + b


def dot(a, b):
    return lax.dot_general(a, b, (((1,), (0,)), ((), ())), preferred_element_type=F32)


def dot_nt(a, b):
    return lax.dot_general(a, b, (((1,), (1,)), ((), ())), preferred_element_type=F32)


def iota(dims, axis):
    return lax.broadcasted_iota(I32, dims, axis)


def swap_matrix(outer, inner, flip=False):
    n = outer * inner
    row, col = iota((n, n), 0), iota((n, n), 1)
    place = row & (outer - 1)
    source = (outer - 1 - place if flip else place) * inner + (row >> (outer.bit_length() - 1))
    return (col == source).astype(F32).astype(BF16)


def to_wire(rows):
    tail = jnp.concatenate([rows[:, LANES:SQUARE], rows[:, SQUARE + LANES :]], axis=1)
    return rows[:, :LANES], rows[:, SQUARE : SQUARE + LANES], tail


def pack_rows(plan, load, out_ref, stage, sems, flip=False):
    swap = swap_matrix(plan.steps, TILE, flip)
    tails, copies = {}, []

    def send(first, count):
        rows = slice(first, first + count)
        copy = pltpu.make_async_copy(stage.at[:, rows, :], out_ref.at[:, rows, :], sems.at[len(copies)])
        copy.start()
        copies.append(copy)

    for k in range(plan.mom_dev):
        for h in range(plan.pairs // TILE):
            left, right, tail = to_wire(dot(swap, load(k, h)).astype(BF16))
            for i in range(TILE):
                peer, u = plan.place(h, i)
                here = slice(i * plan.steps, (i + 1) * plan.steps)
                row = plan.main_row(k, u)
                stage[peer, row : row + plan.steps, :] = left[here]
                stage[peer, row + plan.steps : row + 2 * plan.steps, :] = right[here]
                tails[peer, k * plan.own + u] = tail[here]
            send(plan.main_row(k, h * plan.sub), plan.sub * 2 * plan.steps)
    for peer in range(plan.peers):
        for first in range(0, plan.mom_dev * plan.own, SLOTS):
            row = plan.main_rows + first // SLOTS * plan.steps
            joined = jnp.concatenate([tails[peer, first + t] for t in range(SLOTS)], axis=1)
            stage[peer, row : row + plan.steps, :] = joined
    send(plan.main_rows, plan.tail_rows)
    for copy in copies:
        copy.wait()


def pack_own_kernel(plan, green_ref, out_ref, stage, out_sems, tiles, sems):
    copies = {}
    for k in range(plan.mom_dev):
        for h in range(plan.pairs // TILE):
            copies[k, h] = pltpu.make_async_copy(
                green_ref.at[k, :, TILE * h : TILE * (h + 1), :], tiles.at[k, h], sems.at[k, h]
            )
            copies[k, h].start()

    def load(k, h):
        copies[k, h].wait()
        return tiles[k, h].reshape(plan.steps * TILE, COMP)

    pack_rows(plan, load, out_ref, stage, out_sems)


def pack_partner_kernel(plan, take_ref, green_ref, out_ref, stage, sems, taken):
    chunk = take_ref.shape[0] // plan.pairs
    take = take_ref[...]
    for k in range(plan.mom_dev):
        for e in range(0, plan.steps, chunk):
            rows = green_ref[k, e : e + chunk].reshape(chunk * plan.pairs, COMP)
            taken[k, e : e + chunk] = dot(take, rows).astype(BF16).reshape(chunk, plan.pairs, COMP)

    def load(k, h):
        return taken[k, :, TILE * h : TILE * (h + 1), :].reshape(plan.steps * TILE, COMP)

    pack_rows(plan, load, out_ref, stage, sems, flip=True)


def each_pair(plan, body, pairs=None):
    first, last = (0, plan.own) if pairs is None else (pairs.start, pairs.stop)
    if plan.own <= 2:
        for u in range(first, last):
            body(u)
    else:
        lax.fori_loop(first, last, lambda u, _: body(u), None)


def pairs_of(plan, piece):
    return range(piece * plan.few, (piece + 1) * plan.few)


def rows_at(row, count):
    return pl.ds(row if isinstance(row, int) else pl.multiple_of(row, count), count)


def my_table(plan, tables_ref, u):
    group = lax.axis_index("energy") // plan.group
    return tables_ref[(u // plan.sub ^ group) * plan.sub + u % plan.sub]


def sandwich_kernel(plan, tables_ref, sand_ref):
    place, want = iota((2 * LANES, 16), 0), iota((2 * LANES, 16), 1)

    def body(u):
        couple = my_table(plan, tables_ref, u)[: BRANCH * 16, :16]
        for h in range(2):
            comp = jnp.where(place < LANES, place, place - (u % SLOTS * TAIL + h * REST))
            valid = (place < LANES) | ((comp >= LANES) & (comp < SQUARE))
            quotient = (comp * 171) >> 11
            first = (valid & (quotient == want)).astype(F32).astype(BF16)
            second = (valid & (comp - ORB * quotient == want)).astype(F32).astype(BF16)
            left = dot_nt(couple, first).astype(BF16)
            right = dot_nt(couple, second).astype(BF16)
            for i in range(BRANCH):
                rows = slice(16 * i, 16 * i + 16)
                product = dot(first, left[rows]) * dot(second, right[rows])
                sand_ref[u, h, :, 2 * LANES * i : 2 * LANES * (i + 1)] = product.astype(BF16)

    each_pair(plan, body)


def toeplitz_kernel(plan, tables_ref, toep_ref):
    mirror = iota((FREQ, 2 * FREQ), 0) + iota((FREQ, 2 * FREQ), 1) == FREQ
    mirror = mirror.astype(F32).astype(BF16)

    def body(u):
        lags = dot(my_table(plan, tables_ref, u)[BRANCH * 16 :, :], mirror)
        for q in range(plan.momenta):
            for i in range(BRANCH):
                n = q * BRANCH + i
                band = jnp.broadcast_to(lags[n : n + 1], (FREQ, 2 * FREQ))
                band = pltpu.roll(band, 0, 1, stride=1, stride_axis=0)
                toep_ref[u, q, i * FREQ : (i + 1) * FREQ, :] = band.astype(BF16)

    each_pair(plan, body)


def edge_kernel(plan, own_ref, *edges):
    odd = lax.axis_index("energy") // plan.group % 2
    near = plan.half * plan.n_mom
    count = plan.few * 2 * plan.steps
    for n in range(0, len(edges), 2):
        side = 1 - odd if n == 0 else odd
        for i in range(near):
            for piece in range(2):
                for k in range(plan.mom_dev):
                    row = plan.main_row(k, piece * plan.few)
                    edges[n + piece][i, k * count : (k + 1) * count, :] = own_ref[
                        side * near + i, row : row + count, :
                    ]
            edges[n][i, plan.few_rows :, :] = own_ref[side * near + i, plan.main_rows :, :]


def gather_rows(plan, ref, u, y, first, flip=False, piece=None, tail_ref=None):
    m, k = divmod(y, plan.mom_dev)
    row, tail = plan.main_row(k, u), plan.tail_row(k, u)
    if piece is not None:
        row = (k * plan.few + u - piece * plan.few) * 2 * plan.steps
        tail = plan.few_rows + tail - plan.main_rows
    order = range(plan.half)
    lefts, rights, tails = [], [], []
    for j in reversed(order) if flip else order:
        peer = (first + j) * plan.n_mom + m
        lefts.append(ref[peer, rows_at(row, plan.steps), :])
        rights.append(ref[peer, rows_at(row + plan.steps, plan.steps), :])
        tails.append((ref if tail_ref is None else tail_ref)[peer, rows_at(tail, plan.steps), :])
    tails = jnp.concatenate(tails, axis=0)
    if plan.shift(k):
        tails = pltpu.roll(tails.astype(F32), LANES - plan.shift(k), 1).astype(BF16)
    return jnp.concatenate([jnp.concatenate(lefts, axis=0), jnp.concatenate(rights, axis=0), tails], axis=1)


def half_and_tail(rows, h):
    return jnp.concatenate([rows[:, h * LANES : (h + 1) * LANES], rows[:, 2 * LANES :]], axis=1)


def self_block(plan, u, green, toep_ref, sand_ref, out_ref):
    summed = []
    for i in range(BRANCH):
        rows = slice(i * FREQ, (i + 1) * FREQ)
        band = jnp.concatenate(
            [
                jnp.concatenate([toep_ref[u, (k - y) % plan.momenta, rows, :] for y in range(plan.momenta)], axis=1)
                for k in range(plan.momenta)
            ],
            axis=0,
        )
        summed.append(dot(band, green).astype(BF16))
    left, right = [
        dot_nt(jnp.concatenate([half_and_tail(rows, h) for rows in summed], axis=1), sand_ref[u, h])
        for h in range(2)
    ]
    tails = left[:, LANES:] + right[:, LANES:]
    left, right = left[:, :LANES].astype(BF16), right[:, :LANES].astype(BF16)
    for y in range(plan.momenta):
        m, k = divmod(y, plan.mom_dev)
        row, tail = plan.main_row(k, u), plan.tail_row(k, u)
        rest = tails[y * FREQ : (y + 1) * FREQ]
        if plan.shift(k):
            rest = pltpu.roll(rest, plan.shift(k), 1)
        rest = rest.astype(BF16)
        for j in range(plan.half):
            peer = j * plan.n_mom + m
            here = slice(j * plan.steps, (j + 1) * plan.steps)
            there = slice(y * FREQ + j * plan.steps, y * FREQ + (j + 1) * plan.steps)
            out_ref[peer, rows_at(row, plan.steps), :] = left[there]
            out_ref[peer, rows_at(row + plan.steps, plan.steps), :] = right[there]
            out_ref[peer, rows_at(tail, plan.steps), :] += rest[here]


def clear_tails(plan, out_ref):
    for peer in range(plan.half * plan.n_mom):
        out_ref[peer, plan.main_rows :, :] = jnp.zeros((plan.tail_rows, LANES), BF16)


def self_late_kernel(plan, own, toep_ref, sand_ref, out_ref):
    clear_tails(plan, out_ref)

    def body(u):
        green = [gather_rows(plan, own, u, y, first) for y in range(plan.momenta) for first in (0, plan.half)]
        self_block(plan, u, jnp.concatenate(green, axis=0), toep_ref, sand_ref, out_ref)

    each_pair(plan, body)


def halo_rows(plan, pieces, u, y, piece, exists):
    rows = gather_rows(plan, pieces[piece], u, y, 0, piece=piece, tail_ref=pieces[0])
    return rows * exists.astype(F32).astype(BF16)


def early_block(plan, own, pieces, toep_ref, sand_ref, stage, piece):
    exists = lax.axis_index("energy") // plan.group > 0

    def body(u):
        green = []
        for y in range(plan.momenta):
            green.append(halo_rows(plan, pieces, u, y, piece, exists))
            green.append(gather_rows(plan, own, u, y, 0))
        self_block(plan, u, jnp.concatenate(green, axis=0), toep_ref, sand_ref, stage)

    each_pair(plan, body, pairs_of(plan, piece))


def send_rows(plan, stage, out_ref, sems, piece, tails):
    near = plan.half * plan.n_mom
    count = plan.few * 2 * plan.steps
    spans = [(plan.main_row(k, piece * plan.few), count) for k in range(plan.mom_dev)]
    if tails:
        spans.append((plan.main_rows, plan.tail_rows))
    copies = []
    for n, (row, rows) in enumerate(spans):
        here = pl.ds(row, rows)
        copies.append(
            pltpu.make_async_copy(stage.at[:, here, :], out_ref.at[pl.ds(0, near), here, :], sems.at[n])
        )
        copies[-1].start()
    return copies


def self_first_kernel(plan, own, piece0, toep_ref, sand_ref, late_ref, out_ref, tails_ref, stage, sems):
    near = plan.half * plan.n_mom
    upper = pltpu.make_async_copy(late_ref, out_ref.at[near:], sems.at[plan.mom_dev])
    upper.start()
    clear_tails(plan, stage)
    early_block(plan, own, [piece0], toep_ref, sand_ref, stage, 0)
    copies = send_rows(plan, stage, out_ref, sems, 0, False)
    tails_ref[...] = stage[:, plan.main_rows :, :]
    for copy in copies:
        copy.wait()
    upper.wait()


def self_second_kernel(plan, own, piece0, piece1, toep_ref, sand_ref, tails_ref, part_ref, out_ref, kept_ref, stage, sems):
    kept_ref[...] = piece1[...]
    stage[:, plan.main_rows :, :] = tails_ref[...]
    early_block(plan, own, [piece0, piece1], toep_ref, sand_ref, stage, 1)
    for copy in send_rows(plan, stage, out_ref, sems, 1, True):
        copy.wait()


def lag_sums(plan, u, partner, green, sand_ref, store):
    partner, green = jnp.concatenate(partner, axis=0), jnp.concatenate(green, axis=0)
    left, right = [dot(half_and_tail(partner, h), sand_ref[u, h]) for h in range(2)]
    for i in range(BRANCH):
        here = slice(2 * LANES * i, 2 * LANES * i + LANES)
        rest = slice(2 * LANES * i + LANES, 2 * LANES * (i + 1))
        applied = jnp.concatenate([left[:, here], right[:, here], left[:, rest] + right[:, rest]], axis=1)
        lagged = dot_nt(applied.astype(BF16), green)
        for q in range(plan.momenta):
            acc = None
            for k in range(plan.momenta):
                y = (k + q) % plan.momenta
                part = lagged[k * FREQ : (k + 1) * FREQ, y * 2 * FREQ : (y + 1) * 2 * FREQ]
                acc = part if acc is None else acc + part
            acc = pltpu.roll(acc, FREQ + 1, 1, stride=1, stride_axis=0)
            store(q, i, jnp.sum(acc, axis=0, keepdims=True))


def phonon_early_kernel(plan, own, partner_ref, sand_ref, out_ref):
    def body(u):
        partner = [gather_rows(plan, partner_ref, u, k, 0, flip=True) for k in range(plan.momenta)]
        green = [gather_rows(plan, own, u, y, first) for y in range(plan.momenta) for first in (0, plan.half)]

        def store(q, i, lags):
            out_ref[u, q * BRANCH + i : q * BRANCH + i + 1, :] = lags

        lag_sums(plan, u, partner, green, sand_ref, store)

    each_pair(plan, body)


def phonon_late_kernel(plan, own, piece0, piece1, partner_ref, sand_ref, early_ref, *refs, scale):
    outs, sums = refs[:-1], refs[-1]
    group = lax.axis_index("energy") // plan.group
    me = lax.axis_index("mom")
    exists = group < plan.n_groups - 1

    def terms(u, piece):
        partner = [gather_rows(plan, partner_ref, u, k, plan.half, flip=True) for k in range(plan.momenta)]
        green = []
        for y in range(plan.momenta):
            green.append(gather_rows(plan, own, u, y, plan.half))
            green.append(halo_rows(plan, [piece0, piece1], u, y, piece, exists))

        def store(q, i, lags):
            n = q * BRANCH + i
            side, row = divmod(n, plan.mom_dev * BRANCH)
            sums[u, side, row : row + 1, :] = (lags + early_ref[u, n : n + 1, :]) * scale

        lag_sums(plan, u, partner, green, sand_ref, store)

    for piece in range(2):
        each_pair(plan, functools.partial(terms, piece=piece), pairs_of(plan, piece))
    for d in range(plan.n_groups):
        for t in range(plan.n_mom):
            for b in range(plan.sub):
                outs[d * plan.n_mom + t][b] = sums[(group ^ d) * plan.sub + b, me ^ t]


def collect_kernel(plan, *refs):
    parts, out_ref = refs[:-1], refs[-1]
    me = lax.axis_index("mom")
    for d in range(plan.n_mom):
        total = sum(ref[...] for ref in parts[d :: plan.n_mom])
        for b in range(plan.sub):
            pair = (me ^ d) * plan.sub + b
            for q in range(plan.mom_dev):
                rows = [total[b, q * BRANCH + i : q * BRANCH + i + 1, :FREQ] for i in range(BRANCH)]
                out_ref[q, pl.ds(pair, 1), :] = jnp.concatenate(rows, axis=1)


def unpack_kernel(plan, wire, out_ref, tiles, sems):
    swap = swap_matrix(TILE, plan.steps)
    copies = []
    for k in range(plan.mom_dev):
        for h in range(plan.pairs // TILE):
            lefts, rights, tails = [], [], []
            for i in range(TILE):
                peer, u = plan.place(h, i)
                row, tail = plan.main_row(k, u), plan.tail_row(k, u)
                lefts.append(wire[peer, row : row + plan.steps, :])
                rights.append(wire[peer, row + plan.steps : row + 2 * plan.steps, :])
                lane = (k * plan.own + u) % SLOTS * TAIL
                tails.append(wire[peer, tail : tail + plan.steps, :][:, lane : lane + TAIL])
            rows = jnp.concatenate([jnp.concatenate(part, axis=0) for part in (lefts, rights, tails)], axis=1)
            moved = dot(swap, rows).astype(BF16)
            left, right = moved[:, :LANES], moved[:, LANES : 2 * LANES]
            tail = moved[:, 2 * LANES :]
            moved = jnp.concatenate([left, tail[:, :REST], right, tail[:, REST:]], axis=1)
            tiles[k, h] = moved.reshape(plan.steps, TILE, COMP)
            copy = pltpu.make_async_copy(
                tiles.at[k, h], out_ref.at[k, :, TILE * h : TILE * (h + 1), :], sems.at[k, h]
            )
            copy.start()
            copies.append(copy)
    for copy in copies:
        copy.wait()


ANY = pl.BlockSpec(memory_space=pl.ANY)
HBM = pl.BlockSpec(memory_space=pltpu.HBM)
VMEM = pl.BlockSpec(memory_space=pltpu.VMEM)


def call(plan, kernel, out_shape, *args, in_specs=None, out_specs=None, scratch=(), flops=1, grant=None, aliases=None):
    outs = jax.tree.map(lambda _: VMEM, out_shape)
    return pl.pallas_call(
        functools.partial(kernel, plan),
        out_shape=out_shape,
        in_specs=in_specs or [VMEM] * len(args),
        out_specs=out_specs or outs,
        scratch_shapes=list(scratch),
        compiler_params=pltpu.CompilerParams(vmem_limit_bytes=grant or SMALL_GRANT * max(1, plan.own // 4)),
        cost_estimate=pl.CostEstimate(flops=flops, bytes_accessed=1, transcendentals=0),
        input_output_aliases=aliases or {},
    )(*args)


def shape(dims, dtype):
    return jax.ShapeDtypeStruct(dims, dtype)


def in_hbm(struct):
    return pltpu.HBM(struct.shape, struct.dtype)


def shards(lesser_green, partner, phonon_green, coupling):
    n_energy, n_mom = lax.axis_size("energy"), lax.axis_size("mom")
    plan = Plan(lesser_green, phonon_green, n_energy, n_mom)
    axes = ("energy", "mom")
    me = lax.axis_index("mom")
    s = lax.axis_index("energy") // plan.group
    wire = shape((plan.peers, plan.rows, LANES), BF16)
    half_peers = plan.half * n_mom
    groups = [[g * plan.peers + i for i in range(plan.peers)] for g in range(plan.n_groups)]
    tiles = (plan.mom_dev, plan.pairs // TILE)

    def exchange(blocks):
        return lax.all_to_all(blocks, axes, split_axis=0, concat_axis=0, axis_index_groups=groups, tiled=True)

    def swap_groups(values, other):
        route = []
        for e in range(n_energy):
            g, j = divmod(e, plan.group)
            to = other(g) if 0 <= other(g) < plan.n_groups else g
            route.append((e, to * plan.group + j))
        return lax.ppermute(values, "energy", route)

    staging = [pltpu.VMEM(wire.shape, BF16), pltpu.SemaphoreType.DMA((tiles[0] * tiles[1] + 1,))]
    tile_scratch = [pltpu.VMEM(tiles + (plan.steps, TILE, COMP), BF16), pltpu.SemaphoreType.DMA(tiles)]
    lag_count = plan.momenta * BRANCH
    lag_rows = -(-lag_count // 16) * 16
    couple = coupling.reshape(plan.pairs_dev, BRANCH, ORB, ORB)
    couple = jnp.pad(couple, ((0, 0), (0, 0), (0, 16 - ORB), (0, FREQ - ORB)))
    phonon = phonon_green.reshape(plan.momenta, plan.pairs_dev, BRANCH, FREQ)
    phonon = jnp.moveaxis(phonon, 1, 0).reshape(plan.pairs_dev, lag_count, FREQ)
    phonon = jnp.pad(phonon, ((0, 0), (0, lag_rows - lag_count), (0, 0)))
    table = jnp.concatenate([couple.reshape(plan.pairs_dev, BRANCH * 16, FREQ), phonon], axis=1)
    table = lax.dynamic_slice_in_dim(table, me * plan.sub, plan.sub, axis=0)
    tables = [table]
    for d in range(1, plan.n_groups):
        tables.append(swap_groups(table, functools.partial(lambda d, g: g ^ d, d)))
    tables = jnp.concatenate(tables, axis=0)
    half_wire = shape((half_peers, plan.rows, LANES), BF16)
    own_wire = call(
        plan,
        pack_own_kernel,
        in_hbm(wire),
        lesser_green,
        in_specs=[HBM],
        out_specs=HBM,
        scratch=staging + tile_scratch,
        grant=LARGE_GRANT,
    )
    own_wire, tables = lax.optimization_barrier((own_wire, tables))
    own = exchange(own_wire)

    sand = call(
        plan, sandwich_kernel, shape((plan.own, 2, 2 * LANES, BRANCH * 2 * LANES), BF16), tables
    )
    chunk = max(1, 256 // plan.pairs)
    source = (jnp.arange(chunk)[:, None] * plan.pairs + partner[None, :]).reshape(-1)
    take = (source[:, None] == jnp.arange(chunk * plan.pairs)[None, :]).astype(BF16)
    partner_wire = call(
        plan,
        pack_partner_kernel,
        in_hbm(wire),
        take,
        lesser_green,
        out_specs=HBM,
        scratch=staging + [pltpu.VMEM(lesser_green.shape, BF16)],
    )
    toep = call(plan, toeplitz_kernel, shape((plan.own, plan.momenta, BRANCH * FREQ, 2 * FREQ), BF16), tables)
    own, sand, toep, partner_wire = lax.optimization_barrier((own, sand, toep, partner_wire))
    partner_blocks = exchange(partner_wire)

    sizes = [shape((half_peers, plan.piece_rows(piece), LANES), BF16) for piece in range(2)]
    edges = call(plan, edge_kernel, sizes * (1 if plan.n_groups == 2 else 2), own)
    before = after = [swap_groups(edge, lambda g: g ^ 1) for edge in edges[:2]]
    if plan.n_groups > 2:
        outer = [swap_groups(edge, lambda g: ((g - 1) ^ 1) + 1) for edge in edges[2:]]
        odd = s % 2 == 1
        before, after = (
            [jnp.where(odd, a, b) for a, b in zip(*order)] for order in ((before, outer), (outer, before))
        )

    late = call(plan, self_late_kernel, half_wire, own, toep, sand)
    scratch = [pltpu.VMEM(half_wire.shape, BF16), pltpu.SemaphoreType.DMA((plan.mom_dev + 1,))]
    part, tails = call(
        plan,
        self_first_kernel,
        [in_hbm(wire), shape((half_peers, plan.tail_rows, LANES), BF16)],
        own,
        before[0],
        toep,
        sand,
        late,
        out_specs=[HBM, VMEM],
        scratch=scratch,
        flops=LONG,
    )
    sigma, kept = call(
        plan,
        self_second_kernel,
        [in_hbm(wire), sizes[1]],
        own,
        *before,
        toep,
        sand,
        tails,
        part,
        in_specs=[VMEM] * 6 + [HBM],
        out_specs=[HBM, VMEM],
        scratch=scratch,
        aliases={6: 0},
    )
    if plan.n_groups == 2:
        after = [after[0], kept]
    arrived = exchange(sigma)

    scale = (plan.momenta * n_energy * plan.steps * COMP) ** -0.5
    early = call(
        plan,
        phonon_early_kernel,
        shape((plan.own, lag_count, LANES), F32),
        own,
        partner_blocks,
        sand,
    )
    side_rows = plan.mom_dev * BRANCH
    parts = list(call(
        plan,
        functools.partial(phonon_late_kernel, scale=scale),
        [shape((plan.sub, side_rows, LANES), F32)] * (plan.n_groups * n_mom),
        own,
        *after,
        partner_blocks,
        sand,
        early,
        scratch=[pltpu.VMEM((plan.own, n_mom, side_rows, LANES), F32)],
    ))
    for d in range(plan.n_groups):
        for t in range(n_mom):
            if d or t:
                route = []
                for e in range(n_energy):
                    g, j = divmod(e, plan.group)
                    for m in range(n_mom):
                        route.append((e * n_mom + m, ((g ^ d) * plan.group + j) * n_mom + (m ^ t)))
                parts[d * n_mom + t] = lax.ppermute(parts[d * n_mom + t], axes, route)
    phonon_self = call(
        plan, collect_kernel, shape((plan.mom_dev, plan.pairs_dev, BRANCH * FREQ), F32), *parts
    )

    self_energy = call(
        plan,
        unpack_kernel,
        shape(lesser_green.shape, BF16),
        arrived,
        out_specs=ANY,
        scratch=tile_scratch,
    )
    return self_energy, phonon_self


def solution(mesh):
    in_specs = (P("mom", "energy", None, None), P(), P(None, "energy", None), P("energy", None))
    out_specs = (P("mom", "energy", None, None), P("mom", "energy", None))
    return jax.shard_map(shards, mesh=mesh, in_specs=in_specs, out_specs=out_specs, check_vma=False)
```

```python
import functools

import jax
import jax.numpy as jnp
from jax import lax
from jax.experimental import pallas as pl
from jax.experimental.pallas import tpu as pltpu
from jax.sharding import PartitionSpec as P

ORB = 12
BRANCH = 3
FREQ = 64
COMP = 288
SQUARE = ORB * ORB
LANES = 128
REST = SQUARE - LANES
TAIL = 2 * REST
SLOTS = LANES // TAIL
TILE = 16
SMALL_GRANT = 16 * 1024 * 1024
LARGE_GRANT = 60 * 1024 * 1024
LONG = 100_000_000_000

BF16 = jnp.bfloat16
F32 = jnp.float32
I32 = jnp.int32


class Plan:
    def __init__(self, green, phonon, n_energy, n_mom):
        self.n_energy, self.n_mom = n_energy, n_mom
        self.mom_dev, self.steps, self.pairs, _ = green.shape
        self.momenta = self.mom_dev * n_mom
        self.pairs_dev = phonon.shape[1]
        self.half = FREQ // self.steps
        self.group = 2 * self.half
        self.n_groups = n_energy // self.group
        self.peers = self.group * n_mom
        self.sub = self.pairs_dev // n_mom
        self.own = self.n_groups * self.sub
        self.main_rows = self.mom_dev * self.own * 2 * self.steps
        self.tail_rows = self.mom_dev * self.own // SLOTS * self.steps
        self.rows = self.main_rows + self.tail_rows
        assert self.half * self.steps == FREQ and n_energy % self.group == 0
        assert self.n_groups & (self.n_groups - 1) == 0 and self.own % 2 == 0
        self.few = self.own // 2
        self.few_rows = self.mom_dev * self.few * 2 * self.steps
        assert self.pairs_dev % n_mom == 0 and self.group * self.pairs_dev == TILE
        assert self.mom_dev * self.own % SLOTS == 0 and self.n_groups % 2 == 0

    def main_row(self, k, u):
        return (k * self.own + u) * 2 * self.steps

    def tail_row(self, k, u):
        return self.main_rows + (k * self.own + u) // SLOTS * self.steps

    def piece_rows(self, piece):
        return self.few_rows + (self.tail_rows if piece == 0 else 0)

    def shift(self, k):
        return k * self.own % SLOTS * TAIL

    def place(self, h, i):
        j, rest = divmod(i, self.pairs_dev)
        m, b = divmod(rest, self.sub)
        return j * self.n_mom + m, h * self.sub + b


def dot(a, b):
    return lax.dot_general(a, b, (((1,), (0,)), ((), ())), preferred_element_type=F32)


def dot_nt(a, b):
    return lax.dot_general(a, b, (((1,), (1,)), ((), ())), preferred_element_type=F32)


def iota(dims, axis):
    return lax.broadcasted_iota(I32, dims, axis)


def swap_matrix(outer, inner, flip=False):
    n = outer * inner
    row, col = iota((n, n), 0), iota((n, n), 1)
    place = row & (outer - 1)
    source = (outer - 1 - place if flip else place) * inner + (row >> (outer.bit_length() - 1))
    return (col == source).astype(F32).astype(BF16)


def to_wire(rows):
    tail = jnp.concatenate([rows[:, LANES:SQUARE], rows[:, SQUARE + LANES :]], axis=1)
    return rows[:, :LANES], rows[:, SQUARE : SQUARE + LANES], tail


def pack_rows(plan, load, stage, send, base=0, flip=False):
    swap = swap_matrix(plan.steps, TILE, flip)
    tails = {}
    for k in range(plan.mom_dev):
        for h in range(plan.pairs // TILE):
            left, right, tail = to_wire(dot(swap, load(k, h)).astype(BF16))
            for i in range(TILE):
                peer, u = plan.place(h, i)
                here = slice(i * plan.steps, (i + 1) * plan.steps)
                row = base + plan.main_row(k, u)
                stage[peer, row : row + plan.steps, :] = left[here]
                stage[peer, row + plan.steps : row + 2 * plan.steps, :] = right[here]
                tails[peer, k * plan.own + u] = tail[here]
            send(base + plan.main_row(k, h * plan.sub), plan.sub * 2 * plan.steps)
    for peer in range(plan.peers):
        for first in range(0, plan.mom_dev * plan.own, SLOTS):
            row = base + plan.main_rows + first // SLOTS * plan.steps
            joined = jnp.concatenate([tails[peer, first + t] for t in range(SLOTS)], axis=1)
            stage[peer, row : row + plan.steps, :] = joined
    send(base + plan.main_rows, plan.tail_rows)


def pack_kernel(plan, partner_hbm, green_hbm, out_ref, stage, green, taken, partner, in_sems, out_sems):
    keys = [(k, h) for k in range(plan.mom_dev) for h in range(plan.pairs // TILE)]
    loads = {}
    for n, (k, h) in enumerate(keys):
        here = pl.ds(TILE * h, TILE)
        loads[k, h] = pltpu.make_async_copy(green_hbm.at[k, :, here, :], green.at[k, :, here, :], in_sems.at[n])
        loads[k, h].start()
    scalars = pltpu.make_async_copy(partner_hbm, partner, in_sems.at[len(keys)])
    scalars.start()
    copies = []

    def send(first, count):
        rows = pl.ds(first, count)
        copy = pltpu.make_async_copy(stage.at[:, rows, :], out_ref.at[:, rows, :], out_sems.at[len(copies)])
        copy.start()
        copies.append(copy)

    def load(k, h):
        loads[k, h].wait()
        return green[k, :, TILE * h : TILE * (h + 1), :].reshape(plan.steps * TILE, COMP)

    pack_rows(plan, load, stage, send)

    scalars.wait()
    chunk = max(1, 2 * LANES // plan.pairs)
    width = chunk * plan.pairs
    row, col = iota((plan.pairs, width), 0), iota((plan.pairs, width), 1)
    source = jnp.zeros((plan.pairs, width), I32)
    for p in range(plan.pairs):
        source = jnp.where(row == p, partner[p], source)
    take = [(col == source + e * plan.pairs).astype(F32).astype(BF16) for e in range(chunk)]
    take = jnp.concatenate(take, axis=0)
    for k in range(plan.mom_dev):
        for e in range(0, plan.steps, chunk):
            rows = green[k, e : e + chunk].reshape(width, COMP)
            taken[k, e : e + chunk] = dot(take, rows).astype(BF16).reshape(chunk, plan.pairs, COMP)

    def load_taken(k, h):
        return taken[k, :, TILE * h : TILE * (h + 1), :].reshape(plan.steps * TILE, COMP)

    pack_rows(plan, load_taken, stage, send, base=plan.rows, flip=True)
    for copy in copies:
        copy.wait()


def each_pair(plan, body, pairs=None):
    first, last = (0, plan.own) if pairs is None else (pairs.start, pairs.stop)
    if plan.own <= 2:
        for u in range(first, last):
            body(u)
    else:
        lax.fori_loop(first, last, lambda u, _: body(u), None)


def pairs_of(plan, piece):
    return range(piece * plan.few, (piece + 1) * plan.few)


def rows_at(row, count):
    return pl.ds(row if isinstance(row, int) else pl.multiple_of(row, count), count)


def my_table(plan, tables_ref, u):
    group = lax.axis_index("energy") // plan.group
    return tables_ref[(u // plan.sub ^ group) * plan.sub + u % plan.sub]


def sandwich_kernel(plan, tables_ref, sand_ref, copy_ref, sem):
    place, want = iota((2 * LANES, 16), 0), iota((2 * LANES, 16), 1)

    def body(u):
        couple = my_table(plan, tables_ref, u)[: BRANCH * 16, :16]
        for h in range(2):
            comp = jnp.where(place < LANES, place, place - (u % SLOTS * TAIL + h * REST))
            valid = (place < LANES) | ((comp >= LANES) & (comp < SQUARE))
            quotient = (comp * 171) >> 11
            first = (valid & (quotient == want)).astype(F32).astype(BF16)
            second = (valid & (comp - ORB * quotient == want)).astype(F32).astype(BF16)
            left = dot_nt(couple, first).astype(BF16)
            right = dot_nt(couple, second).astype(BF16)
            for i in range(BRANCH):
                rows = slice(16 * i, 16 * i + 16)
                product = dot(first, left[rows]) * dot(second, right[rows])
                sand_ref[u, h, :, 2 * LANES * i : 2 * LANES * (i + 1)] = product.astype(BF16)

    each_pair(plan, body)
    copy = pltpu.make_async_copy(sand_ref, copy_ref, sem)
    copy.start()
    copy.wait()


def toeplitz_kernel(plan, tables_ref, toep_ref):
    mirror = iota((FREQ, 2 * FREQ), 0) + iota((FREQ, 2 * FREQ), 1) == FREQ
    mirror = mirror.astype(F32).astype(BF16)

    def body(u):
        lags = dot(my_table(plan, tables_ref, u)[BRANCH * 16 :, :], mirror)
        for q in range(plan.momenta):
            for i in range(BRANCH):
                n = q * BRANCH + i
                band = jnp.broadcast_to(lags[n : n + 1], (FREQ, 2 * FREQ))
                band = pltpu.roll(band, 0, 1, stride=1, stride_axis=0)
                toep_ref[u, q, i * FREQ : (i + 1) * FREQ, :] = band.astype(BF16)

    each_pair(plan, body)


def edge_kernel(plan, own_ref, *edges):
    odd = lax.axis_index("energy") // plan.group % 2
    near = plan.half * plan.n_mom
    count = plan.few * 2 * plan.steps
    for n in range(0, len(edges), 2):
        side = 1 - odd if n == 0 else odd
        for i in range(near):
            for piece in range(2):
                for k in range(plan.mom_dev):
                    row = plan.main_row(k, piece * plan.few)
                    edges[n + piece][i, k * count : (k + 1) * count, :] = own_ref[
                        side * near + i, row : row + count, :
                    ]
            edges[n][i, plan.few_rows :, :] = own_ref[side * near + i, plan.main_rows : plan.rows, :]


def gather_rows(plan, ref, u, y, first, base=0, flip=False, piece=None, tail_ref=None):
    m, k = divmod(y, plan.mom_dev)
    row, tail = base + plan.main_row(k, u), base + plan.tail_row(k, u)
    if piece is not None:
        row = (k * plan.few + u - piece * plan.few) * 2 * plan.steps
        tail = plan.few_rows + tail - plan.main_rows
    order = range(plan.half)
    lefts, rights, tails = [], [], []
    for j in reversed(order) if flip else order:
        peer = (first + j) * plan.n_mom + m
        lefts.append(ref[peer, rows_at(row, plan.steps), :])
        rights.append(ref[peer, rows_at(row + plan.steps, plan.steps), :])
        tails.append((ref if tail_ref is None else tail_ref)[peer, rows_at(tail, plan.steps), :])
    tails = jnp.concatenate(tails, axis=0)
    if plan.shift(k):
        tails = pltpu.roll(tails.astype(F32), LANES - plan.shift(k), 1).astype(BF16)
    return jnp.concatenate([jnp.concatenate(lefts, axis=0), jnp.concatenate(rights, axis=0), tails], axis=1)


def half_and_tail(rows, h):
    return jnp.concatenate([rows[:, h * LANES : (h + 1) * LANES], rows[:, 2 * LANES :]], axis=1)


def self_block(plan, u, green, toep_ref, sand_ref, out_ref):
    summed = []
    for i in range(BRANCH):
        rows = slice(i * FREQ, (i + 1) * FREQ)
        band = jnp.concatenate(
            [
                jnp.concatenate([toep_ref[u, (k - y) % plan.momenta, rows, :] for y in range(plan.momenta)], axis=1)
                for k in range(plan.momenta)
            ],
            axis=0,
        )
        summed.append(dot(band, green).astype(BF16))
    left, right = [
        dot_nt(jnp.concatenate([half_and_tail(rows, h) for rows in summed], axis=1), sand_ref[u, h])
        for h in range(2)
    ]
    tails = left[:, LANES:] + right[:, LANES:]
    left, right = left[:, :LANES].astype(BF16), right[:, :LANES].astype(BF16)
    for y in range(plan.momenta):
        m, k = divmod(y, plan.mom_dev)
        row, tail = plan.main_row(k, u), plan.tail_row(k, u)
        rest = tails[y * FREQ : (y + 1) * FREQ]
        if plan.shift(k):
            rest = pltpu.roll(rest, plan.shift(k), 1)
        rest = rest.astype(BF16)
        for j in range(plan.half):
            peer = j * plan.n_mom + m
            here = slice(j * plan.steps, (j + 1) * plan.steps)
            there = slice(y * FREQ + j * plan.steps, y * FREQ + (j + 1) * plan.steps)
            out_ref[peer, rows_at(row, plan.steps), :] = left[there]
            out_ref[peer, rows_at(row + plan.steps, plan.steps), :] = right[there]
            out_ref[peer, rows_at(tail, plan.steps), :] += rest[here]


def clear_tails(plan, out_ref):
    for peer in range(plan.half * plan.n_mom):
        out_ref[peer, plan.main_rows :, :] = jnp.zeros((plan.tail_rows, LANES), BF16)


def self_late_kernel(plan, own, toep_ref, sand_ref, out_ref):
    clear_tails(plan, out_ref)

    def body(u):
        green = [gather_rows(plan, own, u, y, first) for y in range(plan.momenta) for first in (0, plan.half)]
        self_block(plan, u, jnp.concatenate(green, axis=0), toep_ref, sand_ref, out_ref)

    each_pair(plan, body)


def halo_rows(plan, pieces, u, y, piece, exists):
    rows = gather_rows(plan, pieces[piece], u, y, 0, piece=piece, tail_ref=pieces[0])
    return rows * exists.astype(F32).astype(BF16)


def early_block(plan, own, pieces, toep_ref, sand_ref, stage, piece):
    exists = lax.axis_index("energy") // plan.group > 0

    def body(u):
        green = []
        for y in range(plan.momenta):
            green.append(halo_rows(plan, pieces, u, y, piece, exists))
            green.append(gather_rows(plan, own, u, y, 0))
        self_block(plan, u, jnp.concatenate(green, axis=0), toep_ref, sand_ref, stage)

    each_pair(plan, body, pairs_of(plan, piece))


def send_rows(plan, stage, out_ref, sems, piece, tails):
    near = plan.half * plan.n_mom
    count = plan.few * 2 * plan.steps
    spans = [(plan.main_row(k, piece * plan.few), count) for k in range(plan.mom_dev)]
    if tails:
        spans.append((plan.main_rows, plan.tail_rows))
    copies = []
    for n, (row, rows) in enumerate(spans):
        here = pl.ds(row, rows)
        copies.append(
            pltpu.make_async_copy(stage.at[:, here, :], out_ref.at[pl.ds(0, near), here, :], sems.at[n])
        )
        copies[-1].start()
    return copies


def self_first_kernel(plan, own, piece0, toep_ref, sand_ref, late_ref, out_ref, tails_ref, stage, sems):
    near = plan.half * plan.n_mom
    upper = pltpu.make_async_copy(late_ref, out_ref.at[near:], sems.at[plan.mom_dev])
    upper.start()
    clear_tails(plan, stage)
    early_block(plan, own, [piece0], toep_ref, sand_ref, stage, 0)
    copies = send_rows(plan, stage, out_ref, sems, 0, False)
    tails_ref[...] = stage[:, plan.main_rows :, :]
    for copy in copies:
        copy.wait()
    upper.wait()


def self_second_kernel(plan, own, piece0, piece1, toep_ref, sand_ref, tails_ref, part_ref, out_ref, stage, sems):
    stage[:, plan.main_rows :, :] = tails_ref[...]
    early_block(plan, own, [piece0, piece1], toep_ref, sand_ref, stage, 1)
    for copy in send_rows(plan, stage, out_ref, sems, 1, True):
        copy.wait()


def lag_sums(plan, u, partner, green, sand_ref, store):
    partner, green = jnp.concatenate(partner, axis=0), jnp.concatenate(green, axis=0)
    left, right = [dot(half_and_tail(partner, h), sand_ref[u, h]) for h in range(2)]
    for i in range(BRANCH):
        here = slice(2 * LANES * i, 2 * LANES * i + LANES)
        rest = slice(2 * LANES * i + LANES, 2 * LANES * (i + 1))
        applied = jnp.concatenate([left[:, here], right[:, here], left[:, rest] + right[:, rest]], axis=1)
        lagged = dot_nt(applied.astype(BF16), green)
        for q in range(plan.momenta):
            acc = None
            for k in range(plan.momenta):
                y = (k + q) % plan.momenta
                part = lagged[k * FREQ : (k + 1) * FREQ, y * 2 * FREQ : (y + 1) * 2 * FREQ]
                acc = part if acc is None else acc + part
            acc = pltpu.roll(acc, FREQ + 1, 1, stride=1, stride_axis=0)
            store(q, i, jnp.sum(acc, axis=0, keepdims=True))


def phonon_early_kernel(plan, own, sand_ref, out_ref):
    def body(u):
        partner = [gather_rows(plan, own, u, k, 0, base=plan.rows, flip=True) for k in range(plan.momenta)]
        green = [gather_rows(plan, own, u, y, first) for y in range(plan.momenta) for first in (0, plan.half)]

        def store(q, i, lags):
            out_ref[u, q * BRANCH + i : q * BRANCH + i + 1, :] = lags

        lag_sums(plan, u, partner, green, sand_ref, store)

    each_pair(plan, body)


def phonon_late_kernel(plan, own, piece0, piece1, sand_hbm, early_ref, *refs, scale):
    *outs, sums, sand_ref, sem = refs
    load = pltpu.make_async_copy(sand_hbm, sand_ref, sem)
    load.start()
    group = lax.axis_index("energy") // plan.group
    me = lax.axis_index("mom")
    exists = group < plan.n_groups - 1

    def terms(u, piece):
        partner = [gather_rows(plan, own, u, k, plan.half, base=plan.rows, flip=True) for k in range(plan.momenta)]
        green = []
        for y in range(plan.momenta):
            green.append(gather_rows(plan, own, u, y, plan.half))
            green.append(halo_rows(plan, [piece0, piece1], u, y, piece, exists))

        def store(q, i, lags):
            n = q * BRANCH + i
            side, row = divmod(n, plan.mom_dev * BRANCH)
            sums[u, side, row : row + 1, :] = (lags + early_ref[u, n : n + 1, :]) * scale

        lag_sums(plan, u, partner, green, sand_ref, store)

    load.wait()
    for piece in range(2):
        each_pair(plan, functools.partial(terms, piece=piece), pairs_of(plan, piece))
    for d in range(plan.n_groups):
        for t in range(plan.n_mom):
            for b in range(plan.sub):
                outs[d * plan.n_mom + t][b] = sums[(group ^ d) * plan.sub + b, me ^ t]


def collect_kernel(plan, *refs):
    parts, out_ref = refs[:-1], refs[-1]
    me = lax.axis_index("mom")
    for d in range(plan.n_mom):
        total = sum(ref[...] for ref in parts[d :: plan.n_mom])
        for b in range(plan.sub):
            pair = (me ^ d) * plan.sub + b
            for q in range(plan.mom_dev):
                rows = [total[b, q * BRANCH + i : q * BRANCH + i + 1, :FREQ] for i in range(BRANCH)]
                out_ref[q, pl.ds(pair, 1), :] = jnp.concatenate(rows, axis=1)


def unpack_kernel(plan, wire, out_ref, tiles, sems):
    swap = swap_matrix(TILE, plan.steps)
    copies = []
    for k in range(plan.mom_dev):
        for h in range(plan.pairs // TILE):
            lefts, rights, tails = [], [], []
            for i in range(TILE):
                peer, u = plan.place(h, i)
                row, tail = plan.main_row(k, u), plan.tail_row(k, u)
                lefts.append(wire[peer, row : row + plan.steps, :])
                rights.append(wire[peer, row + plan.steps : row + 2 * plan.steps, :])
                lane = (k * plan.own + u) % SLOTS * TAIL
                tails.append(wire[peer, tail : tail + plan.steps, :][:, lane : lane + TAIL])
            rows = jnp.concatenate([jnp.concatenate(part, axis=0) for part in (lefts, rights, tails)], axis=1)
            moved = dot(swap, rows).astype(BF16)
            left, right = moved[:, :LANES], moved[:, LANES : 2 * LANES]
            tail = moved[:, 2 * LANES :]
            moved = jnp.concatenate([left, tail[:, :REST], right, tail[:, REST:]], axis=1)
            tiles[k, h] = moved.reshape(plan.steps, TILE, COMP)
            copy = pltpu.make_async_copy(
                tiles.at[k, h], out_ref.at[k, :, TILE * h : TILE * (h + 1), :], sems.at[k, h]
            )
            copy.start()
            copies.append(copy)
    for copy in copies:
        copy.wait()


ANY = pl.BlockSpec(memory_space=pl.ANY)
HBM = pl.BlockSpec(memory_space=pltpu.HBM)
VMEM = pl.BlockSpec(memory_space=pltpu.VMEM)


def call(plan, kernel, out_shape, *args, in_specs=None, out_specs=None, scratch=(), flops=1, grant=None, aliases=None):
    outs = jax.tree.map(lambda _: VMEM, out_shape)
    return pl.pallas_call(
        functools.partial(kernel, plan),
        out_shape=out_shape,
        in_specs=in_specs or [VMEM] * len(args),
        out_specs=out_specs or outs,
        scratch_shapes=list(scratch),
        compiler_params=pltpu.CompilerParams(vmem_limit_bytes=grant or SMALL_GRANT * max(1, plan.own // 4)),
        cost_estimate=pl.CostEstimate(flops=flops, bytes_accessed=1, transcendentals=0),
        input_output_aliases=aliases or {},
    )(*args)


def shape(dims, dtype):
    return jax.ShapeDtypeStruct(dims, dtype)


def in_hbm(struct):
    return pltpu.HBM(struct.shape, struct.dtype)


def shards(lesser_green, partner, phonon_green, coupling):
    n_energy, n_mom = lax.axis_size("energy"), lax.axis_size("mom")
    plan = Plan(lesser_green, phonon_green, n_energy, n_mom)
    axes = ("energy", "mom")
    me = lax.axis_index("mom")
    s = lax.axis_index("energy") // plan.group
    wire = shape((plan.peers, plan.rows, LANES), BF16)
    half_peers = plan.half * n_mom
    groups = [[g * plan.peers + i for i in range(plan.peers)] for g in range(plan.n_groups)]
    tiles = (plan.mom_dev, plan.pairs // TILE)

    def exchange(blocks):
        return lax.all_to_all(blocks, axes, split_axis=0, concat_axis=0, axis_index_groups=groups, tiled=True)

    def swap_groups(values, other):
        route = []
        for e in range(n_energy):
            g, j = divmod(e, plan.group)
            to = other(g) if 0 <= other(g) < plan.n_groups else g
            route.append((e, to * plan.group + j))
        return lax.ppermute(values, "energy", route)

    half_wire = shape((half_peers, plan.rows, LANES), BF16)
    both = (plan.peers, 2 * plan.rows, LANES)
    blocks = exchange(
        call(
            plan,
            pack_kernel,
            in_hbm(shape(both, BF16)),
            partner,
            lesser_green,
            in_specs=[HBM, HBM],
            out_specs=HBM,
            scratch=[
                pltpu.VMEM(both, BF16),
                pltpu.VMEM(lesser_green.shape, BF16),
                pltpu.VMEM(lesser_green.shape, BF16),
                pltpu.SMEM((plan.pairs,), I32),
                pltpu.SemaphoreType.DMA((tiles[0] * tiles[1] + 1,)),
                pltpu.SemaphoreType.DMA((2 * (tiles[0] * tiles[1] + 1),)),
            ],
            grant=LARGE_GRANT,
        )
    )

    lag_count = plan.momenta * BRANCH
    lag_rows = -(-lag_count // 16) * 16
    couple = coupling.reshape(plan.pairs_dev, BRANCH, ORB, ORB)
    couple = jnp.pad(couple, ((0, 0), (0, 0), (0, 16 - ORB), (0, FREQ - ORB)))
    phonon = phonon_green.reshape(plan.momenta, plan.pairs_dev, BRANCH, FREQ)
    phonon = jnp.moveaxis(phonon, 1, 0).reshape(plan.pairs_dev, lag_count, FREQ)
    phonon = jnp.pad(phonon, ((0, 0), (0, lag_rows - lag_count), (0, 0)))
    table = jnp.concatenate([couple.reshape(plan.pairs_dev, BRANCH * 16, FREQ), phonon], axis=1)
    table = lax.dynamic_slice_in_dim(table, me * plan.sub, plan.sub, axis=0)
    tables = [table]
    for d in range(1, plan.n_groups):
        tables.append(swap_groups(table, functools.partial(lambda d, g: g ^ d, d)))
    tables = jnp.concatenate(tables, axis=0)
    sand_shape = shape((plan.own, 2, 2 * LANES, BRANCH * 2 * LANES), BF16)
    sand, sand_copy = call(
        plan,
        sandwich_kernel,
        [sand_shape, in_hbm(sand_shape)],
        tables,
        out_specs=[VMEM, HBM],
        scratch=[pltpu.SemaphoreType.DMA],
    )
    toep = call(plan, toeplitz_kernel, shape((plan.own, plan.momenta, BRANCH * FREQ, 2 * FREQ), BF16), tables)
    blocks, sand, sand_copy, toep = lax.optimization_barrier((blocks, sand, sand_copy, toep))

    sizes = [shape((half_peers, plan.piece_rows(piece), LANES), BF16) for piece in range(2)]
    edges = call(plan, edge_kernel, sizes * (1 if plan.n_groups == 2 else 2), blocks)
    before = after = [swap_groups(edge, lambda g: g ^ 1) for edge in edges[:2]]
    if plan.n_groups > 2:
        outer = [swap_groups(edge, lambda g: ((g - 1) ^ 1) + 1) for edge in edges[2:]]
        odd = s % 2 == 1
        before, after = (
            [jnp.where(odd, a, b) for a, b in zip(*order)] for order in ((before, outer), (outer, before))
        )

    late = call(plan, self_late_kernel, half_wire, blocks, toep, sand)
    early = call(plan, phonon_early_kernel, shape((plan.own, lag_count, LANES), F32), blocks, sand)
    late, early = lax.optimization_barrier((late, early))
    scratch = [pltpu.VMEM(half_wire.shape, BF16), pltpu.SemaphoreType.DMA((plan.mom_dev + 1,))]
    part, tails = call(
        plan,
        self_first_kernel,
        [in_hbm(wire), shape((half_peers, plan.tail_rows, LANES), BF16)],
        blocks,
        before[0],
        toep,
        sand,
        late,
        out_specs=[HBM, VMEM],
        scratch=scratch,
        flops=LONG,
    )
    sigma = call(
        plan,
        self_second_kernel,
        in_hbm(wire),
        blocks,
        *before,
        toep,
        sand,
        tails,
        part,
        in_specs=[VMEM] * 6 + [HBM],
        out_specs=HBM,
        scratch=scratch,
        aliases={6: 0},
    )
    sigma, early = lax.optimization_barrier((sigma, early))
    arrived = exchange(sigma)

    scale = (plan.momenta * n_energy * plan.steps * COMP) ** -0.5
    side_rows = plan.mom_dev * BRANCH
    parts = list(
        call(
            plan,
            functools.partial(phonon_late_kernel, scale=scale),
            [shape((plan.sub, side_rows, LANES), F32)] * (plan.n_groups * n_mom),
            blocks,
            *after,
            sand_copy,
            early,
            in_specs=[VMEM, VMEM, VMEM, HBM, VMEM],
            scratch=[
                pltpu.VMEM((plan.own, n_mom, side_rows, LANES), F32),
                pltpu.VMEM(sand_shape.shape, BF16),
                pltpu.SemaphoreType.DMA,
            ],
        )
    )
    for d in range(plan.n_groups):
        for t in range(n_mom):
            if d or t:
                route = []
                for e in range(n_energy):
                    g, j = divmod(e, plan.group)
                    for m in range(n_mom):
                        route.append((e * n_mom + m, ((g ^ d) * plan.group + j) * n_mom + (m ^ t)))
                parts[d * n_mom + t] = lax.ppermute(parts[d * n_mom + t], axes, route)
    phonon_self = call(
        plan, collect_kernel, shape((plan.mom_dev, plan.pairs_dev, BRANCH * FREQ), F32), *parts
    )

    self_energy = call(
        plan,
        unpack_kernel,
        shape(lesser_green.shape, BF16),
        arrived,
        out_specs=ANY,
        scratch=[pltpu.VMEM(tiles + (plan.steps, TILE, COMP), BF16), pltpu.SemaphoreType.DMA(tiles)],
    )
    return self_energy, phonon_self


def solution(mesh):
    in_specs = (P("mom", "energy", None, None), P(), P(None, "energy", None), P("energy", None))
    out_specs = (P("mom", "energy", None, None), P("mom", "energy", None))
    return jax.shard_map(shards, mesh=mesh, in_specs=in_specs, out_specs=out_specs, check_vma=False)
```

```python
import functools

import jax
import jax.numpy as jnp
from jax import lax
from jax.experimental import pallas as pl
from jax.experimental.pallas import tpu as pltpu
from jax.sharding import PartitionSpec as P

ORB = 12
BRANCH = 3
FREQ = 64
COMP = 288
SQUARE = ORB * ORB
LANES = 128
REST = SQUARE - LANES
TAIL = 2 * REST
SLOTS = LANES // TAIL
TILE = 16
SMALL_GRANT = 16 * 1024 * 1024
LARGE_GRANT = 60 * 1024 * 1024
LONG = 100_000_000_000

BF16 = jnp.bfloat16
F32 = jnp.float32
I32 = jnp.int32


class Plan:
    def __init__(self, green, phonon, n_energy, n_mom):
        self.n_energy, self.n_mom = n_energy, n_mom
        self.mom_dev, self.steps, self.pairs, _ = green.shape
        self.momenta = self.mom_dev * n_mom
        self.pairs_dev = phonon.shape[1]
        self.half = FREQ // self.steps
        self.group = 2 * self.half
        self.n_groups = n_energy // self.group
        self.peers = self.group * n_mom
        self.sub = self.pairs_dev // n_mom
        self.own = self.n_groups * self.sub
        self.main_rows = self.mom_dev * self.own * 2 * self.steps
        self.tail_rows = self.mom_dev * self.own // SLOTS * self.steps
        self.rows = self.main_rows + self.tail_rows
        assert self.half * self.steps == FREQ and n_energy % self.group == 0
        assert self.n_groups & (self.n_groups - 1) == 0
        assert self.pairs_dev % n_mom == 0 and self.group * self.pairs_dev == TILE
        assert self.mom_dev * self.own % SLOTS == 0 and self.n_groups % 2 == 0

    def main_row(self, k, u):
        return (k * self.own + u) * 2 * self.steps

    def tail_row(self, k, u):
        return self.main_rows + (k * self.own + u) // SLOTS * self.steps

    def shift(self, k):
        return k * self.own % SLOTS * TAIL

    def place(self, h, i):
        j, rest = divmod(i, self.pairs_dev)
        m, b = divmod(rest, self.sub)
        return j * self.n_mom + m, h * self.sub + b


def dot(a, b):
    return lax.dot_general(a, b, (((1,), (0,)), ((), ())), preferred_element_type=F32)


def dot_nt(a, b):
    return lax.dot_general(a, b, (((1,), (1,)), ((), ())), preferred_element_type=F32)


def iota(dims, axis):
    return lax.broadcasted_iota(I32, dims, axis)


def swap_matrix(outer, inner, flip=False):
    n = outer * inner
    row, col = iota((n, n), 0), iota((n, n), 1)
    place = row & (outer - 1)
    source = (outer - 1 - place if flip else place) * inner + (row >> (outer.bit_length() - 1))
    return (col == source).astype(F32).astype(BF16)


def to_wire(rows):
    tail = jnp.concatenate([rows[:, LANES:SQUARE], rows[:, SQUARE + LANES :]], axis=1)
    return rows[:, :LANES], rows[:, SQUARE : SQUARE + LANES], tail


def pack_rows(plan, load, out_ref, stage, sems, flip=False):
    swap = swap_matrix(plan.steps, TILE, flip)
    tails, copies = {}, []

    def send(first, count):
        rows = slice(first, first + count)
        copy = pltpu.make_async_copy(stage.at[:, rows, :], out_ref.at[:, rows, :], sems.at[len(copies)])
        copy.start()
        copies.append(copy)

    for k in range(plan.mom_dev):
        for h in range(plan.pairs // TILE):
            left, right, tail = to_wire(dot(swap, load(k, h)).astype(BF16))
            for i in range(TILE):
                peer, u = plan.place(h, i)
                here = slice(i * plan.steps, (i + 1) * plan.steps)
                row = plan.main_row(k, u)
                stage[peer, row : row + plan.steps, :] = left[here]
                stage[peer, row + plan.steps : row + 2 * plan.steps, :] = right[here]
                tails[peer, k * plan.own + u] = tail[here]
            send(plan.main_row(k, h * plan.sub), plan.sub * 2 * plan.steps)
    for peer in range(plan.peers):
        for first in range(0, plan.mom_dev * plan.own, SLOTS):
            row = plan.main_rows + first // SLOTS * plan.steps
            joined = jnp.concatenate([tails[peer, first + t] for t in range(SLOTS)], axis=1)
            stage[peer, row : row + plan.steps, :] = joined
    send(plan.main_rows, plan.tail_rows)
    for copy in copies:
        copy.wait()


def pack_own_kernel(plan, green_ref, out_ref, stage, out_sems, tiles, sems):
    copies = {}
    for k in range(plan.mom_dev):
        for h in range(plan.pairs // TILE):
            copies[k, h] = pltpu.make_async_copy(
                green_ref.at[k, :, TILE * h : TILE * (h + 1), :], tiles.at[k, h], sems.at[k, h]
            )
            copies[k, h].start()

    def load(k, h):
        copies[k, h].wait()
        return tiles[k, h].reshape(plan.steps * TILE, COMP)

    pack_rows(plan, load, out_ref, stage, out_sems)


def pack_partner_kernel(plan, take_ref, green_ref, out_ref, stage, sems, taken):
    chunk = take_ref.shape[0] // plan.pairs
    take = take_ref[...]
    for k in range(plan.mom_dev):
        for e in range(0, plan.steps, chunk):
            rows = green_ref[k, e : e + chunk].reshape(chunk * plan.pairs, COMP)
            taken[k, e : e + chunk] = dot(take, rows).astype(BF16).reshape(chunk, plan.pairs, COMP)

    def load(k, h):
        return taken[k, :, TILE * h : TILE * (h + 1), :].reshape(plan.steps * TILE, COMP)

    pack_rows(plan, load, out_ref, stage, sems, flip=True)


def each_pair(plan, body):
    if plan.own <= 2:
        for u in range(plan.own):
            body(u)
    else:
        lax.fori_loop(0, plan.own, lambda u, _: body(u), None)


def rows_at(row, count):
    return pl.ds(row if isinstance(row, int) else pl.multiple_of(row, count), count)


def my_table(plan, tables_ref, u):
    group = lax.axis_index("energy") // plan.group
    return tables_ref[(u // plan.sub ^ group) * plan.sub + u % plan.sub]


def sandwich_kernel(plan, tables_ref, sand_ref):
    place, want = iota((2 * LANES, 16), 0), iota((2 * LANES, 16), 1)

    def body(u):
        couple = my_table(plan, tables_ref, u)[: BRANCH * 16, :16]
        for h in range(2):
            comp = jnp.where(place < LANES, place, place - (u % SLOTS * TAIL + h * REST))
            valid = (place < LANES) | ((comp >= LANES) & (comp < SQUARE))
            quotient = (comp * 171) >> 11
            first = (valid & (quotient == want)).astype(F32).astype(BF16)
            second = (valid & (comp - ORB * quotient == want)).astype(F32).astype(BF16)
            left = dot_nt(couple, first).astype(BF16)
            right = dot_nt(couple, second).astype(BF16)
            for i in range(BRANCH):
                rows = slice(16 * i, 16 * i + 16)
                product = dot(first, left[rows]) * dot(second, right[rows])
                sand_ref[u, h, :, 2 * LANES * i : 2 * LANES * (i + 1)] = product.astype(BF16)

    each_pair(plan, body)


def toeplitz_kernel(plan, tables_ref, toep_ref):
    mirror = iota((FREQ, 2 * FREQ), 0) + iota((FREQ, 2 * FREQ), 1) == FREQ
    mirror = mirror.astype(F32).astype(BF16)

    def body(u):
        lags = dot(my_table(plan, tables_ref, u)[BRANCH * 16 :, :], mirror)
        for q in range(plan.momenta):
            for i in range(BRANCH):
                n = q * BRANCH + i
                band = jnp.broadcast_to(lags[n : n + 1], (FREQ, 2 * FREQ))
                band = pltpu.roll(band, 0, 1, stride=1, stride_axis=0)
                toep_ref[u, q, i * FREQ : (i + 1) * FREQ, :] = band.astype(BF16)

    each_pair(plan, body)


def edge_kernel(plan, own_ref, *edges):
    odd = lax.axis_index("energy") // plan.group % 2
    near = plan.half * plan.n_mom
    for edge, side in zip(edges, (1 - odd, odd)):
        for i in range(near):
            edge[i] = own_ref[side * near + i]


def gather_rows(plan, ref, u, y, first, flip=False):
    m, k = divmod(y, plan.mom_dev)
    row, tail = plan.main_row(k, u), plan.tail_row(k, u)
    order = range(plan.half)
    lefts, rights, tails = [], [], []
    for j in reversed(order) if flip else order:
        peer = (first + j) * plan.n_mom + m
        lefts.append(ref[peer, rows_at(row, plan.steps), :])
        rights.append(ref[peer, rows_at(row + plan.steps, plan.steps), :])
        tails.append(ref[peer, rows_at(tail, plan.steps), :])
    tails = jnp.concatenate(tails, axis=0)
    if plan.shift(k):
        tails = pltpu.roll(tails.astype(F32), LANES - plan.shift(k), 1).astype(BF16)
    return jnp.concatenate([jnp.concatenate(lefts, axis=0), jnp.concatenate(rights, axis=0), tails], axis=1)


def half_and_tail(rows, h):
    return jnp.concatenate([rows[:, h * LANES : (h + 1) * LANES], rows[:, 2 * LANES :]], axis=1)


def self_block(plan, u, green, toep_ref, sand_ref, out_ref):
    summed = []
    for i in range(BRANCH):
        rows = slice(i * FREQ, (i + 1) * FREQ)
        band = jnp.concatenate(
            [
                jnp.concatenate([toep_ref[u, (k - y) % plan.momenta, rows, :] for y in range(plan.momenta)], axis=1)
                for k in range(plan.momenta)
            ],
            axis=0,
        )
        summed.append(dot(band, green).astype(BF16))
    left, right = [
        dot_nt(jnp.concatenate([half_and_tail(rows, h) for rows in summed], axis=1), sand_ref[u, h])
        for h in range(2)
    ]
    tails = left[:, LANES:] + right[:, LANES:]
    left, right = left[:, :LANES].astype(BF16), right[:, :LANES].astype(BF16)
    for y in range(plan.momenta):
        m, k = divmod(y, plan.mom_dev)
        row, tail = plan.main_row(k, u), plan.tail_row(k, u)
        rest = tails[y * FREQ : (y + 1) * FREQ]
        if plan.shift(k):
            rest = pltpu.roll(rest, plan.shift(k), 1)
        rest = rest.astype(BF16)
        for j in range(plan.half):
            peer = j * plan.n_mom + m
            here = slice(j * plan.steps, (j + 1) * plan.steps)
            there = slice(y * FREQ + j * plan.steps, y * FREQ + (j + 1) * plan.steps)
            out_ref[peer, rows_at(row, plan.steps), :] = left[there]
            out_ref[peer, rows_at(row + plan.steps, plan.steps), :] = right[there]
            out_ref[peer, rows_at(tail, plan.steps), :] += rest[here]


def clear_tails(plan, out_ref):
    for peer in range(plan.half * plan.n_mom):
        out_ref[peer, plan.main_rows :, :] = jnp.zeros((plan.tail_rows, LANES), BF16)


def self_late_kernel(plan, own, toep_ref, sand_ref, out_ref):
    clear_tails(plan, out_ref)

    def body(u):
        green = [gather_rows(plan, own, u, y, first) for y in range(plan.momenta) for first in (0, plan.half)]
        self_block(plan, u, jnp.concatenate(green, axis=0), toep_ref, sand_ref, out_ref)

    each_pair(plan, body)


def self_early_kernel(plan, own, far, toep_ref, sand_ref, late_ref, out_ref, stage, halo, sems):
    has = (lax.axis_index("energy") // plan.group > 0).astype(F32).astype(BF16)
    near = plan.half * plan.n_mom
    load = pltpu.make_async_copy(far, halo, sems.at[0])
    load.start()
    upper = pltpu.make_async_copy(late_ref, out_ref.at[near:], sems.at[1])
    upper.start()
    clear_tails(plan, stage)
    load.wait()

    def body(u):
        green = []
        for y in range(plan.momenta):
            green.append(gather_rows(plan, halo, u, y, 0) * has)
            green.append(gather_rows(plan, own, u, y, 0))
        self_block(plan, u, jnp.concatenate(green, axis=0), toep_ref, sand_ref, stage)

    each_pair(plan, body)
    lower = pltpu.make_async_copy(stage, out_ref.at[:near], sems.at[2])
    lower.start()
    lower.wait()
    upper.wait()


def lag_sums(plan, u, partner, green, sand_ref, store):
    partner, green = jnp.concatenate(partner, axis=0), jnp.concatenate(green, axis=0)
    left, right = [dot(half_and_tail(partner, h), sand_ref[u, h]) for h in range(2)]
    for i in range(BRANCH):
        here = slice(2 * LANES * i, 2 * LANES * i + LANES)
        rest = slice(2 * LANES * i + LANES, 2 * LANES * (i + 1))
        applied = jnp.concatenate([left[:, here], right[:, here], left[:, rest] + right[:, rest]], axis=1)
        lagged = dot_nt(applied.astype(BF16), green)
        for q in range(plan.momenta):
            acc = None
            for k in range(plan.momenta):
                y = (k + q) % plan.momenta
                part = lagged[k * FREQ : (k + 1) * FREQ, y * 2 * FREQ : (y + 1) * 2 * FREQ]
                acc = part if acc is None else acc + part
            acc = pltpu.roll(acc, FREQ + 1, 1, stride=1, stride_axis=0)
            store(q, i, jnp.sum(acc, axis=0, keepdims=True))


def phonon_early_kernel(plan, own, partner_ref, sand_ref, out_ref):
    def body(u):
        partner = [gather_rows(plan, partner_ref, u, k, 0, flip=True) for k in range(plan.momenta)]
        green = [gather_rows(plan, own, u, y, first) for y in range(plan.momenta) for first in (0, plan.half)]

        def store(q, i, lags):
            out_ref[u, q * BRANCH + i : q * BRANCH + i + 1, :] = lags

        lag_sums(plan, u, partner, green, sand_ref, store)

    each_pair(plan, body)


def phonon_late_kernel(plan, own, halo, partner_ref, sand_ref, early_ref, *refs, scale):
    outs, sums = refs[:-1], refs[-1]
    group = lax.axis_index("energy") // plan.group
    me = lax.axis_index("mom")
    has = (group < plan.n_groups - 1).astype(F32).astype(BF16)

    def body(u):
        partner = [gather_rows(plan, partner_ref, u, k, plan.half, flip=True) for k in range(plan.momenta)]
        green = []
        for y in range(plan.momenta):
            green.append(gather_rows(plan, own, u, y, plan.half))
            green.append(gather_rows(plan, halo, u, y, 0) * has)

        def store(q, i, lags):
            n = q * BRANCH + i
            side, row = divmod(n, plan.mom_dev * BRANCH)
            sums[u, side, row : row + 1, :] = (lags + early_ref[u, n : n + 1, :]) * scale

        lag_sums(plan, u, partner, green, sand_ref, store)

    each_pair(plan, body)
    for d in range(plan.n_groups):
        for t in range(plan.n_mom):
            for b in range(plan.sub):
                outs[d * plan.n_mom + t][b] = sums[(group ^ d) * plan.sub + b, me ^ t]


def collect_kernel(plan, *refs):
    parts, out_ref = refs[:-1], refs[-1]
    me = lax.axis_index("mom")
    for d in range(plan.n_mom):
        total = sum(ref[...] for ref in parts[d :: plan.n_mom])
        for b in range(plan.sub):
            pair = (me ^ d) * plan.sub + b
            for q in range(plan.mom_dev):
                rows = [total[b, q * BRANCH + i : q * BRANCH + i + 1, :FREQ] for i in range(BRANCH)]
                out_ref[q, pl.ds(pair, 1), :] = jnp.concatenate(rows, axis=1)


def unpack_kernel(plan, wire, out_ref, tiles, sems):
    swap = swap_matrix(TILE, plan.steps)
    copies = []
    for k in range(plan.mom_dev):
        for h in range(plan.pairs // TILE):
            lefts, rights, tails = [], [], []
            for i in range(TILE):
                peer, u = plan.place(h, i)
                row, tail = plan.main_row(k, u), plan.tail_row(k, u)
                lefts.append(wire[peer, row : row + plan.steps, :])
                rights.append(wire[peer, row + plan.steps : row + 2 * plan.steps, :])
                lane = (k * plan.own + u) % SLOTS * TAIL
                tails.append(wire[peer, tail : tail + plan.steps, :][:, lane : lane + TAIL])
            rows = jnp.concatenate([jnp.concatenate(part, axis=0) for part in (lefts, rights, tails)], axis=1)
            moved = dot(swap, rows).astype(BF16)
            left, right = moved[:, :LANES], moved[:, LANES : 2 * LANES]
            tail = moved[:, 2 * LANES :]
            moved = jnp.concatenate([left, tail[:, :REST], right, tail[:, REST:]], axis=1)
            tiles[k, h] = moved.reshape(plan.steps, TILE, COMP)
            copy = pltpu.make_async_copy(
                tiles.at[k, h], out_ref.at[k, :, TILE * h : TILE * (h + 1), :], sems.at[k, h]
            )
            copy.start()
            copies.append(copy)
    for copy in copies:
        copy.wait()


ANY = pl.BlockSpec(memory_space=pl.ANY)
HBM = pl.BlockSpec(memory_space=pltpu.HBM)
VMEM = pl.BlockSpec(memory_space=pltpu.VMEM)


def call(plan, kernel, out_shape, *args, in_specs=None, out_specs=None, scratch=(), flops=1, grant=None):
    outs = jax.tree.map(lambda _: VMEM, out_shape)
    return pl.pallas_call(
        functools.partial(kernel, plan),
        out_shape=out_shape,
        in_specs=in_specs or [VMEM] * len(args),
        out_specs=out_specs or outs,
        scratch_shapes=list(scratch),
        compiler_params=pltpu.CompilerParams(vmem_limit_bytes=grant or SMALL_GRANT * max(1, plan.own // 4)),
        cost_estimate=pl.CostEstimate(flops=flops, bytes_accessed=1, transcendentals=0),
    )(*args)


def shape(dims, dtype):
    return jax.ShapeDtypeStruct(dims, dtype)


def in_hbm(struct):
    return pltpu.HBM(struct.shape, struct.dtype)


def shards(lesser_green, partner, phonon_green, coupling):
    n_energy, n_mom = lax.axis_size("energy"), lax.axis_size("mom")
    plan = Plan(lesser_green, phonon_green, n_energy, n_mom)
    axes = ("energy", "mom")
    me = lax.axis_index("mom")
    s = lax.axis_index("energy") // plan.group
    wire = shape((plan.peers, plan.rows, LANES), BF16)
    half_peers = plan.half * n_mom
    groups = [[g * plan.peers + i for i in range(plan.peers)] for g in range(plan.n_groups)]
    tiles = (plan.mom_dev, plan.pairs // TILE)

    def exchange(blocks):
        return lax.all_to_all(blocks, axes, split_axis=0, concat_axis=0, axis_index_groups=groups, tiled=True)

    def swap_groups(values, other):
        route = []
        for e in range(n_energy):
            g, j = divmod(e, plan.group)
            to = other(g) if 0 <= other(g) < plan.n_groups else g
            route.append((e, to * plan.group + j))
        return lax.ppermute(values, "energy", route)

    staging = [pltpu.VMEM(wire.shape, BF16), pltpu.SemaphoreType.DMA((tiles[0] * tiles[1] + 1,))]
    tile_scratch = [pltpu.VMEM(tiles + (plan.steps, TILE, COMP), BF16), pltpu.SemaphoreType.DMA(tiles)]
    half_wire = shape((half_peers, plan.rows, LANES), BF16)
    own = exchange(
        call(
            plan,
            pack_own_kernel,
            in_hbm(wire),
            lesser_green,
            in_specs=[HBM],
            out_specs=HBM,
            scratch=staging + tile_scratch,
            grant=LARGE_GRANT,
        )
    )

    lag_count = plan.momenta * BRANCH
    lag_rows = -(-lag_count // 16) * 16
    couple = coupling.reshape(plan.pairs_dev, BRANCH, ORB, ORB)
    couple = jnp.pad(couple, ((0, 0), (0, 0), (0, 16 - ORB), (0, FREQ - ORB)))
    phonon = phonon_green.reshape(plan.momenta, plan.pairs_dev, BRANCH, FREQ)
    phonon = jnp.moveaxis(phonon, 1, 0).reshape(plan.pairs_dev, lag_count, FREQ)
    phonon = jnp.pad(phonon, ((0, 0), (0, lag_rows - lag_count), (0, 0)))
    table = jnp.concatenate([couple.reshape(plan.pairs_dev, BRANCH * 16, FREQ), phonon], axis=1)
    table = lax.dynamic_slice_in_dim(table, me * plan.sub, plan.sub, axis=0)
    tables = [table]
    for d in range(1, plan.n_groups):
        tables.append(swap_groups(table, functools.partial(lambda d, g: g ^ d, d)))
    tables = jnp.concatenate(tables, axis=0)
    chunk = max(1, 256 // plan.pairs)
    source = (jnp.arange(chunk)[:, None] * plan.pairs + partner[None, :]).reshape(-1)
    take = (source[:, None] == jnp.arange(chunk * plan.pairs)[None, :]).astype(BF16)
    partner_wire = call(
        plan,
        pack_partner_kernel,
        in_hbm(wire),
        take,
        lesser_green,
        out_specs=HBM,
        scratch=staging + [pltpu.VMEM(lesser_green.shape, BF16)],
    )
    own, tables, partner_wire = lax.optimization_barrier((own, tables, partner_wire))

    edges = call(plan, edge_kernel, [half_wire] * (1 if plan.n_groups == 2 else 2), own)
    before = after = inner = swap_groups(edges[0], lambda g: g ^ 1)
    if plan.n_groups > 2:
        outer = swap_groups(edges[1], lambda g: ((g - 1) ^ 1) + 1)
        odd = s % 2 == 1
        before = jnp.where(odd, inner, outer)
        after = jnp.where(odd, outer, inner)

    toep = call(
        plan,
        toeplitz_kernel,
        shape((plan.own, plan.momenta, BRANCH * FREQ, 2 * FREQ), BF16),
        tables,
        flops=LONG,
    )
    toep, partner_wire = lax.optimization_barrier((toep, partner_wire))
    partner_blocks = exchange(partner_wire)

    sand = call(
        plan,
        sandwich_kernel,
        shape((plan.own, 2, 2 * LANES, BRANCH * 2 * LANES), BF16),
        tables,
        flops=LONG,
    )
    late = call(plan, self_late_kernel, half_wire, own, toep, sand)
    sigma = call(
        plan,
        self_early_kernel,
        in_hbm(wire),
        own,
        before,
        toep,
        sand,
        late,
        in_specs=[VMEM, ANY, VMEM, VMEM, VMEM],
        out_specs=HBM,
        scratch=[
            pltpu.VMEM(half_wire.shape, BF16),
            pltpu.VMEM(half_wire.shape, BF16),
            pltpu.SemaphoreType.DMA((3,)),
        ],
    )
    arrived = exchange(sigma)

    scale = (plan.momenta * n_energy * plan.steps * COMP) ** -0.5
    early = call(
        plan,
        phonon_early_kernel,
        shape((plan.own, lag_count, LANES), F32),
        own,
        partner_blocks,
        sand,
    )
    side_rows = plan.mom_dev * BRANCH
    parts = list(call(
        plan,
        functools.partial(phonon_late_kernel, scale=scale),
        [shape((plan.sub, side_rows, LANES), F32)] * (plan.n_groups * n_mom),
        own,
        after,
        partner_blocks,
        sand,
        early,
        scratch=[pltpu.VMEM((plan.own, n_mom, side_rows, LANES), F32)],
    ))
    for d in range(plan.n_groups):
        for t in range(n_mom):
            if d or t:
                route = []
                for e in range(n_energy):
                    g, j = divmod(e, plan.group)
                    for m in range(n_mom):
                        route.append((e * n_mom + m, ((g ^ d) * plan.group + j) * n_mom + (m ^ t)))
                parts[d * n_mom + t] = lax.ppermute(parts[d * n_mom + t], axes, route)
    phonon_self = call(
        plan, collect_kernel, shape((plan.mom_dev, plan.pairs_dev, BRANCH * FREQ), F32), *parts
    )

    self_energy = call(
        plan,
        unpack_kernel,
        shape(lesser_green.shape, BF16),
        arrived,
        out_specs=ANY,
        scratch=tile_scratch,
    )
    return self_energy, phonon_self


def solution(mesh):
    in_specs = (P("mom", "energy", None, None), P(), P(None, "energy", None), P("energy", None))
    out_specs = (P("mom", "energy", None, None), P("mom", "energy", None))
    return jax.shard_map(shards, mesh=mesh, in_specs=in_specs, out_specs=out_specs, check_vma=False)
```

```python
import functools

import jax
import jax.numpy as jnp
from jax import lax
from jax.experimental import pallas as pl
from jax.experimental.pallas import tpu as pltpu
from jax.sharding import PartitionSpec as P

ORB = 12
BRANCH = 3
FREQ = 64
COMP = 288
SQUARE = ORB * ORB
LANES = 128
REST = SQUARE - LANES
TAIL = 2 * REST
SLOTS = LANES // TAIL
TILE = 16
SMALL_GRANT = 16 * 1024 * 1024
LARGE_GRANT = 60 * 1024 * 1024
LONG = 100_000_000_000

BF16 = jnp.bfloat16
F32 = jnp.float32
I32 = jnp.int32


class Plan:
    def __init__(self, green, phonon, n_energy, n_mom):
        self.n_energy, self.n_mom = n_energy, n_mom
        self.mom_dev, self.steps, self.pairs, _ = green.shape
        self.momenta = self.mom_dev * n_mom
        self.pairs_dev = phonon.shape[1]
        self.half = FREQ // self.steps
        self.group = 2 * self.half
        self.n_groups = n_energy // self.group
        self.peers = self.group * n_mom
        self.sub = self.pairs_dev // n_mom
        self.own = self.n_groups * self.sub
        self.main_rows = self.mom_dev * self.own * 2 * self.steps
        self.tail_rows = self.mom_dev * self.own // SLOTS * self.steps
        self.rows = self.main_rows + self.tail_rows
        assert self.half * self.steps == FREQ and n_energy % self.group == 0
        assert self.n_groups & (self.n_groups - 1) == 0 and self.own % 2 == 0
        self.few = self.own // 2
        self.few_rows = self.mom_dev * self.few * 2 * self.steps
        assert self.pairs_dev % n_mom == 0 and self.group * self.pairs_dev == TILE
        assert self.mom_dev * self.own % SLOTS == 0 and self.n_groups % 2 == 0

    def main_row(self, k, u):
        return (k * self.own + u) * 2 * self.steps

    def tail_row(self, k, u):
        return self.main_rows + (k * self.own + u) // SLOTS * self.steps

    def piece_rows(self, piece):
        return self.few_rows + (self.tail_rows if piece == 0 else 0)

    def shift(self, k):
        return k * self.own % SLOTS * TAIL

    def place(self, h, i):
        j, rest = divmod(i, self.pairs_dev)
        m, b = divmod(rest, self.sub)
        return j * self.n_mom + m, h * self.sub + b


def dot(a, b):
    return lax.dot_general(a, b, (((1,), (0,)), ((), ())), preferred_element_type=F32)


def dot_nt(a, b):
    return lax.dot_general(a, b, (((1,), (1,)), ((), ())), preferred_element_type=F32)


def iota(dims, axis):
    return lax.broadcasted_iota(I32, dims, axis)


def swap_matrix(outer, inner, flip=False):
    n = outer * inner
    row, col = iota((n, n), 0), iota((n, n), 1)
    place = row & (outer - 1)
    source = (outer - 1 - place if flip else place) * inner + (row >> (outer.bit_length() - 1))
    return (col == source).astype(F32).astype(BF16)


def to_wire(rows):
    tail = jnp.concatenate([rows[:, LANES:SQUARE], rows[:, SQUARE + LANES :]], axis=1)
    return rows[:, :LANES], rows[:, SQUARE : SQUARE + LANES], tail


def pack_rows(plan, load, stage, send, base=0, flip=False):
    swap = swap_matrix(plan.steps, TILE, flip)
    tails = {}
    for k in range(plan.mom_dev):
        for h in range(plan.pairs // TILE):
            left, right, tail = to_wire(dot(swap, load(k, h)).astype(BF16))
            for i in range(TILE):
                peer, u = plan.place(h, i)
                here = slice(i * plan.steps, (i + 1) * plan.steps)
                row = base + plan.main_row(k, u)
                stage[peer, row : row + plan.steps, :] = left[here]
                stage[peer, row + plan.steps : row + 2 * plan.steps, :] = right[here]
                tails[peer, k * plan.own + u] = tail[here]
            send(base + plan.main_row(k, h * plan.sub), plan.sub * 2 * plan.steps)
    for peer in range(plan.peers):
        for first in range(0, plan.mom_dev * plan.own, SLOTS):
            row = base + plan.main_rows + first // SLOTS * plan.steps
            joined = jnp.concatenate([tails[peer, first + t] for t in range(SLOTS)], axis=1)
            stage[peer, row : row + plan.steps, :] = joined
    send(base + plan.main_rows, plan.tail_rows)


def pack_kernel(plan, partner_hbm, green_hbm, out_ref, stage, green, taken, partner, in_sems, out_sems):
    keys = [(k, h) for k in range(plan.mom_dev) for h in range(plan.pairs // TILE)]
    loads = {}
    for n, (k, h) in enumerate(keys):
        here = pl.ds(TILE * h, TILE)
        loads[k, h] = pltpu.make_async_copy(green_hbm.at[k, :, here, :], green.at[k, :, here, :], in_sems.at[n])
        loads[k, h].start()
    scalars = pltpu.make_async_copy(partner_hbm, partner, in_sems.at[len(keys)])
    scalars.start()
    copies = []

    def send(first, count):
        rows = pl.ds(first, count)
        copy = pltpu.make_async_copy(stage.at[:, rows, :], out_ref.at[:, rows, :], out_sems.at[len(copies)])
        copy.start()
        copies.append(copy)

    def load(k, h):
        loads[k, h].wait()
        return green[k, :, TILE * h : TILE * (h + 1), :].reshape(plan.steps * TILE, COMP)

    pack_rows(plan, load, stage, send)

    scalars.wait()
    chunk = max(1, 2 * LANES // plan.pairs)
    width = chunk * plan.pairs
    row, col = iota((plan.pairs, width), 0), iota((plan.pairs, width), 1)
    source = jnp.zeros((plan.pairs, width), I32)
    for p in range(plan.pairs):
        source = jnp.where(row == p, partner[p], source)
    take = [(col == source + e * plan.pairs).astype(F32).astype(BF16) for e in range(chunk)]
    take = jnp.concatenate(take, axis=0)
    for k in range(plan.mom_dev):
        for e in range(0, plan.steps, chunk):
            rows = green[k, e : e + chunk].reshape(width, COMP)
            taken[k, e : e + chunk] = dot(take, rows).astype(BF16).reshape(chunk, plan.pairs, COMP)

    def load_taken(k, h):
        return taken[k, :, TILE * h : TILE * (h + 1), :].reshape(plan.steps * TILE, COMP)

    pack_rows(plan, load_taken, stage, send, base=plan.rows, flip=True)
    for copy in copies:
        copy.wait()


def each_pair(plan, body, pairs=None):
    first, last = (0, plan.own) if pairs is None else (pairs.start, pairs.stop)
    if plan.own <= 2:
        for u in range(first, last):
            body(u)
    else:
        lax.fori_loop(first, last, lambda u, _: body(u), None)


def pairs_of(plan, piece):
    return range(piece * plan.few, (piece + 1) * plan.few)


def rows_at(row, count):
    return pl.ds(row if isinstance(row, int) else pl.multiple_of(row, count), count)


def my_table(plan, tables_ref, u):
    group = lax.axis_index("energy") // plan.group
    return tables_ref[(u // plan.sub ^ group) * plan.sub + u % plan.sub]


def sandwich_kernel(plan, tables_ref, sand_ref, copy_ref, sem):
    place, want = iota((2 * LANES, 16), 0), iota((2 * LANES, 16), 1)

    def body(u):
        couple = my_table(plan, tables_ref, u)[: BRANCH * 16, :16]
        for h in range(2):
            comp = jnp.where(place < LANES, place, place - (u % SLOTS * TAIL + h * REST))
            valid = (place < LANES) | ((comp >= LANES) & (comp < SQUARE))
            quotient = (comp * 171) >> 11
            first = (valid & (quotient == want)).astype(F32).astype(BF16)
            second = (valid & (comp - ORB * quotient == want)).astype(F32).astype(BF16)
            left = dot_nt(couple, first).astype(BF16)
            right = dot_nt(couple, second).astype(BF16)
            for i in range(BRANCH):
                rows = slice(16 * i, 16 * i + 16)
                product = dot(first, left[rows]) * dot(second, right[rows])
                sand_ref[u, h, :, 2 * LANES * i : 2 * LANES * (i + 1)] = product.astype(BF16)

    each_pair(plan, body)
    copy = pltpu.make_async_copy(sand_ref, copy_ref, sem)
    copy.start()
    copy.wait()


def toeplitz_kernel(plan, tables_ref, toep_ref):
    mirror = iota((FREQ, 2 * FREQ), 0) + iota((FREQ, 2 * FREQ), 1) == FREQ
    mirror = mirror.astype(F32).astype(BF16)

    def body(u):
        lags = dot(my_table(plan, tables_ref, u)[BRANCH * 16 :, :], mirror)
        for q in range(plan.momenta):
            for i in range(BRANCH):
                n = q * BRANCH + i
                band = jnp.broadcast_to(lags[n : n + 1], (FREQ, 2 * FREQ))
                band = pltpu.roll(band, 0, 1, stride=1, stride_axis=0)
                toep_ref[u, q, i * FREQ : (i + 1) * FREQ, :] = band.astype(BF16)

    each_pair(plan, body)


def edge_kernel(plan, own_ref, *edges):
    odd = lax.axis_index("energy") // plan.group % 2
    near = plan.half * plan.n_mom
    count = plan.few * 2 * plan.steps
    for n in range(0, len(edges), 2):
        side = 1 - odd if n == 0 else odd
        for i in range(near):
            for piece in range(2):
                for k in range(plan.mom_dev):
                    row = plan.main_row(k, piece * plan.few)
                    edges[n + piece][i, k * count : (k + 1) * count, :] = own_ref[
                        side * near + i, row : row + count, :
                    ]
            edges[n][i, plan.few_rows :, :] = own_ref[side * near + i, plan.main_rows : plan.rows, :]


def gather_rows(plan, ref, u, y, first, base=0, flip=False, piece=None, tail_ref=None):
    m, k = divmod(y, plan.mom_dev)
    row, tail = base + plan.main_row(k, u), base + plan.tail_row(k, u)
    if piece is not None:
        row = (k * plan.few + u - piece * plan.few) * 2 * plan.steps
        tail = plan.few_rows + tail - plan.main_rows
    order = range(plan.half)
    lefts, rights, tails = [], [], []
    for j in reversed(order) if flip else order:
        peer = (first + j) * plan.n_mom + m
        lefts.append(ref[peer, rows_at(row, plan.steps), :])
        rights.append(ref[peer, rows_at(row + plan.steps, plan.steps), :])
        tails.append((ref if tail_ref is None else tail_ref)[peer, rows_at(tail, plan.steps), :])
    tails = jnp.concatenate(tails, axis=0)
    if plan.shift(k):
        tails = pltpu.roll(tails.astype(F32), LANES - plan.shift(k), 1).astype(BF16)
    return jnp.concatenate([jnp.concatenate(lefts, axis=0), jnp.concatenate(rights, axis=0), tails], axis=1)


def half_and_tail(rows, h):
    return jnp.concatenate([rows[:, h * LANES : (h + 1) * LANES], rows[:, 2 * LANES :]], axis=1)


def self_block(plan, u, green, toep_ref, sand_ref, out_ref):
    summed = []
    for i in range(BRANCH):
        rows = slice(i * FREQ, (i + 1) * FREQ)
        band = jnp.concatenate(
            [
                jnp.concatenate([toep_ref[u, (k - y) % plan.momenta, rows, :] for y in range(plan.momenta)], axis=1)
                for k in range(plan.momenta)
            ],
            axis=0,
        )
        summed.append(dot(band, green).astype(BF16))
    left, right = [
        dot_nt(jnp.concatenate([half_and_tail(rows, h) for rows in summed], axis=1), sand_ref[u, h])
        for h in range(2)
    ]
    tails = left[:, LANES:] + right[:, LANES:]
    left, right = left[:, :LANES].astype(BF16), right[:, :LANES].astype(BF16)
    for y in range(plan.momenta):
        m, k = divmod(y, plan.mom_dev)
        row, tail = plan.main_row(k, u), plan.tail_row(k, u)
        rest = tails[y * FREQ : (y + 1) * FREQ]
        if plan.shift(k):
            rest = pltpu.roll(rest, plan.shift(k), 1)
        rest = rest.astype(BF16)
        for j in range(plan.half):
            peer = j * plan.n_mom + m
            here = slice(j * plan.steps, (j + 1) * plan.steps)
            there = slice(y * FREQ + j * plan.steps, y * FREQ + (j + 1) * plan.steps)
            out_ref[peer, rows_at(row, plan.steps), :] = left[there]
            out_ref[peer, rows_at(row + plan.steps, plan.steps), :] = right[there]
            out_ref[peer, rows_at(tail, plan.steps), :] += rest[here]


def clear_tails(plan, out_ref):
    for peer in range(plan.half * plan.n_mom):
        out_ref[peer, plan.main_rows :, :] = jnp.zeros((plan.tail_rows, LANES), BF16)


def self_late_kernel(plan, own, toep_ref, sand_ref, out_ref):
    clear_tails(plan, out_ref)

    def body(u):
        green = [gather_rows(plan, own, u, y, first) for y in range(plan.momenta) for first in (0, plan.half)]
        self_block(plan, u, jnp.concatenate(green, axis=0), toep_ref, sand_ref, out_ref)

    each_pair(plan, body)


def halo_rows(plan, pieces, u, y, piece, exists):
    rows = gather_rows(plan, pieces[piece], u, y, 0, piece=piece, tail_ref=pieces[0])
    return rows * exists.astype(F32).astype(BF16)


def early_block(plan, own, pieces, toep_ref, sand_ref, stage, piece):
    exists = lax.axis_index("energy") // plan.group > 0

    def body(u):
        green = []
        for y in range(plan.momenta):
            green.append(halo_rows(plan, pieces, u, y, piece, exists))
            green.append(gather_rows(plan, own, u, y, 0))
        self_block(plan, u, jnp.concatenate(green, axis=0), toep_ref, sand_ref, stage)

    each_pair(plan, body, pairs_of(plan, piece))


def send_rows(plan, stage, out_ref, sems, piece, tails):
    near = plan.half * plan.n_mom
    count = plan.few * 2 * plan.steps
    spans = [(plan.main_row(k, piece * plan.few), count) for k in range(plan.mom_dev)]
    if tails:
        spans.append((plan.main_rows, plan.tail_rows))
    copies = []
    for n, (row, rows) in enumerate(spans):
        here = pl.ds(row, rows)
        copies.append(
            pltpu.make_async_copy(stage.at[:, here, :], out_ref.at[pl.ds(0, near), here, :], sems.at[n])
        )
        copies[-1].start()
    return copies


def self_first_kernel(plan, own, piece0, toep_ref, sand_ref, late_ref, out_ref, tails_ref, stage, sems):
    near = plan.half * plan.n_mom
    upper = pltpu.make_async_copy(late_ref, out_ref.at[near:], sems.at[plan.mom_dev])
    upper.start()
    clear_tails(plan, stage)
    early_block(plan, own, [piece0], toep_ref, sand_ref, stage, 0)
    copies = send_rows(plan, stage, out_ref, sems, 0, False)
    tails_ref[...] = stage[:, plan.main_rows :, :]
    for copy in copies:
        copy.wait()
    upper.wait()


def self_second_kernel(plan, own, piece0, piece1, toep_ref, sand_ref, tails_ref, part_ref, out_ref, stage, sems):
    stage[:, plan.main_rows :, :] = tails_ref[...]
    early_block(plan, own, [piece0, piece1], toep_ref, sand_ref, stage, 1)
    for copy in send_rows(plan, stage, out_ref, sems, 1, True):
        copy.wait()


def lag_sums(plan, u, partner, green, sand_ref, store):
    partner, green = jnp.concatenate(partner, axis=0), jnp.concatenate(green, axis=0)
    left, right = [dot(half_and_tail(partner, h), sand_ref[u, h]) for h in range(2)]
    for i in range(BRANCH):
        here = slice(2 * LANES * i, 2 * LANES * i + LANES)
        rest = slice(2 * LANES * i + LANES, 2 * LANES * (i + 1))
        applied = jnp.concatenate([left[:, here], right[:, here], left[:, rest] + right[:, rest]], axis=1)
        lagged = dot_nt(applied.astype(BF16), green)
        for q in range(plan.momenta):
            acc = None
            for k in range(plan.momenta):
                y = (k + q) % plan.momenta
                part = lagged[k * FREQ : (k + 1) * FREQ, y * 2 * FREQ : (y + 1) * 2 * FREQ]
                acc = part if acc is None else acc + part
            acc = pltpu.roll(acc, FREQ + 1, 1, stride=1, stride_axis=0)
            store(q, i, jnp.sum(acc, axis=0, keepdims=True))


def phonon_early_kernel(plan, own, sand_ref, out_ref):
    def body(u):
        partner = [gather_rows(plan, own, u, k, 0, base=plan.rows, flip=True) for k in range(plan.momenta)]
        green = [gather_rows(plan, own, u, y, first) for y in range(plan.momenta) for first in (0, plan.half)]

        def store(q, i, lags):
            out_ref[u, q * BRANCH + i : q * BRANCH + i + 1, :] = lags

        lag_sums(plan, u, partner, green, sand_ref, store)

    each_pair(plan, body)


def phonon_late_kernel(plan, own, piece0, piece1, sand_hbm, early_ref, *refs, scale):
    *outs, sums, sand_ref, sem = refs
    load = pltpu.make_async_copy(sand_hbm, sand_ref, sem)
    load.start()
    group = lax.axis_index("energy") // plan.group
    me = lax.axis_index("mom")
    exists = group < plan.n_groups - 1

    def terms(u, piece):
        partner = [gather_rows(plan, own, u, k, plan.half, base=plan.rows, flip=True) for k in range(plan.momenta)]
        green = []
        for y in range(plan.momenta):
            green.append(gather_rows(plan, own, u, y, plan.half))
            green.append(halo_rows(plan, [piece0, piece1], u, y, piece, exists))

        def store(q, i, lags):
            n = q * BRANCH + i
            side, row = divmod(n, plan.mom_dev * BRANCH)
            sums[u, side, row : row + 1, :] = (lags + early_ref[u, n : n + 1, :]) * scale

        lag_sums(plan, u, partner, green, sand_ref, store)

    load.wait()
    for piece in range(2):
        each_pair(plan, functools.partial(terms, piece=piece), pairs_of(plan, piece))
    for d in range(plan.n_groups):
        for t in range(plan.n_mom):
            for b in range(plan.sub):
                outs[d * plan.n_mom + t][b] = sums[(group ^ d) * plan.sub + b, me ^ t]


def collect_kernel(plan, *refs):
    parts, out_ref = refs[:-1], refs[-1]
    me = lax.axis_index("mom")
    for d in range(plan.n_mom):
        total = sum(ref[...] for ref in parts[d :: plan.n_mom])
        for b in range(plan.sub):
            pair = (me ^ d) * plan.sub + b
            for q in range(plan.mom_dev):
                rows = [total[b, q * BRANCH + i : q * BRANCH + i + 1, :FREQ] for i in range(BRANCH)]
                out_ref[q, pl.ds(pair, 1), :] = jnp.concatenate(rows, axis=1)


def unpack_kernel(plan, wire, out_ref, tiles, sems):
    swap = swap_matrix(TILE, plan.steps)
    copies = []
    for k in range(plan.mom_dev):
        for h in range(plan.pairs // TILE):
            lefts, rights, tails = [], [], []
            for i in range(TILE):
                peer, u = plan.place(h, i)
                row, tail = plan.main_row(k, u), plan.tail_row(k, u)
                lefts.append(wire[peer, row : row + plan.steps, :])
                rights.append(wire[peer, row + plan.steps : row + 2 * plan.steps, :])
                lane = (k * plan.own + u) % SLOTS * TAIL
                tails.append(wire[peer, tail : tail + plan.steps, :][:, lane : lane + TAIL])
            rows = jnp.concatenate([jnp.concatenate(part, axis=0) for part in (lefts, rights, tails)], axis=1)
            moved = dot(swap, rows).astype(BF16)
            left, right = moved[:, :LANES], moved[:, LANES : 2 * LANES]
            tail = moved[:, 2 * LANES :]
            moved = jnp.concatenate([left, tail[:, :REST], right, tail[:, REST:]], axis=1)
            tiles[k, h] = moved.reshape(plan.steps, TILE, COMP)
            copy = pltpu.make_async_copy(
                tiles.at[k, h], out_ref.at[k, :, TILE * h : TILE * (h + 1), :], sems.at[k, h]
            )
            copy.start()
            copies.append(copy)
    for copy in copies:
        copy.wait()


ANY = pl.BlockSpec(memory_space=pl.ANY)
HBM = pl.BlockSpec(memory_space=pltpu.HBM)
VMEM = pl.BlockSpec(memory_space=pltpu.VMEM)


def call(plan, kernel, out_shape, *args, in_specs=None, out_specs=None, scratch=(), flops=1, grant=None, aliases=None):
    outs = jax.tree.map(lambda _: VMEM, out_shape)
    return pl.pallas_call(
        functools.partial(kernel, plan),
        out_shape=out_shape,
        in_specs=in_specs or [VMEM] * len(args),
        out_specs=out_specs or outs,
        scratch_shapes=list(scratch),
        compiler_params=pltpu.CompilerParams(vmem_limit_bytes=grant or SMALL_GRANT * max(1, plan.own // 4)),
        cost_estimate=pl.CostEstimate(flops=flops, bytes_accessed=1, transcendentals=0),
        input_output_aliases=aliases or {},
    )(*args)


def shape(dims, dtype):
    return jax.ShapeDtypeStruct(dims, dtype)


def in_hbm(struct):
    return pltpu.HBM(struct.shape, struct.dtype)


def shards(lesser_green, partner, phonon_green, coupling):
    n_energy, n_mom = lax.axis_size("energy"), lax.axis_size("mom")
    plan = Plan(lesser_green, phonon_green, n_energy, n_mom)
    axes = ("energy", "mom")
    me = lax.axis_index("mom")
    s = lax.axis_index("energy") // plan.group
    wire = shape((plan.peers, plan.rows, LANES), BF16)
    half_peers = plan.half * n_mom
    groups = [[g * plan.peers + i for i in range(plan.peers)] for g in range(plan.n_groups)]
    tiles = (plan.mom_dev, plan.pairs // TILE)

    def exchange(blocks):
        return lax.all_to_all(blocks, axes, split_axis=0, concat_axis=0, axis_index_groups=groups, tiled=True)

    def swap_groups(values, other):
        route = []
        for e in range(n_energy):
            g, j = divmod(e, plan.group)
            to = other(g) if 0 <= other(g) < plan.n_groups else g
            route.append((e, to * plan.group + j))
        return lax.ppermute(values, "energy", route)

    half_wire = shape((half_peers, plan.rows, LANES), BF16)
    both = (plan.peers, 2 * plan.rows, LANES)
    blocks = exchange(
        call(
            plan,
            pack_kernel,
            in_hbm(shape(both, BF16)),
            partner,
            lesser_green,
            in_specs=[HBM, HBM],
            out_specs=HBM,
            scratch=[
                pltpu.VMEM(both, BF16),
                pltpu.VMEM(lesser_green.shape, BF16),
                pltpu.VMEM(lesser_green.shape, BF16),
                pltpu.SMEM((plan.pairs,), I32),
                pltpu.SemaphoreType.DMA((tiles[0] * tiles[1] + 1,)),
                pltpu.SemaphoreType.DMA((2 * (tiles[0] * tiles[1] + 1),)),
            ],
            grant=LARGE_GRANT,
        )
    )

    lag_count = plan.momenta * BRANCH
    lag_rows = -(-lag_count // 16) * 16
    couple = coupling.reshape(plan.pairs_dev, BRANCH, ORB, ORB)
    couple = jnp.pad(couple, ((0, 0), (0, 0), (0, 16 - ORB), (0, FREQ - ORB)))
    phonon = phonon_green.reshape(plan.momenta, plan.pairs_dev, BRANCH, FREQ)
    phonon = jnp.moveaxis(phonon, 1, 0).reshape(plan.pairs_dev, lag_count, FREQ)
    phonon = jnp.pad(phonon, ((0, 0), (0, lag_rows - lag_count), (0, 0)))
    table = jnp.concatenate([couple.reshape(plan.pairs_dev, BRANCH * 16, FREQ), phonon], axis=1)
    table = lax.dynamic_slice_in_dim(table, me * plan.sub, plan.sub, axis=0)
    tables = [table]
    for d in range(1, plan.n_groups):
        tables.append(swap_groups(table, functools.partial(lambda d, g: g ^ d, d)))
    tables = jnp.concatenate(tables, axis=0)
    blocks, tables = lax.optimization_barrier((blocks, tables))

    sizes = [shape((half_peers, plan.piece_rows(piece), LANES), BF16) for piece in range(2)]
    edges = call(plan, edge_kernel, sizes * (1 if plan.n_groups == 2 else 2), blocks)
    before = after = [swap_groups(edge, lambda g: g ^ 1) for edge in edges[:2]]
    if plan.n_groups > 2:
        outer = [swap_groups(edge, lambda g: ((g - 1) ^ 1) + 1) for edge in edges[2:]]
        odd = s % 2 == 1
        before, after = (
            [jnp.where(odd, a, b) for a, b in zip(*order)] for order in ((before, outer), (outer, before))
        )

    sand_shape = shape((plan.own, 2, 2 * LANES, BRANCH * 2 * LANES), BF16)
    sand, sand_copy = call(
        plan,
        sandwich_kernel,
        [sand_shape, in_hbm(sand_shape)],
        tables,
        out_specs=[VMEM, HBM],
        scratch=[pltpu.SemaphoreType.DMA],
        flops=LONG,
    )
    toep = call(plan, toeplitz_kernel, shape((plan.own, plan.momenta, BRANCH * FREQ, 2 * FREQ), BF16), tables)
    late = call(plan, self_late_kernel, half_wire, blocks, toep, sand)
    early = call(plan, phonon_early_kernel, shape((plan.own, lag_count, LANES), F32), blocks, sand)
    late, early = lax.optimization_barrier((late, early))
    scratch = [pltpu.VMEM(half_wire.shape, BF16), pltpu.SemaphoreType.DMA((plan.mom_dev + 1,))]
    part, tails = call(
        plan,
        self_first_kernel,
        [in_hbm(wire), shape((half_peers, plan.tail_rows, LANES), BF16)],
        blocks,
        before[0],
        toep,
        sand,
        late,
        out_specs=[HBM, VMEM],
        scratch=scratch,
        flops=LONG,
    )
    sigma = call(
        plan,
        self_second_kernel,
        in_hbm(wire),
        blocks,
        *before,
        toep,
        sand,
        tails,
        part,
        in_specs=[VMEM] * 6 + [HBM],
        out_specs=HBM,
        scratch=scratch,
        aliases={6: 0},
    )
    sigma, early = lax.optimization_barrier((sigma, early))
    arrived = exchange(sigma)

    scale = (plan.momenta * n_energy * plan.steps * COMP) ** -0.5
    side_rows = plan.mom_dev * BRANCH
    parts = list(
        call(
            plan,
            functools.partial(phonon_late_kernel, scale=scale),
            [shape((plan.sub, side_rows, LANES), F32)] * (plan.n_groups * n_mom),
            blocks,
            *after,
            sand_copy,
            early,
            in_specs=[VMEM, VMEM, VMEM, HBM, VMEM],
            scratch=[
                pltpu.VMEM((plan.own, n_mom, side_rows, LANES), F32),
                pltpu.VMEM(sand_shape.shape, BF16),
                pltpu.SemaphoreType.DMA,
            ],
        )
    )
    for d in range(plan.n_groups):
        for t in range(n_mom):
            if d or t:
                route = []
                for e in range(n_energy):
                    g, j = divmod(e, plan.group)
                    for m in range(n_mom):
                        route.append((e * n_mom + m, ((g ^ d) * plan.group + j) * n_mom + (m ^ t)))
                parts[d * n_mom + t] = lax.ppermute(parts[d * n_mom + t], axes, route)
    phonon_self = call(
        plan, collect_kernel, shape((plan.mom_dev, plan.pairs_dev, BRANCH * FREQ), F32), *parts
    )

    self_energy = call(
        plan,
        unpack_kernel,
        shape(lesser_green.shape, BF16),
        arrived,
        out_specs=ANY,
        scratch=[pltpu.VMEM(tiles + (plan.steps, TILE, COMP), BF16), pltpu.SemaphoreType.DMA(tiles)],
    )
    return self_energy, phonon_self


def solution(mesh):
    in_specs = (P("mom", "energy", None, None), P(), P(None, "energy", None), P("energy", None))
    out_specs = (P("mom", "energy", None, None), P("mom", "energy", None))
    return jax.shard_map(shards, mesh=mesh, in_specs=in_specs, out_specs=out_specs, check_vma=False)
```

```python
import functools

import jax
import jax.numpy as jnp
from jax import lax
from jax.experimental import pallas as pl
from jax.experimental.pallas import tpu as pltpu
from jax.sharding import PartitionSpec as P

ORB = 12
BRANCH = 3
FREQ = 64
COMP = 288
SQUARE = ORB * ORB
LANES = 128
REST = SQUARE - LANES
TAIL = 2 * REST
SLOTS = LANES // TAIL
TILE = 16
SMALL_GRANT = 16 * 1024 * 1024
LARGE_GRANT = 60 * 1024 * 1024
LONG = 100_000_000_000

BF16 = jnp.bfloat16
F32 = jnp.float32
I32 = jnp.int32


class Plan:
    def __init__(self, green, phonon, n_energy, n_mom):
        self.n_energy, self.n_mom = n_energy, n_mom
        self.mom_dev, self.steps, self.pairs, _ = green.shape
        self.momenta = self.mom_dev * n_mom
        self.pairs_dev = phonon.shape[1]
        self.group = FREQ // self.steps
        self.n_groups = n_energy // self.group
        self.peers = self.group * n_mom
        self.sub = self.pairs_dev // n_mom
        self.own = self.n_groups * self.sub
        self.block = self.group * self.pairs_dev
        self.main_rows = self.mom_dev * self.own * 2 * self.steps
        self.tail_rows = self.mom_dev * self.own // SLOTS * self.steps
        self.rows = self.main_rows + self.tail_rows
        assert self.group * self.steps == FREQ and n_energy % self.group == 0
        assert self.n_groups & (self.n_groups - 1) == 0
        assert self.pairs_dev % n_mom == 0 and TILE % self.block == 0
        assert self.mom_dev * self.own % SLOTS == 0 and self.n_groups % 2 == 0

    def main_row(self, k, u):
        return (k * self.own + u) * 2 * self.steps

    def tail_row(self, k, u):
        return self.main_rows + (k * self.own + u) // SLOTS * self.steps

    def shift(self, k):
        return k * self.own % SLOTS * TAIL

    def place(self, h, i):
        s, rest = divmod(TILE * h + i, self.block)
        j, rest = divmod(rest, self.pairs_dev)
        m, b = divmod(rest, self.sub)
        return j * self.n_mom + m, s * self.sub + b


def dot(a, b):
    return lax.dot_general(a, b, (((1,), (0,)), ((), ())), preferred_element_type=F32)


def dot_nt(a, b):
    return lax.dot_general(a, b, (((1,), (1,)), ((), ())), preferred_element_type=F32)


def iota(dims, axis):
    return lax.broadcasted_iota(I32, dims, axis)


def swap_matrix(outer, inner, flip=False):
    n = outer * inner
    row, col = iota((n, n), 0), iota((n, n), 1)
    place = row & (outer - 1)
    source = (outer - 1 - place if flip else place) * inner + (row >> (outer.bit_length() - 1))
    return (col == source).astype(F32).astype(BF16)


def to_wire(rows):
    tail = jnp.concatenate([rows[:, LANES:SQUARE], rows[:, SQUARE + LANES :]], axis=1)
    return rows[:, :LANES], rows[:, SQUARE : SQUARE + LANES], tail


def pack_rows(plan, load, out_ref, stage, sems, flip=False):
    swap = swap_matrix(plan.steps, TILE, flip)
    tails, copies = {}, []

    def send(first, count):
        rows = slice(first, first + count)
        copy = pltpu.make_async_copy(stage.at[:, rows, :], out_ref.at[:, rows, :], sems.at[len(copies)])
        copy.start()
        copies.append(copy)

    for k in range(plan.mom_dev):
        for h in range(plan.pairs // TILE):
            left, right, tail = to_wire(dot(swap, load(k, h)).astype(BF16))
            for i in range(TILE):
                peer, u = plan.place(h, i)
                here = slice(i * plan.steps, (i + 1) * plan.steps)
                row = plan.main_row(k, u)
                stage[peer, row : row + plan.steps, :] = left[here]
                stage[peer, row + plan.steps : row + 2 * plan.steps, :] = right[here]
                tails[peer, k * plan.own + u] = tail[here]
            count = TILE // plan.block * plan.sub
            send(plan.main_row(k, h * count), count * 2 * plan.steps)
    for peer in range(plan.peers):
        for first in range(0, plan.mom_dev * plan.own, SLOTS):
            row = plan.main_rows + first // SLOTS * plan.steps
            joined = jnp.concatenate([tails[peer, first + t] for t in range(SLOTS)], axis=1)
            stage[peer, row : row + plan.steps, :] = joined
    send(plan.main_rows, plan.tail_rows)
    for copy in copies:
        copy.wait()


def pack_own_kernel(plan, green_ref, out_ref, stage, out_sems, tiles, sems):
    copies = {}
    for k in range(plan.mom_dev):
        for h in range(plan.pairs // TILE):
            copies[k, h] = pltpu.make_async_copy(
                green_ref.at[k, :, TILE * h : TILE * (h + 1), :], tiles.at[k, h], sems.at[k, h]
            )
            copies[k, h].start()

    def load(k, h):
        copies[k, h].wait()
        return tiles[k, h].reshape(plan.steps * TILE, COMP)

    pack_rows(plan, load, out_ref, stage, out_sems)


def pack_partner_kernel(plan, take_ref, green_ref, out_ref, stage, sems, taken):
    chunk = take_ref.shape[0] // plan.pairs
    take = take_ref[...]
    for k in range(plan.mom_dev):
        for e in range(0, plan.steps, chunk):
            rows = green_ref[k, e : e + chunk].reshape(chunk * plan.pairs, COMP)
            taken[k, e : e + chunk] = dot(take, rows).astype(BF16).reshape(chunk, plan.pairs, COMP)

    def load(k, h):
        return taken[k, :, TILE * h : TILE * (h + 1), :].reshape(plan.steps * TILE, COMP)

    pack_rows(plan, load, out_ref, stage, sems, flip=True)


def each_pair(plan, body):
    if plan.own <= SLOTS:
        for u in range(plan.own):
            body(u)
    else:
        lax.fori_loop(0, plan.own, lambda u, _: body(u), None)


def rows_at(row, count):
    return pl.ds(row if isinstance(row, int) else pl.multiple_of(row, count), count)


def my_table(plan, tables_ref, u):
    group = lax.axis_index("energy") // plan.group
    return tables_ref[(u // plan.sub ^ group) * plan.sub + u % plan.sub]


def sandwich_kernel(plan, tables_ref, sand_ref, copy_ref, sem):
    place, want = iota((2 * LANES, 16), 0), iota((2 * LANES, 16), 1)

    def body(u):
        couple = my_table(plan, tables_ref, u)[: BRANCH * 16, :16]
        for h in range(2):
            comp = jnp.where(place < LANES, place, place - (u % SLOTS * TAIL + h * REST))
            valid = (place < LANES) | ((comp >= LANES) & (comp < SQUARE))
            quotient = (comp * 171) >> 11
            first = (valid & (quotient == want)).astype(F32).astype(BF16)
            second = (valid & (comp - ORB * quotient == want)).astype(F32).astype(BF16)
            left = dot_nt(couple, first).astype(BF16)
            right = dot_nt(couple, second).astype(BF16)
            for i in range(BRANCH):
                rows = slice(16 * i, 16 * i + 16)
                product = dot(first, left[rows]) * dot(second, right[rows])
                sand_ref[u, h, :, 2 * LANES * i : 2 * LANES * (i + 1)] = product.astype(BF16)

    each_pair(plan, body)
    copy = pltpu.make_async_copy(sand_ref, copy_ref, sem)
    copy.start()
    copy.wait()


def toeplitz_kernel(plan, tables_ref, toep_ref):
    mirror = iota((FREQ, 2 * FREQ), 0) + iota((FREQ, 2 * FREQ), 1) == FREQ
    mirror = mirror.astype(F32).astype(BF16)

    def body(u):
        lags = dot(my_table(plan, tables_ref, u)[BRANCH * 16 :, :], mirror)
        for q in range(plan.momenta):
            for i in range(BRANCH):
                n = q * BRANCH + i
                band = jnp.broadcast_to(lags[n : n + 1], (FREQ, 2 * FREQ))
                band = pltpu.roll(band, 0, 1, stride=1, stride_axis=0)
                toep_ref[u, q, i * FREQ : (i + 1) * FREQ, :] = band.astype(BF16)

    each_pair(plan, body)


def gather_rows(plan, ref, u, y, flip=False):
    m, k = divmod(y, plan.mom_dev)
    row, tail = plan.main_row(k, u), plan.tail_row(k, u)
    order = range(plan.group)
    lefts, rights, tails = [], [], []
    for j in reversed(order) if flip else order:
        peer = j * plan.n_mom + m
        lefts.append(ref[peer, rows_at(row, plan.steps), :])
        rights.append(ref[peer, rows_at(row + plan.steps, plan.steps), :])
        tails.append(ref[peer, rows_at(tail, plan.steps), :])
    tails = jnp.concatenate(tails, axis=0)
    if plan.shift(k):
        tails = pltpu.roll(tails.astype(F32), LANES - plan.shift(k), 1).astype(BF16)
    return jnp.concatenate([jnp.concatenate(lefts, axis=0), jnp.concatenate(rights, axis=0), tails], axis=1)


def half_and_tail(rows, h):
    return jnp.concatenate([rows[:, h * LANES : (h + 1) * LANES], rows[:, 2 * LANES :]], axis=1)


def halo_rows(plan, even, odd, u, y, later):
    group = lax.axis_index("energy") // plan.group
    inner = group % 2 == (0 if later else 1)
    exists = group < plan.n_groups - 1 if later else group > 0
    rows = jnp.where(inner, gather_rows(plan, even, u, y), gather_rows(plan, odd, u, y))
    return rows * exists.astype(F32).astype(BF16)


def self_kernel(plan, own, even, odd, toep_ref, sand_ref, out_ref, stage, sems):
    copies = []

    def send(rows):
        copy = pltpu.make_async_copy(stage.at[:, rows, :], out_ref.at[:, rows, :], sems.at[len(copies)])
        copy.start()
        copies.append(copy)

    for peer in range(plan.peers):
        stage[peer, plan.main_rows :, :] = jnp.zeros((plan.tail_rows, LANES), BF16)

    def body(u):
        green = []
        for y in range(plan.momenta):
            green.append(halo_rows(plan, even, odd, u, y, False))
            green.append(gather_rows(plan, own, u, y))
        green = jnp.concatenate(green, axis=0)
        summed = []
        for i in range(BRANCH):
            rows = slice(i * FREQ, (i + 1) * FREQ)
            band = jnp.concatenate(
                [
                    jnp.concatenate(
                        [toep_ref[u, (k - y) % plan.momenta, rows, :] for y in range(plan.momenta)], axis=1
                    )
                    for k in range(plan.momenta)
                ],
                axis=0,
            )
            summed.append(dot(band, green).astype(BF16))
        left, right = [
            dot_nt(jnp.concatenate([half_and_tail(rows, h) for rows in summed], axis=1), sand_ref[u, h])
            for h in range(2)
        ]
        tails = left[:, LANES:] + right[:, LANES:]
        left, right = left[:, :LANES].astype(BF16), right[:, :LANES].astype(BF16)
        for y in range(plan.momenta):
            m, k = divmod(y, plan.mom_dev)
            row, tail = plan.main_row(k, u), plan.tail_row(k, u)
            rest = tails[y * FREQ : (y + 1) * FREQ]
            if plan.shift(k):
                rest = pltpu.roll(rest, plan.shift(k), 1)
            rest = rest.astype(BF16)
            for j in range(plan.group):
                peer = j * plan.n_mom + m
                here = slice(j * plan.steps, (j + 1) * plan.steps)
                there = slice(y * FREQ + j * plan.steps, y * FREQ + (j + 1) * plan.steps)
                stage[peer, rows_at(row, plan.steps), :] = left[there]
                stage[peer, rows_at(row + plan.steps, plan.steps), :] = right[there]
                stage[peer, rows_at(tail, plan.steps), :] += rest[here]
        if isinstance(u, int):
            for k in range(plan.mom_dev):
                send(pl.ds(plan.main_row(k, u), 2 * plan.steps))

    each_pair(plan, body)
    send(pl.ds(plan.main_rows, plan.tail_rows) if copies else pl.ds(0, plan.rows))
    for copy in copies:
        copy.wait()


def lag_sums(plan, u, partner, green, sand_ref, store):
    partner, green = jnp.concatenate(partner, axis=0), jnp.concatenate(green, axis=0)
    left, right = [dot(half_and_tail(partner, h), sand_ref[u, h]) for h in range(2)]
    for i in range(BRANCH):
        here = slice(2 * LANES * i, 2 * LANES * i + LANES)
        rest = slice(2 * LANES * i + LANES, 2 * LANES * (i + 1))
        applied = jnp.concatenate([left[:, here], right[:, here], left[:, rest] + right[:, rest]], axis=1)
        lagged = dot_nt(applied.astype(BF16), green)
        for q in range(plan.momenta):
            acc = None
            for k in range(plan.momenta):
                y = (k + q) % plan.momenta
                part = lagged[k * FREQ : (k + 1) * FREQ, y * 2 * FREQ : (y + 1) * 2 * FREQ]
                acc = part if acc is None else acc + part
            acc = pltpu.roll(acc, FREQ + 1, 1, stride=1, stride_axis=0)
            store(q, i, jnp.sum(acc, axis=0, keepdims=True))


def phonon_kernel(plan, own, even, odd, partner, sand_hbm, *refs, scale):
    *outs, sums, sand_ref, sems = refs
    loads = [pltpu.make_async_copy(sand_hbm.at[u], sand_ref.at[u], sems.at[u]) for u in range(plan.own)]
    for load in loads:
        load.start()
    if plan.own > SLOTS:
        for load in loads:
            load.wait()
    group = lax.axis_index("energy") // plan.group
    me = lax.axis_index("mom")

    def body(u):
        if isinstance(u, int):
            loads[u].wait()
        rows = [gather_rows(plan, partner, u, k, flip=True) for k in range(plan.momenta)]
        green = []
        for y in range(plan.momenta):
            green.append(gather_rows(plan, own, u, y))
            green.append(halo_rows(plan, even, odd, u, y, True))

        def store(q, i, lags):
            side, row = divmod(q * BRANCH + i, plan.mom_dev * BRANCH)
            sums[u, side, row : row + 1, :] = lags * scale

        lag_sums(plan, u, rows, green, sand_ref, store)

    each_pair(plan, body)
    for d in range(plan.n_groups):
        for t in range(plan.n_mom):
            for b in range(plan.sub):
                outs[d * plan.n_mom + t][b] = sums[(group ^ d) * plan.sub + b, me ^ t]


def collect_kernel(plan, *refs):
    parts, out_ref = refs[:-1], refs[-1]
    me = lax.axis_index("mom")
    for d in range(plan.n_mom):
        total = sum(ref[...] for ref in parts[d :: plan.n_mom])
        for b in range(plan.sub):
            pair = (me ^ d) * plan.sub + b
            for q in range(plan.mom_dev):
                rows = [total[b, q * BRANCH + i : q * BRANCH + i + 1, :FREQ] for i in range(BRANCH)]
                out_ref[q, pl.ds(pair, 1), :] = jnp.concatenate(rows, axis=1)


def unpack_kernel(plan, wire, out_ref, tiles, sems):
    swap = swap_matrix(TILE, plan.steps)
    copies = []
    for k in range(plan.mom_dev):
        for h in range(plan.pairs // TILE):
            lefts, rights, tails = [], [], []
            for i in range(TILE):
                peer, u = plan.place(h, i)
                row, tail = plan.main_row(k, u), plan.tail_row(k, u)
                lefts.append(wire[peer, row : row + plan.steps, :])
                rights.append(wire[peer, row + plan.steps : row + 2 * plan.steps, :])
                lane = (k * plan.own + u) % SLOTS * TAIL
                tails.append(wire[peer, tail : tail + plan.steps, :][:, lane : lane + TAIL])
            rows = jnp.concatenate([jnp.concatenate(part, axis=0) for part in (lefts, rights, tails)], axis=1)
            moved = dot(swap, rows).astype(BF16)
            left, right = moved[:, :LANES], moved[:, LANES : 2 * LANES]
            tail = moved[:, 2 * LANES :]
            moved = jnp.concatenate([left, tail[:, :REST], right, tail[:, REST:]], axis=1)
            tiles[k, h] = moved.reshape(plan.steps, TILE, COMP)
            copy = pltpu.make_async_copy(
                tiles.at[k, h], out_ref.at[k, :, TILE * h : TILE * (h + 1), :], sems.at[k, h]
            )
            copy.start()
            copies.append(copy)
    for copy in copies:
        copy.wait()


ANY = pl.BlockSpec(memory_space=pl.ANY)
HBM = pl.BlockSpec(memory_space=pltpu.HBM)
VMEM = pl.BlockSpec(memory_space=pltpu.VMEM)


def call(plan, kernel, out_shape, *args, in_specs=None, out_specs=None, scratch=(), flops=1, grant=None):
    outs = jax.tree.map(lambda _: VMEM, out_shape)
    return pl.pallas_call(
        functools.partial(kernel, plan),
        out_shape=out_shape,
        in_specs=in_specs or [VMEM] * len(args),
        out_specs=out_specs or outs,
        scratch_shapes=list(scratch),
        compiler_params=pltpu.CompilerParams(vmem_limit_bytes=grant or SMALL_GRANT * max(1, plan.own // 4)),
        cost_estimate=pl.CostEstimate(flops=flops, bytes_accessed=1, transcendentals=0),
    )(*args)


def shape(dims, dtype):
    return jax.ShapeDtypeStruct(dims, dtype)


def in_hbm(struct):
    return pltpu.HBM(struct.shape, struct.dtype)


def shards(lesser_green, partner, phonon_green, coupling):
    n_energy, n_mom = lax.axis_size("energy"), lax.axis_size("mom")
    plan = Plan(lesser_green, phonon_green, n_energy, n_mom)
    axes = ("energy", "mom")
    me = lax.axis_index("mom")
    s = lax.axis_index("energy") // plan.group
    wire = shape((plan.peers, plan.rows, LANES), BF16)
    groups = [[g * plan.peers + i for i in range(plan.peers)] for g in range(plan.n_groups)]
    tiles = (plan.mom_dev, plan.pairs // TILE)

    def exchange(blocks):
        return lax.all_to_all(blocks, axes, split_axis=0, concat_axis=0, axis_index_groups=groups, tiled=True)

    def swap_groups(values, other):
        route = []
        for e in range(n_energy):
            g, j = divmod(e, plan.group)
            to = other(g) if 0 <= other(g) < plan.n_groups else g
            route.append((e, to * plan.group + j))
        return lax.ppermute(values, "energy", route)

    staging = [pltpu.VMEM(wire.shape, BF16), pltpu.SemaphoreType.DMA((tiles[0] * tiles[1] + 1,))]
    tile_scratch = [pltpu.VMEM(tiles + (plan.steps, TILE, COMP), BF16), pltpu.SemaphoreType.DMA(tiles)]
    own = exchange(
        call(
            plan,
            pack_own_kernel,
            in_hbm(wire),
            lesser_green,
            in_specs=[HBM],
            out_specs=HBM,
            scratch=staging + tile_scratch,
            grant=LARGE_GRANT,
        )
    )

    lag_count = plan.momenta * BRANCH
    lag_rows = -(-lag_count // 16) * 16
    couple = coupling.reshape(plan.pairs_dev, BRANCH, ORB, ORB)
    couple = jnp.pad(couple, ((0, 0), (0, 0), (0, 16 - ORB), (0, FREQ - ORB)))
    phonon = phonon_green.reshape(plan.momenta, plan.pairs_dev, BRANCH, FREQ)
    phonon = jnp.moveaxis(phonon, 1, 0).reshape(plan.pairs_dev, lag_count, FREQ)
    phonon = jnp.pad(phonon, ((0, 0), (0, lag_rows - lag_count), (0, 0)))
    table = jnp.concatenate([couple.reshape(plan.pairs_dev, BRANCH * 16, FREQ), phonon], axis=1)
    table = lax.dynamic_slice_in_dim(table, me * plan.sub, plan.sub, axis=0)
    tables = [table]
    for d in range(1, plan.n_groups):
        tables.append(swap_groups(table, functools.partial(lambda d, g: g ^ d, d)))
    tables = jnp.concatenate(tables, axis=0)
    chunk = max(1, 256 // plan.pairs)
    source = (jnp.arange(chunk)[:, None] * plan.pairs + partner[None, :]).reshape(-1)
    take = (source[:, None] == jnp.arange(chunk * plan.pairs)[None, :]).astype(BF16)
    partner_wire = call(
        plan,
        pack_partner_kernel,
        in_hbm(wire),
        take,
        lesser_green,
        out_specs=HBM,
        scratch=staging + [pltpu.VMEM(lesser_green.shape, BF16)],
    )
    own, tables, partner_wire = lax.optimization_barrier((own, tables, partner_wire))

    def neighbours(shift):
        route = []
        for e in range(n_energy):
            g, j = divmod(e, plan.group)
            to = ((g - shift) ^ 1) + shift
            for m in range(n_mom):
                if 0 <= to < plan.n_groups:
                    route.append((e * n_mom + m, (to * plan.group + j) * n_mom + m))
                else:
                    route.append((e * n_mom + m, e * n_mom + (m ^ 1)))
        return lax.ppermute(own, axes, route)

    even, odd = neighbours(0), neighbours(1)

    toep = call(
        plan,
        toeplitz_kernel,
        shape((plan.own, plan.momenta, BRANCH * FREQ, 2 * FREQ), BF16),
        tables,
        flops=LONG,
    )
    toep, partner_wire = lax.optimization_barrier((toep, partner_wire))
    partner_blocks = exchange(partner_wire)
    sand_shape = shape((plan.own, 2, 2 * LANES, BRANCH * 2 * LANES), BF16)
    sand, sand_copy = call(
        plan,
        sandwich_kernel,
        [sand_shape, in_hbm(sand_shape)],
        tables,
        out_specs=[VMEM, HBM],
        scratch=[pltpu.SemaphoreType.DMA],
        flops=LONG,
    )
    sigma = call(
        plan,
        self_kernel,
        in_hbm(wire),
        own,
        even,
        odd,
        toep,
        sand,
        out_specs=HBM,
        scratch=[pltpu.VMEM(wire.shape, BF16), pltpu.SemaphoreType.DMA((plan.mom_dev * plan.own + 1,))],
    )
    sigma, sand_copy = lax.optimization_barrier((sigma, sand_copy))
    arrived = exchange(sigma)

    scale = (plan.momenta * n_energy * plan.steps * COMP) ** -0.5
    side_rows = plan.mom_dev * BRANCH
    parts = list(
        call(
            plan,
            functools.partial(phonon_kernel, scale=scale),
            [shape((plan.sub, side_rows, LANES), F32)] * (plan.n_groups * n_mom),
            own,
            even,
            odd,
            partner_blocks,
            sand_copy,
            in_specs=[VMEM] * 4 + [HBM],
            scratch=[
                pltpu.VMEM((plan.own, n_mom, side_rows, LANES), F32),
                pltpu.VMEM(sand_shape.shape, BF16),
                pltpu.SemaphoreType.DMA((plan.own,)),
            ],
        )
    )
    for d in range(plan.n_groups):
        for t in range(n_mom):
            if d or t:
                route = []
                for e in range(n_energy):
                    g, j = divmod(e, plan.group)
                    for m in range(n_mom):
                        route.append((e * n_mom + m, ((g ^ d) * plan.group + j) * n_mom + (m ^ t)))
                parts[d * n_mom + t] = lax.ppermute(parts[d * n_mom + t], axes, route)
    phonon_self = call(
        plan, collect_kernel, shape((plan.mom_dev, plan.pairs_dev, BRANCH * FREQ), F32), *parts
    )

    self_energy = call(
        plan,
        unpack_kernel,
        shape(lesser_green.shape, BF16),
        arrived,
        out_specs=ANY,
        scratch=tile_scratch,
    )
    return self_energy, phonon_self


def solution(mesh):
    in_specs = (P("mom", "energy", None, None), P(), P(None, "energy", None), P("energy", None))
    out_specs = (P("mom", "energy", None, None), P("mom", "energy", None))
    return jax.shard_map(shards, mesh=mesh, in_specs=in_specs, out_specs=out_specs, check_vma=False)
```

```python
import functools

import jax
import jax.numpy as jnp
from jax import lax
from jax.experimental import pallas as pl
from jax.experimental.pallas import tpu as pltpu
from jax.sharding import PartitionSpec as P

ORB = 12
BRANCH = 3
FREQ = 64
COMP = 288
SQUARE = ORB * ORB
LANES = 128
REST = SQUARE - LANES
TAIL = 2 * REST
SLOTS = LANES // TAIL
TILE = 16
SMALL_GRANT = 16 * 1024 * 1024
LARGE_GRANT = 60 * 1024 * 1024
LONG = 100_000_000_000

BF16 = jnp.bfloat16
F32 = jnp.float32
I32 = jnp.int32


class Plan:
    def __init__(self, green, phonon, n_energy, n_mom):
        self.n_energy, self.n_mom = n_energy, n_mom
        self.mom_dev, self.steps, self.pairs, _ = green.shape
        self.momenta = self.mom_dev * n_mom
        self.pairs_dev = phonon.shape[1]
        self.half = FREQ // self.steps
        self.group = 2 * self.half
        self.n_groups = n_energy // self.group
        self.peers = self.group * n_mom
        self.sub = self.pairs_dev // n_mom
        self.own = self.n_groups * self.sub
        self.main_rows = self.mom_dev * self.own * 2 * self.steps
        self.tail_rows = self.mom_dev * self.own // SLOTS * self.steps
        self.rows = self.main_rows + self.tail_rows
        assert self.half * self.steps == FREQ and n_energy % self.group == 0
        for count in (self.n_groups, self.half, n_mom):
            assert count & (count - 1) == 0
        self.sides = 1 if self.n_groups == 2 else 2
        assert self.pairs_dev % n_mom == 0 and self.group * self.pairs_dev == TILE
        assert self.mom_dev * self.own % SLOTS == 0 and self.n_groups % 2 == 0

    def main_row(self, k, u):
        return (k * self.own + u) * 2 * self.steps

    def tail_row(self, k, u):
        return self.main_rows + (k * self.own + u) // SLOTS * self.steps

    def hops(self):
        return [(plane, d) for d in range(self.half) for plane in (1, 0)]

    def shift(self, k):
        return k * self.own % SLOTS * TAIL

    def place(self, h, i):
        j, rest = divmod(i, self.pairs_dev)
        m, b = divmod(rest, self.sub)
        return j * self.n_mom + m, h * self.sub + b


def dot(a, b):
    return lax.dot_general(a, b, (((1,), (0,)), ((), ())), preferred_element_type=F32)


def dot_nt(a, b):
    return lax.dot_general(a, b, (((1,), (1,)), ((), ())), preferred_element_type=F32)


def iota(dims, axis):
    return lax.broadcasted_iota(I32, dims, axis)


def swap_matrix(outer, inner, flip=False):
    n = outer * inner
    row, col = iota((n, n), 0), iota((n, n), 1)
    place = row & (outer - 1)
    source = (outer - 1 - place if flip else place) * inner + (row >> (outer.bit_length() - 1))
    return (col == source).astype(F32).astype(BF16)


def to_wire(rows):
    tail = jnp.concatenate([rows[:, LANES:SQUARE], rows[:, SQUARE + LANES :]], axis=1)
    return rows[:, :LANES], rows[:, SQUARE : SQUARE + LANES], tail


def pack_rows(plan, load, stage, sent, base=0, flip=False):
    swap = swap_matrix(plan.steps, TILE, flip)
    tails = {}
    for k in range(plan.mom_dev):
        for h in range(plan.pairs // TILE):
            left, right, tail = to_wire(dot(swap, load(k, h)).astype(BF16))
            for i in range(TILE):
                peer, u = plan.place(h, i)
                here = slice(i * plan.steps, (i + 1) * plan.steps)
                row = base + plan.main_row(k, u)
                stage[peer, row : row + plan.steps, :] = left[here]
                stage[peer, row + plan.steps : row + 2 * plan.steps, :] = right[here]
                tails[peer, k * plan.own + u] = tail[here]
            sent(base + plan.main_row(k, h * plan.sub), plan.sub * 2 * plan.steps)
    for peer in range(plan.peers):
        for first in range(0, plan.mom_dev * plan.own, SLOTS):
            row = base + plan.main_rows + first // SLOTS * plan.steps
            joined = jnp.concatenate([tails[peer, first + t] for t in range(SLOTS)], axis=1)
            stage[peer, row : row + plan.steps, :] = joined
    sent(base + plan.main_rows, plan.tail_rows)


def pack_kernel(plan, partner_hbm, green_hbm, out_ref, *refs):
    *messages, stage, green, taken, partner, in_sems, out_sems = refs
    keys = [(k, h) for k in range(plan.mom_dev) for h in range(plan.pairs // TILE)]
    loads = {}
    for n, (k, h) in enumerate(keys):
        here = pl.ds(TILE * h, TILE)
        loads[k, h] = pltpu.make_async_copy(green_hbm.at[k, :, here, :], green.at[k, :, here, :], in_sems.at[n])
        loads[k, h].start()
    scalars = pltpu.make_async_copy(partner_hbm, partner, in_sems.at[len(keys)])
    scalars.start()
    copies = []

    def send(first, count):
        rows = pl.ds(first, count)
        copy = pltpu.make_async_copy(stage.at[:, rows, :], out_ref.at[:, rows, :], out_sems.at[len(copies)])
        copy.start()
        copies.append(copy)

    def load(k, h):
        loads[k, h].wait()
        return green[k, :, TILE * h : TILE * (h + 1), :].reshape(plan.steps * TILE, COMP)

    pack_rows(plan, load, stage, send)

    here = lax.axis_index("energy") % plan.group
    later, seat = here // plan.half, here % plan.half
    for message, (plane, d) in zip(messages, plan.hops()):
        chip = (1 - plane ^ later) * plan.half + (seat ^ d)
        for m in range(plan.n_mom):
            message[m] = stage[chip * plan.n_mom + m, : plan.rows, :]

    scalars.wait()
    chunk = max(1, 2 * LANES // plan.pairs)
    width = chunk * plan.pairs
    row, col = iota((plan.pairs, width), 0), iota((plan.pairs, width), 1)
    source = jnp.zeros((plan.pairs, width), I32)
    for p in range(plan.pairs):
        source = jnp.where(row == p, partner[p], source)
    take = [(col == source + e * plan.pairs).astype(F32).astype(BF16) for e in range(chunk)]
    take = jnp.concatenate(take, axis=0)
    for k in range(plan.mom_dev):
        for e in range(0, plan.steps, chunk):
            rows = green[k, e : e + chunk].reshape(width, COMP)
            taken[k, e : e + chunk] = dot(take, rows).astype(BF16).reshape(chunk, plan.pairs, COMP)

    def load_taken(k, h):
        return taken[k, :, TILE * h : TILE * (h + 1), :].reshape(plan.steps * TILE, COMP)

    pack_rows(plan, load_taken, stage, send, base=plan.rows, flip=True)
    for copy in copies:
        copy.wait()


def halo_kernel(plan, *refs):
    messages, outs = dict(zip(plan.hops(), refs)), refs[2 * plan.half :]
    here = lax.axis_index("energy") % plan.group
    plane, seat = here // plan.half, here % plan.half
    me = lax.axis_index("mom")
    for d in range(plan.half):
        first, second = messages[0, d], messages[1, d]
        for t in range(plan.n_mom):
            a, b = first[me ^ t], second[me ^ t]
            if plan.sides == 1:
                outs[t][0, seat ^ d] = a + b
            else:
                outs[t][0, seat ^ d] = jnp.where(plane == 0, a, b)
                outs[t][1, seat ^ d] = jnp.where(plane == 0, b, a)


def each_pair(plan, body):
    if plan.own <= 2:
        for u in range(plan.own):
            body(u)
    else:
        lax.fori_loop(0, plan.own, lambda u, _: body(u), None)


def rows_at(row, count):
    return pl.ds(row if isinstance(row, int) else pl.multiple_of(row, count), count)


def my_table(plan, tables_ref, u):
    group = lax.axis_index("energy") // plan.group
    return tables_ref[(u // plan.sub ^ group) * plan.sub + u % plan.sub]


def sandwich_kernel(plan, tables_ref, sand_ref):
    place, want = iota((2 * LANES, 16), 0), iota((2 * LANES, 16), 1)

    def body(u):
        couple = my_table(plan, tables_ref, u)[: BRANCH * 16, :16]
        for h in range(2):
            comp = jnp.where(place < LANES, place, place - (u % SLOTS * TAIL + h * REST))
            valid = (place < LANES) | ((comp >= LANES) & (comp < SQUARE))
            quotient = (comp * 171) >> 11
            first = (valid & (quotient == want)).astype(F32).astype(BF16)
            second = (valid & (comp - ORB * quotient == want)).astype(F32).astype(BF16)
            left = dot_nt(couple, first).astype(BF16)
            right = dot_nt(couple, second).astype(BF16)
            for i in range(BRANCH):
                rows = slice(16 * i, 16 * i + 16)
                product = dot(first, left[rows]) * dot(second, right[rows])
                sand_ref[u, h, :, 2 * LANES * i : 2 * LANES * (i + 1)] = product.astype(BF16)

    each_pair(plan, body)


def toeplitz_kernel(plan, tables_ref, toep_ref):
    mirror = iota((FREQ, 2 * FREQ), 0) + iota((FREQ, 2 * FREQ), 1) == FREQ
    mirror = mirror.astype(F32).astype(BF16)

    def body(u):
        lags = dot(my_table(plan, tables_ref, u)[BRANCH * 16 :, :], mirror)
        for q in range(plan.momenta):
            for i in range(BRANCH):
                n = q * BRANCH + i
                band = jnp.broadcast_to(lags[n : n + 1], (FREQ, 2 * FREQ))
                band = pltpu.roll(band, 0, 1, stride=1, stride_axis=0)
                toep_ref[u, q, i * FREQ : (i + 1) * FREQ, :] = band.astype(BF16)

    each_pair(plan, body)


def gather_rows(plan, ref, u, y, place, base=0, flip=False):
    m, k = divmod(y, plan.mom_dev)
    row, tail = base + plan.main_row(k, u), base + plan.tail_row(k, u)
    order = range(plan.half)
    lefts, rights, tails = [], [], []
    for j in reversed(order) if flip else order:
        peer = place(j, m)
        lefts.append(ref[peer, rows_at(row, plan.steps), :])
        rights.append(ref[peer, rows_at(row + plan.steps, plan.steps), :])
        tails.append(ref[peer, rows_at(tail, plan.steps), :])
    tails = jnp.concatenate(tails, axis=0)
    if plan.shift(k):
        tails = pltpu.roll(tails.astype(F32), LANES - plan.shift(k), 1).astype(BF16)
    return jnp.concatenate([jnp.concatenate(lefts, axis=0), jnp.concatenate(rights, axis=0), tails], axis=1)


def half_and_tail(rows, h):
    return jnp.concatenate([rows[:, h * LANES : (h + 1) * LANES], rows[:, 2 * LANES :]], axis=1)


def own_rows(plan, blocks, u, y, late):
    return gather_rows(plan, blocks, u, y, lambda j, m: (late * plan.half + j) * plan.n_mom + m)


def partner_rows(plan, blocks, u, k, late):
    place = lambda j, m: (late * plan.half + j) * plan.n_mom + m
    return gather_rows(plan, blocks, u, k, place, base=plan.rows, flip=True)


def halo_rows(plan, halo, u, y, side, has):
    side = min(side, plan.sides - 1)
    rows = gather_rows(plan, halo, u, y, lambda j, m: (m * plan.sides + side) * plan.half + j)
    return rows * has.astype(F32).astype(BF16)


def sort_halo(plan, halos, halo):
    me = lax.axis_index("mom")
    count = plan.sides * plan.half
    for t in range(plan.n_mom):
        for side in range(plan.sides):
            for j in range(plan.half):
                halo[(me ^ t) * count + side * plan.half + j] = halos[t][side, j]


def self_block(plan, u, green, toep_ref, sand_ref, out_ref, late):
    green = jnp.concatenate(green, axis=0)
    summed = []
    for i in range(BRANCH):
        rows = slice(i * FREQ, (i + 1) * FREQ)
        band = jnp.concatenate(
            [
                jnp.concatenate([toep_ref[u, (k - y) % plan.momenta, rows, :] for y in range(plan.momenta)], axis=1)
                for k in range(plan.momenta)
            ],
            axis=0,
        )
        summed.append(dot(band, green).astype(BF16))
    left, right = [
        dot_nt(jnp.concatenate([half_and_tail(rows, h) for rows in summed], axis=1), sand_ref[u, h])
        for h in range(2)
    ]
    tails = left[:, LANES:] + right[:, LANES:]
    left, right = left[:, :LANES].astype(BF16), right[:, :LANES].astype(BF16)
    for y in range(plan.momenta):
        m, k = divmod(y, plan.mom_dev)
        row, tail = plan.main_row(k, u), plan.tail_row(k, u)
        rest = tails[y * FREQ : (y + 1) * FREQ]
        if plan.shift(k):
            rest = pltpu.roll(rest, plan.shift(k), 1)
        rest = rest.astype(BF16)
        for j in range(plan.half):
            peer = (late * plan.half + j) * plan.n_mom + m
            here = slice(j * plan.steps, (j + 1) * plan.steps)
            there = slice(y * FREQ + j * plan.steps, y * FREQ + (j + 1) * plan.steps)
            out_ref[peer, rows_at(row, plan.steps), :] = left[there]
            out_ref[peer, rows_at(row + plan.steps, plan.steps), :] = right[there]
            out_ref[peer, rows_at(tail, plan.steps), :] += rest[here]


def self_kernel(plan, blocks, *refs):
    halos, (toep_ref, sand_ref, out_ref, copy_ref, stage, halo, sems) = refs[: plan.n_mom], refs[plan.n_mom :]
    copies = [pltpu.make_async_copy(sand_ref, copy_ref, sems.at[2])]
    copies[0].start()
    has_before = lax.axis_index("energy") // plan.group > 0
    near = plan.half * plan.n_mom
    sort_halo(plan, halos, halo)
    for peer in range(plan.peers):
        stage[peer, plan.main_rows :, :] = jnp.zeros((plan.tail_rows, LANES), BF16)
    for late in (1, 0):

        def body(u):
            green = []
            for y in range(plan.momenta):
                if late:
                    green.append(own_rows(plan, blocks, u, y, 0))
                else:
                    green.append(halo_rows(plan, halo, u, y, 0, has_before))
                green.append(own_rows(plan, blocks, u, y, late))
            self_block(plan, u, green, toep_ref, sand_ref, stage, late)

        each_pair(plan, body)
        here = pl.ds(late * near, near)
        copies.append(pltpu.make_async_copy(stage.at[here], out_ref.at[here], sems.at[late]))
        copies[-1].start()
    for copy in copies:
        copy.wait()


def lag_sums(plan, u, partner, green, sand_ref, store):
    partner, green = jnp.concatenate(partner, axis=0), jnp.concatenate(green, axis=0)
    left, right = [dot(half_and_tail(partner, h), sand_ref[u, h]) for h in range(2)]
    for i in range(BRANCH):
        here = slice(2 * LANES * i, 2 * LANES * i + LANES)
        rest = slice(2 * LANES * i + LANES, 2 * LANES * (i + 1))
        applied = jnp.concatenate([left[:, here], right[:, here], left[:, rest] + right[:, rest]], axis=1)
        lagged = dot_nt(applied.astype(BF16), green)
        for q in range(plan.momenta):
            acc = None
            for k in range(plan.momenta):
                y = (k + q) % plan.momenta
                part = lagged[k * FREQ : (k + 1) * FREQ, y * 2 * FREQ : (y + 1) * 2 * FREQ]
                acc = part if acc is None else acc + part
            acc = pltpu.roll(acc, FREQ + 1, 1, stride=1, stride_axis=0)
            store(q, i, jnp.sum(acc, axis=0, keepdims=True))


def phonon_kernel(plan, blocks, *refs, scale):
    halos, (sand_hbm, *outs, sums, halo, sand_ref, sem) = refs[: plan.n_mom], refs[plan.n_mom :]
    load = pltpu.make_async_copy(sand_hbm, sand_ref, sem)
    load.start()
    group = lax.axis_index("energy") // plan.group
    me = lax.axis_index("mom")
    has_after = group < plan.n_groups - 1
    sort_halo(plan, halos, halo)
    load.wait()

    def body(u):
        for late in range(2):
            partner = [partner_rows(plan, blocks, u, k, late) for k in range(plan.momenta)]
            green = []
            for y in range(plan.momenta):
                green.append(own_rows(plan, blocks, u, y, late))
                if late:
                    green.append(halo_rows(plan, halo, u, y, 1, has_after))
                else:
                    green.append(own_rows(plan, blocks, u, y, 1))

            def store(q, i, lags):
                side, row = divmod(q * BRANCH + i, plan.mom_dev * BRANCH)
                if late:
                    lags = lags + sums[u, side, row : row + 1, :]
                sums[u, side, row : row + 1, :] = lags * scale if late else lags

            lag_sums(plan, u, partner, green, sand_ref, store)

    each_pair(plan, body)
    for d in range(plan.n_groups):
        for t in range(plan.n_mom):
            for b in range(plan.sub):
                outs[d * plan.n_mom + t][b] = sums[(group ^ d) * plan.sub + b, me ^ t]


def collect_kernel(plan, *refs):
    parts, out_ref = refs[:-1], refs[-1]
    me = lax.axis_index("mom")
    for d in range(plan.n_mom):
        total = sum(ref[...] for ref in parts[d :: plan.n_mom])
        for b in range(plan.sub):
            pair = (me ^ d) * plan.sub + b
            for q in range(plan.mom_dev):
                rows = [total[b, q * BRANCH + i : q * BRANCH + i + 1, :FREQ] for i in range(BRANCH)]
                out_ref[q, pl.ds(pair, 1), :] = jnp.concatenate(rows, axis=1)


def unpack_kernel(plan, wire, out_ref, tiles, sems):
    swap = swap_matrix(TILE, plan.steps)
    copies = []
    for k in range(plan.mom_dev):
        for h in range(plan.pairs // TILE):
            lefts, rights, tails = [], [], []
            for i in range(TILE):
                peer, u = plan.place(h, i)
                row, tail = plan.main_row(k, u), plan.tail_row(k, u)
                lefts.append(wire[peer, row : row + plan.steps, :])
                rights.append(wire[peer, row + plan.steps : row + 2 * plan.steps, :])
                lane = (k * plan.own + u) % SLOTS * TAIL
                tails.append(wire[peer, tail : tail + plan.steps, :][:, lane : lane + TAIL])
            rows = jnp.concatenate([jnp.concatenate(part, axis=0) for part in (lefts, rights, tails)], axis=1)
            moved = dot(swap, rows).astype(BF16)
            left, right = moved[:, :LANES], moved[:, LANES : 2 * LANES]
            tail = moved[:, 2 * LANES :]
            moved = jnp.concatenate([left, tail[:, :REST], right, tail[:, REST:]], axis=1)
            tiles[k, h] = moved.reshape(plan.steps, TILE, COMP)
            copy = pltpu.make_async_copy(
                tiles.at[k, h], out_ref.at[k, :, TILE * h : TILE * (h + 1), :], sems.at[k, h]
            )
            copy.start()
            copies.append(copy)
    for copy in copies:
        copy.wait()


ANY = pl.BlockSpec(memory_space=pl.ANY)
HBM = pl.BlockSpec(memory_space=pltpu.HBM)
VMEM = pl.BlockSpec(memory_space=pltpu.VMEM)


def call(plan, kernel, out_shape, *args, in_specs=None, out_specs=None, scratch=(), flops=1, grant=None):
    outs = jax.tree.map(lambda _: VMEM, out_shape)
    return pl.pallas_call(
        functools.partial(kernel, plan),
        out_shape=out_shape,
        in_specs=in_specs or [VMEM] * len(args),
        out_specs=out_specs or outs,
        scratch_shapes=list(scratch),
        compiler_params=pltpu.CompilerParams(vmem_limit_bytes=grant or SMALL_GRANT * max(1, plan.own // 4)),
        cost_estimate=pl.CostEstimate(flops=flops, bytes_accessed=1, transcendentals=0),
    )(*args)


def shape(dims, dtype):
    return jax.ShapeDtypeStruct(dims, dtype)


def in_hbm(struct):
    return pltpu.HBM(struct.shape, struct.dtype)


def shards(lesser_green, partner, phonon_green, coupling):
    n_energy, n_mom = lax.axis_size("energy"), lax.axis_size("mom")
    plan = Plan(lesser_green, phonon_green, n_energy, n_mom)
    axes = ("energy", "mom")
    me = lax.axis_index("mom")
    s = lax.axis_index("energy") // plan.group
    wire = shape((plan.peers, plan.rows, LANES), BF16)
    groups = [[g * plan.peers + i for i in range(plan.peers)] for g in range(plan.n_groups)]
    tiles = (plan.mom_dev, plan.pairs // TILE)

    def exchange(blocks):
        return lax.all_to_all(blocks, axes, split_axis=0, concat_axis=0, axis_index_groups=groups, tiled=True)

    def swap_groups(values, other):
        route = []
        for e in range(n_energy):
            g, j = divmod(e, plan.group)
            to = other(g) if 0 <= other(g) < plan.n_groups else g
            route.append((e, to * plan.group + j))
        return lax.ppermute(values, "energy", route)

    both = (plan.peers, 2 * plan.rows, LANES)
    message = shape((n_mom, plan.rows, LANES), BF16)
    packed, *messages = call(
        plan,
        pack_kernel,
        [in_hbm(shape(both, BF16))] + [message] * len(plan.hops()),
        partner,
        lesser_green,
        in_specs=[HBM, HBM],
        out_specs=[HBM] + [VMEM] * len(plan.hops()),
        scratch=[
            pltpu.VMEM(both, BF16),
            pltpu.VMEM(lesser_green.shape, BF16),
            pltpu.VMEM(lesser_green.shape, BF16),
            pltpu.SMEM((plan.pairs,), I32),
            pltpu.SemaphoreType.DMA((tiles[0] * tiles[1] + 1,)),
            pltpu.SemaphoreType.DMA((2 * (tiles[0] * tiles[1] + 1),)),
        ],
        grant=LARGE_GRANT,
    )
    lag_count = plan.momenta * BRANCH
    lag_rows = -(-lag_count // 16) * 16
    couple = coupling.reshape(plan.pairs_dev, BRANCH, ORB, ORB)
    couple = jnp.pad(couple, ((0, 0), (0, 0), (0, 16 - ORB), (0, FREQ - ORB)))
    phonon = phonon_green.reshape(plan.momenta, plan.pairs_dev, BRANCH, FREQ)
    phonon = jnp.moveaxis(phonon, 1, 0).reshape(plan.pairs_dev, lag_count, FREQ)
    phonon = jnp.pad(phonon, ((0, 0), (0, lag_rows - lag_count), (0, 0)))
    table = jnp.concatenate([couple.reshape(plan.pairs_dev, BRANCH * 16, FREQ), phonon], axis=1)
    table = lax.dynamic_slice_in_dim(table, me * plan.sub, plan.sub, axis=0)
    messages[0], table = lax.optimization_barrier((messages[0], table))
    tables = [table]
    for d in range(1, plan.n_groups):
        tables.append(swap_groups(table, functools.partial(lambda d, g: g ^ d, d)))
    tables = jnp.concatenate(tables, axis=0)
    blocks = exchange(packed)
    messages[2:], tables = lax.optimization_barrier((messages[2:], tables))

    arrived = []
    for message, (plane, d) in zip(messages, plan.hops()):
        route = []
        for e in range(n_energy):
            g, rest = divmod(e, plan.group)
            later, seat = divmod(rest, plan.half)
            g, to = (g + 1, plane) if later else (g - 1, 1 - plane)
            if 0 <= g < plan.n_groups:
                route.append((e, g * plan.group + to * plan.half + (seat ^ d)))
        arrived.append(lax.ppermute(message, "energy", route))
    side_shape = shape((plan.sides, plan.half, plan.rows, LANES), BF16)
    halos = list(call(plan, halo_kernel, [side_shape] * n_mom, *arrived))
    halos[0], tables = lax.optimization_barrier((halos[0], tables))
    for t in range(1, n_mom):
        halos[t] = lax.ppermute(halos[t], "mom", [(m, m ^ t) for m in range(n_mom)])

    sand_shape = shape((plan.own, 2, 2 * LANES, BRANCH * 2 * LANES), BF16)
    sand = call(plan, sandwich_kernel, sand_shape, tables, flops=LONG)
    toep = call(plan, toeplitz_kernel, shape((plan.own, plan.momenta, BRANCH * FREQ, 2 * FREQ), BF16), tables)
    blocks, halos, sand, toep = lax.optimization_barrier((blocks, halos, sand, toep))

    halo_scratch = pltpu.VMEM((n_mom * plan.sides * plan.half, plan.rows, LANES), BF16)
    sigma, sand_copy = call(
        plan,
        self_kernel,
        [in_hbm(wire), in_hbm(sand_shape)],
        blocks,
        *halos,
        toep,
        sand,
        out_specs=[HBM, HBM],
        scratch=[pltpu.VMEM(wire.shape, BF16), halo_scratch, pltpu.SemaphoreType.DMA((3,))],
    )
    arrived = exchange(sigma)

    scale = (plan.momenta * n_energy * plan.steps * COMP) ** -0.5
    side_rows = plan.mom_dev * BRANCH
    parts = list(
        call(
            plan,
            functools.partial(phonon_kernel, scale=scale),
            [shape((plan.sub, side_rows, LANES), F32)] * (plan.n_groups * n_mom),
            blocks,
            *halos,
            sand_copy,
            in_specs=[VMEM] * (n_mom + 1) + [HBM],
            scratch=[
                pltpu.VMEM((plan.own, n_mom, side_rows, LANES), F32),
                halo_scratch,
                pltpu.VMEM(sand_shape.shape, BF16),
                pltpu.SemaphoreType.DMA,
            ],
        )
    )
    for d in range(plan.n_groups):
        for t in range(n_mom):
            if d or t:
                route = []
                for e in range(n_energy):
                    g, j = divmod(e, plan.group)
                    for m in range(n_mom):
                        route.append((e * n_mom + m, ((g ^ d) * plan.group + j) * n_mom + (m ^ t)))
                parts[d * n_mom + t] = lax.ppermute(parts[d * n_mom + t], axes, route)
    phonon_self = call(
        plan, collect_kernel, shape((plan.mom_dev, plan.pairs_dev, BRANCH * FREQ), F32), *parts
    )

    self_energy = call(
        plan,
        unpack_kernel,
        shape(lesser_green.shape, BF16),
        arrived,
        out_specs=ANY,
        scratch=[pltpu.VMEM(tiles + (plan.steps, TILE, COMP), BF16), pltpu.SemaphoreType.DMA(tiles)],
    )
    return self_energy, phonon_self


def solution(mesh):
    in_specs = (P("mom", "energy", None, None), P(), P(None, "energy", None), P("energy", None))
    out_specs = (P("mom", "energy", None, None), P("mom", "energy", None))
    return jax.shard_map(shards, mesh=mesh, in_specs=in_specs, out_specs=out_specs, check_vma=False)
```

```python
import functools

import jax
import jax.numpy as jnp
from jax import lax
from jax.experimental import pallas as pl
from jax.experimental.pallas import tpu as pltpu
from jax.sharding import PartitionSpec as P

ORB = 12
BRANCH = 3
FREQ = 64
COMP = 288
SQUARE = ORB * ORB
LANES = 128
REST = SQUARE - LANES
TAIL = 2 * REST
SLOTS = LANES // TAIL
TILE = 16
SMALL_GRANT = 16 * 1024 * 1024
LARGE_GRANT = 60 * 1024 * 1024
LONG = 100_000_000_000

BF16 = jnp.bfloat16
F32 = jnp.float32
I32 = jnp.int32


class Plan:
    def __init__(self, green, phonon, n_energy, n_mom):
        self.n_energy, self.n_mom = n_energy, n_mom
        self.mom_dev, self.steps, self.pairs, _ = green.shape
        self.momenta = self.mom_dev * n_mom
        self.pairs_dev = phonon.shape[1]
        self.half = FREQ // self.steps
        self.group = 2 * self.half
        self.n_groups = n_energy // self.group
        self.peers = self.group * n_mom
        self.sub = self.pairs_dev // n_mom
        self.own = self.n_groups * self.sub
        self.main_rows = self.mom_dev * self.own * 2 * self.steps
        self.tail_rows = self.mom_dev * self.own // SLOTS * self.steps
        self.rows = self.main_rows + self.tail_rows
        assert self.half * self.steps == FREQ and n_energy % self.group == 0
        assert self.n_groups & (self.n_groups - 1) == 0
        assert self.pairs_dev == n_mom and self.group * self.pairs_dev == TILE
        assert self.mom_dev * self.own % SLOTS == 0 and self.n_groups % 2 == 0

    def main_row(self, k, u):
        return (k * self.own + u) * 2 * self.steps

    def tail_row(self, k, u):
        return self.main_rows + (k * self.own + u) // SLOTS * self.steps

    def shift(self, k):
        return k * self.own % SLOTS * TAIL


def dot(a, b):
    return lax.dot_general(a, b, (((1,), (0,)), ((), ())), preferred_element_type=F32)


def dot_nt(a, b):
    return lax.dot_general(a, b, (((1,), (1,)), ((), ())), preferred_element_type=F32)


def iota(dims, axis):
    return lax.broadcasted_iota(I32, dims, axis)


def swap_matrix(outer, inner, flip=False):
    n = outer * inner
    row, col = iota((n, n), 0), iota((n, n), 1)
    place = row & (outer - 1)
    source = (outer - 1 - place if flip else place) * inner + (row >> (outer.bit_length() - 1))
    return (col == source).astype(F32).astype(BF16)


def pack_rows(plan, load, out_ref, stage, sems, flip=False):
    swap = swap_matrix(plan.steps, TILE, flip)
    copies = []

    def send(first, count):
        rows = slice(first, first + count)
        copy = pltpu.make_async_copy(stage.at[:, rows, :], out_ref.at[:, rows, :], sems.at[len(copies)])
        copy.start()
        copies.append(copy)

    def put(row, moved):
        for peer in range(plan.peers):
            stage[peer, row : row + plan.steps, :] = moved[peer * plan.steps : (peer + 1) * plan.steps]

    tails = []
    for k in range(plan.mom_dev):
        for h in range(plan.pairs // TILE):
            rows = load(k, h)
            halves = jnp.concatenate([rows[:, :LANES], rows[:, SQUARE : SQUARE + LANES]], axis=1)
            tails += [rows[:, LANES:SQUARE], rows[:, SQUARE + LANES :]]
            moved = dot(swap, halves).astype(BF16)
            row = plan.main_row(k, h)
            put(row, moved[:, :LANES])
            put(row + plan.steps, moved[:, LANES:])
            send(row, 2 * plan.steps)
    for n in range(0, len(tails), 2 * SLOTS):
        joined = jnp.concatenate(tails[n : n + 2 * SLOTS], axis=1)
        put(plan.main_rows + n // (2 * SLOTS) * plan.steps, dot(swap, joined).astype(BF16))
    send(plan.main_rows, plan.tail_rows)
    for copy in copies:
        copy.wait()


def pack_own_kernel(plan, green_ref, out_ref, stage, out_sems, tiles, sems):
    copies = {}
    for k in range(plan.mom_dev):
        for h in range(plan.pairs // TILE):
            copies[k, h] = pltpu.make_async_copy(
                green_ref.at[k, :, TILE * h : TILE * (h + 1), :], tiles.at[k, h], sems.at[k, h]
            )
            copies[k, h].start()

    def load(k, h):
        copies[k, h].wait()
        return tiles[k, h].reshape(plan.steps * TILE, COMP)

    pack_rows(plan, load, out_ref, stage, out_sems)


def pack_partner_kernel(plan, take_ref, green_ref, out_ref, stage, sems, taken):
    chunk = take_ref.shape[0] // plan.pairs
    take = take_ref[...]
    for k in range(plan.mom_dev):
        for e in range(0, plan.steps, chunk):
            rows = green_ref[k, e : e + chunk].reshape(chunk * plan.pairs, COMP)
            taken[k, e : e + chunk] = dot(take, rows).astype(BF16).reshape(chunk, plan.pairs, COMP)

    def load(k, h):
        return taken[k, :, TILE * h : TILE * (h + 1), :].reshape(plan.steps * TILE, COMP)

    pack_rows(plan, load, out_ref, stage, sems, flip=True)


def each_pair(plan, body):
    if plan.own <= 2:
        for u in range(plan.own):
            body(u)
    else:
        lax.fori_loop(0, plan.own, lambda u, _: body(u), None)


def rows_at(row, count):
    return pl.ds(row if isinstance(row, int) else pl.multiple_of(row, count), count)


def my_table(plan, tables_ref, u):
    group = lax.axis_index("energy") // plan.group
    return tables_ref[(u // plan.sub ^ group) * plan.sub + u % plan.sub]


def sandwich_kernel(plan, tables_ref, sand_ref):
    place, want = iota((2 * LANES, 16), 0), iota((2 * LANES, 16), 1)

    def body(u):
        couple = my_table(plan, tables_ref, u)[: BRANCH * 16, :16]
        for h in range(2):
            comp = jnp.where(place < LANES, place, place - (u % SLOTS * TAIL + h * REST))
            valid = (place < LANES) | ((comp >= LANES) & (comp < SQUARE))
            quotient = (comp * 171) >> 11
            first = (valid & (quotient == want)).astype(F32).astype(BF16)
            second = (valid & (comp - ORB * quotient == want)).astype(F32).astype(BF16)
            left = dot_nt(couple, first).astype(BF16)
            right = dot_nt(couple, second).astype(BF16)
            for i in range(BRANCH):
                rows = slice(16 * i, 16 * i + 16)
                product = dot(first, left[rows]) * dot(second, right[rows])
                sand_ref[u, h, :, 2 * LANES * i : 2 * LANES * (i + 1)] = product.astype(BF16)

    each_pair(plan, body)


def toeplitz_kernel(plan, tables_ref, toep_ref):
    mirror = iota((FREQ, 2 * FREQ), 0) + iota((FREQ, 2 * FREQ), 1) == FREQ
    mirror = mirror.astype(F32).astype(BF16)

    def body(u):
        lags = dot(my_table(plan, tables_ref, u)[BRANCH * 16 :, :], mirror)
        for q in range(plan.momenta):
            for i in range(BRANCH):
                n = q * BRANCH + i
                band = jnp.broadcast_to(lags[n : n + 1], (FREQ, 2 * FREQ))
                band = pltpu.roll(band, 0, 1, stride=1, stride_axis=0)
                toep_ref[u, q, i * FREQ : (i + 1) * FREQ, :] = band.astype(BF16)

    each_pair(plan, body)


def gather_rows(plan, ref, u, y, first, flip=False):
    m, k = divmod(y, plan.mom_dev)
    row, tail = plan.main_row(k, u), plan.tail_row(k, u)
    order = range(plan.half)
    lefts, rights, tails = [], [], []
    for j in reversed(order) if flip else order:
        peer = (first + j) * plan.n_mom + m
        lefts.append(ref[peer, rows_at(row, plan.steps), :])
        rights.append(ref[peer, rows_at(row + plan.steps, plan.steps), :])
        tails.append(ref[peer, rows_at(tail, plan.steps), :])
    tails = jnp.concatenate(tails, axis=0)
    if plan.shift(k):
        tails = pltpu.roll(tails.astype(F32), LANES - plan.shift(k), 1).astype(BF16)
    return jnp.concatenate([jnp.concatenate(lefts, axis=0), jnp.concatenate(rights, axis=0), tails], axis=1)


def half_and_tail(rows, h):
    return jnp.concatenate([rows[:, h * LANES : (h + 1) * LANES], rows[:, 2 * LANES :]], axis=1)


def self_block(plan, u, green, toep_ref, sand_ref, out_ref):
    summed = []
    for i in range(BRANCH):
        rows = slice(i * FREQ, (i + 1) * FREQ)
        band = jnp.concatenate(
            [
                jnp.concatenate([toep_ref[u, (k - y) % plan.momenta, rows, :] for y in range(plan.momenta)], axis=1)
                for k in range(plan.momenta)
            ],
            axis=0,
        )
        summed.append(dot(band, green).astype(BF16))
    left, right = [
        dot_nt(jnp.concatenate([half_and_tail(rows, h) for rows in summed], axis=1), sand_ref[u, h])
        for h in range(2)
    ]
    tails = left[:, LANES:] + right[:, LANES:]
    left, right = left[:, :LANES].astype(BF16), right[:, :LANES].astype(BF16)
    for y in range(plan.momenta):
        m, k = divmod(y, plan.mom_dev)
        row, tail = plan.main_row(k, u), plan.tail_row(k, u)
        rest = tails[y * FREQ : (y + 1) * FREQ]
        if plan.shift(k):
            rest = pltpu.roll(rest, plan.shift(k), 1)
        rest = rest.astype(BF16)
        for j in range(plan.half):
            peer = j * plan.n_mom + m
            here = slice(j * plan.steps, (j + 1) * plan.steps)
            there = slice(y * FREQ + j * plan.steps, y * FREQ + (j + 1) * plan.steps)
            out_ref[peer, rows_at(row, plan.steps), :] = left[there]
            out_ref[peer, rows_at(row + plan.steps, plan.steps), :] = right[there]
            out_ref[peer, rows_at(tail, plan.steps), :] += rest[here]


def clear_tails(plan, out_ref):
    for peer in range(plan.half * plan.n_mom):
        out_ref[peer, plan.main_rows :, :] = jnp.zeros((plan.tail_rows, LANES), BF16)


def self_late_kernel(plan, own, toep_ref, sand_ref, out_ref):
    clear_tails(plan, out_ref)

    def body(u):
        green = [gather_rows(plan, own, u, y, first) for y in range(plan.momenta) for first in (0, plan.half)]
        self_block(plan, u, jnp.concatenate(green, axis=0), toep_ref, sand_ref, out_ref)

    each_pair(plan, body)


def self_early_kernel(plan, own, far, toep_ref, sand_ref, late_ref, out_ref, stage, halo, sems):
    has = (lax.axis_index("energy") // plan.group > 0).astype(F32).astype(BF16)
    near = plan.half * plan.n_mom
    load = pltpu.make_async_copy(far, halo, sems.at[0])
    load.start()
    upper = pltpu.make_async_copy(late_ref, out_ref.at[near:], sems.at[1])
    upper.start()
    clear_tails(plan, stage)
    load.wait()

    def body(u):
        green = []
        for y in range(plan.momenta):
            green.append(gather_rows(plan, halo, u, y, 0) * has)
            green.append(gather_rows(plan, own, u, y, 0))
        self_block(plan, u, jnp.concatenate(green, axis=0), toep_ref, sand_ref, stage)

    each_pair(plan, body)
    lower = pltpu.make_async_copy(stage, out_ref.at[:near], sems.at[2])
    lower.start()
    lower.wait()
    upper.wait()


def lag_sums(plan, u, partner, green, sand_ref, store):
    partner, green = jnp.concatenate(partner, axis=0), jnp.concatenate(green, axis=0)
    left, right = [dot(half_and_tail(partner, h), sand_ref[u, h]) for h in range(2)]
    for i in range(BRANCH):
        here = slice(2 * LANES * i, 2 * LANES * i + LANES)
        rest = slice(2 * LANES * i + LANES, 2 * LANES * (i + 1))
        applied = jnp.concatenate([left[:, here], right[:, here], left[:, rest] + right[:, rest]], axis=1)
        lagged = dot_nt(applied.astype(BF16), green)
        for q in range(plan.momenta):
            acc = None
            for k in range(plan.momenta):
                y = (k + q) % plan.momenta
                part = lagged[k * FREQ : (k + 1) * FREQ, y * 2 * FREQ : (y + 1) * 2 * FREQ]
                acc = part if acc is None else acc + part
            acc = pltpu.roll(acc, FREQ + 1, 1, stride=1, stride_axis=0)
            store(q, i, jnp.sum(acc, axis=0, keepdims=True))


def phonon_early_kernel(plan, own, partner_ref, sand_ref, out_ref):
    def body(u):
        partner = [gather_rows(plan, partner_ref, u, k, 0, flip=True) for k in range(plan.momenta)]
        green = [gather_rows(plan, own, u, y, first) for y in range(plan.momenta) for first in (0, plan.half)]

        def store(q, i, lags):
            out_ref[u, q * BRANCH + i : q * BRANCH + i + 1, :] = lags

        lag_sums(plan, u, partner, green, sand_ref, store)

    each_pair(plan, body)


def phonon_late_kernel(plan, own, halo, partner_ref, sand_ref, early_ref, *refs, scale):
    outs, sums = refs[:-1], refs[-1]
    group = lax.axis_index("energy") // plan.group
    me = lax.axis_index("mom")
    has = (group < plan.n_groups - 1).astype(F32).astype(BF16)

    def body(u):
        partner = [gather_rows(plan, partner_ref, u, k, plan.half, flip=True) for k in range(plan.momenta)]
        green = []
        for y in range(plan.momenta):
            green.append(gather_rows(plan, own, u, y, plan.half))
            green.append(gather_rows(plan, halo, u, y, 0) * has)

        def store(q, i, lags):
            n = q * BRANCH + i
            side, row = divmod(n, plan.mom_dev * BRANCH)
            sums[u, side, row : row + 1, :] = (lags + early_ref[u, n : n + 1, :]) * scale

        lag_sums(plan, u, partner, green, sand_ref, store)

    each_pair(plan, body)
    for d in range(plan.n_groups):
        for t in range(plan.n_mom):
            for b in range(plan.sub):
                outs[d * plan.n_mom + t][b] = sums[(group ^ d) * plan.sub + b, me ^ t]


def collect_kernel(plan, *refs):
    parts, out_ref = refs[:-1], refs[-1]
    me = lax.axis_index("mom")
    for d in range(plan.n_mom):
        total = sum(ref[...] for ref in parts[d :: plan.n_mom])
        for b in range(plan.sub):
            pair = (me ^ d) * plan.sub + b
            for q in range(plan.mom_dev):
                rows = [total[b, q * BRANCH + i : q * BRANCH + i + 1, :FREQ] for i in range(BRANCH)]
                out_ref[q, pl.ds(pair, 1), :] = jnp.concatenate(rows, axis=1)


def unpack_kernel(plan, wire, out_ref, tiles, sems):
    swap = swap_matrix(TILE, plan.steps)

    def rows_of(row):
        return jnp.concatenate([wire[peer, row : row + plan.steps, :] for peer in range(plan.peers)], axis=0)

    tails = {}
    for first in range(0, plan.mom_dev * plan.own, SLOTS):
        moved = dot(swap, rows_of(plan.main_rows + first // SLOTS * plan.steps))
        for t in range(SLOTS):
            tails[first + t] = moved[:, t * TAIL : (t + 1) * TAIL]
    copies = []
    for k in range(plan.mom_dev):
        for h in range(plan.pairs // TILE):
            row = plan.main_row(k, h)
            moved = dot(swap, jnp.concatenate([rows_of(row), rows_of(row + plan.steps)], axis=1))
            tail = tails[k * plan.own + h]
            moved = jnp.concatenate([moved[:, :LANES], tail[:, :REST], moved[:, LANES:], tail[:, REST:]], axis=1)
            tiles[k, h] = moved.astype(BF16).reshape(plan.steps, TILE, COMP)
            copy = pltpu.make_async_copy(
                tiles.at[k, h], out_ref.at[k, :, TILE * h : TILE * (h + 1), :], sems.at[k, h]
            )
            copy.start()
            copies.append(copy)
    for copy in copies:
        copy.wait()


ANY = pl.BlockSpec(memory_space=pl.ANY)
HBM = pl.BlockSpec(memory_space=pltpu.HBM)
VMEM = pl.BlockSpec(memory_space=pltpu.VMEM)


def call(plan, kernel, out_shape, *args, in_specs=None, out_specs=None, scratch=(), flops=1, grant=None):
    outs = jax.tree.map(lambda _: VMEM, out_shape)
    return pl.pallas_call(
        functools.partial(kernel, plan),
        out_shape=out_shape,
        in_specs=in_specs or [VMEM] * len(args),
        out_specs=out_specs or outs,
        scratch_shapes=list(scratch),
        compiler_params=pltpu.CompilerParams(vmem_limit_bytes=grant or SMALL_GRANT * max(1, plan.own // 4)),
        cost_estimate=pl.CostEstimate(flops=flops, bytes_accessed=1, transcendentals=0),
    )(*args)


def shape(dims, dtype):
    return jax.ShapeDtypeStruct(dims, dtype)


def in_hbm(struct):
    return pltpu.HBM(struct.shape, struct.dtype)


def shards(lesser_green, partner, phonon_green, coupling):
    n_energy, n_mom = lax.axis_size("energy"), lax.axis_size("mom")
    plan = Plan(lesser_green, phonon_green, n_energy, n_mom)
    axes = ("energy", "mom")
    me = lax.axis_index("mom")
    s = lax.axis_index("energy") // plan.group
    wire = shape((plan.peers, plan.rows, LANES), BF16)
    half_peers = plan.half * n_mom
    groups = [[g * plan.peers + i for i in range(plan.peers)] for g in range(plan.n_groups)]
    tiles = (plan.mom_dev, plan.pairs // TILE)

    def exchange(blocks):
        return lax.all_to_all(blocks, axes, split_axis=0, concat_axis=0, axis_index_groups=groups, tiled=True)

    def swap_groups(values, other):
        route = []
        for e in range(n_energy):
            g, j = divmod(e, plan.group)
            to = other(g) if 0 <= other(g) < plan.n_groups else g
            route.append((e, to * plan.group + j))
        return lax.ppermute(values, "energy", route)

    staging = [pltpu.VMEM(wire.shape, BF16), pltpu.SemaphoreType.DMA((tiles[0] * tiles[1] + 1,))]
    tile_scratch = [pltpu.VMEM(tiles + (plan.steps, TILE, COMP), BF16), pltpu.SemaphoreType.DMA(tiles)]
    half_wire = shape((half_peers, plan.rows, LANES), BF16)
    own = exchange(
        call(
            plan,
            pack_own_kernel,
            in_hbm(wire),
            lesser_green,
            in_specs=[HBM],
            out_specs=HBM,
            scratch=staging + tile_scratch,
            grant=LARGE_GRANT,
        )
    )

    lag_count = plan.momenta * BRANCH
    lag_rows = -(-lag_count // 16) * 16
    couple = coupling.reshape(plan.pairs_dev, BRANCH, ORB, ORB)
    couple = jnp.pad(couple, ((0, 0), (0, 0), (0, 16 - ORB), (0, FREQ - ORB)))
    phonon = phonon_green.reshape(plan.momenta, plan.pairs_dev, BRANCH, FREQ)
    phonon = jnp.moveaxis(phonon, 1, 0).reshape(plan.pairs_dev, lag_count, FREQ)
    phonon = jnp.pad(phonon, ((0, 0), (0, lag_rows - lag_count), (0, 0)))
    table = jnp.concatenate([couple.reshape(plan.pairs_dev, BRANCH * 16, FREQ), phonon], axis=1)
    table = lax.dynamic_slice_in_dim(table, me * plan.sub, plan.sub, axis=0)
    tables = [table]
    for d in range(1, plan.n_groups):
        tables.append(swap_groups(table, functools.partial(lambda d, g: g ^ d, d)))
    tables = jnp.concatenate(tables, axis=0)
    sand = call(
        plan, sandwich_kernel, shape((plan.own, 2, 2 * LANES, BRANCH * 2 * LANES), BF16), tables
    )
    chunk = max(1, 256 // plan.pairs)
    source = (jnp.arange(chunk)[:, None] * plan.pairs + partner[None, :]).reshape(-1)
    take = (source[:, None] == jnp.arange(chunk * plan.pairs)[None, :]).astype(BF16)
    partner_wire = call(
        plan,
        pack_partner_kernel,
        in_hbm(wire),
        take,
        lesser_green,
        out_specs=HBM,
        scratch=staging + [pltpu.VMEM(lesser_green.shape, BF16)],
    )
    own, tables, sand, partner_wire = lax.optimization_barrier((own, tables, sand, partner_wire))

    odd = s % 2

    def edge(side):
        return lax.dynamic_slice_in_dim(own, side * half_peers, half_peers, axis=0)

    before = after = inner = swap_groups(edge(1 - odd), lambda g: g ^ 1)
    if plan.n_groups > 2:
        outer = swap_groups(edge(odd), lambda g: ((g - 1) ^ 1) + 1)
        before = jnp.where(odd == 1, inner, outer)
        after = jnp.where(odd == 1, outer, inner)

    toep = call(
        plan,
        toeplitz_kernel,
        shape((plan.own, plan.momenta, BRANCH * FREQ, 2 * FREQ), BF16),
        tables,
        flops=LONG,
    )
    toep, partner_wire = lax.optimization_barrier((toep, partner_wire))
    partner_blocks = exchange(partner_wire)

    late = call(plan, self_late_kernel, half_wire, own, toep, sand)
    sigma = call(
        plan,
        self_early_kernel,
        in_hbm(wire),
        own,
        before,
        toep,
        sand,
        late,
        in_specs=[VMEM, ANY, VMEM, VMEM, VMEM],
        out_specs=HBM,
        scratch=[
            pltpu.VMEM(half_wire.shape, BF16),
            pltpu.VMEM(half_wire.shape, BF16),
            pltpu.SemaphoreType.DMA((3,)),
        ],
        flops=LONG,
    )
    arrived = exchange(sigma)

    scale = (plan.momenta * n_energy * plan.steps * COMP) ** -0.5
    early = call(
        plan,
        phonon_early_kernel,
        shape((plan.own, lag_count, LANES), F32),
        own,
        partner_blocks,
        sand,
    )
    side_rows = plan.mom_dev * BRANCH
    parts = list(call(
        plan,
        functools.partial(phonon_late_kernel, scale=scale),
        [shape((plan.sub, side_rows, LANES), F32)] * (plan.n_groups * n_mom),
        own,
        after,
        partner_blocks,
        sand,
        early,
        scratch=[pltpu.VMEM((plan.own, n_mom, side_rows, LANES), F32)],
    ))
    for d in range(plan.n_groups):
        for t in range(n_mom):
            if d or t:
                route = []
                for e in range(n_energy):
                    g, j = divmod(e, plan.group)
                    for m in range(n_mom):
                        route.append((e * n_mom + m, ((g ^ d) * plan.group + j) * n_mom + (m ^ t)))
                parts[d * n_mom + t] = lax.ppermute(parts[d * n_mom + t], axes, route)
    phonon_self = call(
        plan, collect_kernel, shape((plan.mom_dev, plan.pairs_dev, BRANCH * FREQ), F32), *parts
    )

    self_energy = call(
        plan,
        unpack_kernel,
        shape(lesser_green.shape, BF16),
        arrived,
        out_specs=ANY,
        scratch=tile_scratch,
    )
    return self_energy, phonon_self


def solution(mesh):
    in_specs = (P("mom", "energy", None, None), P(), P(None, "energy", None), P("energy", None))
    out_specs = (P("mom", "energy", None, None), P("mom", "energy", None))
    return jax.shard_map(shards, mesh=mesh, in_specs=in_specs, out_specs=out_specs, check_vma=False)
```

```python
import functools

import jax
import jax.numpy as jnp
from jax import lax
from jax.experimental import pallas as pl
from jax.experimental.pallas import tpu as pltpu
from jax.sharding import PartitionSpec as P

ORB = 12
BRANCH = 3
FREQ = 64
COMP = 288
SQUARE = ORB * ORB
LANES = 128
REST = SQUARE - LANES
TAIL = 2 * REST
SLOTS = LANES // TAIL
TILE = 16
SMALL_GRANT = 16 * 1024 * 1024
LARGE_GRANT = 60 * 1024 * 1024
LONG = 100_000_000_000

BF16 = jnp.bfloat16
F32 = jnp.float32
I32 = jnp.int32


class Plan:
    def __init__(self, green, phonon, n_energy, n_mom):
        self.n_energy, self.n_mom = n_energy, n_mom
        self.mom_dev, self.steps, self.pairs, _ = green.shape
        self.momenta = self.mom_dev * n_mom
        self.pairs_dev = phonon.shape[1]
        self.half = FREQ // self.steps
        self.group = 2 * self.half
        self.n_groups = n_energy // self.group
        self.peers = self.group * n_mom
        self.sub = self.pairs_dev // n_mom
        self.own = self.n_groups * self.sub
        self.main_rows = self.mom_dev * self.own * 2 * self.steps
        self.tail_rows = self.mom_dev * self.own // SLOTS * self.steps
        self.rows = self.main_rows + self.tail_rows
        assert self.half * self.steps == FREQ and n_energy % self.group == 0
        assert self.n_groups & (self.n_groups - 1) == 0
        assert self.pairs_dev == n_mom and self.group * self.pairs_dev == TILE
        assert self.mom_dev * self.own % SLOTS == 0 and self.n_groups % 2 == 0

    def main_row(self, k, u):
        return (k * self.own + u) * 2 * self.steps

    def tail_row(self, k, u):
        return self.main_rows + (k * self.own + u) // SLOTS * self.steps

    def shift(self, k):
        return k * self.own % SLOTS * TAIL


def dot(a, b):
    return lax.dot_general(a, b, (((1,), (0,)), ((), ())), preferred_element_type=F32)


def dot_nt(a, b):
    return lax.dot_general(a, b, (((1,), (1,)), ((), ())), preferred_element_type=F32)


def iota(dims, axis):
    return lax.broadcasted_iota(I32, dims, axis)


def swap_matrix(outer, inner, flip=False):
    n = outer * inner
    row, col = iota((n, n), 0), iota((n, n), 1)
    place = row & (outer - 1)
    source = (outer - 1 - place if flip else place) * inner + (row >> (outer.bit_length() - 1))
    return (col == source).astype(F32).astype(BF16)


def pack_rows(plan, load, out_ref, stage, sems, flip=False):
    swap = swap_matrix(plan.steps, TILE, flip)
    copies = []

    def send(first, count):
        rows = slice(first, first + count)
        copy = pltpu.make_async_copy(stage.at[:, rows, :], out_ref.at[:, rows, :], sems.at[len(copies)])
        copy.start()
        copies.append(copy)

    def put(row, moved):
        for peer in range(plan.peers):
            stage[peer, row : row + plan.steps, :] = moved[peer * plan.steps : (peer + 1) * plan.steps]

    tails = []
    for k in range(plan.mom_dev):
        for h in range(plan.pairs // TILE):
            rows = load(k, h)
            halves = jnp.concatenate([rows[:, :LANES], rows[:, SQUARE : SQUARE + LANES]], axis=1)
            tails += [rows[:, LANES:SQUARE], rows[:, SQUARE + LANES :]]
            moved = dot(swap, halves).astype(BF16)
            row = plan.main_row(k, h)
            put(row, moved[:, :LANES])
            put(row + plan.steps, moved[:, LANES:])
            send(row, 2 * plan.steps)
    for n in range(0, len(tails), 2 * SLOTS):
        joined = jnp.concatenate(tails[n : n + 2 * SLOTS], axis=1)
        put(plan.main_rows + n // (2 * SLOTS) * plan.steps, dot(swap, joined).astype(BF16))
    send(plan.main_rows, plan.tail_rows)
    for copy in copies:
        copy.wait()


def pack_own_kernel(plan, green_ref, out_ref, stage, out_sems, tiles, sems):
    copies = {}
    for k in range(plan.mom_dev):
        for h in range(plan.pairs // TILE):
            copies[k, h] = pltpu.make_async_copy(
                green_ref.at[k, :, TILE * h : TILE * (h + 1), :], tiles.at[k, h], sems.at[k, h]
            )
            copies[k, h].start()

    def load(k, h):
        copies[k, h].wait()
        return tiles[k, h].reshape(plan.steps * TILE, COMP)

    pack_rows(plan, load, out_ref, stage, out_sems)


def pack_partner_kernel(plan, take_ref, green_ref, out_ref, stage, sems, taken):
    chunk = take_ref.shape[0] // plan.pairs
    take = take_ref[...]
    for k in range(plan.mom_dev):
        for e in range(0, plan.steps, chunk):
            rows = green_ref[k, e : e + chunk].reshape(chunk * plan.pairs, COMP)
            taken[k, e : e + chunk] = dot(take, rows).astype(BF16).reshape(chunk, plan.pairs, COMP)

    def load(k, h):
        return taken[k, :, TILE * h : TILE * (h + 1), :].reshape(plan.steps * TILE, COMP)

    pack_rows(plan, load, out_ref, stage, sems, flip=True)


def each_pair(plan, body):
    if plan.own <= 2:
        for u in range(plan.own):
            body(u)
    else:
        lax.fori_loop(0, plan.own, lambda u, _: body(u), None)


def rows_at(row, count):
    return pl.ds(row if isinstance(row, int) else pl.multiple_of(row, count), count)


def my_table(plan, tables_ref, u):
    group = lax.axis_index("energy") // plan.group
    return tables_ref[(u // plan.sub ^ group) * plan.sub + u % plan.sub]


def sandwich_kernel(plan, tables_ref, sand_ref):
    place, want = iota((2 * LANES, 16), 0), iota((2 * LANES, 16), 1)

    def body(u):
        couple = my_table(plan, tables_ref, u)[: BRANCH * 16, :16]
        for h in range(2):
            comp = jnp.where(place < LANES, place, place - (u % SLOTS * TAIL + h * REST))
            valid = (place < LANES) | ((comp >= LANES) & (comp < SQUARE))
            quotient = (comp * 171) >> 11
            first = (valid & (quotient == want)).astype(F32).astype(BF16)
            second = (valid & (comp - ORB * quotient == want)).astype(F32).astype(BF16)
            left = dot_nt(couple, first).astype(BF16)
            right = dot_nt(couple, second).astype(BF16)
            for i in range(BRANCH):
                rows = slice(16 * i, 16 * i + 16)
                product = dot(first, left[rows]) * dot(second, right[rows])
                sand_ref[u, h, :, 2 * LANES * i : 2 * LANES * (i + 1)] = product.astype(BF16)

    each_pair(plan, body)


def toeplitz_kernel(plan, tables_ref, toep_ref):
    mirror = iota((FREQ, 2 * FREQ), 0) + iota((FREQ, 2 * FREQ), 1) == FREQ
    mirror = mirror.astype(F32).astype(BF16)

    def body(u):
        lags = dot(my_table(plan, tables_ref, u)[BRANCH * 16 :, :], mirror)
        for q in range(plan.momenta):
            for i in range(BRANCH):
                n = q * BRANCH + i
                band = jnp.broadcast_to(lags[n : n + 1], (FREQ, 2 * FREQ))
                band = pltpu.roll(band, 0, 1, stride=1, stride_axis=0)
                toep_ref[u, q, i * FREQ : (i + 1) * FREQ, :] = band.astype(BF16)

    each_pair(plan, body)


def edge_kernel(plan, own_ref, *edges):
    odd = lax.axis_index("energy") // plan.group % 2
    near = plan.half * plan.n_mom
    for edge, side in zip(edges, (1 - odd, odd)):
        for i in range(near):
            edge[i] = own_ref[side * near + i]


def gather_rows(plan, ref, u, y, first, flip=False):
    m, k = divmod(y, plan.mom_dev)
    row, tail = plan.main_row(k, u), plan.tail_row(k, u)
    order = range(plan.half)
    lefts, rights, tails = [], [], []
    for j in reversed(order) if flip else order:
        peer = (first + j) * plan.n_mom + m
        lefts.append(ref[peer, rows_at(row, plan.steps), :])
        rights.append(ref[peer, rows_at(row + plan.steps, plan.steps), :])
        tails.append(ref[peer, rows_at(tail, plan.steps), :])
    tails = jnp.concatenate(tails, axis=0)
    if plan.shift(k):
        tails = pltpu.roll(tails.astype(F32), LANES - plan.shift(k), 1).astype(BF16)
    return jnp.concatenate([jnp.concatenate(lefts, axis=0), jnp.concatenate(rights, axis=0), tails], axis=1)


def half_and_tail(rows, h):
    return jnp.concatenate([rows[:, h * LANES : (h + 1) * LANES], rows[:, 2 * LANES :]], axis=1)


def self_block(plan, u, green, toep_ref, sand_ref, out_ref):
    summed = []
    for i in range(BRANCH):
        rows = slice(i * FREQ, (i + 1) * FREQ)
        band = jnp.concatenate(
            [
                jnp.concatenate([toep_ref[u, (k - y) % plan.momenta, rows, :] for y in range(plan.momenta)], axis=1)
                for k in range(plan.momenta)
            ],
            axis=0,
        )
        summed.append(dot(band, green).astype(BF16))
    left, right = [
        dot_nt(jnp.concatenate([half_and_tail(rows, h) for rows in summed], axis=1), sand_ref[u, h])
        for h in range(2)
    ]
    tails = left[:, LANES:] + right[:, LANES:]
    left, right = left[:, :LANES].astype(BF16), right[:, :LANES].astype(BF16)
    for y in range(plan.momenta):
        m, k = divmod(y, plan.mom_dev)
        row, tail = plan.main_row(k, u), plan.tail_row(k, u)
        rest = tails[y * FREQ : (y + 1) * FREQ]
        if plan.shift(k):
            rest = pltpu.roll(rest, plan.shift(k), 1)
        rest = rest.astype(BF16)
        for j in range(plan.half):
            peer = j * plan.n_mom + m
            here = slice(j * plan.steps, (j + 1) * plan.steps)
            there = slice(y * FREQ + j * plan.steps, y * FREQ + (j + 1) * plan.steps)
            out_ref[peer, rows_at(row, plan.steps), :] = left[there]
            out_ref[peer, rows_at(row + plan.steps, plan.steps), :] = right[there]
            out_ref[peer, rows_at(tail, plan.steps), :] += rest[here]


def clear_tails(plan, out_ref):
    for peer in range(plan.half * plan.n_mom):
        out_ref[peer, plan.main_rows :, :] = jnp.zeros((plan.tail_rows, LANES), BF16)


def self_late_kernel(plan, own, toep_ref, sand_ref, out_ref):
    clear_tails(plan, out_ref)

    def body(u):
        green = [gather_rows(plan, own, u, y, first) for y in range(plan.momenta) for first in (0, plan.half)]
        self_block(plan, u, jnp.concatenate(green, axis=0), toep_ref, sand_ref, out_ref)

    each_pair(plan, body)


def self_early_kernel(plan, own, far, toep_ref, sand_ref, late_ref, out_ref, stage, halo, sems):
    has = (lax.axis_index("energy") // plan.group > 0).astype(F32).astype(BF16)
    near = plan.half * plan.n_mom
    load = pltpu.make_async_copy(far, halo, sems.at[0])
    load.start()
    upper = pltpu.make_async_copy(late_ref, out_ref.at[near:], sems.at[1])
    upper.start()
    clear_tails(plan, stage)
    load.wait()

    def body(u):
        green = []
        for y in range(plan.momenta):
            green.append(gather_rows(plan, halo, u, y, 0) * has)
            green.append(gather_rows(plan, own, u, y, 0))
        self_block(plan, u, jnp.concatenate(green, axis=0), toep_ref, sand_ref, stage)

    each_pair(plan, body)
    lower = pltpu.make_async_copy(stage, out_ref.at[:near], sems.at[2])
    lower.start()
    lower.wait()
    upper.wait()


def lag_sums(plan, u, partner, green, sand_ref, store):
    partner, green = jnp.concatenate(partner, axis=0), jnp.concatenate(green, axis=0)
    left, right = [dot(half_and_tail(partner, h), sand_ref[u, h]) for h in range(2)]
    for i in range(BRANCH):
        here = slice(2 * LANES * i, 2 * LANES * i + LANES)
        rest = slice(2 * LANES * i + LANES, 2 * LANES * (i + 1))
        applied = jnp.concatenate([left[:, here], right[:, here], left[:, rest] + right[:, rest]], axis=1)
        lagged = dot_nt(applied.astype(BF16), green)
        for q in range(plan.momenta):
            acc = None
            for k in range(plan.momenta):
                y = (k + q) % plan.momenta
                part = lagged[k * FREQ : (k + 1) * FREQ, y * 2 * FREQ : (y + 1) * 2 * FREQ]
                acc = part if acc is None else acc + part
            acc = pltpu.roll(acc, FREQ + 1, 1, stride=1, stride_axis=0)
            store(q, i, jnp.sum(acc, axis=0, keepdims=True))


def phonon_early_kernel(plan, own, partner_ref, sand_ref, out_ref):
    def body(u):
        partner = [gather_rows(plan, partner_ref, u, k, 0, flip=True) for k in range(plan.momenta)]
        green = [gather_rows(plan, own, u, y, first) for y in range(plan.momenta) for first in (0, plan.half)]

        def store(q, i, lags):
            out_ref[u, q * BRANCH + i : q * BRANCH + i + 1, :] = lags

        lag_sums(plan, u, partner, green, sand_ref, store)

    each_pair(plan, body)


def phonon_late_kernel(plan, own, halo, partner_ref, sand_ref, early_ref, *refs, scale):
    outs, sums = refs[:-1], refs[-1]
    group = lax.axis_index("energy") // plan.group
    me = lax.axis_index("mom")
    has = (group < plan.n_groups - 1).astype(F32).astype(BF16)

    def body(u):
        partner = [gather_rows(plan, partner_ref, u, k, plan.half, flip=True) for k in range(plan.momenta)]
        green = []
        for y in range(plan.momenta):
            green.append(gather_rows(plan, own, u, y, plan.half))
            green.append(gather_rows(plan, halo, u, y, 0) * has)

        def store(q, i, lags):
            n = q * BRANCH + i
            side, row = divmod(n, plan.mom_dev * BRANCH)
            sums[u, side, row : row + 1, :] = (lags + early_ref[u, n : n + 1, :]) * scale

        lag_sums(plan, u, partner, green, sand_ref, store)

    each_pair(plan, body)
    for d in range(plan.n_groups):
        for t in range(plan.n_mom):
            for b in range(plan.sub):
                outs[d * plan.n_mom + t][b] = sums[(group ^ d) * plan.sub + b, me ^ t]


def collect_kernel(plan, *refs):
    parts, out_ref = refs[:-1], refs[-1]
    me = lax.axis_index("mom")
    for d in range(plan.n_mom):
        total = sum(ref[...] for ref in parts[d :: plan.n_mom])
        for b in range(plan.sub):
            pair = (me ^ d) * plan.sub + b
            for q in range(plan.mom_dev):
                rows = [total[b, q * BRANCH + i : q * BRANCH + i + 1, :FREQ] for i in range(BRANCH)]
                out_ref[q, pl.ds(pair, 1), :] = jnp.concatenate(rows, axis=1)


def unpack_kernel(plan, wire, out_ref, tiles, sems):
    swap = swap_matrix(TILE, plan.steps)

    def rows_of(row):
        return jnp.concatenate([wire[peer, row : row + plan.steps, :] for peer in range(plan.peers)], axis=0)

    tails = {}
    for first in range(0, plan.mom_dev * plan.own, SLOTS):
        moved = dot(swap, rows_of(plan.main_rows + first // SLOTS * plan.steps))
        for t in range(SLOTS):
            tails[first + t] = moved[:, t * TAIL : (t + 1) * TAIL]
    copies = []
    for k in range(plan.mom_dev):
        for h in range(plan.pairs // TILE):
            row = plan.main_row(k, h)
            moved = dot(swap, jnp.concatenate([rows_of(row), rows_of(row + plan.steps)], axis=1))
            tail = tails[k * plan.own + h]
            moved = jnp.concatenate([moved[:, :LANES], tail[:, :REST], moved[:, LANES:], tail[:, REST:]], axis=1)
            tiles[k, h] = moved.astype(BF16).reshape(plan.steps, TILE, COMP)
            copy = pltpu.make_async_copy(
                tiles.at[k, h], out_ref.at[k, :, TILE * h : TILE * (h + 1), :], sems.at[k, h]
            )
            copy.start()
            copies.append(copy)
    for copy in copies:
        copy.wait()


ANY = pl.BlockSpec(memory_space=pl.ANY)
HBM = pl.BlockSpec(memory_space=pltpu.HBM)
VMEM = pl.BlockSpec(memory_space=pltpu.VMEM)


def call(plan, kernel, out_shape, *args, in_specs=None, out_specs=None, scratch=(), flops=1, grant=None):
    outs = jax.tree.map(lambda _: VMEM, out_shape)
    return pl.pallas_call(
        functools.partial(kernel, plan),
        out_shape=out_shape,
        in_specs=in_specs or [VMEM] * len(args),
        out_specs=out_specs or outs,
        scratch_shapes=list(scratch),
        compiler_params=pltpu.CompilerParams(vmem_limit_bytes=grant or SMALL_GRANT * max(1, plan.own // 4)),
        cost_estimate=pl.CostEstimate(flops=flops, bytes_accessed=1, transcendentals=0),
    )(*args)


def shape(dims, dtype):
    return jax.ShapeDtypeStruct(dims, dtype)


def in_hbm(struct):
    return pltpu.HBM(struct.shape, struct.dtype)


def in_vmem(struct):
    return pltpu.VMEM(struct.shape, struct.dtype)


def shards(lesser_green, partner, phonon_green, coupling):
    n_energy, n_mom = lax.axis_size("energy"), lax.axis_size("mom")
    plan = Plan(lesser_green, phonon_green, n_energy, n_mom)
    axes = ("energy", "mom")
    me = lax.axis_index("mom")
    s = lax.axis_index("energy") // plan.group
    wire = shape((plan.peers, plan.rows, LANES), BF16)
    half_peers = plan.half * n_mom
    groups = [[g * plan.peers + i for i in range(plan.peers)] for g in range(plan.n_groups)]
    tiles = (plan.mom_dev, plan.pairs // TILE)

    def exchange(blocks):
        return lax.all_to_all(blocks, axes, split_axis=0, concat_axis=0, axis_index_groups=groups, tiled=True)

    def swap_groups(values, other):
        route = []
        for e in range(n_energy):
            g, j = divmod(e, plan.group)
            to = other(g) if 0 <= other(g) < plan.n_groups else g
            route.append((e, to * plan.group + j))
        return lax.ppermute(values, "energy", route)

    staging = [pltpu.VMEM(wire.shape, BF16), pltpu.SemaphoreType.DMA((tiles[0] * tiles[1] + 1,))]
    tile_scratch = [pltpu.VMEM(tiles + (plan.steps, TILE, COMP), BF16), pltpu.SemaphoreType.DMA(tiles)]
    half_wire = shape((half_peers, plan.rows, LANES), BF16)
    own = exchange(
        call(
            plan,
            pack_own_kernel,
            in_hbm(wire),
            lesser_green,
            in_specs=[HBM],
            out_specs=HBM,
            scratch=staging + tile_scratch,
            grant=LARGE_GRANT,
        )
    )

    lag_count = plan.momenta * BRANCH
    lag_rows = -(-lag_count // 16) * 16
    couple = coupling.reshape(plan.pairs_dev, BRANCH, ORB, ORB)
    couple = jnp.pad(couple, ((0, 0), (0, 0), (0, 16 - ORB), (0, FREQ - ORB)))
    phonon = phonon_green.reshape(plan.momenta, plan.pairs_dev, BRANCH, FREQ)
    phonon = jnp.moveaxis(phonon, 1, 0).reshape(plan.pairs_dev, lag_count, FREQ)
    phonon = jnp.pad(phonon, ((0, 0), (0, lag_rows - lag_count), (0, 0)))
    table = jnp.concatenate([couple.reshape(plan.pairs_dev, BRANCH * 16, FREQ), phonon], axis=1)
    table = lax.dynamic_slice_in_dim(table, me * plan.sub, plan.sub, axis=0)
    tables = [table]
    for d in range(1, plan.n_groups):
        tables.append(swap_groups(table, functools.partial(lambda d, g: g ^ d, d)))
    tables = jnp.concatenate(tables, axis=0)
    sand = call(
        plan, sandwich_kernel, shape((plan.own, 2, 2 * LANES, BRANCH * 2 * LANES), BF16), tables
    )
    chunk = max(1, 256 // plan.pairs)
    source = (jnp.arange(chunk)[:, None] * plan.pairs + partner[None, :]).reshape(-1)
    take = (source[:, None] == jnp.arange(chunk * plan.pairs)[None, :]).astype(BF16)
    partner_wire = call(
        plan,
        pack_partner_kernel,
        in_hbm(wire),
        take,
        lesser_green,
        out_specs=HBM,
        scratch=staging + [pltpu.VMEM(lesser_green.shape, BF16)],
    )
    own, tables, sand, partner_wire = lax.optimization_barrier((own, tables, sand, partner_wire))

    edges = call(plan, edge_kernel, [in_vmem(half_wire)] * (1 if plan.n_groups == 2 else 2), own)
    before = after = inner = swap_groups(edges[0], lambda g: g ^ 1)
    if plan.n_groups > 2:
        outer = swap_groups(edges[1], lambda g: ((g - 1) ^ 1) + 1)
        odd = s % 2 == 1
        before = jnp.where(odd, inner, outer)
        after = jnp.where(odd, outer, inner)

    toep = call(
        plan,
        toeplitz_kernel,
        shape((plan.own, plan.momenta, BRANCH * FREQ, 2 * FREQ), BF16),
        tables,
        flops=LONG,
    )
    toep, partner_wire = lax.optimization_barrier((toep, partner_wire))
    partner_blocks = exchange(partner_wire)

    late = call(plan, self_late_kernel, half_wire, own, toep, sand)
    sigma = call(
        plan,
        self_early_kernel,
        in_hbm(wire),
        own,
        before,
        toep,
        sand,
        late,
        in_specs=[VMEM, ANY, VMEM, VMEM, VMEM],
        out_specs=HBM,
        scratch=[
            pltpu.VMEM(half_wire.shape, BF16),
            pltpu.VMEM(half_wire.shape, BF16),
            pltpu.SemaphoreType.DMA((3,)),
        ],
        flops=LONG,
    )
    arrived = exchange(sigma)

    scale = (plan.momenta * n_energy * plan.steps * COMP) ** -0.5
    early = call(
        plan,
        phonon_early_kernel,
        shape((plan.own, lag_count, LANES), F32),
        own,
        partner_blocks,
        sand,
    )
    side_rows = plan.mom_dev * BRANCH
    parts = list(call(
        plan,
        functools.partial(phonon_late_kernel, scale=scale),
        [shape((plan.sub, side_rows, LANES), F32)] * (plan.n_groups * n_mom),
        own,
        after,
        partner_blocks,
        sand,
        early,
        scratch=[pltpu.VMEM((plan.own, n_mom, side_rows, LANES), F32)],
    ))
    for d in range(plan.n_groups):
        for t in range(n_mom):
            if d or t:
                route = []
                for e in range(n_energy):
                    g, j = divmod(e, plan.group)
                    for m in range(n_mom):
                        route.append((e * n_mom + m, ((g ^ d) * plan.group + j) * n_mom + (m ^ t)))
                parts[d * n_mom + t] = lax.ppermute(parts[d * n_mom + t], axes, route)
    phonon_self = call(
        plan, collect_kernel, shape((plan.mom_dev, plan.pairs_dev, BRANCH * FREQ), F32), *parts
    )

    self_energy = call(
        plan,
        unpack_kernel,
        shape(lesser_green.shape, BF16),
        arrived,
        out_specs=ANY,
        scratch=tile_scratch,
    )
    return self_energy, phonon_self


def solution(mesh):
    in_specs = (P("mom", "energy", None, None), P(), P(None, "energy", None), P("energy", None))
    out_specs = (P("mom", "energy", None, None), P("mom", "energy", None))
    return jax.shard_map(shards, mesh=mesh, in_specs=in_specs, out_specs=out_specs, check_vma=False)
```

```python
import functools

import jax
import jax.numpy as jnp
from jax import lax
from jax.experimental import pallas as pl
from jax.experimental.pallas import tpu as pltpu
from jax.sharding import PartitionSpec as P

ORB = 12
BRANCH = 3
FREQ = 64
COMP = 288
SQUARE = ORB * ORB
LANES = 128
REST = SQUARE - LANES
TAIL = 2 * REST
SLOTS = LANES // TAIL
TILE = 16
SMALL_GRANT = 16 * 1024 * 1024
LARGE_GRANT = 60 * 1024 * 1024
LONG = 100_000_000_000

BF16 = jnp.bfloat16
F32 = jnp.float32
I32 = jnp.int32


class Plan:
    def __init__(self, green, phonon, n_energy, n_mom):
        self.n_energy, self.n_mom = n_energy, n_mom
        self.mom_dev, self.steps, self.pairs, _ = green.shape
        self.momenta = self.mom_dev * n_mom
        self.pairs_dev = phonon.shape[1]
        self.half = FREQ // self.steps
        self.group = 2 * self.half
        self.n_groups = n_energy // self.group
        self.peers = self.group * n_mom
        self.sub = self.pairs_dev // n_mom
        self.own = self.n_groups * self.sub
        self.main_rows = self.mom_dev * self.own * 2 * self.steps
        self.tail_rows = self.mom_dev * self.own // SLOTS * self.steps
        self.rows = self.main_rows + self.tail_rows
        assert self.half * self.steps == FREQ and n_energy % self.group == 0
        assert self.n_groups & (self.n_groups - 1) == 0
        assert self.pairs_dev == n_mom and self.group * self.pairs_dev == TILE
        assert self.mom_dev * self.own % SLOTS == 0 and self.n_groups % 2 == 0

    def main_row(self, k, u):
        return (k * self.own + u) * 2 * self.steps

    def tail_row(self, k, u):
        return self.main_rows + (k * self.own + u) // SLOTS * self.steps

    def shift(self, k):
        return k * self.own % SLOTS * TAIL


def dot(a, b):
    return lax.dot_general(a, b, (((1,), (0,)), ((), ())), preferred_element_type=F32)


def dot_nt(a, b):
    return lax.dot_general(a, b, (((1,), (1,)), ((), ())), preferred_element_type=F32)


def iota(dims, axis):
    return lax.broadcasted_iota(I32, dims, axis)


def swap_matrix(outer, inner, flip=False):
    n = outer * inner
    row, col = iota((n, n), 0), iota((n, n), 1)
    place = row & (outer - 1)
    source = (outer - 1 - place if flip else place) * inner + (row >> (outer.bit_length() - 1))
    return (col == source).astype(F32).astype(BF16)


def pack_rows(plan, load, out_ref, stage, sems, flip=False):
    swap = swap_matrix(plan.steps, TILE, flip)
    copies = []

    def send(first, count):
        rows = slice(first, first + count)
        copy = pltpu.make_async_copy(stage.at[:, rows, :], out_ref.at[:, rows, :], sems.at[len(copies)])
        copy.start()
        copies.append(copy)

    def put(row, moved):
        for peer in range(plan.peers):
            stage[peer, row : row + plan.steps, :] = moved[peer * plan.steps : (peer + 1) * plan.steps]

    tails = []
    for k in range(plan.mom_dev):
        for h in range(plan.pairs // TILE):
            rows = load(k, h)
            halves = jnp.concatenate([rows[:, :LANES], rows[:, SQUARE : SQUARE + LANES]], axis=1)
            tails += [rows[:, LANES:SQUARE], rows[:, SQUARE + LANES :]]
            moved = dot(swap, halves).astype(BF16)
            row = plan.main_row(k, h)
            put(row, moved[:, :LANES])
            put(row + plan.steps, moved[:, LANES:])
            send(row, 2 * plan.steps)
    for n in range(0, len(tails), 2 * SLOTS):
        joined = jnp.concatenate(tails[n : n + 2 * SLOTS], axis=1)
        put(plan.main_rows + n // (2 * SLOTS) * plan.steps, dot(swap, joined).astype(BF16))
    send(plan.main_rows, plan.tail_rows)
    for copy in copies:
        copy.wait()


def pack_own_kernel(plan, green_ref, out_ref, stage, out_sems, tiles, sems):
    copies = {}
    for k in range(plan.mom_dev):
        for h in range(plan.pairs // TILE):
            copies[k, h] = pltpu.make_async_copy(
                green_ref.at[k, :, TILE * h : TILE * (h + 1), :], tiles.at[k, h], sems.at[k, h]
            )
            copies[k, h].start()

    def load(k, h):
        copies[k, h].wait()
        return tiles[k, h].reshape(plan.steps * TILE, COMP)

    pack_rows(plan, load, out_ref, stage, out_sems)


def pack_partner_kernel(plan, take_ref, green_ref, out_ref, stage, sems, taken):
    chunk = take_ref.shape[0] // plan.pairs
    take = take_ref[...]
    for k in range(plan.mom_dev):
        for e in range(0, plan.steps, chunk):
            rows = green_ref[k, e : e + chunk].reshape(chunk * plan.pairs, COMP)
            taken[k, e : e + chunk] = dot(take, rows).astype(BF16).reshape(chunk, plan.pairs, COMP)

    def load(k, h):
        return taken[k, :, TILE * h : TILE * (h + 1), :].reshape(plan.steps * TILE, COMP)

    pack_rows(plan, load, out_ref, stage, sems, flip=True)


def each_pair(plan, body):
    if plan.own <= 2:
        for u in range(plan.own):
            body(u)
    else:
        lax.fori_loop(0, plan.own, lambda u, _: body(u), None)


def rows_at(row, count):
    return pl.ds(row if isinstance(row, int) else pl.multiple_of(row, count), count)


def my_table(plan, tables_ref, u):
    group = lax.axis_index("energy") // plan.group
    return tables_ref[(u // plan.sub ^ group) * plan.sub + u % plan.sub]


def sandwich_kernel(plan, tables_ref, sand_ref):
    place, want = iota((2 * LANES, 16), 0), iota((2 * LANES, 16), 1)

    def body(u):
        couple = my_table(plan, tables_ref, u)[: BRANCH * 16, :16]
        for h in range(2):
            comp = jnp.where(place < LANES, place, place - (u % SLOTS * TAIL + h * REST))
            valid = (place < LANES) | ((comp >= LANES) & (comp < SQUARE))
            quotient = (comp * 171) >> 11
            first = (valid & (quotient == want)).astype(F32).astype(BF16)
            second = (valid & (comp - ORB * quotient == want)).astype(F32).astype(BF16)
            left = dot_nt(couple, first).astype(BF16)
            right = dot_nt(couple, second).astype(BF16)
            for i in range(BRANCH):
                rows = slice(16 * i, 16 * i + 16)
                product = dot(first, left[rows]) * dot(second, right[rows])
                sand_ref[u, h, :, 2 * LANES * i : 2 * LANES * (i + 1)] = product.astype(BF16)

    each_pair(plan, body)


def pace_kernel(plan, tables_ref, out_ref):
    out_ref[...] = tables_ref[...]


def toeplitz_kernel(plan, tables_ref, toep_ref):
    mirror = iota((FREQ, 2 * FREQ), 0) + iota((FREQ, 2 * FREQ), 1) == FREQ
    mirror = mirror.astype(F32).astype(BF16)

    def body(u):
        lags = dot(my_table(plan, tables_ref, u)[BRANCH * 16 :, :], mirror)
        for q in range(plan.momenta):
            for i in range(BRANCH):
                n = q * BRANCH + i
                band = jnp.broadcast_to(lags[n : n + 1], (FREQ, 2 * FREQ))
                band = pltpu.roll(band, 0, 1, stride=1, stride_axis=0)
                toep_ref[u, q, i * FREQ : (i + 1) * FREQ, :] = band.astype(BF16)

    each_pair(plan, body)


def gather_rows(plan, ref, u, y, first, flip=False):
    m, k = divmod(y, plan.mom_dev)
    row, tail = plan.main_row(k, u), plan.tail_row(k, u)
    order = range(plan.half)
    lefts, rights, tails = [], [], []
    for j in reversed(order) if flip else order:
        peer = (first + j) * plan.n_mom + m
        lefts.append(ref[peer, rows_at(row, plan.steps), :])
        rights.append(ref[peer, rows_at(row + plan.steps, plan.steps), :])
        tails.append(ref[peer, rows_at(tail, plan.steps), :])
    tails = jnp.concatenate(tails, axis=0)
    if plan.shift(k):
        tails = pltpu.roll(tails.astype(F32), LANES - plan.shift(k), 1).astype(BF16)
    return jnp.concatenate([jnp.concatenate(lefts, axis=0), jnp.concatenate(rights, axis=0), tails], axis=1)


def half_and_tail(rows, h):
    return jnp.concatenate([rows[:, h * LANES : (h + 1) * LANES], rows[:, 2 * LANES :]], axis=1)


def self_block(plan, u, green, toep_ref, sand_ref, out_ref):
    summed = []
    for i in range(BRANCH):
        rows = slice(i * FREQ, (i + 1) * FREQ)
        band = jnp.concatenate(
            [
                jnp.concatenate([toep_ref[u, (k - y) % plan.momenta, rows, :] for y in range(plan.momenta)], axis=1)
                for k in range(plan.momenta)
            ],
            axis=0,
        )
        summed.append(dot(band, green).astype(BF16))
    left, right = [
        dot_nt(jnp.concatenate([half_and_tail(rows, h) for rows in summed], axis=1), sand_ref[u, h])
        for h in range(2)
    ]
    tails = left[:, LANES:] + right[:, LANES:]
    left, right = left[:, :LANES].astype(BF16), right[:, :LANES].astype(BF16)
    for y in range(plan.momenta):
        m, k = divmod(y, plan.mom_dev)
        row, tail = plan.main_row(k, u), plan.tail_row(k, u)
        rest = tails[y * FREQ : (y + 1) * FREQ]
        if plan.shift(k):
            rest = pltpu.roll(rest, plan.shift(k), 1)
        rest = rest.astype(BF16)
        for j in range(plan.half):
            peer = j * plan.n_mom + m
            here = slice(j * plan.steps, (j + 1) * plan.steps)
            there = slice(y * FREQ + j * plan.steps, y * FREQ + (j + 1) * plan.steps)
            out_ref[peer, rows_at(row, plan.steps), :] = left[there]
            out_ref[peer, rows_at(row + plan.steps, plan.steps), :] = right[there]
            out_ref[peer, rows_at(tail, plan.steps), :] += rest[here]


def clear_tails(plan, out_ref):
    for peer in range(plan.half * plan.n_mom):
        out_ref[peer, plan.main_rows :, :] = jnp.zeros((plan.tail_rows, LANES), BF16)


def self_late_kernel(plan, own, toep_ref, sand_ref, out_ref):
    clear_tails(plan, out_ref)

    def body(u):
        green = [gather_rows(plan, own, u, y, first) for y in range(plan.momenta) for first in (0, plan.half)]
        self_block(plan, u, jnp.concatenate(green, axis=0), toep_ref, sand_ref, out_ref)

    each_pair(plan, body)


def self_early_kernel(plan, own, far, toep_ref, sand_ref, late_ref, out_ref, stage, halo, sems):
    has = (lax.axis_index("energy") // plan.group > 0).astype(F32).astype(BF16)
    near = plan.half * plan.n_mom
    load = pltpu.make_async_copy(far, halo, sems.at[0])
    load.start()
    upper = pltpu.make_async_copy(late_ref, out_ref.at[near:], sems.at[1])
    upper.start()
    clear_tails(plan, stage)
    load.wait()

    def body(u):
        green = []
        for y in range(plan.momenta):
            green.append(gather_rows(plan, halo, u, y, 0) * has)
            green.append(gather_rows(plan, own, u, y, 0))
        self_block(plan, u, jnp.concatenate(green, axis=0), toep_ref, sand_ref, stage)

    each_pair(plan, body)
    lower = pltpu.make_async_copy(stage, out_ref.at[:near], sems.at[2])
    lower.start()
    lower.wait()
    upper.wait()


def lag_sums(plan, u, partner, green, sand_ref, store):
    partner, green = jnp.concatenate(partner, axis=0), jnp.concatenate(green, axis=0)
    left, right = [dot(half_and_tail(partner, h), sand_ref[u, h]) for h in range(2)]
    for i in range(BRANCH):
        here = slice(2 * LANES * i, 2 * LANES * i + LANES)
        rest = slice(2 * LANES * i + LANES, 2 * LANES * (i + 1))
        applied = jnp.concatenate([left[:, here], right[:, here], left[:, rest] + right[:, rest]], axis=1)
        lagged = dot_nt(applied.astype(BF16), green)
        for q in range(plan.momenta):
            acc = None
            for k in range(plan.momenta):
                y = (k + q) % plan.momenta
                part = lagged[k * FREQ : (k + 1) * FREQ, y * 2 * FREQ : (y + 1) * 2 * FREQ]
                acc = part if acc is None else acc + part
            acc = pltpu.roll(acc, FREQ + 1, 1, stride=1, stride_axis=0)
            store(q, i, jnp.sum(acc, axis=0, keepdims=True))


def phonon_early_kernel(plan, own, partner_ref, sand_ref, out_ref):
    def body(u):
        partner = [gather_rows(plan, partner_ref, u, k, 0, flip=True) for k in range(plan.momenta)]
        green = [gather_rows(plan, own, u, y, first) for y in range(plan.momenta) for first in (0, plan.half)]

        def store(q, i, lags):
            out_ref[u, q * BRANCH + i : q * BRANCH + i + 1, :] = lags

        lag_sums(plan, u, partner, green, sand_ref, store)

    each_pair(plan, body)


def phonon_late_kernel(plan, own, halo, partner_ref, sand_ref, early_ref, *refs, scale):
    outs, sums = refs[:-1], refs[-1]
    group = lax.axis_index("energy") // plan.group
    me = lax.axis_index("mom")
    has = (group < plan.n_groups - 1).astype(F32).astype(BF16)

    def body(u):
        partner = [gather_rows(plan, partner_ref, u, k, plan.half, flip=True) for k in range(plan.momenta)]
        green = []
        for y in range(plan.momenta):
            green.append(gather_rows(plan, own, u, y, plan.half))
            green.append(gather_rows(plan, halo, u, y, 0) * has)

        def store(q, i, lags):
            n = q * BRANCH + i
            side, row = divmod(n, plan.mom_dev * BRANCH)
            sums[u, side, row : row + 1, :] = (lags + early_ref[u, n : n + 1, :]) * scale

        lag_sums(plan, u, partner, green, sand_ref, store)

    each_pair(plan, body)
    for d in range(plan.n_groups):
        for t in range(plan.n_mom):
            for b in range(plan.sub):
                outs[d * plan.n_mom + t][b] = sums[(group ^ d) * plan.sub + b, me ^ t]


def collect(plan, parts, out_ref):
    me = lax.axis_index("mom")
    for d in range(plan.n_mom):
        total = sum(ref[...] for ref in parts[d :: plan.n_mom])
        for b in range(plan.sub):
            pair = (me ^ d) * plan.sub + b
            for q in range(plan.mom_dev):
                rows = [total[b, q * BRANCH + i : q * BRANCH + i + 1, :FREQ] for i in range(BRANCH)]
                out_ref[q, pl.ds(pair, 1), :] = jnp.concatenate(rows, axis=1)


def unpack_kernel(plan, wire, *refs):
    *parts, out_ref, lags_ref, tiles, sems = refs
    swap = swap_matrix(TILE, plan.steps)

    def rows_of(row):
        return jnp.concatenate([wire[peer, row : row + plan.steps, :] for peer in range(plan.peers)], axis=0)

    tails = {}
    for first in range(0, plan.mom_dev * plan.own, SLOTS):
        moved = dot(swap, rows_of(plan.main_rows + first // SLOTS * plan.steps))
        for t in range(SLOTS):
            tails[first + t] = moved[:, t * TAIL : (t + 1) * TAIL]
    copies = []
    for k in range(plan.mom_dev):
        for h in range(plan.pairs // TILE):
            row = plan.main_row(k, h)
            moved = dot(swap, jnp.concatenate([rows_of(row), rows_of(row + plan.steps)], axis=1))
            tail = tails[k * plan.own + h]
            moved = jnp.concatenate([moved[:, :LANES], tail[:, :REST], moved[:, LANES:], tail[:, REST:]], axis=1)
            tiles[k, h] = moved.astype(BF16).reshape(plan.steps, TILE, COMP)
            copy = pltpu.make_async_copy(
                tiles.at[k, h], out_ref.at[k, :, TILE * h : TILE * (h + 1), :], sems.at[k, h]
            )
            copy.start()
            copies.append(copy)
    collect(plan, parts, lags_ref)
    for copy in copies:
        copy.wait()


ANY = pl.BlockSpec(memory_space=pl.ANY)
HBM = pl.BlockSpec(memory_space=pltpu.HBM)
VMEM = pl.BlockSpec(memory_space=pltpu.VMEM)


def call(plan, kernel, out_shape, *args, in_specs=None, out_specs=None, scratch=(), flops=1, grant=None):
    outs = jax.tree.map(lambda _: VMEM, out_shape)
    return pl.pallas_call(
        functools.partial(kernel, plan),
        out_shape=out_shape,
        in_specs=in_specs or [VMEM] * len(args),
        out_specs=out_specs or outs,
        scratch_shapes=list(scratch),
        compiler_params=pltpu.CompilerParams(vmem_limit_bytes=grant or SMALL_GRANT * max(1, plan.own // 4)),
        cost_estimate=pl.CostEstimate(flops=flops, bytes_accessed=1, transcendentals=0),
    )(*args)


def shape(dims, dtype):
    return jax.ShapeDtypeStruct(dims, dtype)


def in_hbm(struct):
    return pltpu.HBM(struct.shape, struct.dtype)


def shards(lesser_green, partner, phonon_green, coupling):
    n_energy, n_mom = lax.axis_size("energy"), lax.axis_size("mom")
    plan = Plan(lesser_green, phonon_green, n_energy, n_mom)
    axes = ("energy", "mom")
    me = lax.axis_index("mom")
    s = lax.axis_index("energy") // plan.group
    wire = shape((plan.peers, plan.rows, LANES), BF16)
    half_peers = plan.half * n_mom
    groups = [[g * plan.peers + i for i in range(plan.peers)] for g in range(plan.n_groups)]
    tiles = (plan.mom_dev, plan.pairs // TILE)

    def exchange(blocks):
        return lax.all_to_all(blocks, axes, split_axis=0, concat_axis=0, axis_index_groups=groups, tiled=True)

    def swap_groups(values, other):
        route = []
        for e in range(n_energy):
            g, j = divmod(e, plan.group)
            to = other(g) if 0 <= other(g) < plan.n_groups else g
            route.append((e, to * plan.group + j))
        return lax.ppermute(values, "energy", route)

    staging = [pltpu.VMEM(wire.shape, BF16), pltpu.SemaphoreType.DMA((tiles[0] * tiles[1] + 1,))]
    tile_scratch = [pltpu.VMEM(tiles + (plan.steps, TILE, COMP), BF16), pltpu.SemaphoreType.DMA(tiles)]
    half_wire = shape((half_peers, plan.rows, LANES), BF16)
    own = exchange(
        call(
            plan,
            pack_own_kernel,
            in_hbm(wire),
            lesser_green,
            in_specs=[HBM],
            out_specs=HBM,
            scratch=staging + tile_scratch,
            grant=LARGE_GRANT,
        )
    )

    lag_count = plan.momenta * BRANCH
    lag_rows = -(-lag_count // 16) * 16
    couple = coupling.reshape(plan.pairs_dev, BRANCH, ORB, ORB)
    couple = jnp.pad(couple, ((0, 0), (0, 0), (0, 16 - ORB), (0, FREQ - ORB)))
    phonon = phonon_green.reshape(plan.momenta, plan.pairs_dev, BRANCH, FREQ)
    phonon = jnp.moveaxis(phonon, 1, 0).reshape(plan.pairs_dev, lag_count, FREQ)
    phonon = jnp.pad(phonon, ((0, 0), (0, lag_rows - lag_count), (0, 0)))
    table = jnp.concatenate([couple.reshape(plan.pairs_dev, BRANCH * 16, FREQ), phonon], axis=1)
    table = lax.dynamic_slice_in_dim(table, me * plan.sub, plan.sub, axis=0)
    tables = [table]
    for d in range(1, plan.n_groups):
        tables.append(swap_groups(table, functools.partial(lambda d, g: g ^ d, d)))
    tables = jnp.concatenate(tables, axis=0)
    sand = call(
        plan, sandwich_kernel, shape((plan.own, 2, 2 * LANES, BRANCH * 2 * LANES), BF16), tables
    )
    chunk = max(1, 256 // plan.pairs)
    source = (jnp.arange(chunk)[:, None] * plan.pairs + partner[None, :]).reshape(-1)
    take = (source[:, None] == jnp.arange(chunk * plan.pairs)[None, :]).astype(BF16)
    partner_wire = call(
        plan,
        pack_partner_kernel,
        in_hbm(wire),
        take,
        lesser_green,
        out_specs=HBM,
        scratch=staging + [pltpu.VMEM(lesser_green.shape, BF16)],
    )
    toep = call(plan, toeplitz_kernel, shape((plan.own, plan.momenta, BRANCH * FREQ, 2 * FREQ), BF16), tables)
    own, tables, sand, toep, partner_wire = lax.optimization_barrier((own, tables, sand, toep, partner_wire))

    odd = s % 2

    def edge(side):
        return lax.dynamic_slice_in_dim(own, side * half_peers, half_peers, axis=0)

    before = after = inner = swap_groups(edge(1 - odd), lambda g: g ^ 1)
    if plan.n_groups > 2:
        outer = swap_groups(edge(odd), lambda g: ((g - 1) ^ 1) + 1)
        before = jnp.where(odd == 1, inner, outer)
        after = jnp.where(odd == 1, outer, inner)

    paced = call(plan, pace_kernel, shape(tables.shape, BF16), tables, flops=LONG)
    paced, partner_wire = lax.optimization_barrier((paced, partner_wire))
    partner_blocks = exchange(partner_wire)

    late = call(plan, self_late_kernel, half_wire, own, toep, sand)
    sigma = call(
        plan,
        self_early_kernel,
        in_hbm(wire),
        own,
        before,
        toep,
        sand,
        late,
        in_specs=[VMEM, ANY, VMEM, VMEM, VMEM],
        out_specs=HBM,
        scratch=[
            pltpu.VMEM(half_wire.shape, BF16),
            pltpu.VMEM(half_wire.shape, BF16),
            pltpu.SemaphoreType.DMA((3,)),
        ],
        flops=LONG,
    )
    arrived = exchange(sigma)

    scale = (plan.momenta * n_energy * plan.steps * COMP) ** -0.5
    early = call(
        plan,
        phonon_early_kernel,
        shape((plan.own, lag_count, LANES), F32),
        own,
        partner_blocks,
        sand,
    )
    side_rows = plan.mom_dev * BRANCH
    parts = list(call(
        plan,
        functools.partial(phonon_late_kernel, scale=scale),
        [shape((plan.sub, side_rows, LANES), F32)] * (plan.n_groups * n_mom),
        own,
        after,
        partner_blocks,
        sand,
        early,
        scratch=[pltpu.VMEM((plan.own, n_mom, side_rows, LANES), F32)],
    ))
    for d in range(plan.n_groups):
        for t in range(n_mom):
            if d or t:
                route = []
                for e in range(n_energy):
                    g, j = divmod(e, plan.group)
                    for m in range(n_mom):
                        route.append((e * n_mom + m, ((g ^ d) * plan.group + j) * n_mom + (m ^ t)))
                parts[d * n_mom + t] = lax.ppermute(parts[d * n_mom + t], axes, route)
    return call(
        plan,
        unpack_kernel,
        [
            shape(lesser_green.shape, BF16),
            shape((plan.mom_dev, plan.pairs_dev, BRANCH * FREQ), F32),
        ],
        arrived,
        *parts,
        out_specs=[ANY, VMEM],
        scratch=[pltpu.VMEM(tiles + (plan.steps, TILE, COMP), BF16), pltpu.SemaphoreType.DMA(tiles)],
    )


def solution(mesh):
    in_specs = (P("mom", "energy", None, None), P(), P(None, "energy", None), P("energy", None))
    out_specs = (P("mom", "energy", None, None), P("mom", "energy", None))
    return jax.shard_map(shards, mesh=mesh, in_specs=in_specs, out_specs=out_specs, check_vma=False)
```

```python
import functools

import jax
import jax.numpy as jnp
from jax import lax
from jax.experimental import pallas as pl
from jax.experimental.pallas import tpu as pltpu
from jax.sharding import PartitionSpec as P

ORB = 12
BRANCH = 3
FREQ = 64
COMP = 288
SQUARE = ORB * ORB
LANES = 128
REST = SQUARE - LANES
TAIL = 2 * REST
SLOTS = LANES // TAIL
TILE = 16
SMALL_GRANT = 16 * 1024 * 1024
LARGE_GRANT = 60 * 1024 * 1024
LONG = 100_000_000_000

BF16 = jnp.bfloat16
F32 = jnp.float32
I32 = jnp.int32


class Plan:
    def __init__(self, green, phonon, n_energy, n_mom):
        self.n_energy, self.n_mom = n_energy, n_mom
        self.mom_dev, self.steps, self.pairs, _ = green.shape
        self.momenta = self.mom_dev * n_mom
        self.pairs_dev = phonon.shape[1]
        self.half = FREQ // self.steps
        self.group = 2 * self.half
        self.n_groups = n_energy // self.group
        self.peers = self.group * n_mom
        self.sub = self.pairs_dev // n_mom
        self.own = self.n_groups * self.sub
        self.main_rows = self.mom_dev * self.own * 2 * self.steps
        self.tail_rows = self.mom_dev * self.own // SLOTS * self.steps
        self.rows = self.main_rows + self.tail_rows
        assert self.half * self.steps == FREQ and n_energy % self.group == 0
        assert self.n_groups & (self.n_groups - 1) == 0
        assert self.pairs_dev == n_mom and self.group * self.pairs_dev == TILE
        assert self.mom_dev * self.own % SLOTS == 0 and self.n_groups % 2 == 0

    def main_row(self, k, u):
        return (k * self.own + u) * 2 * self.steps

    def tail_row(self, k, u):
        return self.main_rows + (k * self.own + u) // SLOTS * self.steps

    def shift(self, k):
        return k * self.own % SLOTS * TAIL


def dot(a, b):
    return lax.dot_general(a, b, (((1,), (0,)), ((), ())), preferred_element_type=F32)


def dot_nt(a, b):
    return lax.dot_general(a, b, (((1,), (1,)), ((), ())), preferred_element_type=F32)


def iota(dims, axis):
    return lax.broadcasted_iota(I32, dims, axis)


def swap_matrix(outer, inner, flip=False):
    n = outer * inner
    row, col = iota((n, n), 0), iota((n, n), 1)
    place = row & (outer - 1)
    source = (outer - 1 - place if flip else place) * inner + (row >> (outer.bit_length() - 1))
    return (col == source).astype(F32).astype(BF16)


def pack_rows(plan, load, out_ref, stage, sems, flip=False):
    swap = swap_matrix(plan.steps, TILE, flip)
    copies = []

    def send(first, count):
        rows = slice(first, first + count)
        copy = pltpu.make_async_copy(stage.at[:, rows, :], out_ref.at[:, rows, :], sems.at[len(copies)])
        copy.start()
        copies.append(copy)

    def put(row, moved):
        for peer in range(plan.peers):
            stage[peer, row : row + plan.steps, :] = moved[peer * plan.steps : (peer + 1) * plan.steps]

    tails = []
    for k in range(plan.mom_dev):
        for h in range(plan.pairs // TILE):
            rows = load(k, h)
            halves = jnp.concatenate([rows[:, :LANES], rows[:, SQUARE : SQUARE + LANES]], axis=1)
            tails += [rows[:, LANES:SQUARE], rows[:, SQUARE + LANES :]]
            moved = dot(swap, halves).astype(BF16)
            row = plan.main_row(k, h)
            put(row, moved[:, :LANES])
            send(row, plan.steps)
            put(row + plan.steps, moved[:, LANES:])
            send(row + plan.steps, plan.steps)
    for n in range(0, len(tails), 2 * SLOTS):
        joined = jnp.concatenate(tails[n : n + 2 * SLOTS], axis=1)
        put(plan.main_rows + n // (2 * SLOTS) * plan.steps, dot(swap, joined).astype(BF16))
    send(plan.main_rows, plan.tail_rows)
    for copy in copies:
        copy.wait()


def pack_own_kernel(plan, green_ref, out_ref, stage, out_sems, tiles, sems):
    copies = {}
    for k in range(plan.mom_dev):
        for h in range(plan.pairs // TILE):
            for part in range(2):
                steps = pl.ds(part * plan.steps // 2, plan.steps // 2)
                copies[k, h, part] = pltpu.make_async_copy(
                    green_ref.at[k, steps, TILE * h : TILE * (h + 1), :], tiles.at[k, h, steps], sems.at[k, h, part]
                )
                copies[k, h, part].start()

    def load(k, h):
        for part in range(2):
            copies[k, h, part].wait()
        return tiles[k, h].reshape(plan.steps * TILE, COMP)

    pack_rows(plan, load, out_ref, stage, out_sems)


def pack_partner_kernel(plan, take_ref, green_ref, out_ref, stage, sems, taken):
    chunk = take_ref.shape[0] // plan.pairs
    take = take_ref[...]
    for k in range(plan.mom_dev):
        for e in range(0, plan.steps, chunk):
            rows = green_ref[k, e : e + chunk].reshape(chunk * plan.pairs, COMP)
            taken[k, e : e + chunk] = dot(take, rows).astype(BF16).reshape(chunk, plan.pairs, COMP)

    def load(k, h):
        return taken[k, :, TILE * h : TILE * (h + 1), :].reshape(plan.steps * TILE, COMP)

    pack_rows(plan, load, out_ref, stage, sems, flip=True)


def each_pair(plan, body):
    if plan.own <= 2:
        for u in range(plan.own):
            body(u)
    else:
        lax.fori_loop(0, plan.own, lambda u, _: body(u), None)


def rows_at(row, count):
    return pl.ds(row if isinstance(row, int) else pl.multiple_of(row, count), count)


def my_table(plan, tables_ref, u):
    group = lax.axis_index("energy") // plan.group
    return tables_ref[(u // plan.sub ^ group) * plan.sub + u % plan.sub]


def sandwich_kernel(plan, tables_ref, sand_ref):
    place, want = iota((2 * LANES, 16), 0), iota((2 * LANES, 16), 1)

    def body(u):
        couple = my_table(plan, tables_ref, u)[: BRANCH * 16, :16]
        for h in range(2):
            comp = jnp.where(place < LANES, place, place - (u % SLOTS * TAIL + h * REST))
            valid = (place < LANES) | ((comp >= LANES) & (comp < SQUARE))
            quotient = (comp * 171) >> 11
            first = (valid & (quotient == want)).astype(F32).astype(BF16)
            second = (valid & (comp - ORB * quotient == want)).astype(F32).astype(BF16)
            left = dot_nt(couple, first).astype(BF16)
            right = dot_nt(couple, second).astype(BF16)
            for i in range(BRANCH):
                rows = slice(16 * i, 16 * i + 16)
                product = dot(first, left[rows]) * dot(second, right[rows])
                sand_ref[u, h, :, 2 * LANES * i : 2 * LANES * (i + 1)] = product.astype(BF16)

    each_pair(plan, body)


def pace_kernel(plan, tables_ref, out_ref):
    out_ref[...] = tables_ref[...]


def toeplitz_kernel(plan, tables_ref, toep_ref):
    mirror = iota((FREQ, 2 * FREQ), 0) + iota((FREQ, 2 * FREQ), 1) == FREQ
    mirror = mirror.astype(F32).astype(BF16)

    def body(u):
        lags = dot(my_table(plan, tables_ref, u)[BRANCH * 16 :, :], mirror)
        for q in range(plan.momenta):
            for i in range(BRANCH):
                n = q * BRANCH + i
                band = jnp.broadcast_to(lags[n : n + 1], (FREQ, 2 * FREQ))
                band = pltpu.roll(band, 0, 1, stride=1, stride_axis=0)
                toep_ref[u, q, i * FREQ : (i + 1) * FREQ, :] = band.astype(BF16)

    each_pair(plan, body)


def gather_rows(plan, ref, u, y, first, flip=False):
    m, k = divmod(y, plan.mom_dev)
    row, tail = plan.main_row(k, u), plan.tail_row(k, u)
    order = range(plan.half)
    lefts, rights, tails = [], [], []
    for j in reversed(order) if flip else order:
        peer = (first + j) * plan.n_mom + m
        lefts.append(ref[peer, rows_at(row, plan.steps), :])
        rights.append(ref[peer, rows_at(row + plan.steps, plan.steps), :])
        tails.append(ref[peer, rows_at(tail, plan.steps), :])
    tails = jnp.concatenate(tails, axis=0)
    if plan.shift(k):
        tails = pltpu.roll(tails.astype(F32), LANES - plan.shift(k), 1).astype(BF16)
    return jnp.concatenate([jnp.concatenate(lefts, axis=0), jnp.concatenate(rights, axis=0), tails], axis=1)


def half_and_tail(rows, h):
    return jnp.concatenate([rows[:, h * LANES : (h + 1) * LANES], rows[:, 2 * LANES :]], axis=1)


def self_block(plan, u, green, toep_ref, sand_ref, out_ref):
    summed = []
    for i in range(BRANCH):
        rows = slice(i * FREQ, (i + 1) * FREQ)
        band = jnp.concatenate(
            [
                jnp.concatenate([toep_ref[u, (k - y) % plan.momenta, rows, :] for y in range(plan.momenta)], axis=1)
                for k in range(plan.momenta)
            ],
            axis=0,
        )
        summed.append(dot(band, green).astype(BF16))
    left, right = [
        dot_nt(jnp.concatenate([half_and_tail(rows, h) for rows in summed], axis=1), sand_ref[u, h])
        for h in range(2)
    ]
    tails = left[:, LANES:] + right[:, LANES:]
    left, right = left[:, :LANES].astype(BF16), right[:, :LANES].astype(BF16)
    for y in range(plan.momenta):
        m, k = divmod(y, plan.mom_dev)
        row, tail = plan.main_row(k, u), plan.tail_row(k, u)
        rest = tails[y * FREQ : (y + 1) * FREQ]
        if plan.shift(k):
            rest = pltpu.roll(rest, plan.shift(k), 1)
        rest = rest.astype(BF16)
        for j in range(plan.half):
            peer = j * plan.n_mom + m
            here = slice(j * plan.steps, (j + 1) * plan.steps)
            there = slice(y * FREQ + j * plan.steps, y * FREQ + (j + 1) * plan.steps)
            out_ref[peer, rows_at(row, plan.steps), :] = left[there]
            out_ref[peer, rows_at(row + plan.steps, plan.steps), :] = right[there]
            out_ref[peer, rows_at(tail, plan.steps), :] += rest[here]


def clear_tails(plan, out_ref):
    for peer in range(plan.half * plan.n_mom):
        out_ref[peer, plan.main_rows :, :] = jnp.zeros((plan.tail_rows, LANES), BF16)


def self_late_kernel(plan, own, toep_ref, sand_ref, out_ref):
    clear_tails(plan, out_ref)

    def body(u):
        green = [gather_rows(plan, own, u, y, first) for y in range(plan.momenta) for first in (0, plan.half)]
        self_block(plan, u, jnp.concatenate(green, axis=0), toep_ref, sand_ref, out_ref)

    each_pair(plan, body)


def self_early_kernel(plan, own, far, toep_ref, sand_ref, late_ref, out_ref, stage, halo, sems):
    has = (lax.axis_index("energy") // plan.group > 0).astype(F32).astype(BF16)
    near = plan.half * plan.n_mom
    load = pltpu.make_async_copy(far, halo, sems.at[0])
    load.start()
    upper = pltpu.make_async_copy(late_ref, out_ref.at[near:], sems.at[1])
    upper.start()
    clear_tails(plan, stage)
    load.wait()

    def body(u):
        green = []
        for y in range(plan.momenta):
            green.append(gather_rows(plan, halo, u, y, 0) * has)
            green.append(gather_rows(plan, own, u, y, 0))
        self_block(plan, u, jnp.concatenate(green, axis=0), toep_ref, sand_ref, stage)

    each_pair(plan, body)
    lower = pltpu.make_async_copy(stage, out_ref.at[:near], sems.at[2])
    lower.start()
    lower.wait()
    upper.wait()


def lag_sums(plan, u, partner, green, sand_ref, store):
    partner, green = jnp.concatenate(partner, axis=0), jnp.concatenate(green, axis=0)
    left, right = [dot(half_and_tail(partner, h), sand_ref[u, h]) for h in range(2)]
    for i in range(BRANCH):
        here = slice(2 * LANES * i, 2 * LANES * i + LANES)
        rest = slice(2 * LANES * i + LANES, 2 * LANES * (i + 1))
        applied = jnp.concatenate([left[:, here], right[:, here], left[:, rest] + right[:, rest]], axis=1)
        lagged = dot_nt(applied.astype(BF16), green)
        for q in range(plan.momenta):
            acc = None
            for k in range(plan.momenta):
                y = (k + q) % plan.momenta
                part = lagged[k * FREQ : (k + 1) * FREQ, y * 2 * FREQ : (y + 1) * 2 * FREQ]
                acc = part if acc is None else acc + part
            acc = pltpu.roll(acc, FREQ + 1, 1, stride=1, stride_axis=0)
            store(q, i, jnp.sum(acc, axis=0, keepdims=True))


def phonon_early_kernel(plan, own, partner_ref, sand_ref, out_ref):
    def body(u):
        partner = [gather_rows(plan, partner_ref, u, k, 0, flip=True) for k in range(plan.momenta)]
        green = [gather_rows(plan, own, u, y, first) for y in range(plan.momenta) for first in (0, plan.half)]

        def store(q, i, lags):
            out_ref[u, q * BRANCH + i : q * BRANCH + i + 1, :] = lags

        lag_sums(plan, u, partner, green, sand_ref, store)

    each_pair(plan, body)


def phonon_late_kernel(plan, own, halo, partner_ref, sand_ref, early_ref, *refs, scale):
    outs, sums = refs[:-1], refs[-1]
    group = lax.axis_index("energy") // plan.group
    me = lax.axis_index("mom")
    has = (group < plan.n_groups - 1).astype(F32).astype(BF16)

    def body(u):
        partner = [gather_rows(plan, partner_ref, u, k, plan.half, flip=True) for k in range(plan.momenta)]
        green = []
        for y in range(plan.momenta):
            green.append(gather_rows(plan, own, u, y, plan.half))
            green.append(gather_rows(plan, halo, u, y, 0) * has)

        def store(q, i, lags):
            n = q * BRANCH + i
            side, row = divmod(n, plan.mom_dev * BRANCH)
            sums[u, side, row : row + 1, :] = (lags + early_ref[u, n : n + 1, :]) * scale

        lag_sums(plan, u, partner, green, sand_ref, store)

    each_pair(plan, body)
    for d in range(plan.n_groups):
        for t in range(plan.n_mom):
            for b in range(plan.sub):
                outs[d * plan.n_mom + t][b] = sums[(group ^ d) * plan.sub + b, me ^ t]


def collect(plan, parts, out_ref):
    me = lax.axis_index("mom")
    for d in range(plan.n_mom):
        total = sum(ref[...] for ref in parts[d :: plan.n_mom])
        for b in range(plan.sub):
            pair = (me ^ d) * plan.sub + b
            for q in range(plan.mom_dev):
                rows = [total[b, q * BRANCH + i : q * BRANCH + i + 1, :FREQ] for i in range(BRANCH)]
                out_ref[q, pl.ds(pair, 1), :] = jnp.concatenate(rows, axis=1)


def unpack_kernel(plan, wire, *refs):
    *parts, out_ref, lags_hbm, tiles, lags, sems, lag_sem = refs
    collect(plan, parts, lags)
    lag_copy = pltpu.make_async_copy(lags, lags_hbm, lag_sem)
    lag_copy.start()
    swap = swap_matrix(TILE, plan.steps)

    def rows_of(row):
        return jnp.concatenate([wire[peer, row : row + plan.steps, :] for peer in range(plan.peers)], axis=0)

    tails = {}
    for first in range(0, plan.mom_dev * plan.own, SLOTS):
        moved = dot(swap, rows_of(plan.main_rows + first // SLOTS * plan.steps))
        for t in range(SLOTS):
            tails[first + t] = moved[:, t * TAIL : (t + 1) * TAIL]
    copies = []
    for k in range(plan.mom_dev):
        for h in range(plan.pairs // TILE):
            row = plan.main_row(k, h)
            moved = dot(swap, jnp.concatenate([rows_of(row), rows_of(row + plan.steps)], axis=1))
            tail = tails[k * plan.own + h]
            moved = jnp.concatenate([moved[:, :LANES], tail[:, :REST], moved[:, LANES:], tail[:, REST:]], axis=1)
            tiles[k, h] = moved.astype(BF16).reshape(plan.steps, TILE, COMP)
            copy = pltpu.make_async_copy(
                tiles.at[k, h], out_ref.at[k, :, TILE * h : TILE * (h + 1), :], sems.at[k, h]
            )
            copy.start()
            copies.append(copy)
    for copy in copies:
        copy.wait()
    lag_copy.wait()


ANY = pl.BlockSpec(memory_space=pl.ANY)
HBM = pl.BlockSpec(memory_space=pltpu.HBM)
VMEM = pl.BlockSpec(memory_space=pltpu.VMEM)


def call(plan, kernel, out_shape, *args, in_specs=None, out_specs=None, scratch=(), flops=1, grant=None):
    outs = jax.tree.map(lambda _: VMEM, out_shape)
    return pl.pallas_call(
        functools.partial(kernel, plan),
        out_shape=out_shape,
        in_specs=in_specs or [VMEM] * len(args),
        out_specs=out_specs or outs,
        scratch_shapes=list(scratch),
        compiler_params=pltpu.CompilerParams(vmem_limit_bytes=grant or SMALL_GRANT * max(1, plan.own // 4)),
        cost_estimate=pl.CostEstimate(flops=flops, bytes_accessed=1, transcendentals=0),
    )(*args)


def shape(dims, dtype):
    return jax.ShapeDtypeStruct(dims, dtype)


def in_hbm(struct):
    return pltpu.HBM(struct.shape, struct.dtype)


def shards(lesser_green, partner, phonon_green, coupling):
    n_energy, n_mom = lax.axis_size("energy"), lax.axis_size("mom")
    plan = Plan(lesser_green, phonon_green, n_energy, n_mom)
    axes = ("energy", "mom")
    me = lax.axis_index("mom")
    s = lax.axis_index("energy") // plan.group
    wire = shape((plan.peers, plan.rows, LANES), BF16)
    half_peers = plan.half * n_mom
    groups = [[g * plan.peers + i for i in range(plan.peers)] for g in range(plan.n_groups)]
    tiles = (plan.mom_dev, plan.pairs // TILE)

    def exchange(blocks):
        return lax.all_to_all(blocks, axes, split_axis=0, concat_axis=0, axis_index_groups=groups, tiled=True)

    def swap_groups(values, other):
        route = []
        for e in range(n_energy):
            g, j = divmod(e, plan.group)
            to = other(g) if 0 <= other(g) < plan.n_groups else g
            route.append((e, to * plan.group + j))
        return lax.ppermute(values, "energy", route)

    staging = [pltpu.VMEM(wire.shape, BF16), pltpu.SemaphoreType.DMA((2 * tiles[0] * tiles[1] + 1,))]
    tile_scratch = [pltpu.VMEM(tiles + (plan.steps, TILE, COMP), BF16), pltpu.SemaphoreType.DMA(tiles + (2,))]
    half_wire = shape((half_peers, plan.rows, LANES), BF16)
    own = exchange(
        call(
            plan,
            pack_own_kernel,
            in_hbm(wire),
            lesser_green,
            in_specs=[HBM],
            out_specs=HBM,
            scratch=staging + tile_scratch,
            grant=LARGE_GRANT,
        )
    )

    lag_count = plan.momenta * BRANCH
    lag_rows = -(-lag_count // 16) * 16
    couple = coupling.reshape(plan.pairs_dev, BRANCH, ORB, ORB)
    couple = jnp.pad(couple, ((0, 0), (0, 0), (0, 16 - ORB), (0, FREQ - ORB)))
    phonon = phonon_green.reshape(plan.momenta, plan.pairs_dev, BRANCH, FREQ)
    phonon = jnp.moveaxis(phonon, 1, 0).reshape(plan.pairs_dev, lag_count, FREQ)
    phonon = jnp.pad(phonon, ((0, 0), (0, lag_rows - lag_count), (0, 0)))
    table = jnp.concatenate([couple.reshape(plan.pairs_dev, BRANCH * 16, FREQ), phonon], axis=1)
    table = lax.dynamic_slice_in_dim(table, me * plan.sub, plan.sub, axis=0)
    tables = [table]
    for d in range(1, plan.n_groups):
        tables.append(swap_groups(table, functools.partial(lambda d, g: g ^ d, d)))
    tables = jnp.concatenate(tables, axis=0)
    sand = call(
        plan, sandwich_kernel, shape((plan.own, 2, 2 * LANES, BRANCH * 2 * LANES), BF16), tables
    )
    chunk = max(1, 256 // plan.pairs)
    source = (jnp.arange(chunk)[:, None] * plan.pairs + partner[None, :]).reshape(-1)
    take = (source[:, None] == jnp.arange(chunk * plan.pairs)[None, :]).astype(BF16)
    partner_wire = call(
        plan,
        pack_partner_kernel,
        in_hbm(wire),
        take,
        lesser_green,
        out_specs=HBM,
        scratch=staging + [pltpu.VMEM(lesser_green.shape, BF16)],
    )
    toep = call(plan, toeplitz_kernel, shape((plan.own, plan.momenta, BRANCH * FREQ, 2 * FREQ), BF16), tables)
    own, tables, sand, toep, partner_wire = lax.optimization_barrier((own, tables, sand, toep, partner_wire))

    odd = s % 2

    def edge(side):
        return lax.dynamic_slice_in_dim(own, side * half_peers, half_peers, axis=0)

    before = after = inner = swap_groups(edge(1 - odd), lambda g: g ^ 1)
    if plan.n_groups > 2:
        outer = swap_groups(edge(odd), lambda g: ((g - 1) ^ 1) + 1)
        before = jnp.where(odd == 1, inner, outer)
        after = jnp.where(odd == 1, outer, inner)

    paced = call(plan, pace_kernel, shape(tables.shape, BF16), tables, flops=LONG)
    paced, partner_wire = lax.optimization_barrier((paced, partner_wire))
    partner_blocks = exchange(partner_wire)

    late = call(plan, self_late_kernel, half_wire, own, toep, sand)
    sigma = call(
        plan,
        self_early_kernel,
        in_hbm(wire),
        own,
        before,
        toep,
        sand,
        late,
        in_specs=[VMEM, ANY, VMEM, VMEM, VMEM],
        out_specs=HBM,
        scratch=[
            pltpu.VMEM(half_wire.shape, BF16),
            pltpu.VMEM(half_wire.shape, BF16),
            pltpu.SemaphoreType.DMA((3,)),
        ],
        flops=LONG,
    )
    arrived = exchange(sigma)

    scale = (plan.momenta * n_energy * plan.steps * COMP) ** -0.5
    early = call(
        plan,
        phonon_early_kernel,
        shape((plan.own, lag_count, LANES), F32),
        own,
        partner_blocks,
        sand,
    )
    side_rows = plan.mom_dev * BRANCH
    parts = list(call(
        plan,
        functools.partial(phonon_late_kernel, scale=scale),
        [shape((plan.sub, side_rows, LANES), F32)] * (plan.n_groups * n_mom),
        own,
        after,
        partner_blocks,
        sand,
        early,
        scratch=[pltpu.VMEM((plan.own, n_mom, side_rows, LANES), F32)],
    ))
    for d in range(plan.n_groups):
        for t in range(n_mom):
            if d or t:
                route = []
                for e in range(n_energy):
                    g, j = divmod(e, plan.group)
                    for m in range(n_mom):
                        route.append((e * n_mom + m, ((g ^ d) * plan.group + j) * n_mom + (m ^ t)))
                parts[d * n_mom + t] = lax.ppermute(parts[d * n_mom + t], axes, route)
    return call(
        plan,
        unpack_kernel,
        [
            shape(lesser_green.shape, BF16),
            shape((plan.mom_dev, plan.pairs_dev, BRANCH * FREQ), F32),
        ],
        arrived,
        *parts,
        out_specs=[ANY, ANY],
        scratch=[
            pltpu.VMEM(tiles + (plan.steps, TILE, COMP), BF16),
            pltpu.VMEM((plan.mom_dev, plan.pairs_dev, BRANCH * FREQ), F32),
            pltpu.SemaphoreType.DMA(tiles),
            pltpu.SemaphoreType.DMA,
        ],
    )


def solution(mesh):
    in_specs = (P("mom", "energy", None, None), P(), P(None, "energy", None), P("energy", None))
    out_specs = (P("mom", "energy", None, None), P("mom", "energy", None))
    return jax.shard_map(shards, mesh=mesh, in_specs=in_specs, out_specs=out_specs, check_vma=False)
```

```python
import functools

import jax
import jax.numpy as jnp
from jax import lax
from jax.experimental import pallas as pl
from jax.experimental.pallas import tpu as pltpu
from jax.sharding import PartitionSpec as P

ORB = 12
BRANCH = 3
FREQ = 64
COMP = 288
SQUARE = ORB * ORB
LANES = 128
REST = SQUARE - LANES
TAIL = 2 * REST
SLOTS = LANES // TAIL
TILE = 16
SMALL_GRANT = 16 * 1024 * 1024
LARGE_GRANT = 60 * 1024 * 1024
LONG = 100_000_000_000

BF16 = jnp.bfloat16
F32 = jnp.float32
I32 = jnp.int32


class Plan:
    def __init__(self, green, phonon, n_energy, n_mom):
        self.n_energy, self.n_mom = n_energy, n_mom
        self.mom_dev, self.steps, self.pairs, _ = green.shape
        self.momenta = self.mom_dev * n_mom
        self.pairs_dev = phonon.shape[1]
        self.half = FREQ // self.steps
        self.group = 2 * self.half
        self.n_groups = n_energy // self.group
        self.peers = self.group * n_mom
        self.sub = self.pairs_dev // n_mom
        self.own = self.n_groups * self.sub
        self.main_rows = self.mom_dev * self.own * 2 * self.steps
        self.tail_rows = self.mom_dev * self.own // SLOTS * self.steps
        self.rows = self.main_rows + self.tail_rows
        assert self.half * self.steps == FREQ and n_energy % self.group == 0
        assert self.n_groups & (self.n_groups - 1) == 0
        assert self.pairs_dev == n_mom and self.group * self.pairs_dev == TILE
        assert self.mom_dev * self.own % SLOTS == 0 and self.n_groups % 2 == 0

    def main_row(self, k, u):
        return (k * self.own + u) * 2 * self.steps

    def tail_row(self, k, u):
        return self.main_rows + (k * self.own + u) // SLOTS * self.steps

    def shift(self, k):
        return k * self.own % SLOTS * TAIL


def dot(a, b):
    return lax.dot_general(a, b, (((1,), (0,)), ((), ())), preferred_element_type=F32)


def dot_nt(a, b):
    return lax.dot_general(a, b, (((1,), (1,)), ((), ())), preferred_element_type=F32)


def iota(dims, axis):
    return lax.broadcasted_iota(I32, dims, axis)


def swap_matrix(outer, inner, flip=False):
    n = outer * inner
    row, col = iota((n, n), 0), iota((n, n), 1)
    place = row & (outer - 1)
    source = (outer - 1 - place if flip else place) * inner + (row >> (outer.bit_length() - 1))
    return (col == source).astype(F32).astype(BF16)


def pack_rows(plan, load, out_ref, stage, sems, flip=False):
    swap = swap_matrix(plan.steps, TILE, flip)
    copies = []

    def send(first, count):
        rows = slice(first, first + count)
        copy = pltpu.make_async_copy(stage.at[:, rows, :], out_ref.at[:, rows, :], sems.at[len(copies)])
        copy.start()
        copies.append(copy)

    def put(row, moved):
        for peer in range(plan.peers):
            stage[peer, row : row + plan.steps, :] = moved[peer * plan.steps : (peer + 1) * plan.steps]

    tails = []
    for k in range(plan.mom_dev):
        for h in range(plan.pairs // TILE):
            rows = load(k, h)
            halves = jnp.concatenate([rows[:, :LANES], rows[:, SQUARE : SQUARE + LANES]], axis=1)
            tails += [rows[:, LANES:SQUARE], rows[:, SQUARE + LANES :]]
            moved = dot(swap, halves).astype(BF16)
            row = plan.main_row(k, h)
            put(row, moved[:, :LANES])
            put(row + plan.steps, moved[:, LANES:])
            send(row, 2 * plan.steps)
    for n in range(0, len(tails), 2 * SLOTS):
        joined = jnp.concatenate(tails[n : n + 2 * SLOTS], axis=1)
        put(plan.main_rows + n // (2 * SLOTS) * plan.steps, dot(swap, joined).astype(BF16))
    send(plan.main_rows, plan.tail_rows)
    for copy in copies:
        copy.wait()


def pack_own_kernel(plan, green_ref, out_ref, stage, out_sems, tiles, sems):
    copies = {}
    for k in range(plan.mom_dev):
        for h in range(plan.pairs // TILE):
            copies[k, h] = pltpu.make_async_copy(
                green_ref.at[k, :, TILE * h : TILE * (h + 1), :], tiles.at[k, h], sems.at[k, h]
            )
            copies[k, h].start()

    def load(k, h):
        copies[k, h].wait()
        return tiles[k, h].reshape(plan.steps * TILE, COMP)

    pack_rows(plan, load, out_ref, stage, out_sems)


def pack_partner_kernel(plan, take_ref, green_ref, out_ref, stage, sems, taken):
    chunk = take_ref.shape[0] // plan.pairs
    take = take_ref[...]
    for k in range(plan.mom_dev):
        for e in range(0, plan.steps, chunk):
            rows = green_ref[k, e : e + chunk].reshape(chunk * plan.pairs, COMP)
            taken[k, e : e + chunk] = dot(take, rows).astype(BF16).reshape(chunk, plan.pairs, COMP)

    def load(k, h):
        return taken[k, :, TILE * h : TILE * (h + 1), :].reshape(plan.steps * TILE, COMP)

    pack_rows(plan, load, out_ref, stage, sems, flip=True)


def each_pair(plan, body):
    if plan.own <= 2:
        for u in range(plan.own):
            body(u)
    else:
        lax.fori_loop(0, plan.own, lambda u, _: body(u), None)


def rows_at(row, count):
    return pl.ds(row if isinstance(row, int) else pl.multiple_of(row, count), count)


def my_table(plan, tables_ref, u):
    group = lax.axis_index("energy") // plan.group
    return tables_ref[(u // plan.sub ^ group) * plan.sub + u % plan.sub]


def sandwich_kernel(plan, tables_ref, sand_ref):
    place, want = iota((2 * LANES, 16), 0), iota((2 * LANES, 16), 1)

    def body(u):
        couple = my_table(plan, tables_ref, u)[: BRANCH * 16, :16]
        for h in range(2):
            comp = jnp.where(place < LANES, place, place - (u % SLOTS * TAIL + h * REST))
            valid = (place < LANES) | ((comp >= LANES) & (comp < SQUARE))
            quotient = (comp * 171) >> 11
            first = (valid & (quotient == want)).astype(F32).astype(BF16)
            second = (valid & (comp - ORB * quotient == want)).astype(F32).astype(BF16)
            left = dot_nt(couple, first).astype(BF16)
            right = dot_nt(couple, second).astype(BF16)
            for i in range(BRANCH):
                rows = slice(16 * i, 16 * i + 16)
                product = dot(first, left[rows]) * dot(second, right[rows])
                sand_ref[u, h, :, 2 * LANES * i : 2 * LANES * (i + 1)] = product.astype(BF16)

    each_pair(plan, body)


def pace_kernel(plan, tables_ref, out_ref):
    out_ref[...] = tables_ref[...]


def toeplitz_kernel(plan, tables_ref, toep_ref):
    mirror = iota((FREQ, 2 * FREQ), 0) + iota((FREQ, 2 * FREQ), 1) == FREQ
    mirror = mirror.astype(F32).astype(BF16)

    def body(u):
        lags = dot(my_table(plan, tables_ref, u)[BRANCH * 16 :, :], mirror)
        for q in range(plan.momenta):
            for i in range(BRANCH):
                n = q * BRANCH + i
                band = jnp.broadcast_to(lags[n : n + 1], (FREQ, 2 * FREQ))
                band = pltpu.roll(band, 0, 1, stride=1, stride_axis=0)
                toep_ref[u, q, i * FREQ : (i + 1) * FREQ, :] = band.astype(BF16)

    each_pair(plan, body)


def gather_rows(plan, ref, u, y, first, flip=False):
    m, k = divmod(y, plan.mom_dev)
    row, tail = plan.main_row(k, u), plan.tail_row(k, u)
    order = range(plan.half)
    lefts, rights, tails = [], [], []
    for j in reversed(order) if flip else order:
        peer = (first + j) * plan.n_mom + m
        lefts.append(ref[peer, rows_at(row, plan.steps), :])
        rights.append(ref[peer, rows_at(row + plan.steps, plan.steps), :])
        tails.append(ref[peer, rows_at(tail, plan.steps), :])
    tails = jnp.concatenate(tails, axis=0)
    if plan.shift(k):
        tails = pltpu.roll(tails.astype(F32), LANES - plan.shift(k), 1).astype(BF16)
    return jnp.concatenate([jnp.concatenate(lefts, axis=0), jnp.concatenate(rights, axis=0), tails], axis=1)


def half_and_tail(rows, h):
    return jnp.concatenate([rows[:, h * LANES : (h + 1) * LANES], rows[:, 2 * LANES :]], axis=1)


def self_block(plan, u, green, toep_ref, sand_ref, out_ref):
    summed = []
    for i in range(BRANCH):
        rows = slice(i * FREQ, (i + 1) * FREQ)
        band = jnp.concatenate(
            [
                jnp.concatenate([toep_ref[u, (k - y) % plan.momenta, rows, :] for y in range(plan.momenta)], axis=1)
                for k in range(plan.momenta)
            ],
            axis=0,
        )
        summed.append(dot(band, green).astype(BF16))
    left, right = [
        dot_nt(jnp.concatenate([half_and_tail(rows, h) for rows in summed], axis=1), sand_ref[u, h])
        for h in range(2)
    ]
    tails = left[:, LANES:] + right[:, LANES:]
    left, right = left[:, :LANES].astype(BF16), right[:, :LANES].astype(BF16)
    for y in range(plan.momenta):
        m, k = divmod(y, plan.mom_dev)
        row, tail = plan.main_row(k, u), plan.tail_row(k, u)
        rest = tails[y * FREQ : (y + 1) * FREQ]
        if plan.shift(k):
            rest = pltpu.roll(rest, plan.shift(k), 1)
        rest = rest.astype(BF16)
        for j in range(plan.half):
            peer = j * plan.n_mom + m
            here = slice(j * plan.steps, (j + 1) * plan.steps)
            there = slice(y * FREQ + j * plan.steps, y * FREQ + (j + 1) * plan.steps)
            out_ref[peer, rows_at(row, plan.steps), :] = left[there]
            out_ref[peer, rows_at(row + plan.steps, plan.steps), :] = right[there]
            out_ref[peer, rows_at(tail, plan.steps), :] += rest[here]


def clear_tails(plan, out_ref):
    for peer in range(plan.half * plan.n_mom):
        out_ref[peer, plan.main_rows :, :] = jnp.zeros((plan.tail_rows, LANES), BF16)


def self_late_kernel(plan, own, toep_ref, sand_ref, out_ref):
    clear_tails(plan, out_ref)

    def body(u):
        green = [gather_rows(plan, own, u, y, first) for y in range(plan.momenta) for first in (0, plan.half)]
        self_block(plan, u, jnp.concatenate(green, axis=0), toep_ref, sand_ref, out_ref)

    each_pair(plan, body)


def self_early_kernel(plan, own, far, toep_ref, sand_ref, late_ref, out_ref, stage, halo, sems):
    has = (lax.axis_index("energy") // plan.group > 0).astype(F32).astype(BF16)
    near = plan.half * plan.n_mom
    load = pltpu.make_async_copy(far, halo, sems.at[0])
    load.start()
    upper = pltpu.make_async_copy(late_ref, out_ref.at[near:], sems.at[1])
    upper.start()
    clear_tails(plan, stage)
    load.wait()

    def body(u):
        green = []
        for y in range(plan.momenta):
            green.append(gather_rows(plan, halo, u, y, 0) * has)
            green.append(gather_rows(plan, own, u, y, 0))
        self_block(plan, u, jnp.concatenate(green, axis=0), toep_ref, sand_ref, stage)

    each_pair(plan, body)
    lower = pltpu.make_async_copy(stage, out_ref.at[:near], sems.at[2])
    lower.start()
    lower.wait()
    upper.wait()


def lag_sums(plan, u, partner, green, sand_ref, store):
    partner, green = jnp.concatenate(partner, axis=0), jnp.concatenate(green, axis=0)
    left, right = [dot(half_and_tail(partner, h), sand_ref[u, h]) for h in range(2)]
    for i in range(BRANCH):
        here = slice(2 * LANES * i, 2 * LANES * i + LANES)
        rest = slice(2 * LANES * i + LANES, 2 * LANES * (i + 1))
        applied = jnp.concatenate([left[:, here], right[:, here], left[:, rest] + right[:, rest]], axis=1)
        lagged = dot_nt(applied.astype(BF16), green)
        for q in range(plan.momenta):
            acc = None
            for k in range(plan.momenta):
                y = (k + q) % plan.momenta
                part = lagged[k * FREQ : (k + 1) * FREQ, y * 2 * FREQ : (y + 1) * 2 * FREQ]
                acc = part if acc is None else acc + part
            acc = pltpu.roll(acc, FREQ + 1, 1, stride=1, stride_axis=0)
            store(q, i, jnp.sum(acc, axis=0, keepdims=True))


def phonon_early_kernel(plan, own, partner_ref, sand_ref, out_ref):
    def body(u):
        partner = [gather_rows(plan, partner_ref, u, k, 0, flip=True) for k in range(plan.momenta)]
        green = [gather_rows(plan, own, u, y, first) for y in range(plan.momenta) for first in (0, plan.half)]

        def store(q, i, lags):
            out_ref[u, q * BRANCH + i : q * BRANCH + i + 1, :] = lags

        lag_sums(plan, u, partner, green, sand_ref, store)

    each_pair(plan, body)


def phonon_late_kernel(plan, own, halo, partner_ref, sand_ref, early_ref, *refs, scale):
    outs, sums = refs[:-1], refs[-1]
    group = lax.axis_index("energy") // plan.group
    me = lax.axis_index("mom")
    has = (group < plan.n_groups - 1).astype(F32).astype(BF16)

    def body(u):
        partner = [gather_rows(plan, partner_ref, u, k, plan.half, flip=True) for k in range(plan.momenta)]
        green = []
        for y in range(plan.momenta):
            green.append(gather_rows(plan, own, u, y, plan.half))
            green.append(gather_rows(plan, halo, u, y, 0) * has)

        def store(q, i, lags):
            n = q * BRANCH + i
            side, row = divmod(n, plan.mom_dev * BRANCH)
            sums[u, side, row : row + 1, :] = (lags + early_ref[u, n : n + 1, :]) * scale

        lag_sums(plan, u, partner, green, sand_ref, store)

    each_pair(plan, body)
    for d in range(plan.n_groups):
        for t in range(plan.n_mom):
            for b in range(plan.sub):
                outs[d * plan.n_mom + t][b] = sums[(group ^ d) * plan.sub + b, me ^ t]


def collect(plan, parts, out_ref):
    me = lax.axis_index("mom")
    for d in range(plan.n_mom):
        total = sum(ref[...] for ref in parts[d :: plan.n_mom])
        for b in range(plan.sub):
            pair = (me ^ d) * plan.sub + b
            for q in range(plan.mom_dev):
                rows = [total[b, q * BRANCH + i : q * BRANCH + i + 1, :FREQ] for i in range(BRANCH)]
                out_ref[q, pl.ds(pair, 1), :] = jnp.concatenate(rows, axis=1)


def unpack_kernel(plan, wire, *refs):
    *parts, out_ref, lags_hbm, tiles, lags, sems, lag_sem = refs
    collect(plan, parts, lags)
    lag_copy = pltpu.make_async_copy(lags, lags_hbm, lag_sem)
    lag_copy.start()
    swap = swap_matrix(TILE, plan.steps)

    def rows_of(row):
        return jnp.concatenate([wire[peer, row : row + plan.steps, :] for peer in range(plan.peers)], axis=0)

    tails = {}
    for first in range(0, plan.mom_dev * plan.own, SLOTS):
        moved = dot(swap, rows_of(plan.main_rows + first // SLOTS * plan.steps))
        for t in range(SLOTS):
            tails[first + t] = moved[:, t * TAIL : (t + 1) * TAIL]
    copies = []
    for k in range(plan.mom_dev):
        for h in range(plan.pairs // TILE):
            row = plan.main_row(k, h)
            moved = dot(swap, jnp.concatenate([rows_of(row), rows_of(row + plan.steps)], axis=1))
            tail = tails[k * plan.own + h]
            moved = jnp.concatenate([moved[:, :LANES], tail[:, :REST], moved[:, LANES:], tail[:, REST:]], axis=1)
            tiles[k, h] = moved.astype(BF16).reshape(plan.steps, TILE, COMP)
            copy = pltpu.make_async_copy(
                tiles.at[k, h], out_ref.at[k, :, TILE * h : TILE * (h + 1), :], sems.at[k, h]
            )
            copy.start()
            copies.append(copy)
    for copy in copies:
        copy.wait()
    lag_copy.wait()


ANY = pl.BlockSpec(memory_space=pl.ANY)
HBM = pl.BlockSpec(memory_space=pltpu.HBM)
VMEM = pl.BlockSpec(memory_space=pltpu.VMEM)


def call(plan, kernel, out_shape, *args, in_specs=None, out_specs=None, scratch=(), flops=1, grant=None):
    outs = jax.tree.map(lambda _: VMEM, out_shape)
    return pl.pallas_call(
        functools.partial(kernel, plan),
        out_shape=out_shape,
        in_specs=in_specs or [VMEM] * len(args),
        out_specs=out_specs or outs,
        scratch_shapes=list(scratch),
        compiler_params=pltpu.CompilerParams(vmem_limit_bytes=grant or SMALL_GRANT * max(1, plan.own // 4)),
        cost_estimate=pl.CostEstimate(flops=flops, bytes_accessed=1, transcendentals=0),
    )(*args)


def shape(dims, dtype):
    return jax.ShapeDtypeStruct(dims, dtype)


def in_hbm(struct):
    return pltpu.HBM(struct.shape, struct.dtype)


def shards(lesser_green, partner, phonon_green, coupling):
    n_energy, n_mom = lax.axis_size("energy"), lax.axis_size("mom")
    plan = Plan(lesser_green, phonon_green, n_energy, n_mom)
    axes = ("energy", "mom")
    me = lax.axis_index("mom")
    s = lax.axis_index("energy") // plan.group
    wire = shape((plan.peers, plan.rows, LANES), BF16)
    half_peers = plan.half * n_mom
    groups = [[g * plan.peers + i for i in range(plan.peers)] for g in range(plan.n_groups)]
    tiles = (plan.mom_dev, plan.pairs // TILE)

    def exchange(blocks):
        return lax.all_to_all(blocks, axes, split_axis=0, concat_axis=0, axis_index_groups=groups, tiled=True)

    def swap_groups(values, other):
        route = []
        for e in range(n_energy):
            g, j = divmod(e, plan.group)
            to = other(g) if 0 <= other(g) < plan.n_groups else g
            route.append((e, to * plan.group + j))
        return lax.ppermute(values, "energy", route)

    staging = [pltpu.VMEM(wire.shape, BF16), pltpu.SemaphoreType.DMA((tiles[0] * tiles[1] + 1,))]
    tile_scratch = [pltpu.VMEM(tiles + (plan.steps, TILE, COMP), BF16), pltpu.SemaphoreType.DMA(tiles)]
    half_wire = shape((half_peers, plan.rows, LANES), BF16)
    own = exchange(
        call(
            plan,
            pack_own_kernel,
            in_hbm(wire),
            lesser_green,
            in_specs=[HBM],
            out_specs=HBM,
            scratch=staging + tile_scratch,
            grant=LARGE_GRANT,
        )
    )

    lag_count = plan.momenta * BRANCH
    lag_rows = -(-lag_count // 16) * 16
    couple = coupling.reshape(plan.pairs_dev, BRANCH, ORB, ORB)
    couple = jnp.pad(couple, ((0, 0), (0, 0), (0, 16 - ORB), (0, FREQ - ORB)))
    phonon = phonon_green.reshape(plan.momenta, plan.pairs_dev, BRANCH, FREQ)
    phonon = jnp.moveaxis(phonon, 1, 0).reshape(plan.pairs_dev, lag_count, FREQ)
    phonon = jnp.pad(phonon, ((0, 0), (0, lag_rows - lag_count), (0, 0)))
    table = jnp.concatenate([couple.reshape(plan.pairs_dev, BRANCH * 16, FREQ), phonon], axis=1)
    table = lax.dynamic_slice_in_dim(table, me * plan.sub, plan.sub, axis=0)
    tables = [table]
    for d in range(1, plan.n_groups):
        tables.append(swap_groups(table, functools.partial(lambda d, g: g ^ d, d)))
    tables = jnp.concatenate(tables, axis=0)
    sand = call(
        plan, sandwich_kernel, shape((plan.own, 2, 2 * LANES, BRANCH * 2 * LANES), BF16), tables
    )
    chunk = max(1, 256 // plan.pairs)
    source = (jnp.arange(chunk)[:, None] * plan.pairs + partner[None, :]).reshape(-1)
    take = (source[:, None] == jnp.arange(chunk * plan.pairs)[None, :]).astype(BF16)
    partner_wire = call(
        plan,
        pack_partner_kernel,
        in_hbm(wire),
        take,
        lesser_green,
        out_specs=HBM,
        scratch=staging + [pltpu.VMEM(lesser_green.shape, BF16)],
    )
    own, tables, sand, partner_wire = lax.optimization_barrier((own, tables, sand, partner_wire))

    odd = s % 2

    def edge(side):
        return lax.dynamic_slice_in_dim(own, side * half_peers, half_peers, axis=0)

    before = after = inner = swap_groups(edge(1 - odd), lambda g: g ^ 1)
    if plan.n_groups > 2:
        outer = swap_groups(edge(odd), lambda g: ((g - 1) ^ 1) + 1)
        before = jnp.where(odd == 1, inner, outer)
        after = jnp.where(odd == 1, outer, inner)

    paced = call(plan, pace_kernel, shape(tables.shape, BF16), tables, flops=LONG)
    paced, partner_wire = lax.optimization_barrier((paced, partner_wire))
    partner_blocks = exchange(partner_wire)
    toep = call(
        plan,
        toeplitz_kernel,
        shape((plan.own, plan.momenta, BRANCH * FREQ, 2 * FREQ), BF16),
        tables,
        flops=LONG,
    )

    late = call(plan, self_late_kernel, half_wire, own, toep, sand)
    sigma = call(
        plan,
        self_early_kernel,
        in_hbm(wire),
        own,
        before,
        toep,
        sand,
        late,
        in_specs=[VMEM, ANY, VMEM, VMEM, VMEM],
        out_specs=HBM,
        scratch=[
            pltpu.VMEM(half_wire.shape, BF16),
            pltpu.VMEM(half_wire.shape, BF16),
            pltpu.SemaphoreType.DMA((3,)),
        ],
        flops=LONG,
    )
    arrived = exchange(sigma)

    scale = (plan.momenta * n_energy * plan.steps * COMP) ** -0.5
    early = call(
        plan,
        phonon_early_kernel,
        shape((plan.own, lag_count, LANES), F32),
        own,
        partner_blocks,
        sand,
    )
    side_rows = plan.mom_dev * BRANCH
    parts = list(call(
        plan,
        functools.partial(phonon_late_kernel, scale=scale),
        [shape((plan.sub, side_rows, LANES), F32)] * (plan.n_groups * n_mom),
        own,
        after,
        partner_blocks,
        sand,
        early,
        scratch=[pltpu.VMEM((plan.own, n_mom, side_rows, LANES), F32)],
    ))
    for d in range(plan.n_groups):
        for t in range(n_mom):
            if d or t:
                route = []
                for e in range(n_energy):
                    g, j = divmod(e, plan.group)
                    for m in range(n_mom):
                        route.append((e * n_mom + m, ((g ^ d) * plan.group + j) * n_mom + (m ^ t)))
                parts[d * n_mom + t] = lax.ppermute(parts[d * n_mom + t], axes, route)
    return call(
        plan,
        unpack_kernel,
        [
            shape(lesser_green.shape, BF16),
            shape((plan.mom_dev, plan.pairs_dev, BRANCH * FREQ), F32),
        ],
        arrived,
        *parts,
        out_specs=[ANY, ANY],
        scratch=[
            pltpu.VMEM(tiles + (plan.steps, TILE, COMP), BF16),
            pltpu.VMEM((plan.mom_dev, plan.pairs_dev, BRANCH * FREQ), F32),
            pltpu.SemaphoreType.DMA(tiles),
            pltpu.SemaphoreType.DMA,
        ],
    )


def solution(mesh):
    in_specs = (P("mom", "energy", None, None), P(), P(None, "energy", None), P("energy", None))
    out_specs = (P("mom", "energy", None, None), P("mom", "energy", None))
    return jax.shard_map(shards, mesh=mesh, in_specs=in_specs, out_specs=out_specs, check_vma=False)
```

```python
import functools

import jax
import jax.numpy as jnp
from jax import lax
from jax.experimental import pallas as pl
from jax.experimental.pallas import tpu as pltpu
from jax.sharding import PartitionSpec as P

ORB = 12
BRANCH = 3
FREQ = 64
COMP = 288
SQUARE = ORB * ORB
LANES = 128
REST = SQUARE - LANES
TAIL = 2 * REST
SLOTS = LANES // TAIL
TILE = 16
SMALL_GRANT = 16 * 1024 * 1024
LARGE_GRANT = 60 * 1024 * 1024
LONG = 100_000_000_000

BF16 = jnp.bfloat16
F32 = jnp.float32
I32 = jnp.int32


class Plan:
    def __init__(self, green, phonon, n_energy, n_mom):
        self.n_energy, self.n_mom = n_energy, n_mom
        self.mom_dev, self.steps, self.pairs, _ = green.shape
        self.momenta = self.mom_dev * n_mom
        self.pairs_dev = phonon.shape[1]
        self.half = FREQ // self.steps
        self.group = 2 * self.half
        self.n_groups = n_energy // self.group
        self.peers = self.group * n_mom
        self.sub = self.pairs_dev // n_mom
        self.own = self.n_groups * self.sub
        self.main_rows = self.mom_dev * self.own * 2 * self.steps
        self.tail_rows = self.mom_dev * self.own // SLOTS * self.steps
        self.rows = self.main_rows + self.tail_rows
        assert self.half * self.steps == FREQ and n_energy % self.group == 0
        assert self.n_groups & (self.n_groups - 1) == 0
        assert self.pairs_dev == n_mom and self.group * self.pairs_dev == TILE
        assert self.mom_dev * self.own % SLOTS == 0 and self.n_groups % 2 == 0

    def main_row(self, k, u):
        return (k * self.own + u) * 2 * self.steps

    def tail_row(self, k, u):
        return self.main_rows + (k * self.own + u) // SLOTS * self.steps

    def shift(self, k):
        return k * self.own % SLOTS * TAIL


def dot(a, b):
    return lax.dot_general(a, b, (((1,), (0,)), ((), ())), preferred_element_type=F32)


def dot_nt(a, b):
    return lax.dot_general(a, b, (((1,), (1,)), ((), ())), preferred_element_type=F32)


def iota(dims, axis):
    return lax.broadcasted_iota(I32, dims, axis)


def swap_matrix(outer, inner, flip=False):
    n = outer * inner
    row, col = iota((n, n), 0), iota((n, n), 1)
    place = row & (outer - 1)
    source = (outer - 1 - place if flip else place) * inner + (row >> (outer.bit_length() - 1))
    return (col == source).astype(F32).astype(BF16)


def pack_rows(plan, load, out_ref, stage, sems, flip=False):
    swap = swap_matrix(plan.steps, TILE, flip)
    copies = []

    def send(first, count):
        rows = slice(first, first + count)
        copy = pltpu.make_async_copy(stage.at[:, rows, :], out_ref.at[:, rows, :], sems.at[len(copies)])
        copy.start()
        copies.append(copy)

    def put(row, moved):
        for peer in range(plan.peers):
            stage[peer, row : row + plan.steps, :] = moved[peer * plan.steps : (peer + 1) * plan.steps]

    tails = []
    for k in range(plan.mom_dev):
        for h in range(plan.pairs // TILE):
            rows = load(k, h)
            halves = jnp.concatenate([rows[:, :LANES], rows[:, SQUARE : SQUARE + LANES]], axis=1)
            tails += [rows[:, LANES:SQUARE], rows[:, SQUARE + LANES :]]
            moved = dot(swap, halves).astype(BF16)
            row = plan.main_row(k, h)
            put(row, moved[:, :LANES])
            put(row + plan.steps, moved[:, LANES:])
            send(row, 2 * plan.steps)
    for n in range(0, len(tails), 2 * SLOTS):
        joined = jnp.concatenate(tails[n : n + 2 * SLOTS], axis=1)
        put(plan.main_rows + n // (2 * SLOTS) * plan.steps, dot(swap, joined).astype(BF16))
    send(plan.main_rows, plan.tail_rows)
    for copy in copies:
        copy.wait()


def pack_own_kernel(plan, green_ref, out_ref, stage, out_sems, tiles, sems):
    copies = {}
    for k in range(plan.mom_dev):
        for h in range(plan.pairs // TILE):
            copies[k, h] = pltpu.make_async_copy(
                green_ref.at[k, :, TILE * h : TILE * (h + 1), :], tiles.at[k, h], sems.at[k, h]
            )
            copies[k, h].start()

    def load(k, h):
        copies[k, h].wait()
        return tiles[k, h].reshape(plan.steps * TILE, COMP)

    pack_rows(plan, load, out_ref, stage, out_sems)


def pack_partner_kernel(plan, take_ref, green_ref, out_ref, stage, sems, taken):
    chunk = take_ref.shape[0] // plan.pairs
    take = take_ref[...]
    for k in range(plan.mom_dev):
        for e in range(0, plan.steps, chunk):
            rows = green_ref[k, e : e + chunk].reshape(chunk * plan.pairs, COMP)
            taken[k, e : e + chunk] = dot(take, rows).astype(BF16).reshape(chunk, plan.pairs, COMP)

    def load(k, h):
        return taken[k, :, TILE * h : TILE * (h + 1), :].reshape(plan.steps * TILE, COMP)

    pack_rows(plan, load, out_ref, stage, sems, flip=True)


def each_pair(plan, body):
    if plan.own <= 2:
        for u in range(plan.own):
            body(u)
    else:
        lax.fori_loop(0, plan.own, lambda u, _: body(u), None)


def rows_at(row, count):
    return pl.ds(row if isinstance(row, int) else pl.multiple_of(row, count), count)


def my_table(plan, tables_ref, u):
    group = lax.axis_index("energy") // plan.group
    return tables_ref[(u // plan.sub ^ group) * plan.sub + u % plan.sub]


def sandwich_kernel(plan, tables_ref, sand_ref):
    place, want = iota((2 * LANES, 16), 0), iota((2 * LANES, 16), 1)

    def body(u):
        couple = my_table(plan, tables_ref, u)[: BRANCH * 16, :16]
        for h in range(2):
            comp = jnp.where(place < LANES, place, place - (u % SLOTS * TAIL + h * REST))
            valid = (place < LANES) | ((comp >= LANES) & (comp < SQUARE))
            quotient = (comp * 171) >> 11
            first = (valid & (quotient == want)).astype(F32).astype(BF16)
            second = (valid & (comp - ORB * quotient == want)).astype(F32).astype(BF16)
            left = dot_nt(couple, first).astype(BF16)
            right = dot_nt(couple, second).astype(BF16)
            for i in range(BRANCH):
                rows = slice(16 * i, 16 * i + 16)
                product = dot(first, left[rows]) * dot(second, right[rows])
                sand_ref[u, h, :, 2 * LANES * i : 2 * LANES * (i + 1)] = product.astype(BF16)

    each_pair(plan, body)


def pace_kernel(plan, tables_ref, out_ref):
    out_ref[...] = tables_ref[...]


def toeplitz_kernel(plan, tables_ref, toep_ref):
    mirror = iota((FREQ, 2 * FREQ), 0) + iota((FREQ, 2 * FREQ), 1) == FREQ
    mirror = mirror.astype(F32).astype(BF16)

    def body(u):
        lags = dot(my_table(plan, tables_ref, u)[BRANCH * 16 :, :], mirror)
        for q in range(plan.momenta):
            for i in range(BRANCH):
                n = q * BRANCH + i
                band = jnp.broadcast_to(lags[n : n + 1], (FREQ, 2 * FREQ))
                band = pltpu.roll(band, 0, 1, stride=1, stride_axis=0)
                toep_ref[u, q, i * FREQ : (i + 1) * FREQ, :] = band.astype(BF16)

    each_pair(plan, body)


def gather_rows(plan, ref, u, y, first, flip=False):
    m, k = divmod(y, plan.mom_dev)
    row, tail = plan.main_row(k, u), plan.tail_row(k, u)
    order = range(plan.half)
    lefts, rights, tails = [], [], []
    for j in reversed(order) if flip else order:
        peer = (first + j) * plan.n_mom + m
        lefts.append(ref[peer, rows_at(row, plan.steps), :])
        rights.append(ref[peer, rows_at(row + plan.steps, plan.steps), :])
        tails.append(ref[peer, rows_at(tail, plan.steps), :])
    tails = jnp.concatenate(tails, axis=0)
    if plan.shift(k):
        tails = pltpu.roll(tails.astype(F32), LANES - plan.shift(k), 1).astype(BF16)
    return jnp.concatenate([jnp.concatenate(lefts, axis=0), jnp.concatenate(rights, axis=0), tails], axis=1)


def half_and_tail(rows, h):
    return jnp.concatenate([rows[:, h * LANES : (h + 1) * LANES], rows[:, 2 * LANES :]], axis=1)


def self_block(plan, u, green, toep_ref, sand_ref, out_ref):
    summed = []
    for i in range(BRANCH):
        rows = slice(i * FREQ, (i + 1) * FREQ)
        band = jnp.concatenate(
            [
                jnp.concatenate([toep_ref[u, (k - y) % plan.momenta, rows, :] for y in range(plan.momenta)], axis=1)
                for k in range(plan.momenta)
            ],
            axis=0,
        )
        summed.append(dot(band, green).astype(BF16))
    left, right = [
        dot_nt(jnp.concatenate([half_and_tail(rows, h) for rows in summed], axis=1), sand_ref[u, h])
        for h in range(2)
    ]
    tails = left[:, LANES:] + right[:, LANES:]
    left, right = left[:, :LANES].astype(BF16), right[:, :LANES].astype(BF16)
    for y in range(plan.momenta):
        m, k = divmod(y, plan.mom_dev)
        row, tail = plan.main_row(k, u), plan.tail_row(k, u)
        rest = tails[y * FREQ : (y + 1) * FREQ]
        if plan.shift(k):
            rest = pltpu.roll(rest, plan.shift(k), 1)
        rest = rest.astype(BF16)
        for j in range(plan.half):
            peer = j * plan.n_mom + m
            here = slice(j * plan.steps, (j + 1) * plan.steps)
            there = slice(y * FREQ + j * plan.steps, y * FREQ + (j + 1) * plan.steps)
            out_ref[peer, rows_at(row, plan.steps), :] = left[there]
            out_ref[peer, rows_at(row + plan.steps, plan.steps), :] = right[there]
            out_ref[peer, rows_at(tail, plan.steps), :] += rest[here]


def clear_tails(plan, out_ref):
    for peer in range(plan.half * plan.n_mom):
        out_ref[peer, plan.main_rows :, :] = jnp.zeros((plan.tail_rows, LANES), BF16)


def self_late_kernel(plan, own, toep_ref, sand_ref, out_ref):
    clear_tails(plan, out_ref)

    def body(u):
        green = [gather_rows(plan, own, u, y, first) for y in range(plan.momenta) for first in (0, plan.half)]
        self_block(plan, u, jnp.concatenate(green, axis=0), toep_ref, sand_ref, out_ref)

    each_pair(plan, body)


def self_early_kernel(plan, own, far, toep_ref, sand_ref, late_ref, out_ref, stage, halo, sems):
    has = (lax.axis_index("energy") // plan.group > 0).astype(F32).astype(BF16)
    near = plan.half * plan.n_mom
    load = pltpu.make_async_copy(far, halo, sems.at[0])
    load.start()
    upper = pltpu.make_async_copy(late_ref, out_ref.at[near:], sems.at[1])
    upper.start()
    clear_tails(plan, stage)
    load.wait()

    def body(u):
        green = []
        for y in range(plan.momenta):
            green.append(gather_rows(plan, halo, u, y, 0) * has)
            green.append(gather_rows(plan, own, u, y, 0))
        self_block(plan, u, jnp.concatenate(green, axis=0), toep_ref, sand_ref, stage)

    each_pair(plan, body)
    lower = pltpu.make_async_copy(stage, out_ref.at[:near], sems.at[2])
    lower.start()
    lower.wait()
    upper.wait()


def lag_sums(plan, u, partner, green, sand_ref, store):
    partner, green = jnp.concatenate(partner, axis=0), jnp.concatenate(green, axis=0)
    left, right = [dot(half_and_tail(partner, h), sand_ref[u, h]) for h in range(2)]
    for i in range(BRANCH):
        here = slice(2 * LANES * i, 2 * LANES * i + LANES)
        rest = slice(2 * LANES * i + LANES, 2 * LANES * (i + 1))
        applied = jnp.concatenate([left[:, here], right[:, here], left[:, rest] + right[:, rest]], axis=1)
        lagged = dot_nt(applied.astype(BF16), green)
        for q in range(plan.momenta):
            acc = None
            for k in range(plan.momenta):
                y = (k + q) % plan.momenta
                part = lagged[k * FREQ : (k + 1) * FREQ, y * 2 * FREQ : (y + 1) * 2 * FREQ]
                acc = part if acc is None else acc + part
            acc = pltpu.roll(acc, FREQ + 1, 1, stride=1, stride_axis=0)
            store(q, i, jnp.sum(acc, axis=0, keepdims=True))


def phonon_early_kernel(plan, own, partner_ref, sand_ref, out_ref):
    def body(u):
        partner = [gather_rows(plan, partner_ref, u, k, 0, flip=True) for k in range(plan.momenta)]
        green = [gather_rows(plan, own, u, y, first) for y in range(plan.momenta) for first in (0, plan.half)]

        def store(q, i, lags):
            out_ref[u, q * BRANCH + i : q * BRANCH + i + 1, :] = lags

        lag_sums(plan, u, partner, green, sand_ref, store)

    each_pair(plan, body)


def phonon_late_kernel(plan, own, halo, partner_ref, sand_ref, early_ref, *refs, scale):
    outs, sums = refs[:-1], refs[-1]
    group = lax.axis_index("energy") // plan.group
    me = lax.axis_index("mom")
    has = (group < plan.n_groups - 1).astype(F32).astype(BF16)

    def body(u):
        partner = [gather_rows(plan, partner_ref, u, k, plan.half, flip=True) for k in range(plan.momenta)]
        green = []
        for y in range(plan.momenta):
            green.append(gather_rows(plan, own, u, y, plan.half))
            green.append(gather_rows(plan, halo, u, y, 0) * has)

        def store(q, i, lags):
            n = q * BRANCH + i
            side, row = divmod(n, plan.mom_dev * BRANCH)
            sums[u, side, row : row + 1, :] = (lags + early_ref[u, n : n + 1, :]) * scale

        lag_sums(plan, u, partner, green, sand_ref, store)

    each_pair(plan, body)
    for d in range(plan.n_groups):
        for t in range(plan.n_mom):
            for b in range(plan.sub):
                outs[d * plan.n_mom + t][b] = sums[(group ^ d) * plan.sub + b, me ^ t]


def collect(plan, parts, out_ref):
    me = lax.axis_index("mom")
    for d in range(plan.n_mom):
        total = sum(ref[...] for ref in parts[d :: plan.n_mom])
        for b in range(plan.sub):
            pair = (me ^ d) * plan.sub + b
            for q in range(plan.mom_dev):
                rows = [total[b, q * BRANCH + i : q * BRANCH + i + 1, :FREQ] for i in range(BRANCH)]
                out_ref[q, pl.ds(pair, 1), :] = jnp.concatenate(rows, axis=1)


def unpack_kernel(plan, wire, *refs):
    *parts, out_ref, lags_hbm, tiles, lags, sems, lag_sem = refs
    collect(plan, parts, lags)
    lag_copy = pltpu.make_async_copy(lags, lags_hbm, lag_sem)
    lag_copy.start()
    swap = swap_matrix(TILE, plan.steps)

    def rows_of(row):
        return jnp.concatenate([wire[peer, row : row + plan.steps, :] for peer in range(plan.peers)], axis=0)

    tails = {}
    for first in range(0, plan.mom_dev * plan.own, SLOTS):
        moved = dot(swap, rows_of(plan.main_rows + first // SLOTS * plan.steps))
        for t in range(SLOTS):
            tails[first + t] = moved[:, t * TAIL : (t + 1) * TAIL]
    copies = []
    for k in range(plan.mom_dev):
        for h in range(plan.pairs // TILE):
            row = plan.main_row(k, h)
            moved = dot(swap, jnp.concatenate([rows_of(row), rows_of(row + plan.steps)], axis=1))
            tail = tails[k * plan.own + h]
            moved = jnp.concatenate([moved[:, :LANES], tail[:, :REST], moved[:, LANES:], tail[:, REST:]], axis=1)
            tiles[k, h] = moved.astype(BF16).reshape(plan.steps, TILE, COMP)
            copy = pltpu.make_async_copy(
                tiles.at[k, h], out_ref.at[k, :, TILE * h : TILE * (h + 1), :], sems.at[k, h]
            )
            copy.start()
            copies.append(copy)
    for copy in copies:
        copy.wait()
    lag_copy.wait()


ANY = pl.BlockSpec(memory_space=pl.ANY)
HBM = pl.BlockSpec(memory_space=pltpu.HBM)
VMEM = pl.BlockSpec(memory_space=pltpu.VMEM)


def call(plan, kernel, out_shape, *args, in_specs=None, out_specs=None, scratch=(), flops=1, grant=None):
    outs = jax.tree.map(lambda _: VMEM, out_shape)
    return pl.pallas_call(
        functools.partial(kernel, plan),
        out_shape=out_shape,
        in_specs=in_specs or [VMEM] * len(args),
        out_specs=out_specs or outs,
        scratch_shapes=list(scratch),
        compiler_params=pltpu.CompilerParams(vmem_limit_bytes=grant or SMALL_GRANT * max(1, plan.own // 4)),
        cost_estimate=pl.CostEstimate(flops=flops, bytes_accessed=1, transcendentals=0),
    )(*args)


def shape(dims, dtype):
    return jax.ShapeDtypeStruct(dims, dtype)


def in_hbm(struct):
    return pltpu.HBM(struct.shape, struct.dtype)


def shards(lesser_green, partner, phonon_green, coupling):
    n_energy, n_mom = lax.axis_size("energy"), lax.axis_size("mom")
    plan = Plan(lesser_green, phonon_green, n_energy, n_mom)
    axes = ("energy", "mom")
    me = lax.axis_index("mom")
    s = lax.axis_index("energy") // plan.group
    wire = shape((plan.peers, plan.rows, LANES), BF16)
    half_peers = plan.half * n_mom
    groups = [[g * plan.peers + i for i in range(plan.peers)] for g in range(plan.n_groups)]
    tiles = (plan.mom_dev, plan.pairs // TILE)

    def exchange(blocks):
        return lax.all_to_all(blocks, axes, split_axis=0, concat_axis=0, axis_index_groups=groups, tiled=True)

    def swap_groups(values, other):
        route = []
        for e in range(n_energy):
            g, j = divmod(e, plan.group)
            to = other(g) if 0 <= other(g) < plan.n_groups else g
            route.append((e, to * plan.group + j))
        return lax.ppermute(values, "energy", route)

    staging = [pltpu.VMEM(wire.shape, BF16), pltpu.SemaphoreType.DMA((tiles[0] * tiles[1] + 1,))]
    tile_scratch = [pltpu.VMEM(tiles + (plan.steps, TILE, COMP), BF16), pltpu.SemaphoreType.DMA(tiles)]
    half_wire = shape((half_peers, plan.rows, LANES), BF16)
    own = exchange(
        call(
            plan,
            pack_own_kernel,
            in_hbm(wire),
            lesser_green,
            in_specs=[HBM],
            out_specs=HBM,
            scratch=staging + tile_scratch,
            grant=LARGE_GRANT,
        )
    )

    lag_count = plan.momenta * BRANCH
    lag_rows = -(-lag_count // 16) * 16
    couple = coupling.reshape(plan.pairs_dev, BRANCH, ORB, ORB)
    couple = jnp.pad(couple, ((0, 0), (0, 0), (0, 16 - ORB), (0, FREQ - ORB)))
    phonon = phonon_green.reshape(plan.momenta, plan.pairs_dev, BRANCH, FREQ)
    phonon = jnp.moveaxis(phonon, 1, 0).reshape(plan.pairs_dev, lag_count, FREQ)
    phonon = jnp.pad(phonon, ((0, 0), (0, lag_rows - lag_count), (0, 0)))
    table = jnp.concatenate([couple.reshape(plan.pairs_dev, BRANCH * 16, FREQ), phonon], axis=1)
    table = lax.dynamic_slice_in_dim(table, me * plan.sub, plan.sub, axis=0)
    tables = [table]
    for d in range(1, plan.n_groups):
        tables.append(swap_groups(table, functools.partial(lambda d, g: g ^ d, d)))
    tables = jnp.concatenate(tables, axis=0)
    sand = call(
        plan, sandwich_kernel, shape((plan.own, 2, 2 * LANES, BRANCH * 2 * LANES), BF16), tables
    )
    chunk = max(1, 256 // plan.pairs)
    source = (jnp.arange(chunk)[:, None] * plan.pairs + partner[None, :]).reshape(-1)
    take = (source[:, None] == jnp.arange(chunk * plan.pairs)[None, :]).astype(BF16)
    partner_wire = call(
        plan,
        pack_partner_kernel,
        in_hbm(wire),
        take,
        lesser_green,
        out_specs=HBM,
        scratch=staging + [pltpu.VMEM(lesser_green.shape, BF16)],
    )
    own, tables, sand, partner_wire = lax.optimization_barrier((own, tables, sand, partner_wire))

    odd = s % 2

    def edge(side):
        return lax.dynamic_slice_in_dim(own, side * half_peers, half_peers, axis=0)

    before = after = inner = swap_groups(edge(1 - odd), lambda g: g ^ 1)
    if plan.n_groups > 2:
        outer = swap_groups(edge(odd), lambda g: ((g - 1) ^ 1) + 1)
        before = jnp.where(odd == 1, inner, outer)
        after = jnp.where(odd == 1, outer, inner)

    paced = call(plan, pace_kernel, shape(tables.shape, BF16), tables, flops=LONG)
    paced, partner_wire = lax.optimization_barrier((paced, partner_wire))
    partner_blocks = exchange(partner_wire)
    toep = call(
        plan,
        toeplitz_kernel,
        shape((plan.own, plan.momenta, BRANCH * FREQ, 2 * FREQ), BF16),
        tables,
    )

    late = call(plan, self_late_kernel, half_wire, own, toep, sand)
    sigma = call(
        plan,
        self_early_kernel,
        in_hbm(wire),
        own,
        before,
        toep,
        sand,
        late,
        in_specs=[VMEM, ANY, VMEM, VMEM, VMEM],
        out_specs=HBM,
        scratch=[
            pltpu.VMEM(half_wire.shape, BF16),
            pltpu.VMEM(half_wire.shape, BF16),
            pltpu.SemaphoreType.DMA((3,)),
        ],
        flops=LONG,
    )
    arrived = exchange(sigma)

    scale = (plan.momenta * n_energy * plan.steps * COMP) ** -0.5
    early = call(
        plan,
        phonon_early_kernel,
        shape((plan.own, lag_count, LANES), F32),
        own,
        partner_blocks,
        sand,
    )
    side_rows = plan.mom_dev * BRANCH
    parts = list(call(
        plan,
        functools.partial(phonon_late_kernel, scale=scale),
        [shape((plan.sub, side_rows, LANES), F32)] * (plan.n_groups * n_mom),
        own,
        after,
        partner_blocks,
        sand,
        early,
        scratch=[pltpu.VMEM((plan.own, n_mom, side_rows, LANES), F32)],
    ))
    for d in range(plan.n_groups):
        for t in range(n_mom):
            if d or t:
                route = []
                for e in range(n_energy):
                    g, j = divmod(e, plan.group)
                    for m in range(n_mom):
                        route.append((e * n_mom + m, ((g ^ d) * plan.group + j) * n_mom + (m ^ t)))
                parts[d * n_mom + t] = lax.ppermute(parts[d * n_mom + t], axes, route)
    return call(
        plan,
        unpack_kernel,
        [
            shape(lesser_green.shape, BF16),
            shape((plan.mom_dev, plan.pairs_dev, BRANCH * FREQ), F32),
        ],
        arrived,
        *parts,
        out_specs=[ANY, ANY],
        scratch=[
            pltpu.VMEM(tiles + (plan.steps, TILE, COMP), BF16),
            pltpu.VMEM((plan.mom_dev, plan.pairs_dev, BRANCH * FREQ), F32),
            pltpu.SemaphoreType.DMA(tiles),
            pltpu.SemaphoreType.DMA,
        ],
    )


def solution(mesh):
    in_specs = (P("mom", "energy", None, None), P(), P(None, "energy", None), P("energy", None))
    out_specs = (P("mom", "energy", None, None), P("mom", "energy", None))
    return jax.shard_map(shards, mesh=mesh, in_specs=in_specs, out_specs=out_specs, check_vma=False)
```

```python
import functools

import jax
import jax.numpy as jnp
from jax import lax
from jax.experimental import pallas as pl
from jax.experimental.pallas import tpu as pltpu
from jax.sharding import PartitionSpec as P

ORB = 12
BRANCH = 3
FREQ = 64
COMP = 288
SQUARE = ORB * ORB
LANES = 128
REST = SQUARE - LANES
TAIL = 2 * REST
SLOTS = LANES // TAIL
TILE = 16
SMALL_GRANT = 16 * 1024 * 1024
LARGE_GRANT = 60 * 1024 * 1024
LONG = 100_000_000_000

BF16 = jnp.bfloat16
F32 = jnp.float32
I32 = jnp.int32


class Plan:
    def __init__(self, green, phonon, n_energy, n_mom):
        self.n_energy, self.n_mom = n_energy, n_mom
        self.mom_dev, self.steps, self.pairs, _ = green.shape
        self.momenta = self.mom_dev * n_mom
        self.pairs_dev = phonon.shape[1]
        self.half = FREQ // self.steps
        self.group = 2 * self.half
        self.n_groups = n_energy // self.group
        self.peers = self.group * n_mom
        self.sub = self.pairs_dev // n_mom
        self.own = self.n_groups * self.sub
        self.main_rows = self.mom_dev * self.own * 2 * self.steps
        self.tail_rows = self.mom_dev * self.own // SLOTS * self.steps
        self.rows = self.main_rows + self.tail_rows
        assert self.half * self.steps == FREQ and n_energy % self.group == 0
        assert self.n_groups & (self.n_groups - 1) == 0
        assert self.pairs_dev == n_mom and self.group * self.pairs_dev == TILE
        assert self.mom_dev * self.own % SLOTS == 0 and self.n_groups % 2 == 0

    def main_row(self, k, u):
        return (k * self.own + u) * 2 * self.steps

    def tail_row(self, k, u):
        return self.main_rows + (k * self.own + u) // SLOTS * self.steps

    def shift(self, k):
        return k * self.own % SLOTS * TAIL


def dot(a, b):
    return lax.dot_general(a, b, (((1,), (0,)), ((), ())), preferred_element_type=F32)


def dot_nt(a, b):
    return lax.dot_general(a, b, (((1,), (1,)), ((), ())), preferred_element_type=F32)


def iota(dims, axis):
    return lax.broadcasted_iota(I32, dims, axis)


def swap_matrix(outer, inner, flip=False):
    n = outer * inner
    row, col = iota((n, n), 0), iota((n, n), 1)
    place = row & (outer - 1)
    source = (outer - 1 - place if flip else place) * inner + (row >> (outer.bit_length() - 1))
    return (col == source).astype(F32).astype(BF16)


def pack_rows(plan, load, out_ref, stage, sems, flip=False):
    swap = swap_matrix(plan.steps, TILE, flip)
    copies = []

    def send(first, last):
        rows = slice(first, last)
        copy = pltpu.make_async_copy(stage.at[:, rows, :], out_ref.at[:, rows, :], sems.at[len(copies)])
        copy.start()
        copies.append(copy)

    def put(row, moved):
        for peer in range(plan.peers):
            stage[peer, row : row + plan.steps, :] = moved[peer * plan.steps : (peer + 1) * plan.steps]

    tails = []
    for k in range(plan.mom_dev):
        last = k == plan.mom_dev - 1
        for h in range(plan.pairs // TILE):
            rows = load(k, h)
            halves = jnp.concatenate([rows[:, :LANES], rows[:, SQUARE : SQUARE + LANES]], axis=1)
            tails += [rows[:, LANES:SQUARE], rows[:, SQUARE + LANES :]]
            moved = dot(swap, halves).astype(BF16)
            row = plan.main_row(k, h)
            put(row, moved[:, :LANES])
            put(row + plan.steps, moved[:, LANES:])
        if last:
            for n in range(0, len(tails), 2 * SLOTS):
                joined = jnp.concatenate(tails[n : n + 2 * SLOTS], axis=1)
                put(plan.main_rows + n // (2 * SLOTS) * plan.steps, dot(swap, joined).astype(BF16))
        send(plan.main_row(k, 0), plan.rows if last else plan.main_row(k + 1, 0))
    for copy in copies:
        copy.wait()


def pack_own_kernel(plan, green_ref, out_ref, stage, out_sems, green, sems):
    copies = [pltpu.make_async_copy(green_ref.at[k], green.at[k], sems.at[k]) for k in range(plan.mom_dev)]
    for copy in copies:
        copy.start()

    def load(k, h):
        if h == 0:
            copies[k].wait()
        return green[k, :, TILE * h : TILE * (h + 1), :].reshape(plan.steps * TILE, COMP)

    pack_rows(plan, load, out_ref, stage, out_sems)


def pack_partner_kernel(plan, take_ref, green_ref, out_ref, stage, sems, taken):
    chunk = take_ref.shape[0] // plan.pairs
    take = take_ref[...]
    for k in range(plan.mom_dev):
        for e in range(0, plan.steps, chunk):
            rows = green_ref[k, e : e + chunk].reshape(chunk * plan.pairs, COMP)
            taken[k, e : e + chunk] = dot(take, rows).astype(BF16).reshape(chunk, plan.pairs, COMP)

    def load(k, h):
        return taken[k, :, TILE * h : TILE * (h + 1), :].reshape(plan.steps * TILE, COMP)

    pack_rows(plan, load, out_ref, stage, sems, flip=True)


def each_pair(plan, body):
    if plan.own <= 2:
        for u in range(plan.own):
            body(u)
    else:
        lax.fori_loop(0, plan.own, lambda u, _: body(u), None)


def rows_at(row, count):
    return pl.ds(row if isinstance(row, int) else pl.multiple_of(row, count), count)


def my_table(plan, tables_ref, u):
    group = lax.axis_index("energy") // plan.group
    return tables_ref[(u // plan.sub ^ group) * plan.sub + u % plan.sub]


def sandwich_kernel(plan, tables_ref, sand_ref):
    place, want = iota((2 * LANES, 16), 0), iota((2 * LANES, 16), 1)

    def body(u):
        couple = my_table(plan, tables_ref, u)[: BRANCH * 16, :16]
        for h in range(2):
            comp = jnp.where(place < LANES, place, place - (u % SLOTS * TAIL + h * REST))
            valid = (place < LANES) | ((comp >= LANES) & (comp < SQUARE))
            quotient = (comp * 171) >> 11
            first = (valid & (quotient == want)).astype(F32).astype(BF16)
            second = (valid & (comp - ORB * quotient == want)).astype(F32).astype(BF16)
            left = dot_nt(couple, first).astype(BF16)
            right = dot_nt(couple, second).astype(BF16)
            for i in range(BRANCH):
                rows = slice(16 * i, 16 * i + 16)
                product = dot(first, left[rows]) * dot(second, right[rows])
                sand_ref[u, h, :, 2 * LANES * i : 2 * LANES * (i + 1)] = product.astype(BF16)

    each_pair(plan, body)


def pace_kernel(plan, tables_ref, out_ref):
    out_ref[...] = tables_ref[...]


def toeplitz_kernel(plan, tables_ref, toep_ref):
    mirror = iota((FREQ, 2 * FREQ), 0) + iota((FREQ, 2 * FREQ), 1) == FREQ
    mirror = mirror.astype(F32).astype(BF16)

    def body(u):
        lags = dot(my_table(plan, tables_ref, u)[BRANCH * 16 :, :], mirror)
        for q in range(plan.momenta):
            for i in range(BRANCH):
                n = q * BRANCH + i
                band = jnp.broadcast_to(lags[n : n + 1], (FREQ, 2 * FREQ))
                band = pltpu.roll(band, 0, 1, stride=1, stride_axis=0)
                toep_ref[u, q, i * FREQ : (i + 1) * FREQ, :] = band.astype(BF16)

    each_pair(plan, body)


def gather_rows(plan, ref, u, y, first, flip=False):
    m, k = divmod(y, plan.mom_dev)
    row, tail = plan.main_row(k, u), plan.tail_row(k, u)
    order = range(plan.half)
    lefts, rights, tails = [], [], []
    for j in reversed(order) if flip else order:
        peer = (first + j) * plan.n_mom + m
        lefts.append(ref[peer, rows_at(row, plan.steps), :])
        rights.append(ref[peer, rows_at(row + plan.steps, plan.steps), :])
        tails.append(ref[peer, rows_at(tail, plan.steps), :])
    tails = jnp.concatenate(tails, axis=0)
    if plan.shift(k):
        tails = pltpu.roll(tails.astype(F32), LANES - plan.shift(k), 1).astype(BF16)
    return jnp.concatenate([jnp.concatenate(lefts, axis=0), jnp.concatenate(rights, axis=0), tails], axis=1)


def half_and_tail(rows, h):
    return jnp.concatenate([rows[:, h * LANES : (h + 1) * LANES], rows[:, 2 * LANES :]], axis=1)


def self_block(plan, u, green, toep_ref, sand_ref, out_ref):
    summed = []
    for i in range(BRANCH):
        rows = slice(i * FREQ, (i + 1) * FREQ)
        band = jnp.concatenate(
            [
                jnp.concatenate([toep_ref[u, (k - y) % plan.momenta, rows, :] for y in range(plan.momenta)], axis=1)
                for k in range(plan.momenta)
            ],
            axis=0,
        )
        summed.append(dot(band, green).astype(BF16))
    left, right = [
        dot_nt(jnp.concatenate([half_and_tail(rows, h) for rows in summed], axis=1), sand_ref[u, h])
        for h in range(2)
    ]
    tails = left[:, LANES:] + right[:, LANES:]
    left, right = left[:, :LANES].astype(BF16), right[:, :LANES].astype(BF16)
    for y in range(plan.momenta):
        m, k = divmod(y, plan.mom_dev)
        row, tail = plan.main_row(k, u), plan.tail_row(k, u)
        rest = tails[y * FREQ : (y + 1) * FREQ]
        if plan.shift(k):
            rest = pltpu.roll(rest, plan.shift(k), 1)
        rest = rest.astype(BF16)
        for j in range(plan.half):
            peer = j * plan.n_mom + m
            here = slice(j * plan.steps, (j + 1) * plan.steps)
            there = slice(y * FREQ + j * plan.steps, y * FREQ + (j + 1) * plan.steps)
            out_ref[peer, rows_at(row, plan.steps), :] = left[there]
            out_ref[peer, rows_at(row + plan.steps, plan.steps), :] = right[there]
            out_ref[peer, rows_at(tail, plan.steps), :] += rest[here]


def clear_tails(plan, out_ref):
    for peer in range(plan.half * plan.n_mom):
        out_ref[peer, plan.main_rows :, :] = jnp.zeros((plan.tail_rows, LANES), BF16)


def self_late_kernel(plan, own, toep_ref, sand_ref, out_ref):
    clear_tails(plan, out_ref)

    def body(u):
        green = [gather_rows(plan, own, u, y, first) for y in range(plan.momenta) for first in (0, plan.half)]
        self_block(plan, u, jnp.concatenate(green, axis=0), toep_ref, sand_ref, out_ref)

    each_pair(plan, body)


def self_early_kernel(plan, own, far, toep_ref, sand_ref, late_ref, out_ref, stage, halo, sems):
    has = (lax.axis_index("energy") // plan.group > 0).astype(F32).astype(BF16)
    near = plan.half * plan.n_mom
    load = pltpu.make_async_copy(far, halo, sems.at[0])
    load.start()
    upper = pltpu.make_async_copy(late_ref, out_ref.at[near:], sems.at[1])
    upper.start()
    clear_tails(plan, stage)
    load.wait()

    def body(u):
        green = []
        for y in range(plan.momenta):
            green.append(gather_rows(plan, halo, u, y, 0) * has)
            green.append(gather_rows(plan, own, u, y, 0))
        self_block(plan, u, jnp.concatenate(green, axis=0), toep_ref, sand_ref, stage)

    each_pair(plan, body)
    lower = pltpu.make_async_copy(stage, out_ref.at[:near], sems.at[2])
    lower.start()
    lower.wait()
    upper.wait()


def lag_sums(plan, u, partner, green, sand_ref, store):
    partner, green = jnp.concatenate(partner, axis=0), jnp.concatenate(green, axis=0)
    left, right = [dot(half_and_tail(partner, h), sand_ref[u, h]) for h in range(2)]
    for i in range(BRANCH):
        here = slice(2 * LANES * i, 2 * LANES * i + LANES)
        rest = slice(2 * LANES * i + LANES, 2 * LANES * (i + 1))
        applied = jnp.concatenate([left[:, here], right[:, here], left[:, rest] + right[:, rest]], axis=1)
        lagged = dot_nt(applied.astype(BF16), green)
        for q in range(plan.momenta):
            acc = None
            for k in range(plan.momenta):
                y = (k + q) % plan.momenta
                part = lagged[k * FREQ : (k + 1) * FREQ, y * 2 * FREQ : (y + 1) * 2 * FREQ]
                acc = part if acc is None else acc + part
            acc = pltpu.roll(acc, FREQ + 1, 1, stride=1, stride_axis=0)
            store(q, i, jnp.sum(acc, axis=0, keepdims=True))


def phonon_early_kernel(plan, own, partner_ref, sand_ref, out_ref):
    def body(u):
        partner = [gather_rows(plan, partner_ref, u, k, 0, flip=True) for k in range(plan.momenta)]
        green = [gather_rows(plan, own, u, y, first) for y in range(plan.momenta) for first in (0, plan.half)]

        def store(q, i, lags):
            out_ref[u, q * BRANCH + i : q * BRANCH + i + 1, :] = lags

        lag_sums(plan, u, partner, green, sand_ref, store)

    each_pair(plan, body)


def phonon_late_kernel(plan, own, halo, partner_ref, sand_ref, early_ref, *refs, scale):
    outs, sums = refs[:-1], refs[-1]
    group = lax.axis_index("energy") // plan.group
    me = lax.axis_index("mom")
    has = (group < plan.n_groups - 1).astype(F32).astype(BF16)

    def body(u):
        partner = [gather_rows(plan, partner_ref, u, k, plan.half, flip=True) for k in range(plan.momenta)]
        green = []
        for y in range(plan.momenta):
            green.append(gather_rows(plan, own, u, y, plan.half))
            green.append(gather_rows(plan, halo, u, y, 0) * has)

        def store(q, i, lags):
            n = q * BRANCH + i
            side, row = divmod(n, plan.mom_dev * BRANCH)
            sums[u, side, row : row + 1, :] = (lags + early_ref[u, n : n + 1, :]) * scale

        lag_sums(plan, u, partner, green, sand_ref, store)

    each_pair(plan, body)
    for d in range(plan.n_groups):
        for t in range(plan.n_mom):
            for b in range(plan.sub):
                outs[d * plan.n_mom + t][b] = sums[(group ^ d) * plan.sub + b, me ^ t]


def collect(plan, parts, out_ref):
    me = lax.axis_index("mom")
    for d in range(plan.n_mom):
        total = sum(ref[...] for ref in parts[d :: plan.n_mom])
        for b in range(plan.sub):
            pair = (me ^ d) * plan.sub + b
            for q in range(plan.mom_dev):
                rows = [total[b, q * BRANCH + i : q * BRANCH + i + 1, :FREQ] for i in range(BRANCH)]
                out_ref[q, pl.ds(pair, 1), :] = jnp.concatenate(rows, axis=1)


def unpack_kernel(plan, wire, *refs):
    *parts, out_ref, lags_hbm, tiles, lags, sems, lag_sem = refs
    collect(plan, parts, lags)
    lag_copy = pltpu.make_async_copy(lags, lags_hbm, lag_sem)
    lag_copy.start()
    swap = swap_matrix(TILE, plan.steps)

    def rows_of(row):
        return jnp.concatenate([wire[peer, row : row + plan.steps, :] for peer in range(plan.peers)], axis=0)

    tails = {}
    for first in range(0, plan.mom_dev * plan.own, SLOTS):
        moved = dot(swap, rows_of(plan.main_rows + first // SLOTS * plan.steps))
        for t in range(SLOTS):
            tails[first + t] = moved[:, t * TAIL : (t + 1) * TAIL]
    copies = []
    for k in range(plan.mom_dev):
        for h in range(plan.pairs // TILE):
            row = plan.main_row(k, h)
            moved = dot(swap, jnp.concatenate([rows_of(row), rows_of(row + plan.steps)], axis=1))
            tail = tails[k * plan.own + h]
            moved = jnp.concatenate([moved[:, :LANES], tail[:, :REST], moved[:, LANES:], tail[:, REST:]], axis=1)
            tiles[k, h] = moved.astype(BF16).reshape(plan.steps, TILE, COMP)
            copy = pltpu.make_async_copy(
                tiles.at[k, h], out_ref.at[k, :, TILE * h : TILE * (h + 1), :], sems.at[k, h]
            )
            copy.start()
            copies.append(copy)
    for copy in copies:
        copy.wait()
    lag_copy.wait()


ANY = pl.BlockSpec(memory_space=pl.ANY)
HBM = pl.BlockSpec(memory_space=pltpu.HBM)
VMEM = pl.BlockSpec(memory_space=pltpu.VMEM)


def call(plan, kernel, out_shape, *args, in_specs=None, out_specs=None, scratch=(), flops=1, grant=None):
    outs = jax.tree.map(lambda _: VMEM, out_shape)
    return pl.pallas_call(
        functools.partial(kernel, plan),
        out_shape=out_shape,
        in_specs=in_specs or [VMEM] * len(args),
        out_specs=out_specs or outs,
        scratch_shapes=list(scratch),
        compiler_params=pltpu.CompilerParams(vmem_limit_bytes=grant or SMALL_GRANT * max(1, plan.own // 4)),
        cost_estimate=pl.CostEstimate(flops=flops, bytes_accessed=1, transcendentals=0),
    )(*args)


def shape(dims, dtype):
    return jax.ShapeDtypeStruct(dims, dtype)


def in_hbm(struct):
    return pltpu.HBM(struct.shape, struct.dtype)


def shards(lesser_green, partner, phonon_green, coupling):
    n_energy, n_mom = lax.axis_size("energy"), lax.axis_size("mom")
    plan = Plan(lesser_green, phonon_green, n_energy, n_mom)
    axes = ("energy", "mom")
    me = lax.axis_index("mom")
    s = lax.axis_index("energy") // plan.group
    wire = shape((plan.peers, plan.rows, LANES), BF16)
    half_peers = plan.half * n_mom
    groups = [[g * plan.peers + i for i in range(plan.peers)] for g in range(plan.n_groups)]
    tiles = (plan.mom_dev, plan.pairs // TILE)

    def exchange(blocks):
        return lax.all_to_all(blocks, axes, split_axis=0, concat_axis=0, axis_index_groups=groups, tiled=True)

    def swap_groups(values, other):
        route = []
        for e in range(n_energy):
            g, j = divmod(e, plan.group)
            to = other(g) if 0 <= other(g) < plan.n_groups else g
            route.append((e, to * plan.group + j))
        return lax.ppermute(values, "energy", route)

    staging = [pltpu.VMEM(wire.shape, BF16), pltpu.SemaphoreType.DMA((plan.mom_dev,))]
    half_wire = shape((half_peers, plan.rows, LANES), BF16)
    own = exchange(
        call(
            plan,
            pack_own_kernel,
            in_hbm(wire),
            lesser_green,
            in_specs=[HBM],
            out_specs=HBM,
            scratch=staging + [pltpu.VMEM(lesser_green.shape, BF16), pltpu.SemaphoreType.DMA((plan.mom_dev,))],
            grant=LARGE_GRANT,
        )
    )

    lag_count = plan.momenta * BRANCH
    lag_rows = -(-lag_count // 16) * 16
    couple = coupling.reshape(plan.pairs_dev, BRANCH, ORB, ORB)
    couple = jnp.pad(couple, ((0, 0), (0, 0), (0, 16 - ORB), (0, FREQ - ORB)))
    phonon = phonon_green.reshape(plan.momenta, plan.pairs_dev, BRANCH, FREQ)
    phonon = jnp.moveaxis(phonon, 1, 0).reshape(plan.pairs_dev, lag_count, FREQ)
    phonon = jnp.pad(phonon, ((0, 0), (0, lag_rows - lag_count), (0, 0)))
    table = jnp.concatenate([couple.reshape(plan.pairs_dev, BRANCH * 16, FREQ), phonon], axis=1)
    table = lax.dynamic_slice_in_dim(table, me * plan.sub, plan.sub, axis=0)
    tables = [table]
    for d in range(1, plan.n_groups):
        tables.append(swap_groups(table, functools.partial(lambda d, g: g ^ d, d)))
    tables = jnp.concatenate(tables, axis=0)
    sand = call(
        plan, sandwich_kernel, shape((plan.own, 2, 2 * LANES, BRANCH * 2 * LANES), BF16), tables
    )
    chunk = max(1, 256 // plan.pairs)
    source = (jnp.arange(chunk)[:, None] * plan.pairs + partner[None, :]).reshape(-1)
    take = (source[:, None] == jnp.arange(chunk * plan.pairs)[None, :]).astype(BF16)
    partner_wire = call(
        plan,
        pack_partner_kernel,
        in_hbm(wire),
        take,
        lesser_green,
        out_specs=HBM,
        scratch=staging + [pltpu.VMEM(lesser_green.shape, BF16)],
    )
    own, tables, sand, partner_wire = lax.optimization_barrier((own, tables, sand, partner_wire))

    odd = s % 2

    def edge(side):
        return lax.dynamic_slice_in_dim(own, side * half_peers, half_peers, axis=0)

    before = after = inner = swap_groups(edge(1 - odd), lambda g: g ^ 1)
    if plan.n_groups > 2:
        outer = swap_groups(edge(odd), lambda g: ((g - 1) ^ 1) + 1)
        before = jnp.where(odd == 1, inner, outer)
        after = jnp.where(odd == 1, outer, inner)

    paced = call(plan, pace_kernel, shape(tables.shape, BF16), tables, flops=LONG)
    paced, partner_wire = lax.optimization_barrier((paced, partner_wire))
    partner_blocks = exchange(partner_wire)
    toep = call(
        plan,
        toeplitz_kernel,
        shape((plan.own, plan.momenta, BRANCH * FREQ, 2 * FREQ), BF16),
        tables,
    )

    late = call(plan, self_late_kernel, half_wire, own, toep, sand)
    sigma = call(
        plan,
        self_early_kernel,
        in_hbm(wire),
        own,
        before,
        toep,
        sand,
        late,
        in_specs=[VMEM, ANY, VMEM, VMEM, VMEM],
        out_specs=HBM,
        scratch=[
            pltpu.VMEM(half_wire.shape, BF16),
            pltpu.VMEM(half_wire.shape, BF16),
            pltpu.SemaphoreType.DMA((3,)),
        ],
        flops=LONG,
    )
    arrived = exchange(sigma)

    scale = (plan.momenta * n_energy * plan.steps * COMP) ** -0.5
    early = call(
        plan,
        phonon_early_kernel,
        shape((plan.own, lag_count, LANES), F32),
        own,
        partner_blocks,
        sand,
    )
    side_rows = plan.mom_dev * BRANCH
    parts = list(call(
        plan,
        functools.partial(phonon_late_kernel, scale=scale),
        [shape((plan.sub, side_rows, LANES), F32)] * (plan.n_groups * n_mom),
        own,
        after,
        partner_blocks,
        sand,
        early,
        scratch=[pltpu.VMEM((plan.own, n_mom, side_rows, LANES), F32)],
    ))
    for d in range(plan.n_groups):
        for t in range(n_mom):
            if d or t:
                route = []
                for e in range(n_energy):
                    g, j = divmod(e, plan.group)
                    for m in range(n_mom):
                        route.append((e * n_mom + m, ((g ^ d) * plan.group + j) * n_mom + (m ^ t)))
                parts[d * n_mom + t] = lax.ppermute(parts[d * n_mom + t], axes, route)
    return call(
        plan,
        unpack_kernel,
        [
            shape(lesser_green.shape, BF16),
            shape((plan.mom_dev, plan.pairs_dev, BRANCH * FREQ), F32),
        ],
        arrived,
        *parts,
        out_specs=[ANY, ANY],
        scratch=[
            pltpu.VMEM(tiles + (plan.steps, TILE, COMP), BF16),
            pltpu.VMEM((plan.mom_dev, plan.pairs_dev, BRANCH * FREQ), F32),
            pltpu.SemaphoreType.DMA(tiles),
            pltpu.SemaphoreType.DMA,
        ],
    )


def solution(mesh):
    in_specs = (P("mom", "energy", None, None), P(), P(None, "energy", None), P("energy", None))
    out_specs = (P("mom", "energy", None, None), P("mom", "energy", None))
    return jax.shard_map(shards, mesh=mesh, in_specs=in_specs, out_specs=out_specs, check_vma=False)
```

```python
import functools

import jax
import jax.numpy as jnp
from jax import lax
from jax.experimental import pallas as pl
from jax.experimental.pallas import tpu as pltpu
from jax.sharding import PartitionSpec as P

ORB = 12
BRANCH = 3
FREQ = 64
COMP = 288
SQUARE = ORB * ORB
LANES = 128
REST = SQUARE - LANES
TAIL = 2 * REST
SLOTS = LANES // TAIL
TILE = 16
SMALL_GRANT = 16 * 1024 * 1024
LARGE_GRANT = 60 * 1024 * 1024
LONG = 100_000_000_000

BF16 = jnp.bfloat16
F32 = jnp.float32
I32 = jnp.int32


class Plan:
    def __init__(self, green, phonon, n_energy, n_mom):
        self.n_energy, self.n_mom = n_energy, n_mom
        self.mom_dev, self.steps, self.pairs, _ = green.shape
        self.momenta = self.mom_dev * n_mom
        self.pairs_dev = phonon.shape[1]
        self.half = FREQ // self.steps
        self.group = 2 * self.half
        self.n_groups = n_energy // self.group
        self.peers = self.group * n_mom
        self.sub = self.pairs_dev // n_mom
        self.own = self.n_groups * self.sub
        self.main_rows = self.mom_dev * self.own * 2 * self.steps
        self.tail_rows = self.mom_dev * self.own // SLOTS * self.steps
        self.rows = self.main_rows + self.tail_rows
        assert self.half * self.steps == FREQ and n_energy % self.group == 0
        assert self.n_groups & (self.n_groups - 1) == 0
        assert self.pairs_dev == n_mom and self.group * self.pairs_dev == TILE
        assert self.mom_dev * self.own % SLOTS == 0 and self.n_groups % 2 == 0

    def main_row(self, k, u):
        return (k * self.own + u) * 2 * self.steps

    def tail_row(self, k, u):
        return self.main_rows + (k * self.own + u) // SLOTS * self.steps

    def shift(self, k):
        return k * self.own % SLOTS * TAIL


def dot(a, b):
    return lax.dot_general(a, b, (((1,), (0,)), ((), ())), preferred_element_type=F32)


def dot_nt(a, b):
    return lax.dot_general(a, b, (((1,), (1,)), ((), ())), preferred_element_type=F32)


def iota(dims, axis):
    return lax.broadcasted_iota(I32, dims, axis)


def swap_matrix(outer, inner, flip=False):
    n = outer * inner
    row, col = iota((n, n), 0), iota((n, n), 1)
    place = row & (outer - 1)
    source = (outer - 1 - place if flip else place) * inner + (row >> (outer.bit_length() - 1))
    return (col == source).astype(F32).astype(BF16)


def pack_rows(plan, load, out_ref, stage, sems, flip=False):
    swap = swap_matrix(plan.steps, TILE, flip)
    copies = []

    def send(first, last):
        rows = slice(first, last)
        copy = pltpu.make_async_copy(stage.at[:, rows, :], out_ref.at[:, rows, :], sems.at[len(copies)])
        copy.start()
        copies.append(copy)

    def put(row, moved):
        for peer in range(plan.peers):
            stage[peer, row : row + plan.steps, :] = moved[peer * plan.steps : (peer + 1) * plan.steps]

    tails = []
    for k in range(plan.mom_dev):
        last = k == plan.mom_dev - 1
        for h in range(plan.pairs // TILE):
            rows = load(k, h)
            halves = jnp.concatenate([rows[:, :LANES], rows[:, SQUARE : SQUARE + LANES]], axis=1)
            tails += [rows[:, LANES:SQUARE], rows[:, SQUARE + LANES :]]
            moved = dot(swap, halves).astype(BF16)
            row = plan.main_row(k, h)
            put(row, moved[:, :LANES])
            put(row + plan.steps, moved[:, LANES:])
        if last:
            for n in range(0, len(tails), 2 * SLOTS):
                joined = jnp.concatenate(tails[n : n + 2 * SLOTS], axis=1)
                put(plan.main_rows + n // (2 * SLOTS) * plan.steps, dot(swap, joined).astype(BF16))
        send(plan.main_row(k, 0), plan.rows if last else plan.main_row(k + 1, 0))
    for copy in copies:
        copy.wait()


def pack_own_kernel(plan, green_ref, out_ref, stage, out_sems, green, sems):
    copies = [pltpu.make_async_copy(green_ref.at[k], green.at[k], sems.at[k]) for k in range(plan.mom_dev)]
    for copy in copies:
        copy.start()

    def load(k, h):
        if h == 0:
            copies[k].wait()
        return green[k, :, TILE * h : TILE * (h + 1), :].reshape(plan.steps * TILE, COMP)

    pack_rows(plan, load, out_ref, stage, out_sems)


def pack_partner_kernel(plan, take_ref, green_ref, out_ref, stage, sems, taken):
    chunk = take_ref.shape[0] // plan.pairs
    take = take_ref[...]
    for k in range(plan.mom_dev):
        for e in range(0, plan.steps, chunk):
            rows = green_ref[k, e : e + chunk].reshape(chunk * plan.pairs, COMP)
            taken[k, e : e + chunk] = dot(take, rows).astype(BF16).reshape(chunk, plan.pairs, COMP)

    def load(k, h):
        return taken[k, :, TILE * h : TILE * (h + 1), :].reshape(plan.steps * TILE, COMP)

    pack_rows(plan, load, out_ref, stage, sems, flip=True)


def each_pair(plan, body):
    if plan.own <= 2:
        for u in range(plan.own):
            body(u)
    else:
        lax.fori_loop(0, plan.own, lambda u, _: body(u), None)


def rows_at(row, count):
    return pl.ds(row if isinstance(row, int) else pl.multiple_of(row, count), count)


def my_table(plan, tables_ref, u):
    group = lax.axis_index("energy") // plan.group
    return tables_ref[(u // plan.sub ^ group) * plan.sub + u % plan.sub]


def sandwich_kernel(plan, tables_ref, sand_ref):
    place, want = iota((2 * LANES, 16), 0), iota((2 * LANES, 16), 1)

    def body(u):
        couple = my_table(plan, tables_ref, u)[: BRANCH * 16, :16]
        for h in range(2):
            comp = jnp.where(place < LANES, place, place - (u % SLOTS * TAIL + h * REST))
            valid = (place < LANES) | ((comp >= LANES) & (comp < SQUARE))
            quotient = (comp * 171) >> 11
            first = (valid & (quotient == want)).astype(F32).astype(BF16)
            second = (valid & (comp - ORB * quotient == want)).astype(F32).astype(BF16)
            left = dot_nt(couple, first).astype(BF16)
            right = dot_nt(couple, second).astype(BF16)
            for i in range(BRANCH):
                rows = slice(16 * i, 16 * i + 16)
                product = dot(first, left[rows]) * dot(second, right[rows])
                sand_ref[u, h, :, 2 * LANES * i : 2 * LANES * (i + 1)] = product.astype(BF16)

    each_pair(plan, body)


def pace_kernel(plan, tables_ref, out_ref):
    out_ref[...] = tables_ref[...]


def toeplitz_kernel(plan, tables_ref, toep_ref):
    mirror = iota((FREQ, 2 * FREQ), 0) + iota((FREQ, 2 * FREQ), 1) == FREQ
    mirror = mirror.astype(F32).astype(BF16)

    def body(u):
        lags = dot(my_table(plan, tables_ref, u)[BRANCH * 16 :, :], mirror)
        for q in range(plan.momenta):
            for i in range(BRANCH):
                n = q * BRANCH + i
                band = jnp.broadcast_to(lags[n : n + 1], (FREQ, 2 * FREQ))
                band = pltpu.roll(band, 0, 1, stride=1, stride_axis=0)
                toep_ref[u, q, i * FREQ : (i + 1) * FREQ, :] = band.astype(BF16)

    each_pair(plan, body)


def gather_rows(plan, ref, u, y, first, flip=False):
    m, k = divmod(y, plan.mom_dev)
    row, tail = plan.main_row(k, u), plan.tail_row(k, u)
    order = range(plan.half)
    lefts, rights, tails = [], [], []
    for j in reversed(order) if flip else order:
        peer = (first + j) * plan.n_mom + m
        lefts.append(ref[peer, rows_at(row, plan.steps), :])
        rights.append(ref[peer, rows_at(row + plan.steps, plan.steps), :])
        tails.append(ref[peer, rows_at(tail, plan.steps), :])
    tails = jnp.concatenate(tails, axis=0)
    if plan.shift(k):
        tails = pltpu.roll(tails.astype(F32), LANES - plan.shift(k), 1).astype(BF16)
    return jnp.concatenate([jnp.concatenate(lefts, axis=0), jnp.concatenate(rights, axis=0), tails], axis=1)


def half_and_tail(rows, h):
    return jnp.concatenate([rows[:, h * LANES : (h + 1) * LANES], rows[:, 2 * LANES :]], axis=1)


def self_block(plan, u, green, toep_ref, sand_ref, out_ref):
    summed = []
    for i in range(BRANCH):
        rows = slice(i * FREQ, (i + 1) * FREQ)
        band = jnp.concatenate(
            [
                jnp.concatenate([toep_ref[u, (k - y) % plan.momenta, rows, :] for y in range(plan.momenta)], axis=1)
                for k in range(plan.momenta)
            ],
            axis=0,
        )
        summed.append(dot(band, green).astype(BF16))
    left, right = [
        dot_nt(jnp.concatenate([half_and_tail(rows, h) for rows in summed], axis=1), sand_ref[u, h])
        for h in range(2)
    ]
    tails = left[:, LANES:] + right[:, LANES:]
    left, right = left[:, :LANES].astype(BF16), right[:, :LANES].astype(BF16)
    for y in range(plan.momenta):
        m, k = divmod(y, plan.mom_dev)
        row, tail = plan.main_row(k, u), plan.tail_row(k, u)
        rest = tails[y * FREQ : (y + 1) * FREQ]
        if plan.shift(k):
            rest = pltpu.roll(rest, plan.shift(k), 1)
        rest = rest.astype(BF16)
        for j in range(plan.half):
            peer = j * plan.n_mom + m
            here = slice(j * plan.steps, (j + 1) * plan.steps)
            there = slice(y * FREQ + j * plan.steps, y * FREQ + (j + 1) * plan.steps)
            out_ref[peer, rows_at(row, plan.steps), :] = left[there]
            out_ref[peer, rows_at(row + plan.steps, plan.steps), :] = right[there]
            out_ref[peer, rows_at(tail, plan.steps), :] += rest[here]


def clear_tails(plan, out_ref):
    for peer in range(plan.half * plan.n_mom):
        out_ref[peer, plan.main_rows :, :] = jnp.zeros((plan.tail_rows, LANES), BF16)


def self_late_kernel(plan, own, toep_ref, sand_ref, out_ref):
    clear_tails(plan, out_ref)

    def body(u):
        green = [gather_rows(plan, own, u, y, first) for y in range(plan.momenta) for first in (0, plan.half)]
        self_block(plan, u, jnp.concatenate(green, axis=0), toep_ref, sand_ref, out_ref)

    each_pair(plan, body)


def self_early_kernel(plan, own, far, toep_ref, sand_ref, late_ref, out_ref, stage, halo, sems):
    has = (lax.axis_index("energy") // plan.group > 0).astype(F32).astype(BF16)
    near = plan.half * plan.n_mom
    load = pltpu.make_async_copy(far, halo, sems.at[0])
    load.start()
    upper = pltpu.make_async_copy(late_ref, out_ref.at[near:], sems.at[1])
    upper.start()
    clear_tails(plan, stage)
    load.wait()

    def body(u):
        green = []
        for y in range(plan.momenta):
            green.append(gather_rows(plan, halo, u, y, 0) * has)
            green.append(gather_rows(plan, own, u, y, 0))
        self_block(plan, u, jnp.concatenate(green, axis=0), toep_ref, sand_ref, stage)

    each_pair(plan, body)
    lower = pltpu.make_async_copy(stage, out_ref.at[:near], sems.at[2])
    lower.start()
    lower.wait()
    upper.wait()


def lag_sums(plan, u, partner, green, sand_ref, store):
    partner, green = jnp.concatenate(partner, axis=0), jnp.concatenate(green, axis=0)
    left, right = [dot(half_and_tail(partner, h), sand_ref[u, h]) for h in range(2)]
    for i in range(BRANCH):
        here = slice(2 * LANES * i, 2 * LANES * i + LANES)
        rest = slice(2 * LANES * i + LANES, 2 * LANES * (i + 1))
        applied = jnp.concatenate([left[:, here], right[:, here], left[:, rest] + right[:, rest]], axis=1)
        lagged = dot_nt(applied.astype(BF16), green)
        for q in range(plan.momenta):
            acc = None
            for k in range(plan.momenta):
                y = (k + q) % plan.momenta
                part = lagged[k * FREQ : (k + 1) * FREQ, y * 2 * FREQ : (y + 1) * 2 * FREQ]
                acc = part if acc is None else acc + part
            acc = pltpu.roll(acc, FREQ + 1, 1, stride=1, stride_axis=0)
            store(q, i, jnp.sum(acc, axis=0, keepdims=True))


def phonon_early_kernel(plan, own, partner_ref, sand_ref, out_ref):
    def body(u):
        partner = [gather_rows(plan, partner_ref, u, k, 0, flip=True) for k in range(plan.momenta)]
        green = [gather_rows(plan, own, u, y, first) for y in range(plan.momenta) for first in (0, plan.half)]

        def store(q, i, lags):
            out_ref[u, q * BRANCH + i : q * BRANCH + i + 1, :] = lags

        lag_sums(plan, u, partner, green, sand_ref, store)

    each_pair(plan, body)


def phonon_late_kernel(plan, own, halo, partner_ref, sand_ref, early_ref, *refs, scale):
    outs, sums = refs[:-1], refs[-1]
    group = lax.axis_index("energy") // plan.group
    me = lax.axis_index("mom")
    has = (group < plan.n_groups - 1).astype(F32).astype(BF16)

    def body(u):
        partner = [gather_rows(plan, partner_ref, u, k, plan.half, flip=True) for k in range(plan.momenta)]
        green = []
        for y in range(plan.momenta):
            green.append(gather_rows(plan, own, u, y, plan.half))
            green.append(gather_rows(plan, halo, u, y, 0) * has)

        def store(q, i, lags):
            n = q * BRANCH + i
            side, row = divmod(n, plan.mom_dev * BRANCH)
            sums[u, side, row : row + 1, :] = (lags + early_ref[u, n : n + 1, :]) * scale

        lag_sums(plan, u, partner, green, sand_ref, store)

    each_pair(plan, body)
    for d in range(plan.n_groups):
        for t in range(plan.n_mom):
            for b in range(plan.sub):
                outs[d * plan.n_mom + t][b] = sums[(group ^ d) * plan.sub + b, me ^ t]


def collect(plan, parts, out_ref):
    me = lax.axis_index("mom")
    for d in range(plan.n_mom):
        total = sum(ref[...] for ref in parts[d :: plan.n_mom])
        for b in range(plan.sub):
            pair = (me ^ d) * plan.sub + b
            for q in range(plan.mom_dev):
                rows = [total[b, q * BRANCH + i : q * BRANCH + i + 1, :FREQ] for i in range(BRANCH)]
                out_ref[q, pl.ds(pair, 1), :] = jnp.concatenate(rows, axis=1)


def unpack_kernel(plan, wire, *refs):
    *parts, out_ref, lags_hbm, green, lags, sems, lag_sem = refs
    collect(plan, parts, lags)
    lag_copy = pltpu.make_async_copy(lags, lags_hbm, lag_sem)
    lag_copy.start()
    swap = swap_matrix(TILE, plan.steps)

    def rows_of(row):
        return jnp.concatenate([wire[peer, row : row + plan.steps, :] for peer in range(plan.peers)], axis=0)

    tails = {}
    for first in range(0, plan.mom_dev * plan.own, SLOTS):
        moved = dot(swap, rows_of(plan.main_rows + first // SLOTS * plan.steps))
        for t in range(SLOTS):
            tails[first + t] = moved[:, t * TAIL : (t + 1) * TAIL]
    copies = []
    for k in range(plan.mom_dev):
        for h in range(plan.pairs // TILE):
            row = plan.main_row(k, h)
            moved = dot(swap, jnp.concatenate([rows_of(row), rows_of(row + plan.steps)], axis=1))
            tail = tails[k * plan.own + h]
            moved = jnp.concatenate([moved[:, :LANES], tail[:, :REST], moved[:, LANES:], tail[:, REST:]], axis=1)
            moved = moved.astype(BF16).reshape(plan.steps, TILE, COMP)
            green[k, :, TILE * h : TILE * (h + 1), :] = moved
        copies.append(pltpu.make_async_copy(green.at[k], out_ref.at[k], sems.at[k]))
        copies[-1].start()
    for copy in copies:
        copy.wait()
    lag_copy.wait()


ANY = pl.BlockSpec(memory_space=pl.ANY)
HBM = pl.BlockSpec(memory_space=pltpu.HBM)
VMEM = pl.BlockSpec(memory_space=pltpu.VMEM)


def call(plan, kernel, out_shape, *args, in_specs=None, out_specs=None, scratch=(), flops=1, grant=None):
    outs = jax.tree.map(lambda _: VMEM, out_shape)
    return pl.pallas_call(
        functools.partial(kernel, plan),
        out_shape=out_shape,
        in_specs=in_specs or [VMEM] * len(args),
        out_specs=out_specs or outs,
        scratch_shapes=list(scratch),
        compiler_params=pltpu.CompilerParams(vmem_limit_bytes=grant or SMALL_GRANT * max(1, plan.own // 4)),
        cost_estimate=pl.CostEstimate(flops=flops, bytes_accessed=1, transcendentals=0),
    )(*args)


def shape(dims, dtype):
    return jax.ShapeDtypeStruct(dims, dtype)


def in_hbm(struct):
    return pltpu.HBM(struct.shape, struct.dtype)


def shards(lesser_green, partner, phonon_green, coupling):
    n_energy, n_mom = lax.axis_size("energy"), lax.axis_size("mom")
    plan = Plan(lesser_green, phonon_green, n_energy, n_mom)
    axes = ("energy", "mom")
    me = lax.axis_index("mom")
    s = lax.axis_index("energy") // plan.group
    wire = shape((plan.peers, plan.rows, LANES), BF16)
    half_peers = plan.half * n_mom
    groups = [[g * plan.peers + i for i in range(plan.peers)] for g in range(plan.n_groups)]

    def exchange(blocks):
        return lax.all_to_all(blocks, axes, split_axis=0, concat_axis=0, axis_index_groups=groups, tiled=True)

    def swap_groups(values, other):
        route = []
        for e in range(n_energy):
            g, j = divmod(e, plan.group)
            to = other(g) if 0 <= other(g) < plan.n_groups else g
            route.append((e, to * plan.group + j))
        return lax.ppermute(values, "energy", route)

    staging = [pltpu.VMEM(wire.shape, BF16), pltpu.SemaphoreType.DMA((plan.mom_dev,))]
    half_wire = shape((half_peers, plan.rows, LANES), BF16)
    own = exchange(
        call(
            plan,
            pack_own_kernel,
            in_hbm(wire),
            lesser_green,
            in_specs=[HBM],
            out_specs=HBM,
            scratch=staging + [pltpu.VMEM(lesser_green.shape, BF16), pltpu.SemaphoreType.DMA((plan.mom_dev,))],
            grant=LARGE_GRANT,
        )
    )

    lag_count = plan.momenta * BRANCH
    lag_rows = -(-lag_count // 16) * 16
    couple = coupling.reshape(plan.pairs_dev, BRANCH, ORB, ORB)
    couple = jnp.pad(couple, ((0, 0), (0, 0), (0, 16 - ORB), (0, FREQ - ORB)))
    phonon = phonon_green.reshape(plan.momenta, plan.pairs_dev, BRANCH, FREQ)
    phonon = jnp.moveaxis(phonon, 1, 0).reshape(plan.pairs_dev, lag_count, FREQ)
    phonon = jnp.pad(phonon, ((0, 0), (0, lag_rows - lag_count), (0, 0)))
    table = jnp.concatenate([couple.reshape(plan.pairs_dev, BRANCH * 16, FREQ), phonon], axis=1)
    table = lax.dynamic_slice_in_dim(table, me * plan.sub, plan.sub, axis=0)
    tables = [table]
    for d in range(1, plan.n_groups):
        tables.append(swap_groups(table, functools.partial(lambda d, g: g ^ d, d)))
    tables = jnp.concatenate(tables, axis=0)
    sand = call(
        plan, sandwich_kernel, shape((plan.own, 2, 2 * LANES, BRANCH * 2 * LANES), BF16), tables
    )
    chunk = max(1, 256 // plan.pairs)
    source = (jnp.arange(chunk)[:, None] * plan.pairs + partner[None, :]).reshape(-1)
    take = (source[:, None] == jnp.arange(chunk * plan.pairs)[None, :]).astype(BF16)
    partner_wire = call(
        plan,
        pack_partner_kernel,
        in_hbm(wire),
        take,
        lesser_green,
        out_specs=HBM,
        scratch=staging + [pltpu.VMEM(lesser_green.shape, BF16)],
    )
    own, tables, sand, partner_wire = lax.optimization_barrier((own, tables, sand, partner_wire))

    odd = s % 2

    def edge(side):
        return lax.dynamic_slice_in_dim(own, side * half_peers, half_peers, axis=0)

    before = after = inner = swap_groups(edge(1 - odd), lambda g: g ^ 1)
    if plan.n_groups > 2:
        outer = swap_groups(edge(odd), lambda g: ((g - 1) ^ 1) + 1)
        before = jnp.where(odd == 1, inner, outer)
        after = jnp.where(odd == 1, outer, inner)

    paced = call(plan, pace_kernel, shape(tables.shape, BF16), tables, flops=LONG)
    paced, partner_wire = lax.optimization_barrier((paced, partner_wire))
    partner_blocks = exchange(partner_wire)
    toep = call(
        plan,
        toeplitz_kernel,
        shape((plan.own, plan.momenta, BRANCH * FREQ, 2 * FREQ), BF16),
        tables,
    )

    late = call(plan, self_late_kernel, half_wire, own, toep, sand)
    sigma = call(
        plan,
        self_early_kernel,
        in_hbm(wire),
        own,
        before,
        toep,
        sand,
        late,
        in_specs=[VMEM, ANY, VMEM, VMEM, VMEM],
        out_specs=HBM,
        scratch=[
            pltpu.VMEM(half_wire.shape, BF16),
            pltpu.VMEM(half_wire.shape, BF16),
            pltpu.SemaphoreType.DMA((3,)),
        ],
        flops=LONG,
    )
    arrived = exchange(sigma)

    scale = (plan.momenta * n_energy * plan.steps * COMP) ** -0.5
    early = call(
        plan,
        phonon_early_kernel,
        shape((plan.own, lag_count, LANES), F32),
        own,
        partner_blocks,
        sand,
    )
    side_rows = plan.mom_dev * BRANCH
    parts = list(call(
        plan,
        functools.partial(phonon_late_kernel, scale=scale),
        [shape((plan.sub, side_rows, LANES), F32)] * (plan.n_groups * n_mom),
        own,
        after,
        partner_blocks,
        sand,
        early,
        scratch=[pltpu.VMEM((plan.own, n_mom, side_rows, LANES), F32)],
    ))
    for d in range(plan.n_groups):
        for t in range(n_mom):
            if d or t:
                route = []
                for e in range(n_energy):
                    g, j = divmod(e, plan.group)
                    for m in range(n_mom):
                        route.append((e * n_mom + m, ((g ^ d) * plan.group + j) * n_mom + (m ^ t)))
                parts[d * n_mom + t] = lax.ppermute(parts[d * n_mom + t], axes, route)
    return call(
        plan,
        unpack_kernel,
        [
            shape(lesser_green.shape, BF16),
            shape((plan.mom_dev, plan.pairs_dev, BRANCH * FREQ), F32),
        ],
        arrived,
        *parts,
        out_specs=[ANY, ANY],
        scratch=[
            pltpu.VMEM(lesser_green.shape, BF16),
            pltpu.VMEM((plan.mom_dev, plan.pairs_dev, BRANCH * FREQ), F32),
            pltpu.SemaphoreType.DMA((plan.mom_dev,)),
            pltpu.SemaphoreType.DMA,
        ],
    )


def solution(mesh):
    in_specs = (P("mom", "energy", None, None), P(), P(None, "energy", None), P("energy", None))
    out_specs = (P("mom", "energy", None, None), P("mom", "energy", None))
    return jax.shard_map(shards, mesh=mesh, in_specs=in_specs, out_specs=out_specs, check_vma=False)
```

```python
import functools

import jax
import jax.numpy as jnp
from jax import lax
from jax.experimental import pallas as pl
from jax.experimental.pallas import tpu as pltpu
from jax.sharding import PartitionSpec as P

ORB = 12
BRANCH = 3
FREQ = 64
COMP = 288
SQUARE = ORB * ORB
LANES = 128
REST = SQUARE - LANES
TAIL = 2 * REST
SLOTS = LANES // TAIL
TILE = 16
SMALL_GRANT = 16 * 1024 * 1024
LARGE_GRANT = 60 * 1024 * 1024
LONG = 100_000_000_000

BF16 = jnp.bfloat16
F32 = jnp.float32
I32 = jnp.int32


class Plan:
    def __init__(self, green, phonon, n_energy, n_mom):
        self.n_energy, self.n_mom = n_energy, n_mom
        self.mom_dev, self.steps, self.pairs, _ = green.shape
        self.momenta = self.mom_dev * n_mom
        self.pairs_dev = phonon.shape[1]
        self.half = FREQ // self.steps
        self.group = 2 * self.half
        self.n_groups = n_energy // self.group
        self.peers = self.group * n_mom
        self.sub = self.pairs_dev // n_mom
        self.own = self.n_groups * self.sub
        self.main_rows = self.mom_dev * self.own * 2 * self.steps
        self.tail_rows = self.mom_dev * self.own // SLOTS * self.steps
        self.rows = self.main_rows + self.tail_rows
        assert self.half * self.steps == FREQ and n_energy % self.group == 0
        assert self.n_groups & (self.n_groups - 1) == 0
        assert self.pairs_dev == n_mom and self.group * self.pairs_dev == TILE
        assert self.mom_dev * self.own % SLOTS == 0 and self.n_groups % 2 == 0

    def main_row(self, k, u):
        return (k * self.own + u) * 2 * self.steps

    def tail_row(self, k, u):
        return self.main_rows + (k * self.own + u) // SLOTS * self.steps

    def shift(self, k):
        return k * self.own % SLOTS * TAIL


def dot(a, b):
    return lax.dot_general(a, b, (((1,), (0,)), ((), ())), preferred_element_type=F32)


def dot_nt(a, b):
    return lax.dot_general(a, b, (((1,), (1,)), ((), ())), preferred_element_type=F32)


def iota(dims, axis):
    return lax.broadcasted_iota(I32, dims, axis)


def swap_matrix(outer, inner, flip=False):
    n = outer * inner
    row, col = iota((n, n), 0), iota((n, n), 1)
    place = row & (outer - 1)
    source = (outer - 1 - place if flip else place) * inner + (row >> (outer.bit_length() - 1))
    return (col == source).astype(F32).astype(BF16)


def pack_rows(plan, load, out_ref, stage, sems, flip=False):
    swap = swap_matrix(plan.steps, TILE, flip)
    copies = []

    def send(first, last):
        rows = slice(first, last)
        copy = pltpu.make_async_copy(stage.at[:, rows, :], out_ref.at[:, rows, :], sems.at[len(copies)])
        copy.start()
        copies.append(copy)

    def put(row, moved):
        for peer in range(plan.peers):
            stage[peer, row : row + plan.steps, :] = moved[peer * plan.steps : (peer + 1) * plan.steps]

    tails = []
    for k in range(plan.mom_dev):
        last = k == plan.mom_dev - 1
        for h in range(plan.pairs // TILE):
            rows = load(k, h)
            halves = jnp.concatenate([rows[:, :LANES], rows[:, SQUARE : SQUARE + LANES]], axis=1)
            tails += [rows[:, LANES:SQUARE], rows[:, SQUARE + LANES :]]
            moved = dot(swap, halves).astype(BF16)
            row = plan.main_row(k, h)
            put(row, moved[:, :LANES])
            put(row + plan.steps, moved[:, LANES:])
        if last:
            for n in range(0, len(tails), 2 * SLOTS):
                joined = jnp.concatenate(tails[n : n + 2 * SLOTS], axis=1)
                put(plan.main_rows + n // (2 * SLOTS) * plan.steps, dot(swap, joined).astype(BF16))
        send(plan.main_row(k, 0), plan.rows if last else plan.main_row(k + 1, 0))
    for copy in copies:
        copy.wait()


def pack_own_kernel(plan, green_ref, out_ref, stage, out_sems, green, sems):
    copies = [pltpu.make_async_copy(green_ref.at[k], green.at[k], sems.at[k]) for k in range(plan.mom_dev)]
    for copy in copies:
        copy.start()

    def load(k, h):
        if h == 0:
            copies[k].wait()
        return green[k, :, TILE * h : TILE * (h + 1), :].reshape(plan.steps * TILE, COMP)

    pack_rows(plan, load, out_ref, stage, out_sems)


def pack_partner_kernel(plan, take_ref, green_ref, out_ref, stage, sems, taken):
    chunk = take_ref.shape[0] // plan.pairs
    take = take_ref[...]
    for k in range(plan.mom_dev):
        for e in range(0, plan.steps, chunk):
            rows = green_ref[k, e : e + chunk].reshape(chunk * plan.pairs, COMP)
            taken[k, e : e + chunk] = dot(take, rows).astype(BF16).reshape(chunk, plan.pairs, COMP)

    def load(k, h):
        return taken[k, :, TILE * h : TILE * (h + 1), :].reshape(plan.steps * TILE, COMP)

    pack_rows(plan, load, out_ref, stage, sems, flip=True)


def each_pair(plan, body):
    if plan.own <= 2:
        for u in range(plan.own):
            body(u)
    else:
        lax.fori_loop(0, plan.own, lambda u, _: body(u), None)


def rows_at(row, count):
    return pl.ds(row if isinstance(row, int) else pl.multiple_of(row, count), count)


def my_table(plan, tables_ref, u):
    group = lax.axis_index("energy") // plan.group
    return tables_ref[(u // plan.sub ^ group) * plan.sub + u % plan.sub]


def sandwich_kernel(plan, tables_ref, sand_ref):
    place, want = iota((2 * LANES, 16), 0), iota((2 * LANES, 16), 1)

    def body(u):
        couple = my_table(plan, tables_ref, u)[: BRANCH * 16, :16]
        for h in range(2):
            comp = jnp.where(place < LANES, place, place - (u % SLOTS * TAIL + h * REST))
            valid = (place < LANES) | ((comp >= LANES) & (comp < SQUARE))
            quotient = (comp * 171) >> 11
            first = (valid & (quotient == want)).astype(F32).astype(BF16)
            second = (valid & (comp - ORB * quotient == want)).astype(F32).astype(BF16)
            left = dot_nt(couple, first).astype(BF16)
            right = dot_nt(couple, second).astype(BF16)
            for i in range(BRANCH):
                rows = slice(16 * i, 16 * i + 16)
                product = dot(first, left[rows]) * dot(second, right[rows])
                sand_ref[u, h, :, 2 * LANES * i : 2 * LANES * (i + 1)] = product.astype(BF16)

    each_pair(plan, body)


def pace_kernel(plan, tables_ref, out_ref):
    out_ref[...] = tables_ref[...]


def toeplitz_kernel(plan, tables_ref, toep_ref):
    mirror = iota((FREQ, 2 * FREQ), 0) + iota((FREQ, 2 * FREQ), 1) == FREQ
    mirror = mirror.astype(F32).astype(BF16)

    def body(u):
        lags = dot(my_table(plan, tables_ref, u)[BRANCH * 16 :, :], mirror)
        for q in range(plan.momenta):
            for i in range(BRANCH):
                n = q * BRANCH + i
                band = jnp.broadcast_to(lags[n : n + 1], (FREQ, 2 * FREQ))
                band = pltpu.roll(band, 0, 1, stride=1, stride_axis=0)
                toep_ref[u, q, i * FREQ : (i + 1) * FREQ, :] = band.astype(BF16)

    each_pair(plan, body)


def edge_kernel(plan, own_ref, *refs):
    *edges, sems = refs
    odd = lax.axis_index("energy") // plan.group % 2
    near = plan.half * plan.n_mom
    copies = []
    for n, (edge, side) in enumerate(zip(edges, (1 - odd, odd))):
        copies.append(pltpu.make_async_copy(own_ref.at[pl.ds(side * near, near)], edge, sems.at[n]))
        copies[-1].start()
    for copy in copies:
        copy.wait()


def gather_rows(plan, ref, u, y, first, flip=False):
    m, k = divmod(y, plan.mom_dev)
    row, tail = plan.main_row(k, u), plan.tail_row(k, u)
    order = range(plan.half)
    lefts, rights, tails = [], [], []
    for j in reversed(order) if flip else order:
        peer = (first + j) * plan.n_mom + m
        lefts.append(ref[peer, rows_at(row, plan.steps), :])
        rights.append(ref[peer, rows_at(row + plan.steps, plan.steps), :])
        tails.append(ref[peer, rows_at(tail, plan.steps), :])
    tails = jnp.concatenate(tails, axis=0)
    if plan.shift(k):
        tails = pltpu.roll(tails.astype(F32), LANES - plan.shift(k), 1).astype(BF16)
    return jnp.concatenate([jnp.concatenate(lefts, axis=0), jnp.concatenate(rights, axis=0), tails], axis=1)


def half_and_tail(rows, h):
    return jnp.concatenate([rows[:, h * LANES : (h + 1) * LANES], rows[:, 2 * LANES :]], axis=1)


def self_block(plan, u, green, toep_ref, sand_ref, out_ref):
    summed = []
    for i in range(BRANCH):
        rows = slice(i * FREQ, (i + 1) * FREQ)
        band = jnp.concatenate(
            [
                jnp.concatenate([toep_ref[u, (k - y) % plan.momenta, rows, :] for y in range(plan.momenta)], axis=1)
                for k in range(plan.momenta)
            ],
            axis=0,
        )
        summed.append(dot(band, green).astype(BF16))
    left, right = [
        dot_nt(jnp.concatenate([half_and_tail(rows, h) for rows in summed], axis=1), sand_ref[u, h])
        for h in range(2)
    ]
    tails = left[:, LANES:] + right[:, LANES:]
    left, right = left[:, :LANES].astype(BF16), right[:, :LANES].astype(BF16)
    for y in range(plan.momenta):
        m, k = divmod(y, plan.mom_dev)
        row, tail = plan.main_row(k, u), plan.tail_row(k, u)
        rest = tails[y * FREQ : (y + 1) * FREQ]
        if plan.shift(k):
            rest = pltpu.roll(rest, plan.shift(k), 1)
        rest = rest.astype(BF16)
        for j in range(plan.half):
            peer = j * plan.n_mom + m
            here = slice(j * plan.steps, (j + 1) * plan.steps)
            there = slice(y * FREQ + j * plan.steps, y * FREQ + (j + 1) * plan.steps)
            out_ref[peer, rows_at(row, plan.steps), :] = left[there]
            out_ref[peer, rows_at(row + plan.steps, plan.steps), :] = right[there]
            out_ref[peer, rows_at(tail, plan.steps), :] += rest[here]


def clear_tails(plan, out_ref):
    for peer in range(plan.half * plan.n_mom):
        out_ref[peer, plan.main_rows :, :] = jnp.zeros((plan.tail_rows, LANES), BF16)


def self_late_kernel(plan, own, toep_ref, sand_ref, out_ref):
    clear_tails(plan, out_ref)

    def body(u):
        green = [gather_rows(plan, own, u, y, first) for y in range(plan.momenta) for first in (0, plan.half)]
        self_block(plan, u, jnp.concatenate(green, axis=0), toep_ref, sand_ref, out_ref)

    each_pair(plan, body)


def self_early_kernel(plan, own, far, toep_ref, sand_ref, late_ref, out_ref, stage, halo, sems):
    has = (lax.axis_index("energy") // plan.group > 0).astype(F32).astype(BF16)
    near = plan.half * plan.n_mom
    load = pltpu.make_async_copy(far, halo, sems.at[0])
    load.start()
    upper = pltpu.make_async_copy(late_ref, out_ref.at[near:], sems.at[1])
    upper.start()
    clear_tails(plan, stage)
    load.wait()

    def body(u):
        green = []
        for y in range(plan.momenta):
            green.append(gather_rows(plan, halo, u, y, 0) * has)
            green.append(gather_rows(plan, own, u, y, 0))
        self_block(plan, u, jnp.concatenate(green, axis=0), toep_ref, sand_ref, stage)

    each_pair(plan, body)
    lower = pltpu.make_async_copy(stage, out_ref.at[:near], sems.at[2])
    lower.start()
    lower.wait()
    upper.wait()


def lag_sums(plan, u, partner, green, sand_ref, store):
    partner, green = jnp.concatenate(partner, axis=0), jnp.concatenate(green, axis=0)
    left, right = [dot(half_and_tail(partner, h), sand_ref[u, h]) for h in range(2)]
    for i in range(BRANCH):
        here = slice(2 * LANES * i, 2 * LANES * i + LANES)
        rest = slice(2 * LANES * i + LANES, 2 * LANES * (i + 1))
        applied = jnp.concatenate([left[:, here], right[:, here], left[:, rest] + right[:, rest]], axis=1)
        lagged = dot_nt(applied.astype(BF16), green)
        for q in range(plan.momenta):
            acc = None
            for k in range(plan.momenta):
                y = (k + q) % plan.momenta
                part = lagged[k * FREQ : (k + 1) * FREQ, y * 2 * FREQ : (y + 1) * 2 * FREQ]
                acc = part if acc is None else acc + part
            acc = pltpu.roll(acc, FREQ + 1, 1, stride=1, stride_axis=0)
            store(q, i, jnp.sum(acc, axis=0, keepdims=True))


def phonon_early_kernel(plan, own, partner_ref, sand_ref, out_ref):
    def body(u):
        partner = [gather_rows(plan, partner_ref, u, k, 0, flip=True) for k in range(plan.momenta)]
        green = [gather_rows(plan, own, u, y, first) for y in range(plan.momenta) for first in (0, plan.half)]

        def store(q, i, lags):
            out_ref[u, q * BRANCH + i : q * BRANCH + i + 1, :] = lags

        lag_sums(plan, u, partner, green, sand_ref, store)

    each_pair(plan, body)


def phonon_late_kernel(plan, own, halo, partner_ref, sand_ref, early_ref, *refs, scale):
    outs, sums = refs[:-1], refs[-1]
    group = lax.axis_index("energy") // plan.group
    me = lax.axis_index("mom")
    has = (group < plan.n_groups - 1).astype(F32).astype(BF16)

    def body(u):
        partner = [gather_rows(plan, partner_ref, u, k, plan.half, flip=True) for k in range(plan.momenta)]
        green = []
        for y in range(plan.momenta):
            green.append(gather_rows(plan, own, u, y, plan.half))
            green.append(gather_rows(plan, halo, u, y, 0) * has)

        def store(q, i, lags):
            n = q * BRANCH + i
            side, row = divmod(n, plan.mom_dev * BRANCH)
            sums[u, side, row : row + 1, :] = (lags + early_ref[u, n : n + 1, :]) * scale

        lag_sums(plan, u, partner, green, sand_ref, store)

    each_pair(plan, body)
    for d in range(plan.n_groups):
        for t in range(plan.n_mom):
            for b in range(plan.sub):
                outs[d * plan.n_mom + t][b] = sums[(group ^ d) * plan.sub + b, me ^ t]


def collect(plan, parts, out_ref):
    me = lax.axis_index("mom")
    for d in range(plan.n_mom):
        total = sum(ref[...] for ref in parts[d :: plan.n_mom])
        for b in range(plan.sub):
            pair = (me ^ d) * plan.sub + b
            for q in range(plan.mom_dev):
                rows = [total[b, q * BRANCH + i : q * BRANCH + i + 1, :FREQ] for i in range(BRANCH)]
                out_ref[q, pl.ds(pair, 1), :] = jnp.concatenate(rows, axis=1)


def unpack_kernel(plan, wire, *refs):
    *parts, out_ref, lags_hbm, green, lags, sems, lag_sem = refs
    swap = swap_matrix(TILE, plan.steps)

    def rows_of(row):
        return jnp.concatenate([wire[peer, row : row + plan.steps, :] for peer in range(plan.peers)], axis=0)

    tails = {}
    for first in range(0, plan.mom_dev * plan.own, SLOTS):
        moved = dot(swap, rows_of(plan.main_rows + first // SLOTS * plan.steps))
        for t in range(SLOTS):
            tails[first + t] = moved[:, t * TAIL : (t + 1) * TAIL]
    copies = []
    for k in range(plan.mom_dev):
        for h in range(plan.pairs // TILE):
            row = plan.main_row(k, h)
            moved = dot(swap, jnp.concatenate([rows_of(row), rows_of(row + plan.steps)], axis=1))
            tail = tails[k * plan.own + h]
            moved = jnp.concatenate([moved[:, :LANES], tail[:, :REST], moved[:, LANES:], tail[:, REST:]], axis=1)
            moved = moved.astype(BF16).reshape(plan.steps, TILE, COMP)
            green[k, :, TILE * h : TILE * (h + 1), :] = moved
        copies.append(pltpu.make_async_copy(green.at[k], out_ref.at[k], sems.at[k]))
        copies[-1].start()
    collect(plan, parts, lags)
    lag_copy = pltpu.make_async_copy(lags, lags_hbm, lag_sem)
    lag_copy.start()
    for copy in copies:
        copy.wait()
    lag_copy.wait()


ANY = pl.BlockSpec(memory_space=pl.ANY)
HBM = pl.BlockSpec(memory_space=pltpu.HBM)
VMEM = pl.BlockSpec(memory_space=pltpu.VMEM)


def call(plan, kernel, out_shape, *args, in_specs=None, out_specs=None, scratch=(), flops=1, grant=None):
    outs = jax.tree.map(lambda _: VMEM, out_shape)
    return pl.pallas_call(
        functools.partial(kernel, plan),
        out_shape=out_shape,
        in_specs=in_specs or [VMEM] * len(args),
        out_specs=out_specs or outs,
        scratch_shapes=list(scratch),
        compiler_params=pltpu.CompilerParams(vmem_limit_bytes=grant or SMALL_GRANT * max(1, plan.own // 4)),
        cost_estimate=pl.CostEstimate(flops=flops, bytes_accessed=1, transcendentals=0),
    )(*args)


def shape(dims, dtype):
    return jax.ShapeDtypeStruct(dims, dtype)


def in_hbm(struct):
    return pltpu.HBM(struct.shape, struct.dtype)


def shards(lesser_green, partner, phonon_green, coupling):
    n_energy, n_mom = lax.axis_size("energy"), lax.axis_size("mom")
    plan = Plan(lesser_green, phonon_green, n_energy, n_mom)
    axes = ("energy", "mom")
    me = lax.axis_index("mom")
    s = lax.axis_index("energy") // plan.group
    wire = shape((plan.peers, plan.rows, LANES), BF16)
    half_peers = plan.half * n_mom
    groups = [[g * plan.peers + i for i in range(plan.peers)] for g in range(plan.n_groups)]

    def exchange(blocks):
        return lax.all_to_all(blocks, axes, split_axis=0, concat_axis=0, axis_index_groups=groups, tiled=True)

    def swap_groups(values, other):
        route = []
        for e in range(n_energy):
            g, j = divmod(e, plan.group)
            to = other(g) if 0 <= other(g) < plan.n_groups else g
            route.append((e, to * plan.group + j))
        return lax.ppermute(values, "energy", route)

    staging = [pltpu.VMEM(wire.shape, BF16), pltpu.SemaphoreType.DMA((plan.mom_dev,))]
    half_wire = shape((half_peers, plan.rows, LANES), BF16)
    own = exchange(
        call(
            plan,
            pack_own_kernel,
            in_hbm(wire),
            lesser_green,
            in_specs=[HBM],
            out_specs=HBM,
            scratch=staging + [pltpu.VMEM(lesser_green.shape, BF16), pltpu.SemaphoreType.DMA((plan.mom_dev,))],
            grant=LARGE_GRANT,
        )
    )

    lag_count = plan.momenta * BRANCH
    lag_rows = -(-lag_count // 16) * 16
    couple = coupling.reshape(plan.pairs_dev, BRANCH, ORB, ORB)
    couple = jnp.pad(couple, ((0, 0), (0, 0), (0, 16 - ORB), (0, FREQ - ORB)))
    phonon = phonon_green.reshape(plan.momenta, plan.pairs_dev, BRANCH, FREQ)
    phonon = jnp.moveaxis(phonon, 1, 0).reshape(plan.pairs_dev, lag_count, FREQ)
    phonon = jnp.pad(phonon, ((0, 0), (0, lag_rows - lag_count), (0, 0)))
    table = jnp.concatenate([couple.reshape(plan.pairs_dev, BRANCH * 16, FREQ), phonon], axis=1)
    table = lax.dynamic_slice_in_dim(table, me * plan.sub, plan.sub, axis=0)
    tables = [table]
    for d in range(1, plan.n_groups):
        tables.append(swap_groups(table, functools.partial(lambda d, g: g ^ d, d)))
    tables = jnp.concatenate(tables, axis=0)
    sand = call(
        plan, sandwich_kernel, shape((plan.own, 2, 2 * LANES, BRANCH * 2 * LANES), BF16), tables
    )
    chunk = max(1, 256 // plan.pairs)
    source = (jnp.arange(chunk)[:, None] * plan.pairs + partner[None, :]).reshape(-1)
    take = (source[:, None] == jnp.arange(chunk * plan.pairs)[None, :]).astype(BF16)
    partner_wire = call(
        plan,
        pack_partner_kernel,
        in_hbm(wire),
        take,
        lesser_green,
        out_specs=HBM,
        scratch=staging + [pltpu.VMEM(lesser_green.shape, BF16)],
    )
    own, tables, sand, partner_wire = lax.optimization_barrier((own, tables, sand, partner_wire))

    count = 1 if plan.n_groups == 2 else 2
    edges = call(
        plan,
        edge_kernel,
        [in_hbm(half_wire)] * count,
        own,
        out_specs=[HBM] * count,
        scratch=[pltpu.SemaphoreType.DMA((count,))],
    )
    before = after = inner = swap_groups(edges[0], lambda g: g ^ 1)
    if plan.n_groups > 2:
        outer = swap_groups(edges[1], lambda g: ((g - 1) ^ 1) + 1)
        odd = s % 2 == 1
        before = jnp.where(odd, inner, outer)
        after = jnp.where(odd, outer, inner)

    paced = call(plan, pace_kernel, shape(tables.shape, BF16), tables, flops=LONG)
    paced, partner_wire = lax.optimization_barrier((paced, partner_wire))
    partner_blocks = exchange(partner_wire)
    toep = call(
        plan,
        toeplitz_kernel,
        shape((plan.own, plan.momenta, BRANCH * FREQ, 2 * FREQ), BF16),
        tables,
    )

    late = call(plan, self_late_kernel, half_wire, own, toep, sand)
    sigma = call(
        plan,
        self_early_kernel,
        in_hbm(wire),
        own,
        before,
        toep,
        sand,
        late,
        in_specs=[VMEM, ANY, VMEM, VMEM, VMEM],
        out_specs=HBM,
        scratch=[
            pltpu.VMEM(half_wire.shape, BF16),
            pltpu.VMEM(half_wire.shape, BF16),
            pltpu.SemaphoreType.DMA((3,)),
        ],
        flops=LONG,
    )
    arrived = exchange(sigma)

    scale = (plan.momenta * n_energy * plan.steps * COMP) ** -0.5
    early = call(
        plan,
        phonon_early_kernel,
        shape((plan.own, lag_count, LANES), F32),
        own,
        partner_blocks,
        sand,
    )
    side_rows = plan.mom_dev * BRANCH
    parts = list(call(
        plan,
        functools.partial(phonon_late_kernel, scale=scale),
        [shape((plan.sub, side_rows, LANES), F32)] * (plan.n_groups * n_mom),
        own,
        after,
        partner_blocks,
        sand,
        early,
        scratch=[pltpu.VMEM((plan.own, n_mom, side_rows, LANES), F32)],
    ))
    for d in range(plan.n_groups):
        for t in range(n_mom):
            if d or t:
                route = []
                for e in range(n_energy):
                    g, j = divmod(e, plan.group)
                    for m in range(n_mom):
                        route.append((e * n_mom + m, ((g ^ d) * plan.group + j) * n_mom + (m ^ t)))
                parts[d * n_mom + t] = lax.ppermute(parts[d * n_mom + t], axes, route)
    return call(
        plan,
        unpack_kernel,
        [
            shape(lesser_green.shape, BF16),
            shape((plan.mom_dev, plan.pairs_dev, BRANCH * FREQ), F32),
        ],
        arrived,
        *parts,
        out_specs=[ANY, ANY],
        scratch=[
            pltpu.VMEM(lesser_green.shape, BF16),
            pltpu.VMEM((plan.mom_dev, plan.pairs_dev, BRANCH * FREQ), F32),
            pltpu.SemaphoreType.DMA((plan.mom_dev,)),
            pltpu.SemaphoreType.DMA,
        ],
    )


def solution(mesh):
    in_specs = (P("mom", "energy", None, None), P(), P(None, "energy", None), P("energy", None))
    out_specs = (P("mom", "energy", None, None), P("mom", "energy", None))
    return jax.shard_map(shards, mesh=mesh, in_specs=in_specs, out_specs=out_specs, check_vma=False)
```

```python
import functools

import jax
import jax.numpy as jnp
from jax import lax
from jax.experimental import pallas as pl
from jax.experimental.pallas import tpu as pltpu
from jax.sharding import PartitionSpec as P

ORB = 12
BRANCH = 3
FREQ = 64
COMP = 288
SQUARE = ORB * ORB
LANES = 128
REST = SQUARE - LANES
TAIL = 2 * REST
SLOTS = LANES // TAIL
TILE = 16
SMALL_GRANT = 16 * 1024 * 1024
LARGE_GRANT = 60 * 1024 * 1024
LONG = 100_000_000_000

BF16 = jnp.bfloat16
F32 = jnp.float32
I32 = jnp.int32


class Plan:
    def __init__(self, green, phonon, n_energy, n_mom):
        self.n_energy, self.n_mom = n_energy, n_mom
        self.mom_dev, self.steps, self.pairs, _ = green.shape
        self.momenta = self.mom_dev * n_mom
        self.pairs_dev = phonon.shape[1]
        self.half = FREQ // self.steps
        self.group = 2 * self.half
        self.n_groups = n_energy // self.group
        self.peers = self.group * n_mom
        self.sub = self.pairs_dev // n_mom
        self.own = self.n_groups * self.sub
        self.main_rows = self.mom_dev * self.own * 2 * self.steps
        self.tail_rows = self.mom_dev * self.own // SLOTS * self.steps
        self.rows = self.main_rows + self.tail_rows
        assert self.half * self.steps == FREQ and n_energy % self.group == 0
        assert self.n_groups & (self.n_groups - 1) == 0
        assert self.pairs_dev == n_mom and self.group * self.pairs_dev == TILE
        assert self.mom_dev * self.own % SLOTS == 0 and self.n_groups % 2 == 0

    def main_row(self, k, u):
        return (k * self.own + u) * 2 * self.steps

    def tail_row(self, k, u):
        return self.main_rows + (k * self.own + u) // SLOTS * self.steps

    def shift(self, k):
        return k * self.own % SLOTS * TAIL


def dot(a, b):
    return lax.dot_general(a, b, (((1,), (0,)), ((), ())), preferred_element_type=F32)


def dot_nt(a, b):
    return lax.dot_general(a, b, (((1,), (1,)), ((), ())), preferred_element_type=F32)


def iota(dims, axis):
    return lax.broadcasted_iota(I32, dims, axis)


def swap_matrix(outer, inner, flip=False):
    n = outer * inner
    row, col = iota((n, n), 0), iota((n, n), 1)
    place = row & (outer - 1)
    source = (outer - 1 - place if flip else place) * inner + (row >> (outer.bit_length() - 1))
    return (col == source).astype(F32).astype(BF16)


def pack_rows(plan, load, out_ref, stage, sems, flip=False):
    swap = swap_matrix(plan.steps, TILE, flip)
    copies = []

    def send(first, last):
        rows = slice(first, last)
        copy = pltpu.make_async_copy(stage.at[:, rows, :], out_ref.at[:, rows, :], sems.at[len(copies)])
        copy.start()
        copies.append(copy)

    def put(row, moved):
        for peer in range(plan.peers):
            stage[peer, row : row + plan.steps, :] = moved[peer * plan.steps : (peer + 1) * plan.steps]

    tails = []
    for k in range(plan.mom_dev):
        last = k == plan.mom_dev - 1
        for h in range(plan.pairs // TILE):
            rows = load(k, h)
            halves = jnp.concatenate([rows[:, :LANES], rows[:, SQUARE : SQUARE + LANES]], axis=1)
            tails += [rows[:, LANES:SQUARE], rows[:, SQUARE + LANES :]]
            moved = dot(swap, halves).astype(BF16)
            row = plan.main_row(k, h)
            put(row, moved[:, :LANES])
            put(row + plan.steps, moved[:, LANES:])
        if last:
            for n in range(0, len(tails), 2 * SLOTS):
                joined = jnp.concatenate(tails[n : n + 2 * SLOTS], axis=1)
                put(plan.main_rows + n // (2 * SLOTS) * plan.steps, dot(swap, joined).astype(BF16))
        send(plan.main_row(k, 0), plan.rows if last else plan.main_row(k + 1, 0))
    for copy in copies:
        copy.wait()


def pack_own_kernel(plan, green_ref, out_ref, stage, out_sems, green, sems):
    copies = [pltpu.make_async_copy(green_ref.at[k], green.at[k], sems.at[k]) for k in range(plan.mom_dev)]
    for copy in copies:
        copy.start()

    def load(k, h):
        if h == 0:
            copies[k].wait()
        return green[k, :, TILE * h : TILE * (h + 1), :].reshape(plan.steps * TILE, COMP)

    pack_rows(plan, load, out_ref, stage, out_sems)


def pack_partner_kernel(plan, take_ref, green_ref, out_ref, stage, sems, taken):
    chunk = take_ref.shape[0] // plan.pairs
    take = take_ref[...]
    for k in range(plan.mom_dev):
        for e in range(0, plan.steps, chunk):
            rows = green_ref[k, e : e + chunk].reshape(chunk * plan.pairs, COMP)
            taken[k, e : e + chunk] = dot(take, rows).astype(BF16).reshape(chunk, plan.pairs, COMP)

    def load(k, h):
        return taken[k, :, TILE * h : TILE * (h + 1), :].reshape(plan.steps * TILE, COMP)

    pack_rows(plan, load, out_ref, stage, sems, flip=True)


def each_pair(plan, body):
    if plan.own <= 2:
        for u in range(plan.own):
            body(u)
    else:
        lax.fori_loop(0, plan.own, lambda u, _: body(u), None)


def rows_at(row, count):
    return pl.ds(row if isinstance(row, int) else pl.multiple_of(row, count), count)


def my_table(plan, tables_ref, u):
    group = lax.axis_index("energy") // plan.group
    return tables_ref[(u // plan.sub ^ group) * plan.sub + u % plan.sub]


def sandwich_kernel(plan, tables_ref, sand_ref):
    place, want = iota((2 * LANES, 16), 0), iota((2 * LANES, 16), 1)

    def body(u):
        couple = my_table(plan, tables_ref, u)[: BRANCH * 16, :16]
        for h in range(2):
            comp = jnp.where(place < LANES, place, place - (u % SLOTS * TAIL + h * REST))
            valid = (place < LANES) | ((comp >= LANES) & (comp < SQUARE))
            quotient = (comp * 171) >> 11
            first = (valid & (quotient == want)).astype(F32).astype(BF16)
            second = (valid & (comp - ORB * quotient == want)).astype(F32).astype(BF16)
            left = dot_nt(couple, first).astype(BF16)
            right = dot_nt(couple, second).astype(BF16)
            for i in range(BRANCH):
                rows = slice(16 * i, 16 * i + 16)
                product = dot(first, left[rows]) * dot(second, right[rows])
                sand_ref[u, h, :, 2 * LANES * i : 2 * LANES * (i + 1)] = product.astype(BF16)

    each_pair(plan, body)


def pace_kernel(plan, tables_ref, out_ref):
    out_ref[...] = tables_ref[...]


def toeplitz_kernel(plan, tables_ref, toep_ref):
    mirror = iota((FREQ, 2 * FREQ), 0) + iota((FREQ, 2 * FREQ), 1) == FREQ
    mirror = mirror.astype(F32).astype(BF16)

    def body(u):
        lags = dot(my_table(plan, tables_ref, u)[BRANCH * 16 :, :], mirror)
        for q in range(plan.momenta):
            for i in range(BRANCH):
                n = q * BRANCH + i
                band = jnp.broadcast_to(lags[n : n + 1], (FREQ, 2 * FREQ))
                band = pltpu.roll(band, 0, 1, stride=1, stride_axis=0)
                toep_ref[u, q, i * FREQ : (i + 1) * FREQ, :] = band.astype(BF16)

    each_pair(plan, body)


def gather_rows(plan, ref, u, y, first, flip=False):
    m, k = divmod(y, plan.mom_dev)
    row, tail = plan.main_row(k, u), plan.tail_row(k, u)
    order = range(plan.half)
    lefts, rights, tails = [], [], []
    for j in reversed(order) if flip else order:
        peer = (first + j) * plan.n_mom + m
        lefts.append(ref[peer, rows_at(row, plan.steps), :])
        rights.append(ref[peer, rows_at(row + plan.steps, plan.steps), :])
        tails.append(ref[peer, rows_at(tail, plan.steps), :])
    tails = jnp.concatenate(tails, axis=0)
    if plan.shift(k):
        tails = pltpu.roll(tails.astype(F32), LANES - plan.shift(k), 1).astype(BF16)
    return jnp.concatenate([jnp.concatenate(lefts, axis=0), jnp.concatenate(rights, axis=0), tails], axis=1)


def half_and_tail(rows, h):
    return jnp.concatenate([rows[:, h * LANES : (h + 1) * LANES], rows[:, 2 * LANES :]], axis=1)


def self_block(plan, u, green, toep_ref, sand_ref, out_ref):
    summed = []
    for i in range(BRANCH):
        rows = slice(i * FREQ, (i + 1) * FREQ)
        band = jnp.concatenate(
            [
                jnp.concatenate([toep_ref[u, (k - y) % plan.momenta, rows, :] for y in range(plan.momenta)], axis=1)
                for k in range(plan.momenta)
            ],
            axis=0,
        )
        summed.append(dot(band, green).astype(BF16))
    left, right = [
        dot_nt(jnp.concatenate([half_and_tail(rows, h) for rows in summed], axis=1), sand_ref[u, h])
        for h in range(2)
    ]
    tails = left[:, LANES:] + right[:, LANES:]
    left, right = left[:, :LANES].astype(BF16), right[:, :LANES].astype(BF16)
    for y in range(plan.momenta):
        m, k = divmod(y, plan.mom_dev)
        row, tail = plan.main_row(k, u), plan.tail_row(k, u)
        rest = tails[y * FREQ : (y + 1) * FREQ]
        if plan.shift(k):
            rest = pltpu.roll(rest, plan.shift(k), 1)
        rest = rest.astype(BF16)
        for j in range(plan.half):
            peer = j * plan.n_mom + m
            here = slice(j * plan.steps, (j + 1) * plan.steps)
            there = slice(y * FREQ + j * plan.steps, y * FREQ + (j + 1) * plan.steps)
            out_ref[peer, rows_at(row, plan.steps), :] = left[there]
            out_ref[peer, rows_at(row + plan.steps, plan.steps), :] = right[there]
            out_ref[peer, rows_at(tail, plan.steps), :] += rest[here]


def clear_tails(plan, out_ref):
    for peer in range(plan.half * plan.n_mom):
        out_ref[peer, plan.main_rows :, :] = jnp.zeros((plan.tail_rows, LANES), BF16)


def self_late_kernel(plan, own, toep_ref, sand_ref, out_ref):
    clear_tails(plan, out_ref)

    def body(u):
        green = [gather_rows(plan, own, u, y, first) for y in range(plan.momenta) for first in (0, plan.half)]
        self_block(plan, u, jnp.concatenate(green, axis=0), toep_ref, sand_ref, out_ref)

    each_pair(plan, body)


def self_early_kernel(plan, own, far, toep_ref, sand_ref, late_ref, out_ref, stage, halo, sems):
    has = (lax.axis_index("energy") // plan.group > 0).astype(F32).astype(BF16)
    near = plan.half * plan.n_mom
    load = pltpu.make_async_copy(far, halo, sems.at[0])
    load.start()
    upper = pltpu.make_async_copy(late_ref, out_ref.at[near:], sems.at[1])
    upper.start()
    clear_tails(plan, stage)
    load.wait()

    def body(u):
        green = []
        for y in range(plan.momenta):
            green.append(gather_rows(plan, halo, u, y, 0) * has)
            green.append(gather_rows(plan, own, u, y, 0))
        self_block(plan, u, jnp.concatenate(green, axis=0), toep_ref, sand_ref, stage)

    each_pair(plan, body)
    lower = pltpu.make_async_copy(stage, out_ref.at[:near], sems.at[2])
    lower.start()
    lower.wait()
    upper.wait()


def lag_sums(plan, u, partner, green, sand_ref, store):
    partner, green = jnp.concatenate(partner, axis=0), jnp.concatenate(green, axis=0)
    left, right = [dot(half_and_tail(partner, h), sand_ref[u, h]) for h in range(2)]
    for i in range(BRANCH):
        here = slice(2 * LANES * i, 2 * LANES * i + LANES)
        rest = slice(2 * LANES * i + LANES, 2 * LANES * (i + 1))
        applied = jnp.concatenate([left[:, here], right[:, here], left[:, rest] + right[:, rest]], axis=1)
        lagged = dot_nt(applied.astype(BF16), green)
        for q in range(plan.momenta):
            acc = None
            for k in range(plan.momenta):
                y = (k + q) % plan.momenta
                part = lagged[k * FREQ : (k + 1) * FREQ, y * 2 * FREQ : (y + 1) * 2 * FREQ]
                acc = part if acc is None else acc + part
            acc = pltpu.roll(acc, FREQ + 1, 1, stride=1, stride_axis=0)
            store(q, i, jnp.sum(acc, axis=0, keepdims=True))


def phonon_early_kernel(plan, own, partner_ref, sand_ref, out_ref):
    def body(u):
        partner = [gather_rows(plan, partner_ref, u, k, 0, flip=True) for k in range(plan.momenta)]
        green = [gather_rows(plan, own, u, y, first) for y in range(plan.momenta) for first in (0, plan.half)]

        def store(q, i, lags):
            out_ref[u, q * BRANCH + i : q * BRANCH + i + 1, :] = lags

        lag_sums(plan, u, partner, green, sand_ref, store)

    each_pair(plan, body)


def phonon_late_kernel(plan, own, halo, partner_ref, sand_ref, early_ref, *refs, scale):
    outs, sums = refs[:-1], refs[-1]
    group = lax.axis_index("energy") // plan.group
    me = lax.axis_index("mom")
    has = (group < plan.n_groups - 1).astype(F32).astype(BF16)

    def body(u):
        partner = [gather_rows(plan, partner_ref, u, k, plan.half, flip=True) for k in range(plan.momenta)]
        green = []
        for y in range(plan.momenta):
            green.append(gather_rows(plan, own, u, y, plan.half))
            green.append(gather_rows(plan, halo, u, y, 0) * has)

        def store(q, i, lags):
            n = q * BRANCH + i
            side, row = divmod(n, plan.mom_dev * BRANCH)
            sums[u, side, row : row + 1, :] = (lags + early_ref[u, n : n + 1, :]) * scale

        lag_sums(plan, u, partner, green, sand_ref, store)

    each_pair(plan, body)
    for d in range(plan.n_groups):
        for t in range(plan.n_mom):
            for b in range(plan.sub):
                outs[d * plan.n_mom + t][b] = sums[(group ^ d) * plan.sub + b, me ^ t]


def collect(plan, parts, out_ref):
    me = lax.axis_index("mom")
    totals = [sum(ref[...] for ref in parts[d :: plan.n_mom]) for d in range(plan.n_mom)]
    for q in range(plan.mom_dev):
        pairs = []
        for m in range(plan.n_mom):
            for b in range(plan.sub):
                lags = totals[0][b]
                for d in range(1, plan.n_mom):
                    lags = jnp.where(me ^ d == m, totals[d][b], lags)
                rows = [lags[q * BRANCH + i : q * BRANCH + i + 1, :FREQ] for i in range(BRANCH)]
                pairs.append(jnp.concatenate(rows, axis=1))
        out_ref[q] = jnp.concatenate(pairs, axis=0)


def unpack_kernel(plan, wire, *refs):
    *parts, out_ref, lags_hbm, green, lags, sems, lag_sem = refs
    swap = swap_matrix(TILE, plan.steps)

    def rows_of(row):
        return jnp.concatenate([wire[peer, row : row + plan.steps, :] for peer in range(plan.peers)], axis=0)

    tails = {}
    for first in range(0, plan.mom_dev * plan.own, SLOTS):
        moved = dot(swap, rows_of(plan.main_rows + first // SLOTS * plan.steps))
        for t in range(SLOTS):
            tails[first + t] = moved[:, t * TAIL : (t + 1) * TAIL]
    copies = []
    for k in range(plan.mom_dev):
        for h in range(plan.pairs // TILE):
            row = plan.main_row(k, h)
            moved = dot(swap, jnp.concatenate([rows_of(row), rows_of(row + plan.steps)], axis=1))
            tail = tails[k * plan.own + h]
            moved = jnp.concatenate([moved[:, :LANES], tail[:, :REST], moved[:, LANES:], tail[:, REST:]], axis=1)
            moved = moved.astype(BF16).reshape(plan.steps, TILE, COMP)
            green[k, :, TILE * h : TILE * (h + 1), :] = moved
        copies.append(pltpu.make_async_copy(green.at[k], out_ref.at[k], sems.at[k]))
        copies[-1].start()
    collect(plan, parts, lags)
    lag_copy = pltpu.make_async_copy(lags, lags_hbm, lag_sem)
    lag_copy.start()
    for copy in copies:
        copy.wait()
    lag_copy.wait()


ANY = pl.BlockSpec(memory_space=pl.ANY)
HBM = pl.BlockSpec(memory_space=pltpu.HBM)
VMEM = pl.BlockSpec(memory_space=pltpu.VMEM)


def call(plan, kernel, out_shape, *args, in_specs=None, out_specs=None, scratch=(), flops=1, grant=None):
    outs = jax.tree.map(lambda _: VMEM, out_shape)
    return pl.pallas_call(
        functools.partial(kernel, plan),
        out_shape=out_shape,
        in_specs=in_specs or [VMEM] * len(args),
        out_specs=out_specs or outs,
        scratch_shapes=list(scratch),
        compiler_params=pltpu.CompilerParams(vmem_limit_bytes=grant or SMALL_GRANT * max(1, plan.own // 4)),
        cost_estimate=pl.CostEstimate(flops=flops, bytes_accessed=1, transcendentals=0),
    )(*args)


def shape(dims, dtype):
    return jax.ShapeDtypeStruct(dims, dtype)


def in_hbm(struct):
    return pltpu.HBM(struct.shape, struct.dtype)


def shards(lesser_green, partner, phonon_green, coupling):
    n_energy, n_mom = lax.axis_size("energy"), lax.axis_size("mom")
    plan = Plan(lesser_green, phonon_green, n_energy, n_mom)
    axes = ("energy", "mom")
    me = lax.axis_index("mom")
    s = lax.axis_index("energy") // plan.group
    wire = shape((plan.peers, plan.rows, LANES), BF16)
    half_peers = plan.half * n_mom
    groups = [[g * plan.peers + i for i in range(plan.peers)] for g in range(plan.n_groups)]

    def exchange(blocks):
        return lax.all_to_all(blocks, axes, split_axis=0, concat_axis=0, axis_index_groups=groups, tiled=True)

    def swap_groups(values, other):
        route = []
        for e in range(n_energy):
            g, j = divmod(e, plan.group)
            to = other(g) if 0 <= other(g) < plan.n_groups else g
            route.append((e, to * plan.group + j))
        return lax.ppermute(values, "energy", route)

    staging = [pltpu.VMEM(wire.shape, BF16), pltpu.SemaphoreType.DMA((plan.mom_dev,))]
    half_wire = shape((half_peers, plan.rows, LANES), BF16)
    own = exchange(
        call(
            plan,
            pack_own_kernel,
            in_hbm(wire),
            lesser_green,
            in_specs=[HBM],
            out_specs=HBM,
            scratch=staging + [pltpu.VMEM(lesser_green.shape, BF16), pltpu.SemaphoreType.DMA((plan.mom_dev,))],
            grant=LARGE_GRANT,
        )
    )

    lag_count = plan.momenta * BRANCH
    lag_rows = -(-lag_count // 16) * 16
    couple = coupling.reshape(plan.pairs_dev, BRANCH, ORB, ORB)
    couple = jnp.pad(couple, ((0, 0), (0, 0), (0, 16 - ORB), (0, FREQ - ORB)))
    phonon = phonon_green.reshape(plan.momenta, plan.pairs_dev, BRANCH, FREQ)
    phonon = jnp.moveaxis(phonon, 1, 0).reshape(plan.pairs_dev, lag_count, FREQ)
    phonon = jnp.pad(phonon, ((0, 0), (0, lag_rows - lag_count), (0, 0)))
    table = jnp.concatenate([couple.reshape(plan.pairs_dev, BRANCH * 16, FREQ), phonon], axis=1)
    table = lax.dynamic_slice_in_dim(table, me * plan.sub, plan.sub, axis=0)
    tables = [table]
    for d in range(1, plan.n_groups):
        tables.append(swap_groups(table, functools.partial(lambda d, g: g ^ d, d)))
    tables = jnp.concatenate(tables, axis=0)
    sand = call(
        plan, sandwich_kernel, shape((plan.own, 2, 2 * LANES, BRANCH * 2 * LANES), BF16), tables
    )
    chunk = max(1, 256 // plan.pairs)
    source = (jnp.arange(chunk)[:, None] * plan.pairs + partner[None, :]).reshape(-1)
    take = (source[:, None] == jnp.arange(chunk * plan.pairs)[None, :]).astype(BF16)
    partner_wire = call(
        plan,
        pack_partner_kernel,
        in_hbm(wire),
        take,
        lesser_green,
        out_specs=HBM,
        scratch=staging + [pltpu.VMEM(lesser_green.shape, BF16)],
    )
    own, tables, sand, partner_wire = lax.optimization_barrier((own, tables, sand, partner_wire))

    odd = s % 2

    def edge(side):
        return lax.dynamic_slice_in_dim(own, side * half_peers, half_peers, axis=0)

    before = after = inner = swap_groups(edge(1 - odd), lambda g: g ^ 1)
    if plan.n_groups > 2:
        outer = swap_groups(edge(odd), lambda g: ((g - 1) ^ 1) + 1)
        before = jnp.where(odd == 1, inner, outer)
        after = jnp.where(odd == 1, outer, inner)

    paced = call(plan, pace_kernel, shape(tables.shape, BF16), tables, flops=LONG)
    paced, partner_wire = lax.optimization_barrier((paced, partner_wire))
    partner_blocks = exchange(partner_wire)
    toep = call(
        plan,
        toeplitz_kernel,
        shape((plan.own, plan.momenta, BRANCH * FREQ, 2 * FREQ), BF16),
        tables,
    )

    late = call(plan, self_late_kernel, half_wire, own, toep, sand)
    sigma = call(
        plan,
        self_early_kernel,
        in_hbm(wire),
        own,
        before,
        toep,
        sand,
        late,
        in_specs=[VMEM, ANY, VMEM, VMEM, VMEM],
        out_specs=HBM,
        scratch=[
            pltpu.VMEM(half_wire.shape, BF16),
            pltpu.VMEM(half_wire.shape, BF16),
            pltpu.SemaphoreType.DMA((3,)),
        ],
        flops=LONG,
    )
    arrived = exchange(sigma)

    scale = (plan.momenta * n_energy * plan.steps * COMP) ** -0.5
    early = call(
        plan,
        phonon_early_kernel,
        shape((plan.own, lag_count, LANES), F32),
        own,
        partner_blocks,
        sand,
    )
    side_rows = plan.mom_dev * BRANCH
    parts = list(call(
        plan,
        functools.partial(phonon_late_kernel, scale=scale),
        [shape((plan.sub, side_rows, LANES), F32)] * (plan.n_groups * n_mom),
        own,
        after,
        partner_blocks,
        sand,
        early,
        scratch=[pltpu.VMEM((plan.own, n_mom, side_rows, LANES), F32)],
    ))
    for d in range(plan.n_groups):
        for t in range(n_mom):
            if d or t:
                route = []
                for e in range(n_energy):
                    g, j = divmod(e, plan.group)
                    for m in range(n_mom):
                        route.append((e * n_mom + m, ((g ^ d) * plan.group + j) * n_mom + (m ^ t)))
                parts[d * n_mom + t] = lax.ppermute(parts[d * n_mom + t], axes, route)
    return call(
        plan,
        unpack_kernel,
        [
            shape(lesser_green.shape, BF16),
            shape((plan.mom_dev, plan.pairs_dev, BRANCH * FREQ), F32),
        ],
        arrived,
        *parts,
        out_specs=[ANY, ANY],
        scratch=[
            pltpu.VMEM(lesser_green.shape, BF16),
            pltpu.VMEM((plan.mom_dev, plan.pairs_dev, BRANCH * FREQ), F32),
            pltpu.SemaphoreType.DMA((plan.mom_dev,)),
            pltpu.SemaphoreType.DMA,
        ],
    )


def solution(mesh):
    in_specs = (P("mom", "energy", None, None), P(), P(None, "energy", None), P("energy", None))
    out_specs = (P("mom", "energy", None, None), P("mom", "energy", None))
    return jax.shard_map(shards, mesh=mesh, in_specs=in_specs, out_specs=out_specs, check_vma=False)
```

```python
import functools

import jax
import jax.numpy as jnp
from jax import lax
from jax.experimental import pallas as pl
from jax.experimental.pallas import tpu as pltpu
from jax.sharding import PartitionSpec as P

ORB = 12
BRANCH = 3
FREQ = 64
COMP = 288
SQUARE = ORB * ORB
LANES = 128
REST = SQUARE - LANES
TAIL = 2 * REST
SLOTS = LANES // TAIL
TILE = 16
SMALL_GRANT = 16 * 1024 * 1024
LARGE_GRANT = 60 * 1024 * 1024
LONG = 100_000_000_000

BF16 = jnp.bfloat16
F32 = jnp.float32
I32 = jnp.int32


class Plan:
    def __init__(self, green, phonon, n_energy, n_mom):
        self.n_energy, self.n_mom = n_energy, n_mom
        self.mom_dev, self.steps, self.pairs, _ = green.shape
        self.momenta = self.mom_dev * n_mom
        self.pairs_dev = phonon.shape[1]
        self.half = FREQ // self.steps
        self.group = 2 * self.half
        self.n_groups = n_energy // self.group
        self.peers = self.group * n_mom
        self.sub = self.pairs_dev // n_mom
        self.own = self.n_groups * self.sub
        self.main_rows = self.mom_dev * self.own * 2 * self.steps
        self.tail_rows = self.mom_dev * self.own // SLOTS * self.steps
        self.rows = self.main_rows + self.tail_rows
        assert self.half * self.steps == FREQ and n_energy % self.group == 0
        assert self.n_groups & (self.n_groups - 1) == 0
        assert self.pairs_dev == n_mom and self.group * self.pairs_dev == TILE
        assert self.mom_dev * self.own % SLOTS == 0 and self.n_groups % 2 == 0

    def main_row(self, k, u):
        return (k * self.own + u) * 2 * self.steps

    def tail_row(self, k, u):
        return self.main_rows + (k * self.own + u) // SLOTS * self.steps

    def shift(self, k):
        return k * self.own % SLOTS * TAIL


def dot(a, b):
    return lax.dot_general(a, b, (((1,), (0,)), ((), ())), preferred_element_type=F32)


def dot_nt(a, b):
    return lax.dot_general(a, b, (((1,), (1,)), ((), ())), preferred_element_type=F32)


def iota(dims, axis):
    return lax.broadcasted_iota(I32, dims, axis)


def swap_matrix(outer, inner, flip=False):
    n = outer * inner
    row, col = iota((n, n), 0), iota((n, n), 1)
    place = row & (outer - 1)
    source = (outer - 1 - place if flip else place) * inner + (row >> (outer.bit_length() - 1))
    return (col == source).astype(F32).astype(BF16)


def pack_rows(plan, load, out_ref, stage, sems, flip=False):
    swap = swap_matrix(plan.steps, TILE, flip)
    copies = []

    def send(first, last):
        rows = slice(first, last)
        copy = pltpu.make_async_copy(stage.at[:, rows, :], out_ref.at[:, rows, :], sems.at[len(copies)])
        copy.start()
        copies.append(copy)

    def put(row, moved):
        for peer in range(plan.peers):
            stage[peer, row : row + plan.steps, :] = moved[peer * plan.steps : (peer + 1) * plan.steps]

    tails = []
    for k in range(plan.mom_dev):
        last = k == plan.mom_dev - 1
        for h in range(plan.pairs // TILE):
            rows = load(k, h)
            halves = jnp.concatenate([rows[:, :LANES], rows[:, SQUARE : SQUARE + LANES]], axis=1)
            tails += [rows[:, LANES:SQUARE], rows[:, SQUARE + LANES :]]
            moved = dot(swap, halves).astype(BF16)
            row = plan.main_row(k, h)
            put(row, moved[:, :LANES])
            put(row + plan.steps, moved[:, LANES:])
        if last:
            for n in range(0, len(tails), 2 * SLOTS):
                joined = jnp.concatenate(tails[n : n + 2 * SLOTS], axis=1)
                put(plan.main_rows + n // (2 * SLOTS) * plan.steps, dot(swap, joined).astype(BF16))
        send(plan.main_row(k, 0), plan.rows if last else plan.main_row(k + 1, 0))
    for copy in copies:
        copy.wait()


def pack_own_kernel(plan, green_ref, out_ref, stage, out_sems, green, sems):
    copies = [pltpu.make_async_copy(green_ref.at[k], green.at[k], sems.at[k]) for k in range(plan.mom_dev)]
    for copy in copies:
        copy.start()

    def load(k, h):
        if h == 0:
            copies[k].wait()
        return green[k, :, TILE * h : TILE * (h + 1), :].reshape(plan.steps * TILE, COMP)

    pack_rows(plan, load, out_ref, stage, out_sems)


def pack_partner_kernel(plan, take_ref, green_ref, out_ref, stage, sems, taken):
    chunk = take_ref.shape[0] // plan.pairs
    take = take_ref[...]
    for k in range(plan.mom_dev):
        for e in range(0, plan.steps, chunk):
            rows = green_ref[k, e : e + chunk].reshape(chunk * plan.pairs, COMP)
            taken[k, e : e + chunk] = dot(take, rows).astype(BF16).reshape(chunk, plan.pairs, COMP)

    def load(k, h):
        return taken[k, :, TILE * h : TILE * (h + 1), :].reshape(plan.steps * TILE, COMP)

    pack_rows(plan, load, out_ref, stage, sems, flip=True)


def each_pair(plan, body):
    if plan.own <= 2:
        for u in range(plan.own):
            body(u)
    else:
        lax.fori_loop(0, plan.own, lambda u, _: body(u), None)


def rows_at(row, count):
    return pl.ds(row if isinstance(row, int) else pl.multiple_of(row, count), count)


def my_table(plan, tables_ref, u):
    group = lax.axis_index("energy") // plan.group
    return tables_ref[(u // plan.sub ^ group) * plan.sub + u % plan.sub]


def sandwich_kernel(plan, tables_ref, sand_ref):
    place, want = iota((2 * LANES, 16), 0), iota((2 * LANES, 16), 1)

    def body(u):
        couple = my_table(plan, tables_ref, u)[: BRANCH * 16, :16]
        for h in range(2):
            comp = jnp.where(place < LANES, place, place - (u % SLOTS * TAIL + h * REST))
            valid = (place < LANES) | ((comp >= LANES) & (comp < SQUARE))
            quotient = (comp * 171) >> 11
            first = (valid & (quotient == want)).astype(F32).astype(BF16)
            second = (valid & (comp - ORB * quotient == want)).astype(F32).astype(BF16)
            left = dot_nt(couple, first).astype(BF16)
            right = dot_nt(couple, second).astype(BF16)
            left = jnp.concatenate([left[16 * i : 16 * i + 16] for i in range(BRANCH)], axis=1)
            right = jnp.concatenate([right[16 * i : 16 * i + 16] for i in range(BRANCH)], axis=1)
            sand_ref[u, h] = (dot(first, left) * dot(second, right)).astype(BF16)

    each_pair(plan, body)


def pace_kernel(plan, tables_ref, out_ref):
    out_ref[...] = tables_ref[...]


def toeplitz_kernel(plan, tables_ref, toep_ref):
    mirror = iota((FREQ, 2 * FREQ), 0) + iota((FREQ, 2 * FREQ), 1) == FREQ
    mirror = mirror.astype(F32).astype(BF16)

    def body(u):
        lags = dot(my_table(plan, tables_ref, u)[BRANCH * 16 :, :], mirror)
        for q in range(plan.momenta):
            for i in range(BRANCH):
                n = q * BRANCH + i
                band = jnp.broadcast_to(lags[n : n + 1], (FREQ, 2 * FREQ))
                band = pltpu.roll(band, 0, 1, stride=1, stride_axis=0)
                toep_ref[u, q, i * FREQ : (i + 1) * FREQ, :] = band.astype(BF16)

    each_pair(plan, body)


def gather_rows(plan, ref, u, y, first, flip=False):
    m, k = divmod(y, plan.mom_dev)
    row, tail = plan.main_row(k, u), plan.tail_row(k, u)
    order = range(plan.half)
    lefts, rights, tails = [], [], []
    for j in reversed(order) if flip else order:
        peer = (first + j) * plan.n_mom + m
        lefts.append(ref[peer, rows_at(row, plan.steps), :])
        rights.append(ref[peer, rows_at(row + plan.steps, plan.steps), :])
        tails.append(ref[peer, rows_at(tail, plan.steps), :])
    tails = jnp.concatenate(tails, axis=0)
    if plan.shift(k):
        tails = pltpu.roll(tails.astype(F32), LANES - plan.shift(k), 1).astype(BF16)
    return jnp.concatenate([jnp.concatenate(lefts, axis=0), jnp.concatenate(rights, axis=0), tails], axis=1)


def half_and_tail(rows, h):
    return jnp.concatenate([rows[:, h * LANES : (h + 1) * LANES], rows[:, 2 * LANES :]], axis=1)


def self_block(plan, u, green, toep_ref, sand_ref, out_ref):
    summed = []
    for i in range(BRANCH):
        rows = slice(i * FREQ, (i + 1) * FREQ)
        band = jnp.concatenate(
            [
                jnp.concatenate([toep_ref[u, (k - y) % plan.momenta, rows, :] for y in range(plan.momenta)], axis=1)
                for k in range(plan.momenta)
            ],
            axis=0,
        )
        summed.append(dot(band, green).astype(BF16))
    left, right = [
        dot_nt(jnp.concatenate([half_and_tail(rows, h) for rows in summed], axis=1), sand_ref[u, h])
        for h in range(2)
    ]
    tails = left[:, LANES:] + right[:, LANES:]
    left, right = left[:, :LANES].astype(BF16), right[:, :LANES].astype(BF16)
    for y in range(plan.momenta):
        m, k = divmod(y, plan.mom_dev)
        row, tail = plan.main_row(k, u), plan.tail_row(k, u)
        rest = tails[y * FREQ : (y + 1) * FREQ]
        if plan.shift(k):
            rest = pltpu.roll(rest, plan.shift(k), 1)
        rest = rest.astype(BF16)
        for j in range(plan.half):
            peer = j * plan.n_mom + m
            here = slice(j * plan.steps, (j + 1) * plan.steps)
            there = slice(y * FREQ + j * plan.steps, y * FREQ + (j + 1) * plan.steps)
            out_ref[peer, rows_at(row, plan.steps), :] = left[there]
            out_ref[peer, rows_at(row + plan.steps, plan.steps), :] = right[there]
            out_ref[peer, rows_at(tail, plan.steps), :] += rest[here]


def clear_tails(plan, out_ref):
    for peer in range(plan.half * plan.n_mom):
        out_ref[peer, plan.main_rows :, :] = jnp.zeros((plan.tail_rows, LANES), BF16)


def self_late_kernel(plan, own, toep_ref, sand_ref, out_ref):
    clear_tails(plan, out_ref)

    def body(u):
        green = [gather_rows(plan, own, u, y, first) for y in range(plan.momenta) for first in (0, plan.half)]
        self_block(plan, u, jnp.concatenate(green, axis=0), toep_ref, sand_ref, out_ref)

    each_pair(plan, body)


def self_early_kernel(plan, own, far, toep_ref, sand_ref, late_ref, out_ref, stage, halo, sems):
    has = (lax.axis_index("energy") // plan.group > 0).astype(F32).astype(BF16)
    near = plan.half * plan.n_mom
    load = pltpu.make_async_copy(far, halo, sems.at[0])
    load.start()
    upper = pltpu.make_async_copy(late_ref, out_ref.at[near:], sems.at[1])
    upper.start()
    clear_tails(plan, stage)
    load.wait()

    def body(u):
        green = []
        for y in range(plan.momenta):
            green.append(gather_rows(plan, halo, u, y, 0) * has)
            green.append(gather_rows(plan, own, u, y, 0))
        self_block(plan, u, jnp.concatenate(green, axis=0), toep_ref, sand_ref, stage)

    each_pair(plan, body)
    lower = pltpu.make_async_copy(stage, out_ref.at[:near], sems.at[2])
    lower.start()
    lower.wait()
    upper.wait()


def lag_sums(plan, u, partner, green, sand_ref, store):
    partner, green = jnp.concatenate(partner, axis=0), jnp.concatenate(green, axis=0)
    left, right = [dot(half_and_tail(partner, h), sand_ref[u, h]) for h in range(2)]
    for i in range(BRANCH):
        here = slice(2 * LANES * i, 2 * LANES * i + LANES)
        rest = slice(2 * LANES * i + LANES, 2 * LANES * (i + 1))
        applied = jnp.concatenate([left[:, here], right[:, here], left[:, rest] + right[:, rest]], axis=1)
        lagged = dot_nt(applied.astype(BF16), green)
        for q in range(plan.momenta):
            acc = None
            for k in range(plan.momenta):
                y = (k + q) % plan.momenta
                part = lagged[k * FREQ : (k + 1) * FREQ, y * 2 * FREQ : (y + 1) * 2 * FREQ]
                acc = part if acc is None else acc + part
            acc = pltpu.roll(acc, FREQ + 1, 1, stride=1, stride_axis=0)
            store(q, i, jnp.sum(acc, axis=0, keepdims=True))


def phonon_early_kernel(plan, own, partner_ref, sand_ref, out_ref):
    def body(u):
        partner = [gather_rows(plan, partner_ref, u, k, 0, flip=True) for k in range(plan.momenta)]
        green = [gather_rows(plan, own, u, y, first) for y in range(plan.momenta) for first in (0, plan.half)]

        def store(q, i, lags):
            out_ref[u, q * BRANCH + i : q * BRANCH + i + 1, :] = lags

        lag_sums(plan, u, partner, green, sand_ref, store)

    each_pair(plan, body)


def phonon_late_kernel(plan, own, halo, partner_ref, sand_ref, early_ref, *refs, scale):
    outs, sums = refs[:-1], refs[-1]
    group = lax.axis_index("energy") // plan.group
    me = lax.axis_index("mom")
    has = (group < plan.n_groups - 1).astype(F32).astype(BF16)

    def body(u):
        partner = [gather_rows(plan, partner_ref, u, k, plan.half, flip=True) for k in range(plan.momenta)]
        green = []
        for y in range(plan.momenta):
            green.append(gather_rows(plan, own, u, y, plan.half))
            green.append(gather_rows(plan, halo, u, y, 0) * has)

        def store(q, i, lags):
            n = q * BRANCH + i
            side, row = divmod(n, plan.mom_dev * BRANCH)
            sums[u, side, row : row + 1, :] = (lags + early_ref[u, n : n + 1, :]) * scale

        lag_sums(plan, u, partner, green, sand_ref, store)

    each_pair(plan, body)
    for d in range(plan.n_groups):
        for t in range(plan.n_mom):
            for b in range(plan.sub):
                outs[d * plan.n_mom + t][b] = sums[(group ^ d) * plan.sub + b, me ^ t]


def collect(plan, parts, out_ref):
    me = lax.axis_index("mom")
    totals = [sum(ref[...] for ref in parts[d :: plan.n_mom]) for d in range(plan.n_mom)]
    for q in range(plan.mom_dev):
        pairs = []
        for m in range(plan.n_mom):
            for b in range(plan.sub):
                lags = totals[0][b]
                for d in range(1, plan.n_mom):
                    lags = jnp.where(me ^ d == m, totals[d][b], lags)
                rows = [lags[q * BRANCH + i : q * BRANCH + i + 1, :FREQ] for i in range(BRANCH)]
                pairs.append(jnp.concatenate(rows, axis=1))
        out_ref[q] = jnp.concatenate(pairs, axis=0)


def unpack_kernel(plan, wire, *refs):
    *parts, out_ref, lags_hbm, green, lags, sems, lag_sem = refs
    swap = swap_matrix(TILE, plan.steps)

    def rows_of(row):
        return jnp.concatenate([wire[peer, row : row + plan.steps, :] for peer in range(plan.peers)], axis=0)

    tails = {}
    for first in range(0, plan.mom_dev * plan.own, SLOTS):
        moved = dot(swap, rows_of(plan.main_rows + first // SLOTS * plan.steps))
        for t in range(SLOTS):
            tails[first + t] = moved[:, t * TAIL : (t + 1) * TAIL]
    copies = []
    for k in range(plan.mom_dev):
        for h in range(plan.pairs // TILE):
            row = plan.main_row(k, h)
            moved = dot(swap, jnp.concatenate([rows_of(row), rows_of(row + plan.steps)], axis=1))
            tail = tails[k * plan.own + h]
            moved = jnp.concatenate([moved[:, :LANES], tail[:, :REST], moved[:, LANES:], tail[:, REST:]], axis=1)
            moved = moved.astype(BF16).reshape(plan.steps, TILE, COMP)
            green[k, :, TILE * h : TILE * (h + 1), :] = moved
        copies.append(pltpu.make_async_copy(green.at[k], out_ref.at[k], sems.at[k]))
        copies[-1].start()
    collect(plan, parts, lags)
    lag_copy = pltpu.make_async_copy(lags, lags_hbm, lag_sem)
    lag_copy.start()
    for copy in copies:
        copy.wait()
    lag_copy.wait()


ANY = pl.BlockSpec(memory_space=pl.ANY)
HBM = pl.BlockSpec(memory_space=pltpu.HBM)
VMEM = pl.BlockSpec(memory_space=pltpu.VMEM)


def call(plan, kernel, out_shape, *args, in_specs=None, out_specs=None, scratch=(), flops=1, grant=None):
    outs = jax.tree.map(lambda _: VMEM, out_shape)
    return pl.pallas_call(
        functools.partial(kernel, plan),
        out_shape=out_shape,
        in_specs=in_specs or [VMEM] * len(args),
        out_specs=out_specs or outs,
        scratch_shapes=list(scratch),
        compiler_params=pltpu.CompilerParams(vmem_limit_bytes=grant or SMALL_GRANT * max(1, plan.own // 4)),
        cost_estimate=pl.CostEstimate(flops=flops, bytes_accessed=1, transcendentals=0),
    )(*args)


def shape(dims, dtype):
    return jax.ShapeDtypeStruct(dims, dtype)


def in_hbm(struct):
    return pltpu.HBM(struct.shape, struct.dtype)


def shards(lesser_green, partner, phonon_green, coupling):
    n_energy, n_mom = lax.axis_size("energy"), lax.axis_size("mom")
    plan = Plan(lesser_green, phonon_green, n_energy, n_mom)
    axes = ("energy", "mom")
    me = lax.axis_index("mom")
    s = lax.axis_index("energy") // plan.group
    wire = shape((plan.peers, plan.rows, LANES), BF16)
    half_peers = plan.half * n_mom
    groups = [[g * plan.peers + i for i in range(plan.peers)] for g in range(plan.n_groups)]

    def exchange(blocks):
        return lax.all_to_all(blocks, axes, split_axis=0, concat_axis=0, axis_index_groups=groups, tiled=True)

    def swap_groups(values, other):
        route = []
        for e in range(n_energy):
            g, j = divmod(e, plan.group)
            to = other(g) if 0 <= other(g) < plan.n_groups else g
            route.append((e, to * plan.group + j))
        return lax.ppermute(values, "energy", route)

    staging = [pltpu.VMEM(wire.shape, BF16), pltpu.SemaphoreType.DMA((plan.mom_dev,))]
    half_wire = shape((half_peers, plan.rows, LANES), BF16)
    own = exchange(
        call(
            plan,
            pack_own_kernel,
            in_hbm(wire),
            lesser_green,
            in_specs=[HBM],
            out_specs=HBM,
            scratch=staging + [pltpu.VMEM(lesser_green.shape, BF16), pltpu.SemaphoreType.DMA((plan.mom_dev,))],
            grant=LARGE_GRANT,
        )
    )

    lag_count = plan.momenta * BRANCH
    lag_rows = -(-lag_count // 16) * 16
    couple = coupling.reshape(plan.pairs_dev, BRANCH, ORB, ORB)
    couple = jnp.pad(couple, ((0, 0), (0, 0), (0, 16 - ORB), (0, FREQ - ORB)))
    phonon = phonon_green.reshape(plan.momenta, plan.pairs_dev, BRANCH, FREQ)
    phonon = jnp.moveaxis(phonon, 1, 0).reshape(plan.pairs_dev, lag_count, FREQ)
    phonon = jnp.pad(phonon, ((0, 0), (0, lag_rows - lag_count), (0, 0)))
    table = jnp.concatenate([couple.reshape(plan.pairs_dev, BRANCH * 16, FREQ), phonon], axis=1)
    table = lax.dynamic_slice_in_dim(table, me * plan.sub, plan.sub, axis=0)
    tables = [table]
    for d in range(1, plan.n_groups):
        tables.append(swap_groups(table, functools.partial(lambda d, g: g ^ d, d)))
    tables = jnp.concatenate(tables, axis=0)
    sand = call(
        plan, sandwich_kernel, shape((plan.own, 2, 2 * LANES, BRANCH * 2 * LANES), BF16), tables
    )
    chunk = max(1, 256 // plan.pairs)
    source = (jnp.arange(chunk)[:, None] * plan.pairs + partner[None, :]).reshape(-1)
    take = (source[:, None] == jnp.arange(chunk * plan.pairs)[None, :]).astype(BF16)
    partner_wire = call(
        plan,
        pack_partner_kernel,
        in_hbm(wire),
        take,
        lesser_green,
        out_specs=HBM,
        scratch=staging + [pltpu.VMEM(lesser_green.shape, BF16)],
    )
    own, tables, sand, partner_wire = lax.optimization_barrier((own, tables, sand, partner_wire))

    odd = s % 2

    def edge(side):
        return lax.dynamic_slice_in_dim(own, side * half_peers, half_peers, axis=0)

    before = after = inner = swap_groups(edge(1 - odd), lambda g: g ^ 1)
    if plan.n_groups > 2:
        outer = swap_groups(edge(odd), lambda g: ((g - 1) ^ 1) + 1)
        before = jnp.where(odd == 1, inner, outer)
        after = jnp.where(odd == 1, outer, inner)

    paced = call(plan, pace_kernel, shape(tables.shape, BF16), tables, flops=LONG)
    paced, partner_wire = lax.optimization_barrier((paced, partner_wire))
    partner_blocks = exchange(partner_wire)
    toep = call(
        plan,
        toeplitz_kernel,
        shape((plan.own, plan.momenta, BRANCH * FREQ, 2 * FREQ), BF16),
        tables,
    )

    late = call(plan, self_late_kernel, half_wire, own, toep, sand)
    sigma = call(
        plan,
        self_early_kernel,
        in_hbm(wire),
        own,
        before,
        toep,
        sand,
        late,
        in_specs=[VMEM, ANY, VMEM, VMEM, VMEM],
        out_specs=HBM,
        scratch=[
            pltpu.VMEM(half_wire.shape, BF16),
            pltpu.VMEM(half_wire.shape, BF16),
            pltpu.SemaphoreType.DMA((3,)),
        ],
        flops=LONG,
    )
    arrived = exchange(sigma)

    scale = (plan.momenta * n_energy * plan.steps * COMP) ** -0.5
    early = call(
        plan,
        phonon_early_kernel,
        shape((plan.own, lag_count, LANES), F32),
        own,
        partner_blocks,
        sand,
    )
    side_rows = plan.mom_dev * BRANCH
    parts = list(call(
        plan,
        functools.partial(phonon_late_kernel, scale=scale),
        [shape((plan.sub, side_rows, LANES), F32)] * (plan.n_groups * n_mom),
        own,
        after,
        partner_blocks,
        sand,
        early,
        scratch=[pltpu.VMEM((plan.own, n_mom, side_rows, LANES), F32)],
    ))
    for d in range(plan.n_groups):
        for t in range(n_mom):
            if d or t:
                route = []
                for e in range(n_energy):
                    g, j = divmod(e, plan.group)
                    for m in range(n_mom):
                        route.append((e * n_mom + m, ((g ^ d) * plan.group + j) * n_mom + (m ^ t)))
                parts[d * n_mom + t] = lax.ppermute(parts[d * n_mom + t], axes, route)
    return call(
        plan,
        unpack_kernel,
        [
            shape(lesser_green.shape, BF16),
            shape((plan.mom_dev, plan.pairs_dev, BRANCH * FREQ), F32),
        ],
        arrived,
        *parts,
        out_specs=[ANY, ANY],
        scratch=[
            pltpu.VMEM(lesser_green.shape, BF16),
            pltpu.VMEM((plan.mom_dev, plan.pairs_dev, BRANCH * FREQ), F32),
            pltpu.SemaphoreType.DMA((plan.mom_dev,)),
            pltpu.SemaphoreType.DMA,
        ],
    )


def solution(mesh):
    in_specs = (P("mom", "energy", None, None), P(), P(None, "energy", None), P("energy", None))
    out_specs = (P("mom", "energy", None, None), P("mom", "energy", None))
    return jax.shard_map(shards, mesh=mesh, in_specs=in_specs, out_specs=out_specs, check_vma=False)
```
